128 devices in a mesh: win: 32 (over z, y, core), mlp: 4 (over x).
Axes of the slice: x: 4, y: 4, z: 4, core: 2. Of those that a mesh axis runs over, the one named last changes fastest.
Arguments:
- tokens_in: bfloat16 [150528, 384], P(('win', 'mlp')), may hold values from -6 to 6
- out_grad: bfloat16 [150528, 384], P(('win', 'mlp')), may hold values from -6 to 6
- window_live: int32 [3072], P(('win', 'mlp')), may hold values from 0 to 1, as said below
- region_ids: int32 [150528], P(('win', 'mlp')), may hold values from 0 to 4, as said below
- qkv_weight: float32 [384, 1152], replicated, may hold values from -0.3125 to 0.3125
- proj_weight: float32 [384, 384], replicated, may hold values from -0.875 to 0.875
- rel_table: float32 [169, 12], replicated, may hold values from -4 to 4
- small_params: float32 [3072], replicated, may hold values from -0.9 to 1.75
- fc1_weight: float32 [384, 1536], P(None, 'mlp'), may hold values from -0.3125 to 0.3125
- fc1_bias: float32 [1536], P('mlp'), may hold values from -1.2 to 1.2
- fc2_weight: float32 [1536, 384], P('mlp'), may hold values from -0.15625 to 0.15625
- qkv_row: float32 [384], replicated, as said below
- qkv_col: float32 [1152], replicated, as said below
- proj_row: float32 [384], replicated, as said below
- proj_col: float32 [384], replicated, as said below
- fc1_row: float32 [384], replicated, as said below
- fc1_col: float32 [1536], P('mlp'), as said below
- fc2_row: float32 [1536], P('mlp'), as said below
- fc2_col: float32 [384], replicated, as said below
- fc1_bias_state: float32 [1536], P('mlp'), as said below
- small_state: float32 [3072], replicated, as said below
- table_state: float32 [169, 12], replicated, as said below
Outputs:
- block_out: float32 [150528, 384], P(('win', 'mlp'))
- input_grad: float32 [150528, 384], P(('win', 'mlp'))
- qkv_grad: float32 [384, 1152], P(('win', 'mlp'))
- qkv_row_new: float32 [384], P(('win', 'mlp'))
- qkv_col_new: float32 [1152], replicated
- qkv_new: float32 [384, 1152], P(('win', 'mlp'))
- qkv_new_low: bfloat16 [384, 1152], P(('win', 'mlp'))
- proj_grad: float32 [384, 384], P(('win', 'mlp'))
- proj_row_new: float32 [384], P(('win', 'mlp'))
- proj_col_new: float32 [384], replicated
- proj_new: float32 [384, 384], P(('win', 'mlp'))
- proj_new_low: bfloat16 [384, 384], P(('win', 'mlp'))
- fc1_grad: float32 [384, 1536], P(None, 'mlp')
- fc1_row_new: float32 [384], replicated
- fc1_col_new: float32 [1536], P('mlp')
- fc1_new: float32 [384, 1536], P(None, 'mlp')
- fc1_new_low: bfloat16 [384, 1536], P(None, 'mlp')
- fc2_grad: float32 [1536, 384], P('mlp')
- fc2_row_new: float32 [1536], P('mlp')
- fc2_col_new: float32 [384], replicated
- fc2_new: float32 [1536, 384], P('mlp')
- fc2_new_low: bfloat16 [1536, 384], P('mlp')
- fc1_bias_grad: float32 [1536], P('mlp')
- fc1_bias_state_new: float32 [1536], P('mlp')
- fc1_bias_new: float32 [1536], P('mlp')
- small_grad: float32 [3072], replicated
- small_state_new: float32 [3072], replicated
- small_new: float32 [3072], replicated
- table_grad: float32 [169, 12], replicated
- table_state_new: float32 [169, 12], replicated
- table_new: float32 [169, 12], replicated
The draws below stay inside these ranges and needn't reach their ends.
Inputs may be any that keep to these rules, and one draw needn't show every extreme that they name: `window_live`: on each device's 24 window slots the live ones come first; at least half of each device's slots are live, and in every draw some device has all 24 live. `region_ids`: ids split a window at row and at column 4. `qkv_row`: Positive. `qkv_col`: Positive. `proj_row`: Positive. `proj_col`: Positive. `fc1_row`: Positive. `fc1_col`: Positive. `fc2_row`: Positive. `fc2_col`: Positive. `fc1_bias_state`: Positive. `small_state`: Positive. `table_state`: Positive.
All inputs are finite; a program needn't handle non-finite values.
Results may differ from the reference program's by a relative error of at most 0.0095.
The reference program's roundings to bfloat16 on the way count: a program that leaves them out, or rounds other values in their place, can miss the bound.
Values may be sent and summed in bfloat16 or wider, within the bound.
A program may use at most 128 MiB of HBM per device.

```python
import math
import jax
import jax.numpy as jnp
from jax import lax

D = 384
HEADS = 12
FF = 1536
HEAD_DIM = 32
WIN = 7
SHIFT = 3
STEP = 10
W_DEV = 24
WIN_TOKENS = 49
RELS = 169
WINDOWS = 3072
TOKENS = 150528


def ramped_stats(key, count, base, trend):
    ramp = jnp.arange(count, dtype=jnp.float32) / count
    factor = jnp.exp(jax.random.uniform(key, (count,), jnp.float32, math.log(0.5), math.log(2.0)))
    return base * factor * jnp.power(trend, -ramp)


def draw_window_live(key, part):
    key = jax.random.fold_in(key, 21)
    devices = WINDOWS // W_DEV
    count_key, full_key = jax.random.split(key)
    counts = jax.random.randint(count_key, (devices,), (W_DEV + 1) // 2, W_DEV + 1)
    fullest = jax.random.randint(full_key, (), 0, devices)
    counts = jnp.where(jnp.arange(devices) == fullest, W_DEV, counts)
    slots = jnp.arange(W_DEV)
    return (slots[None, :] < counts[:, None]).astype(jnp.int32).reshape(WINDOWS)


def draw_region_ids(key, part):
    key = jax.random.fold_in(key, 22)
    kinds = jax.random.randint(key, (WINDOWS,), 0, 4)
    kinds = kinds.at[0].set(3)
    position = jnp.arange(WIN_TOKENS)
    lower = (position // WIN >= WIN - SHIFT).astype(jnp.int32)
    right = (position % WIN >= WIN - SHIFT).astype(jnp.int32)
    row_part = jnp.where(kinds[:, None] >= 2, lower[None, :], 0)
    col_part = jnp.where(kinds[:, None] % 2 == 1, right[None, :], 0)
    return (3 * row_part + col_part).astype(jnp.int32).reshape(TOKENS)


def draw_small_params(key, part):
    key = jax.random.fold_in(key, 23)
    noise = jnp.clip(jax.random.normal(key, (8 * D,), jnp.float32), -3.0, 3.0)
    segment = jnp.arange(8 * D) // D
    gain_like = (segment == 0) | (segment == 5)
    return jnp.where(gain_like, 1.0 + 0.25 * noise, 0.3 * noise)


def draw_qkv_row(key, part):
    key = jax.random.fold_in(key, 31)
    trend = 3.0
    return ramped_stats(key, D, 0.07 * TOKENS, trend)


def draw_qkv_col(key, part):
    key = jax.random.fold_in(key, 32)
    trend = 3.0
    return ramped_stats(key, 3 * D, 0.07 * TOKENS, trend)


def draw_proj_row(key, part):
    key = jax.random.fold_in(key, 33)
    trend = 3.0
    return ramped_stats(key, D, 0.14 * TOKENS, trend)


def draw_proj_col(key, part):
    key = jax.random.fold_in(key, 34)
    trend = 3.0
    return ramped_stats(key, D, 0.14 * TOKENS, trend)


def draw_fc1_row(key, part):
    key = jax.random.fold_in(key, 35)
    trend = 3.0
    return ramped_stats(key, D, 0.11 * TOKENS, trend)


def draw_fc1_col(key, part):
    key = jax.random.fold_in(key, 36)
    trend = 3.0
    return ramped_stats(key, FF, 0.11 * TOKENS, trend)


def draw_fc2_row(key, part):
    key = jax.random.fold_in(key, 37)
    trend = 3.0
    return ramped_stats(key, FF, 0.1 * TOKENS, trend)


def draw_fc2_col(key, part):
    key = jax.random.fold_in(key, 38)
    trend = 3.0
    return ramped_stats(key, D, 0.1 * TOKENS, trend)


def draw_fc1_bias_state(key, part):
    key = jax.random.fold_in(key, 39)
    trend = 3.0
    return ramped_stats(key, FF, 0.1 * TOKENS, trend)


def draw_small_state(key, part):
    key = jax.random.fold_in(key, 40)
    trend = 3.0
    return ramped_stats(key, 8 * D, 0.1 * TOKENS, trend)


def draw_table_state(key, part):
    key = jax.random.fold_in(key, 41)
    trend = 3.0
    return ramped_stats(key, RELS * HEADS, 0.0002 * TOKENS, trend).reshape(RELS, HEADS)


def shard_levels(own_key, dims, cuts, smallest, top_value):
    loudness, own = 1.0, jax.random.fold_in(own_key, 6)
    for dim, blocks in cuts:
        draws = jnp.exp(jax.random.uniform(jax.random.fold_in(own, dim), (blocks,), jnp.float32, smallest / len(cuts), top_value / len(cuts)))
        loudness = loudness * jnp.repeat(draws, dims[dim] // blocks).reshape([-1 if axis == dim else 1 for axis in range(len(dims))])
    return loudness


def centred(rng, shape, width, reach, pieces=(), held_as=jnp.bfloat16):
    values = width * jax.random.normal(rng, shape, jnp.float32)
    if pieces:
        values = values * shard_levels(rng, shape, pieces, -0.22, 0.18)
    return jnp.clip(values, -reach, reach).astype(held_as)


def setup_inputs(seed: int = 0) -> dict:
    arg_keys = jax.random.split(jax.random.key(seed), 23)
    tokens_in = centred(arg_keys[0], (TOKENS, D), 1.0, 6.0, ((0, 128),))
    out_grad = centred(arg_keys[1], (TOKENS, D), 1.0, 6.0, ((0, 128),))
    window_live = draw_window_live(jax.random.fold_in(arg_keys[22], 71), 0)
    region_ids = draw_region_ids(jax.random.fold_in(arg_keys[22], 71), 0)
    qkv_weight = centred(arg_keys[4], (D, 3 * D), D ** -0.5, 0.3125, (), jnp.float32)
    proj_weight = centred(arg_keys[5], (D, D), (D // 8) ** -0.5, 0.875, (), jnp.float32)
    rel_table = centred(arg_keys[6], (RELS, HEADS), 1.0, 4.0, (), jnp.float32)
    small_params = draw_small_params(jax.random.fold_in(arg_keys[22], 71), 0)
    fc1_weight = centred(arg_keys[8], (D, FF), D ** -0.5, 0.3125, ((1, 4),), jnp.float32)
    fc1_bias = centred(arg_keys[9], (FF,), 0.3, 1.2, ((0, 4),), jnp.float32)
    fc2_weight = centred(arg_keys[10], (FF, D), FF ** -0.5, 0.15625, ((0, 4),), jnp.float32)
    qkv_row = draw_qkv_row(jax.random.fold_in(arg_keys[22], 71), 0)
    qkv_col = draw_qkv_col(jax.random.fold_in(arg_keys[22], 71), 0)
    proj_row = draw_proj_row(jax.random.fold_in(arg_keys[22], 71), 0)
    proj_col = draw_proj_col(jax.random.fold_in(arg_keys[22], 71), 0)
    fc1_row = draw_fc1_row(jax.random.fold_in(arg_keys[22], 71), 0)
    fc1_col = draw_fc1_col(jax.random.fold_in(arg_keys[22], 71), 0)
    fc2_row = draw_fc2_row(jax.random.fold_in(arg_keys[22], 71), 0)
    fc2_col = draw_fc2_col(jax.random.fold_in(arg_keys[22], 71), 0)
    fc1_bias_state = draw_fc1_bias_state(jax.random.fold_in(arg_keys[22], 71), 0)
    small_state = draw_small_state(jax.random.fold_in(arg_keys[22], 71), 0)
    table_state = draw_table_state(jax.random.fold_in(arg_keys[22], 71), 0)
    return {"tokens_in": tokens_in, "out_grad": out_grad, "window_live": window_live, "region_ids": region_ids, "qkv_weight": qkv_weight, "proj_weight": proj_weight, "rel_table": rel_table, "small_params": small_params, "fc1_weight": fc1_weight, "fc1_bias": fc1_bias, "fc2_weight": fc2_weight, "qkv_row": qkv_row, "qkv_col": qkv_col, "proj_row": proj_row, "proj_col": proj_col, "fc1_row": fc1_row, "fc1_col": fc1_col, "fc2_row": fc2_row, "fc2_col": fc2_col, "fc1_bias_state": fc1_bias_state, "small_state": small_state, "table_state": table_state}


EPS_NORM = 1e-05
EPS_SQ = 1e-30
MASK_FILL = -100.0
CLIP = 1.0
VEC_RATE = 0.3
HIGHEST_PRECISION = lax.Precision.HIGHEST

@jax.custom_vjp
def low(v):
    return lax.optimization_barrier(v.astype(jnp.bfloat16)).astype(jnp.float32)

@jax.custom_vjp
def low_back(v):
    return v

def low_keep(v):
    return (low(v), None)

def low_pass(kept, grad):
    return (grad,)

def back_keep(v):
    return (v, None)

def back_low(kept, grad):
    return (low(grad),)
low.defvjp(low_keep, low_pass)
low_back.defvjp(back_keep, back_low)

def layer_norm(values, gain, shift):
    center = values - lax.optimization_barrier(jnp.mean(values, axis=-1, keepdims=True))
    inverse = lax.rsqrt(lax.optimization_barrier(jnp.mean(center * center, axis=-1, keepdims=True)) + EPS_NORM)
    return center * inverse * gain + shift

def relative_index():
    position = jnp.arange(WIN_TOKENS, dtype=jnp.int32)
    row_of = position // WIN
    col_of = position % WIN
    return (row_of[:, None] - row_of[None, :] + WIN - 1) * (2 * WIN - 1) + col_of[:, None] - col_of[None, :] + WIN - 1

def block_rows(inputs, weights):
    tokens, live, regions = inputs
    qkv_matrix, proj_matrix, table, small, up_matrix, up_shift, down_matrix = weights
    rows = tokens.shape[0]
    windows = rows // WIN_TOKENS
    parts = small.reshape(8, D)
    first = low(layer_norm(tokens, parts[0], parts[1]))
    bias_three = jnp.concatenate([parts[2], jnp.zeros((D,), tokens.dtype), parts[3]])
    projected = jnp.dot(first, low(qkv_matrix), precision=HIGHEST_PRECISION) + bias_three
    projected = low(low_back(projected)).reshape(windows, WIN_TOKENS, 3, HEADS, HEAD_DIM)
    query = projected[:, :, 0]
    keys = projected[:, :, 1]
    values = projected[:, :, 2]
    rel_bias = jnp.transpose(table[relative_index()], (2, 0, 1))
    region_rows = regions.reshape(windows, WIN_TOKENS)
    shift_mask = jnp.where(region_rows[:, :, None] != region_rows[:, None, :], MASK_FILL, 0.0)
    scores = jnp.einsum('wihd,wjhd->whij', query, keys, precision=HIGHEST_PRECISION) * HEAD_DIM ** (-0.5)
    scores = low_back(scores + rel_bias[None] + shift_mask[:, None])
    probs = low(jax.nn.softmax(scores, axis=-1))
    attended = jnp.einsum('whij,wjhd->wihd', probs, values, precision=HIGHEST_PRECISION).reshape(rows, D)
    attended = low(low_back(attended))
    branch = low_back(jnp.dot(attended, low(proj_matrix), precision=HIGHEST_PRECISION) + parts[4])
    middle = tokens + branch
    second = low(layer_norm(middle, parts[5], parts[6]))
    inner = low_back(jnp.dot(second, low(up_matrix), precision=HIGHEST_PRECISION) + up_shift)
    hidden = low(jax.nn.gelu(inner, approximate=False))
    mixed = low_back(jnp.dot(hidden, low(down_matrix), precision=HIGHEST_PRECISION) + parts[7])
    return (middle + mixed) * live[:, None]

def adafactor_matrix(grad, row, col, weight, rate, decay):
    squares = grad * grad + EPS_SQ
    row_new = decay * row + (1.0 - decay) * lax.optimization_barrier(jnp.mean(squares, axis=1))
    col_new = decay * col + (1.0 - decay) * lax.optimization_barrier(jnp.mean(squares, axis=0))
    step = grad * lax.rsqrt(row_new[:, None] * col_new[None, :] / jnp.mean(row_new))
    step = step / jnp.maximum(1.0, jnp.sqrt(jnp.mean(step * step)) / CLIP)
    return (row_new, col_new, weight - rate * step)

def adafactor_vector(grad, state, weight, decay):
    state_new = decay * state + (1.0 - decay) * (grad * grad + EPS_SQ)
    step = grad * lax.rsqrt(state_new)
    step = step / jnp.maximum(1.0, jnp.sqrt(jnp.mean(step * step)) / CLIP)
    return (state_new, weight - VEC_RATE * step)

def reference(tokens_in, out_grad, window_live, region_ids, qkv_weight, proj_weight, rel_table, small_params, fc1_weight, fc1_bias, fc2_weight, qkv_row, qkv_col, proj_row, proj_col, fc1_row, fc1_col, fc2_row, fc2_col, fc1_bias_state, small_state, table_state):
    group_count = WINDOWS // 32
    group_rows = TOKENS // group_count
    live_rows = jnp.repeat(window_live.astype(jnp.float32), WIN_TOKENS).reshape(group_count, group_rows)
    regions = region_ids.reshape(group_count, group_rows)

    def forward(tokens, qkv_matrix, proj_matrix, table, small, up_matrix, up_shift, down_matrix):
        weights = (qkv_matrix, proj_matrix, table, small, up_matrix, up_shift, down_matrix)

        def group_step(inputs):
            return block_rows(inputs, weights)
        outputs = lax.map(jax.checkpoint(group_step), (tokens.reshape(group_count, group_rows, D), live_rows, regions))
        return outputs.reshape(TOKENS, D)
    block_out, pull = jax.vjp(forward, tokens_in.astype(jnp.float32), qkv_weight, proj_weight, rel_table, small_params, fc1_weight, fc1_bias, fc2_weight)
    input_grad, qkv_grad, proj_grad, table_grad, small_grad, fc1_grad, fc1_bias_grad, fc2_grad = pull(out_grad.astype(jnp.float32))
    decay = 1.0 - STEP ** (-0.8)
    qkv_row_new, qkv_col_new, qkv_new = adafactor_matrix(qkv_grad, qkv_row, qkv_col, qkv_weight, D ** (-0.5), decay)
    proj_row_new, proj_col_new, proj_new = adafactor_matrix(proj_grad, proj_row, proj_col, proj_weight, (D // 8) ** (-0.5), decay)
    fc1_row_new, fc1_col_new, fc1_new = adafactor_matrix(fc1_grad, fc1_row, fc1_col, fc1_weight, D ** (-0.5), decay)
    fc2_row_new, fc2_col_new, fc2_new = adafactor_matrix(fc2_grad, fc2_row, fc2_col, fc2_weight, FF ** (-0.5), decay)
    fc1_bias_state_new, fc1_bias_new = adafactor_vector(fc1_bias_grad, fc1_bias_state, fc1_bias, decay)
    small_state_new, small_new = adafactor_vector(small_grad, small_state, small_params, decay)
    table_state_new, table_new = adafactor_vector(table_grad, table_state, rel_table, decay)
    return (block_out, input_grad, qkv_grad, qkv_row_new, qkv_col_new, qkv_new, qkv_new.astype(jnp.bfloat16), proj_grad, proj_row_new, proj_col_new, proj_new, proj_new.astype(jnp.bfloat16), fc1_grad, fc1_row_new, fc1_col_new, fc1_new, fc1_new.astype(jnp.bfloat16), fc2_grad, fc2_row_new, fc2_col_new, fc2_new, fc2_new.astype(jnp.bfloat16), fc1_bias_grad, fc1_bias_state_new, fc1_bias_new, small_grad, small_state_new, small_new, table_grad, table_state_new, table_new)
```

```python
import functools
import math

import jax
import jax.numpy as jnp
from jax import lax
from jax.experimental import pallas as pl
from jax.experimental.pallas import tpu as pltpu
from jax.sharding import PartitionSpec as P

D = 384
FF = 1536
QKV = 3 * D
HEADS = 12
WIN = 7
SPAN = WIN * WIN
STEP = 10
DECAY = 1.0 - STEP ** (-0.8)
EPS_NORM = 1e-05
EPS_SQ = 1e-30
VEC_RATE = 0.3
SCALE = 32 ** (-0.5)
FAR = -1e30

GROUPS = 3
PER = 8
G_TOK = PER * SPAN
G_ROWS = 400
ROWS = GROUPS * G_ROWS
TOK = GROUPS * G_TOK
CHUNK = 64
KEYS = 56
SETS = 3
LANES = 4 * CHUNK

F32 = jnp.float32
BF16 = jnp.bfloat16


def dot(a, b):
    return jnp.dot(a, b, preferred_element_type=F32)


def dot_nt(a, b):
    return lax.dot_general(a, b, (((1,), (1,)), ((), ())), preferred_element_type=F32)


def dot_tn(a, b):
    return lax.dot_general(a, b, (((0,), (0,)), ((), ())), preferred_element_type=F32)


def dot_exact(a, b):
    return jnp.dot(a, b, precision=lax.Precision.HIGHEST, preferred_element_type=F32)


def iota(shape, dim):
    return lax.broadcasted_iota(jnp.int32, shape, dim)


def fold_rows(x):
    total = x[0:8]
    for i in range(1, x.shape[0] // 8):
        total = total + x[8 * i : 8 * i + 8]
    return total


def row_mean(x):
    return jnp.sum(x, axis=1, keepdims=True) * (1.0 / D)


def normalize(x):
    center = x - row_mean(x)
    inverse = lax.rsqrt(row_mean(center * center) + EPS_NORM)
    return center * inverse, inverse


def normalize_back(u, gain, scaled, inverse):
    weighted = u * gain
    return inverse * (weighted - row_mean(weighted) - scaled * row_mean(weighted * scaled))


def gelu_parts(v):
    e = jnp.exp(-0.5 * v * v)
    t = 1.0 / (1.0 + (0.3275911 * 0.5**0.5) * jnp.abs(v))
    poly = 1.061405429 * t - 1.453152027
    poly = poly * t + 1.421413741
    poly = poly * t - 0.284496736
    poly = poly * t + 0.254829592
    tail = (0.5 * e) * (poly * t)
    phi = jnp.where(v < 0.0, tail, 1.0 - tail)
    return v * phi, phi + v * e * (2.0 * math.pi) ** (-0.5)


def barrel(x, amount, right):
    width = x.shape[1]
    for k in range(7):
        step = 1 << k
        moved = pltpu.roll(x, step if right else width - step, 1)
        x = jnp.where((amount & step) != 0, moved, x)
    return x


def embed(i):
    return 13 * (i // WIN) + i % WIN


def chunk_start(w):
    return pl.multiple_of((w // PER) * G_ROWS + (w % PER) * 48, 16)


def prologue(region, table, x_ref, emask, bias, mask, tok):
    for a in range(GROUPS):
        for r in range(0, G_TOK, 56):
            src = a * G_TOK + r
            low = src // 16 * 16
            x_ref[a * G_ROWS + r : a * G_ROWS + r + 56, :] = (
                tok[low : low + 64 if low + 64 <= TOK else TOK, :].astype(F32)[src - low : src - low + 56]
            )
        x_ref[a * G_ROWS + G_TOK : (a + 1) * G_ROWS, :] = jnp.zeros((G_ROWS - G_TOK, D), F32)
    row = iota((LANES, 128), 0)
    lane = iota((LANES, 128), 1)
    for b in range(PER):
        i = row % CHUNK
        keep = (i >= b) & (i < b + SPAN) & (lane // 32 == row // CHUNK)
        emask[b] = jnp.where(keep, 1.0, 0.0).astype(BF16)
    j = iota((KEYS, 256), 0)
    amount = jnp.maximum(84 - embed(j), 0)
    jl = iota((KEYS, LANES), 0)
    il = iota((KEYS, LANES), 1) % CHUNK
    for g in range(SETS):
        base = jnp.zeros((KEYS, LANES), F32)
        for h in range(4):
            wide = jnp.broadcast_to(table[4 * g + h : 4 * g + h + 1, :], (KEYS, 256))
            wide = barrel(wide, amount, False)[:, :128]
            lane_to = iota((128, LANES), 1) - CHUNK * h
            pick = (iota((128, LANES), 0) == embed(lane_to)) & (lane_to >= 0) & (lane_to < SPAN)
            base = base + dot_exact(wide, jnp.where(pick, 1.0, 0.0))
        for b in range(PER):
            moved = pltpu.roll(pltpu.roll(base, b, 0), b, 1) if b else base
            key_ok = (jl >= b) & (jl < b + SPAN)
            query_ok = (il >= b) & (il < b + SPAN)
            bias[b, g] = jnp.where(key_ok, jnp.where(query_ok, moved, 0.0), FAR)
    eye = iota((CHUNK, CHUNK), 0) == iota((CHUNK, CHUNK), 1)
    for w in range(GROUPS * PER):
        start = (w // PER) * G_TOK + (w % PER) * 48
        line = region[:, start : start + CHUNK]
        column = jnp.sum(jnp.where(eye, jnp.broadcast_to(line, (CHUNK, CHUNK)), 0.0), axis=1, keepdims=True)
        wide = jnp.concatenate([line] * 4, axis=1)
        mask[w] = jnp.where(column[:KEYS] != wide, -100.0, 0.0)


def pad_keys(x):
    return jnp.concatenate([x, jnp.zeros((CHUNK - KEYS, x.shape[1]), x.dtype)], axis=0)


def spread(x, keep):
    return jnp.concatenate([x] * 4, axis=0) * keep


def collect(full):
    head = iota((CHUNK, 128), 1) // 32
    parts = [full[CHUNK * h : CHUNK * (h + 1)] for h in range(4)]
    low = jnp.where(head == 0, parts[0], parts[1])
    high = jnp.where(head == 2, parts[2], parts[3])
    return jnp.where(head < 2, low, high)


def block_kernel(
    live_tokens, tok, og, region, wq, wp, table, small, w1, b1, w2,
    out, gin, qkv_g, proj_g, fc1_g, fc2_g, small_g, b1_g, table_g,
    x_ref, xh1, inv1, xh2, inv2, n1, n2, qkv, att, att_b, probs, back, hidden, ig, dqkv, dqkv_b,
    emask, bias, mask, tacc, s1, s2, sums, b1_acc, wq_b, wp_b,
):
    prologue(region, table, x_ref, emask, bias, mask, tok)
    live = live_tokens[0]
    wq_b[...] = wq[...].astype(BF16)
    wp_b[...] = wp[...].astype(BF16)
    sums[...] = jnp.zeros_like(sums)
    b1_acc[...] = jnp.zeros_like(b1_acc)
    tacc[...] = jnp.zeros_like(tacc)
    att[...] = jnp.zeros_like(att)
    dqkv[...] = jnp.zeros_like(dqkv)

    for a in range(GROUPS):
        for r in range(0, G_TOK, 56):
            src = a * G_TOK + r
            low = src // 16 * 16
            rows = og[low : low + 64 if low + 64 <= TOK else TOK, :].astype(F32)[src - low : src - low + 56]
            keep = iota((56, D), 0) + src < live
            x = jnp.where(keep, rows, 0.0)
            s2[r : r + 56, :] = x
            sums[7] += fold_rows(x)
        s2[G_TOK:G_ROWS, :] = jnp.zeros((G_ROWS - G_TOK, D), F32)
        back[a * G_ROWS : (a + 1) * G_ROWS, :] = s2[...].astype(BF16)

    @pl.loop(0, ROWS // 80)
    def _(t):
        for c in range(5):
            rows = pl.ds(pl.multiple_of(t * 80 + c * 16, 16), 16)
            scaled, inverse = normalize(x_ref[rows, :])
            xh1[rows, :] = scaled
            inv1[rows, :] = inverse
            n1[rows, :] = (scaled * small[0:1, :] + small[1:2, :]).astype(BF16)

    for part in range(3):
        shift = None if part == 1 else small[2 + part // 2 : 3 + part // 2, :]

        @pl.loop(0, GROUPS)
        def _(a):
            rows = pl.ds(pl.multiple_of(a * G_ROWS, 16), G_ROWS)
            y = dot(n1[rows, :], wq_b[:, part * D : (part + 1) * D])
            if shift is not None:
                y = y + shift
            qkv[rows, part * D : (part + 1) * D] = y.astype(BF16)

    @pl.loop(0, GROUPS * PER)
    def _(w):
        rows = pl.ds(chunk_start(w), CHUNK)
        b = w % PER
        for g in range(SETS):
            q = qkv[rows, 128 * g : 128 * g + 128]
            k = qkv[rows, D + 128 * g : D + 128 * g + 128]
            v = qkv[rows, 2 * D + 128 * g : 2 * D + 128 * g + 128]
            scores = dot_nt(k, spread(q, emask[b]))[:KEYS] * SCALE + (bias[b, g] + mask[w])
            p = jnp.exp(scores - jnp.max(scores, axis=0, keepdims=True))
            p = p * (1.0 / jnp.sum(p, axis=0, keepdims=True))
            probs[w, g] = p
            o = collect(dot_tn(pad_keys(p).astype(BF16), v))
            i = iota((CHUNK, 128), 0)
            att[rows, 128 * g : 128 * g + 128] += jnp.where((i >= b) & (i < b + SPAN), o, 0.0)

    @pl.loop(0, GROUPS)
    def _(a):
        rows = pl.ds(pl.multiple_of(a * G_ROWS, 16), G_ROWS)
        att_b[rows, :] = att[rows, :].astype(BF16)
        s1[...] = dot(att_b[rows, :], wp_b[...])

        @pl.loop(0, 5)
        def _(t):
            for c in range(5):
                here = pl.multiple_of(t * 80 + c * 16, 16)
                rows = pl.ds(pl.multiple_of(a * G_ROWS + here, 16), 16)
                middle = x_ref[rows, :] + (s1[pl.ds(here, 16), :] + small[4:5, :])
                x_ref[rows, :] = middle
                scaled, inverse = normalize(middle)
                xh2[rows, :] = scaled
                inv2[rows, :] = inverse
                n2[rows, :] = (scaled * small[5:6, :] + small[6:7, :]).astype(BF16)

    @pl.loop(0, 5)
    def _(mt):
        rows = pl.ds(pl.multiple_of(mt * 240, 16), 240)
        for nt in range(6):
            cols = slice(256 * nt, 256 * nt + 256)
            inner = dot(n2[rows, :], w1[:, cols]) + b1[:, cols]
            up = dot_nt(back[rows, :], w2[cols, :])
            total = b1_acc[:, cols]
            for c in range(15):
                act, slope = gelu_parts(inner[16 * c : 16 * c + 16])
                here = pl.ds(pl.multiple_of(mt * 240 + 16 * c, 16), 16)
                hidden[here, cols] = act.astype(BF16)
                grad = (up[16 * c : 16 * c + 16] * slope).astype(BF16)
                ig[here, cols] = grad
                total = total + fold_rows(grad.astype(F32))
            b1_acc[:, cols] = total

    for a in range(GROUPS):
        rows = slice(a * G_ROWS, (a + 1) * G_ROWS)
        s1[...] = dot(hidden[rows, :], w2[...])
        s2[...] = dot_nt(ig[rows, :], w1[...])
        for c in range(25):
            here = slice(16 * c, 16 * c + 16)
            at = slice(a * G_ROWS + 16 * c, a * G_ROWS + 16 * c + 16)
            size = 16 if c < 24 else 8
            src = a * G_TOK + 16 * c
            y = x_ref[at, :] + (s1[here, :] + small[7:8, :])
            keep = iota((16, D), 0) + src < live
            out[src : src + size, :] = jnp.where(keep, y, 0.0)[:size]
            u = s2[here, :]
            scaled = xh2[at, :]
            sums[5] += fold_rows(u * scaled)
            sums[6] += fold_rows(u)
            mg = normalize_back(u, small[5:6, :], scaled, inv2[at, :]) + back[at, :].astype(F32)
            x_ref[at, :] = mg
            low = mg.astype(BF16)
            n2_low = low.astype(F32)
            sums[4] += fold_rows(n2_low)
            att[at, :] = n2_low

    fc2_g[...] = dot_tn(hidden[...], back[...]).astype(fc2_g.dtype)
    fc1_g[...] = dot_tn(n2[...], ig[...]).astype(fc1_g.dtype)

    @pl.loop(0, GROUPS)
    def _(a):
        rows = pl.ds(pl.multiple_of(a * G_ROWS, 16), G_ROWS)
        n2[rows, :] = att[rows, :].astype(BF16)

    proj_g[...] = dot_tn(att_b[...], n2[...]).astype(proj_g.dtype)

    @pl.loop(0, GROUPS)
    def _(a):
        rows = pl.ds(pl.multiple_of(a * G_ROWS, 16), G_ROWS)
        att_b[rows, :] = dot_nt(n2[rows, :], wp_b[...]).astype(BF16)

    @pl.loop(0, GROUPS * PER)
    def _(w):
        rows = pl.ds(chunk_start(w), CHUNK)
        b = w % PER
        for g in range(SETS):
            q = qkv[rows, 128 * g : 128 * g + 128]
            k = qkv[rows, D + 128 * g : D + 128 * g + 128]
            v = qkv[rows, 2 * D + 128 * g : 2 * D + 128 * g + 128]
            keep = emask[b]
            qe = spread(q, keep)
            da = spread(att_b[rows, 128 * g : 128 * g + 128], keep)
            p = probs[w, g]
            dp = dot_nt(v, da)[:KEYS]
            pd = p * dp
            ds = pad_keys(pd - p * jnp.sum(pd, axis=0, keepdims=True)).astype(BF16)
            tacc[b, g] += ds.astype(F32)[:KEYS]
            dv = dot(pad_keys(p).astype(BF16), da)
            dk = dot(ds, qe) * SCALE
            dq = collect(dot_tn(ds, k)) * SCALE
            dqkv[rows, 128 * g : 128 * g + 128] += dq
            dqkv[rows, D + 128 * g : D + 128 * g + 128] += dk
            dqkv[rows, 2 * D + 128 * g : 2 * D + 128 * g + 128] += dv

    @pl.loop(0, ROWS // 80)
    def _(t):
        for c in range(5):
            rows = pl.ds(pl.multiple_of(t * 80 + c * 16, 16), 16)
            low = dqkv[rows, :].astype(BF16)
            dqkv_b[rows, :] = low
            wide = low.astype(F32)
            sums[2] += fold_rows(wide[:, :D])
            sums[3] += fold_rows(wide[:, 2 * D :])

    qkv_g[...] = dot_tn(n1[...], dqkv_b[...]).astype(qkv_g.dtype)

    for a in range(GROUPS):
        rows = slice(a * G_ROWS, (a + 1) * G_ROWS)
        s1[...] = dot_nt(dqkv_b[rows, :], wq_b[...])
        for c in range(25):
            here = slice(16 * c, 16 * c + 16)
            at = slice(a * G_ROWS + 16 * c, a * G_ROWS + 16 * c + 16)
            size = 16 if c < 24 else 8
            src = a * G_TOK + 16 * c
            u = s1[here, :]
            scaled = xh1[at, :]
            sums[0] += fold_rows(u * scaled)
            sums[1] += fold_rows(u)
            y = normalize_back(u, small[0:1, :], scaled, inv1[at, :]) + x_ref[at, :]
            gin[src : src + size, :] = y[:size]

    for part in range(8):
        small_g[part : part + 1, :] = jnp.sum(sums[part], axis=0, keepdims=True)
    b1_g[...] = jnp.sum(b1_acc[...], axis=0, keepdims=True)

    j = iota((KEYS, 256), 0)
    amount = jnp.maximum(84 - embed(j), 0)
    for g in range(SETS):
        total = tacc[0, g]
        for b in range(1, PER):
            total = total + pltpu.roll(pltpu.roll(tacc[b, g], KEYS - b, 0), LANES - b, 1)
        for h in range(4):
            lane_from = iota((LANES, 256), 0) - CHUNK * h
            pick = (iota((LANES, 256), 1) == embed(lane_from)) & (lane_from >= 0) & (lane_from < SPAN)
            wide = barrel(dot_exact(total, jnp.where(pick, 1.0, 0.0)), amount, True)
            wide = jnp.where(j < SPAN, wide, 0.0)
            table_g[4 * g + h : 4 * g + h + 1, :] = jnp.sum(wide, axis=0, keepdims=True)
    table_g[HEADS:, :] = jnp.zeros((16 - HEADS, 256), F32)


def local_block(live_tokens, tok, og, region, wq, wp, table, small, w1, b1, w2, grad_type=BF16):
    sd = jax.ShapeDtypeStruct
    vm = pltpu.VMEM
    return pl.pallas_call(
        block_kernel,
        out_shape=[
            sd((TOK, D), F32),
            sd((TOK, D), F32),
            sd((D, QKV), grad_type),
            sd((D, D), grad_type),
            sd((D, FF), grad_type),
            sd((FF, D), grad_type),
            sd((8, D), F32),
            sd((1, FF), F32),
            sd((16, 256), F32),
        ],
        in_specs=[pl.BlockSpec(memory_space=pltpu.SMEM)] + [pl.BlockSpec(memory_space=vm)] * 10,
        out_specs=[pl.BlockSpec(memory_space=vm)] * 9,
        scratch_shapes=[
            vm((ROWS, D), F32),
            vm((ROWS, D), F32),
            vm((ROWS, 1), F32),
            vm((ROWS, D), F32),
            vm((ROWS, 1), F32),
            vm((ROWS, D), BF16),
            vm((ROWS, D), BF16),
            vm((ROWS, QKV), BF16),
            vm((ROWS, D), F32),
            vm((ROWS, D), BF16),
            vm((GROUPS * PER, SETS, KEYS, LANES), F32),
            vm((ROWS, D), BF16),
            vm((ROWS, FF), BF16),
            vm((ROWS, FF), BF16),
            vm((ROWS, QKV), F32),
            vm((ROWS, QKV), BF16),
            vm((PER, LANES, 128), BF16),
            vm((PER, SETS, KEYS, LANES), F32),
            vm((GROUPS * PER, KEYS, LANES), F32),
            vm((PER, SETS, KEYS, LANES), F32),
            vm((G_ROWS, D), F32),
            vm((G_ROWS, D), F32),
            vm((8, 8, D), F32),
            vm((8, FF), F32),
            vm((D, QKV), BF16),
            vm((D, D), BF16),
        ],
        compiler_params=pltpu.CompilerParams(vmem_limit_bytes=63 * 1024 * 1024),
        cost_estimate=pl.CostEstimate(flops=14_000_000_000, bytes_accessed=20_000_000, transcendentals=3_000_000),
        name="block",
    )(live_tokens, tok, og, region, wq, wp, table, small, w1, b1, w2)


def clip_scale(mean_square):
    return 1.0 / jnp.maximum(1.0, jnp.sqrt(mean_square))


def adafactor_matrix(grad, row, col, weight, rate):
    squares = grad * grad + EPS_SQ
    row_new = DECAY * row + (1.0 - DECAY) * jnp.mean(squares, axis=1)
    col_new = DECAY * col + (1.0 - DECAY) * jnp.mean(squares, axis=0)
    step = grad * lax.rsqrt(row_new[:, None] * col_new[None, :] / jnp.mean(row_new))
    return row_new, col_new, weight - rate * (step * clip_scale(jnp.mean(step * step)))


def vector_update(grad, state, weight):
    state_new = DECAY * state + (1.0 - DECAY) * (grad * grad + EPS_SQ)
    step = grad * lax.rsqrt(state_new)
    return state_new, weight - VEC_RATE * (step * clip_scale(jnp.mean(step * step)))


def per_device(
    tokens_in, out_grad, window_live, region_ids, qkv_weight, proj_weight, rel_table, small_params,
    fc1_weight, fc1_bias, fc2_weight, qkv_row, qkv_col, proj_row, proj_col, fc1_row, fc1_col,
    fc2_row, fc2_col, fc1_bias_state, small_state, table_state,
):
    own = jnp.concatenate([fc1_weight.astype(BF16), fc2_weight.astype(BF16)], axis=0)
    gathered = lax.all_gather(own, "mlp", axis=0)
    w1 = gathered[:, :D].transpose(1, 0, 2).reshape(D, FF)
    w2 = gathered[:, D:].reshape(FF, D)
    b1 = lax.all_gather(fc1_bias, "mlp", axis=0, tiled=True).reshape(1, FF)
    live_tokens = (jnp.sum(window_live) * SPAN).reshape(1)
    region = jnp.pad(region_ids.astype(F32), (0, 104)).reshape(1, 1280)
    table = jnp.pad(rel_table.T, ((0, 4), (0, 87)))
    out, gin, qkv_l, proj_l, fc1_l, fc2_l, small_l, b1_l, table_l = local_block(
        live_tokens, tokens_in, out_grad, region, qkv_weight, proj_weight, table,
        small_params.reshape(8, D), w1, b1, w2,
    )
    qkv_l, proj_l, fc1_l, fc2_l = (g.astype(F32) for g in (qkv_l, proj_l, fc1_l, fc2_l))
    fc1_s = lax.psum_scatter(fc1_l, "mlp", scatter_dimension=1, tiled=True)
    fc2_s = lax.psum_scatter(fc2_l, "mlp", scatter_dimension=0, tiled=True)
    b1_s = lax.psum_scatter(b1_l.reshape(FF), "mlp", scatter_dimension=0, tiled=True)
    up_grad, down_grad, bias_grad = lax.psum((fc1_s, fc2_s, b1_s), "win")
    qkv_whole, proj_whole, small_grad, table_grad = lax.psum(
        (qkv_l, proj_l, small_l.reshape(8 * D), table_l[:HEADS, :169]), ("win", "mlp")
    )
    table_grad = table_grad.T

    up_squares = up_grad * up_grad + EPS_SQ
    down_squares = down_grad * down_grad + EPS_SQ
    fc1_col_new = DECAY * fc1_col + (1.0 - DECAY) * jnp.mean(up_squares, axis=0)
    fc2_row_new = DECAY * fc2_row + (1.0 - DECAY) * jnp.mean(down_squares, axis=1)
    fc1_bias_state_new = DECAY * fc1_bias_state + (1.0 - DECAY) * (bias_grad * bias_grad + EPS_SQ)
    bias_step = bias_grad * lax.rsqrt(fc1_bias_state_new)
    up_rows, up_over, down_cols, down_over, down_total, bias_norm = lax.psum(
        (
            jnp.sum(up_squares, axis=1),
            jnp.sum(up_grad * up_grad / fc1_col_new[None, :], axis=1),
            jnp.sum(down_squares, axis=0),
            jnp.sum(down_grad * down_grad / fc2_row_new[:, None], axis=0),
            jnp.sum(fc2_row_new),
            jnp.sum(bias_step * bias_step),
        ),
        "mlp",
    )
    fc1_row_new = DECAY * fc1_row + (1.0 - DECAY) * up_rows / FF
    fc2_col_new = DECAY * fc2_col + (1.0 - DECAY) * down_cols / FF
    up_mean = jnp.mean(fc1_row_new)
    down_mean = down_total / FF
    up_norm = up_mean * jnp.sum(up_over / fc1_row_new) / (D * FF)
    down_norm = down_mean * jnp.sum(down_over / fc2_col_new) / (D * FF)
    up_step = up_grad * lax.rsqrt(fc1_row_new[:, None] * fc1_col_new[None, :] / up_mean)
    down_step = down_grad * lax.rsqrt(fc2_row_new[:, None] * fc2_col_new[None, :] / down_mean)
    fc1_new = fc1_weight - D ** (-0.5) * (up_step * clip_scale(up_norm))
    fc2_new = fc2_weight - FF ** (-0.5) * (down_step * clip_scale(down_norm))
    fc1_bias_new = fc1_bias - VEC_RATE * (bias_step * clip_scale(bias_norm / FF))

    qkv_row_full, qkv_col_new, qkv_new_full = adafactor_matrix(
        qkv_whole, qkv_row, qkv_col, qkv_weight, D ** (-0.5)
    )
    proj_row_full, proj_col_new, proj_new_full = adafactor_matrix(
        proj_whole, proj_row, proj_col, proj_weight, (D // 8) ** (-0.5)
    )
    start = lax.axis_index(("win", "mlp")) * 3
    mine = lambda full: lax.dynamic_slice_in_dim(full, start, 3, 0)
    qkv_new = mine(qkv_new_full)
    proj_new = mine(proj_new_full)
    small_state_new, small_new = vector_update(small_grad, small_state, small_params)
    table_state_new, table_new = vector_update(table_grad, table_state, rel_table)
    return (
        out, gin,
        mine(qkv_whole), mine(qkv_row_full), qkv_col_new, qkv_new, qkv_new.astype(BF16),
        mine(proj_whole), mine(proj_row_full), proj_col_new, proj_new, proj_new.astype(BF16),
        up_grad, fc1_row_new, fc1_col_new, fc1_new, fc1_new.astype(BF16),
        down_grad, fc2_row_new, fc2_col_new, fc2_new, fc2_new.astype(BF16),
        bias_grad, fc1_bias_state_new, fc1_bias_new,
        small_grad, small_state_new, small_new,
        table_grad, table_state_new, table_new,
    )


def solution(mesh):
    tokens, owner = P(("win", "mlp"), None), P(("win", "mlp"))
    whole, part = P(), P("mlp")
    return jax.shard_map(
        per_device,
        mesh=mesh,
        in_specs=(
            tokens, tokens, owner, owner, whole, whole, whole, whole, P(None, "mlp"), part, P("mlp", None),
            whole, whole, whole, whole, whole, part, part, whole, part, whole, whole,
        ),
        out_specs=(
            tokens, tokens,
            tokens, owner, whole, tokens, tokens,
            tokens, owner, whole, tokens, tokens,
            P(None, "mlp"), whole, part, P(None, "mlp"), P(None, "mlp"),
            P("mlp", None), part, whole, P("mlp", None), P("mlp", None),
            part, part, part,
            whole, whole, whole,
            whole, whole, whole,
        ),
        check_vma=False,
    )
```

```python
import functools
import math

import jax
import jax.numpy as jnp
from jax import lax
from jax.experimental import pallas as pl
from jax.experimental.pallas import tpu as pltpu
from jax.sharding import PartitionSpec as P

D = 384
FF = 1536
QKV = 3 * D
HEADS = 12
WIN = 7
SPAN = WIN * WIN
STEP = 10
DECAY = 1.0 - STEP ** (-0.8)
EPS_NORM = 1e-05
EPS_SQ = 1e-30
VEC_RATE = 0.3
SCALE = 32 ** (-0.5)
FAR = -1e30

GROUPS = 3
PER = 8
G_TOK = PER * SPAN
G_ROWS = 400
ROWS = GROUPS * G_ROWS
TOK = GROUPS * G_TOK
CHUNK = 64
KEYS = 56
SETS = 3
LANES = 4 * CHUNK

MESH = pl.DeviceIdType.MESH
F32 = jnp.float32
BF16 = jnp.bfloat16


def dot(a, b):
    return jnp.dot(a, b, preferred_element_type=F32)


def dot_nt(a, b):
    return lax.dot_general(a, b, (((1,), (1,)), ((), ())), preferred_element_type=F32)


def dot_tn(a, b):
    return lax.dot_general(a, b, (((0,), (0,)), ((), ())), preferred_element_type=F32)


def dot_exact(a, b):
    return jnp.dot(a, b, precision=lax.Precision.HIGHEST, preferred_element_type=F32)


def iota(shape, dim):
    return lax.broadcasted_iota(jnp.int32, shape, dim)


def fold_rows(x):
    total = x[0:8]
    for i in range(1, x.shape[0] // 8):
        total = total + x[8 * i : 8 * i + 8]
    return total


def row_mean(x):
    return jnp.sum(x, axis=1, keepdims=True) * (1.0 / D)


def normalize(x):
    center = x - row_mean(x)
    inverse = lax.rsqrt(row_mean(center * center) + EPS_NORM)
    return center * inverse, inverse


def normalize_back(u, gain, scaled, inverse):
    weighted = u * gain
    return inverse * (weighted - row_mean(weighted) - scaled * row_mean(weighted * scaled))


def gelu_parts(v):
    e = jnp.exp(-0.5 * v * v)
    t = 1.0 / (1.0 + (0.3275911 * 0.5**0.5) * jnp.abs(v))
    poly = 1.061405429 * t - 1.453152027
    poly = poly * t + 1.421413741
    poly = poly * t - 0.284496736
    poly = poly * t + 0.254829592
    tail = (0.5 * e) * (poly * t)
    phi = jnp.where(v < 0.0, tail, 1.0 - tail)
    return v * phi, phi + v * e * (2.0 * math.pi) ** (-0.5)


def barrel(x, amount, right):
    width = x.shape[1]
    for k in range(7):
        step = 1 << k
        moved = pltpu.roll(x, step if right else width - step, 1)
        x = jnp.where((amount & step) != 0, moved, x)
    return x


def embed(i):
    return 13 * (i // WIN) + i % WIN


def chunk_start(w):
    return pl.multiple_of((w // PER) * G_ROWS + (w % PER) * 48, 16)


def prologue(region, table, x_ref, emask, bias, mask, tok):
    for a in range(GROUPS):
        for r in range(0, G_TOK, 56):
            src = a * G_TOK + r
            low = src // 16 * 16
            x_ref[a * G_ROWS + r : a * G_ROWS + r + 56, :] = (
                tok[low : low + 64 if low + 64 <= TOK else TOK, :].astype(F32)[src - low : src - low + 56]
            )
        x_ref[a * G_ROWS + G_TOK : (a + 1) * G_ROWS, :] = jnp.zeros((G_ROWS - G_TOK, D), F32)
    row = iota((LANES, 128), 0)
    lane = iota((LANES, 128), 1)
    for b in range(PER):
        i = row % CHUNK
        keep = (i >= b) & (i < b + SPAN) & (lane // 32 == row // CHUNK)
        emask[b] = jnp.where(keep, 1.0, 0.0).astype(BF16)
    j = iota((KEYS, 256), 0)
    amount = jnp.maximum(84 - embed(j), 0)
    jl = iota((KEYS, LANES), 0)
    il = iota((KEYS, LANES), 1) % CHUNK
    for g in range(SETS):
        base = jnp.zeros((KEYS, LANES), F32)
        for h in range(4):
            wide = jnp.broadcast_to(table[4 * g + h : 4 * g + h + 1, :], (KEYS, 256))
            wide = barrel(wide, amount, False)[:, :128]
            lane_to = iota((128, LANES), 1) - CHUNK * h
            pick = (iota((128, LANES), 0) == embed(lane_to)) & (lane_to >= 0) & (lane_to < SPAN)
            base = base + dot_exact(wide, jnp.where(pick, 1.0, 0.0))
        for b in range(PER):
            moved = pltpu.roll(pltpu.roll(base, b, 0), b, 1) if b else base
            key_ok = (jl >= b) & (jl < b + SPAN)
            query_ok = (il >= b) & (il < b + SPAN)
            bias[b, g] = jnp.where(key_ok, jnp.where(query_ok, moved, 0.0), FAR)
    eye = iota((CHUNK, CHUNK), 0) == iota((CHUNK, CHUNK), 1)
    for w in range(GROUPS * PER):
        start = (w // PER) * G_TOK + (w % PER) * 48
        line = region[:, start : start + CHUNK]
        column = jnp.sum(jnp.where(eye, jnp.broadcast_to(line, (CHUNK, CHUNK)), 0.0), axis=1, keepdims=True)
        wide = jnp.concatenate([line] * 4, axis=1)
        mask[w] = jnp.where(column[:KEYS] != wide, -100.0, 0.0)


def pad_keys(x):
    return jnp.concatenate([x, jnp.zeros((CHUNK - KEYS, x.shape[1]), x.dtype)], axis=0)


def spread(x, keep):
    return jnp.concatenate([x] * 4, axis=0) * keep


def collect(full):
    head = iota((CHUNK, 128), 1) // 32
    parts = [full[CHUNK * h : CHUNK * (h + 1)] for h in range(4)]
    low = jnp.where(head == 0, parts[0], parts[1])
    high = jnp.where(head == 2, parts[2], parts[3])
    return jnp.where(head < 2, low, high)


def block_kernel(
    live_tokens, tok, og, region, wq, wp, table, small, fc1, fc2, fc1_b,
    out, gin, qkv_g, proj_g, fc1_g, fc2_g, small_g, b1_g, table_g,
    x_ref, xh1, inv1, xh2, inv2, n1, n2, qkv, att, att_b, probs, back, hidden, ig, dqkv,
    emask, bias, mask, tacc, s1, s2, sums, b1_acc, wq_b, wp_b, w1, w2, b1,
    ag_send, ag_recv, pair_send, pair_recv,
):
    win, mlp = lax.axis_index("win"), lax.axis_index("mlp")
    core = win % 2
    pair = {"win": win + 1 - 2 * core}
    barrier = pltpu.get_barrier_semaphore()
    for d in range(1, 4):
        pl.semaphore_signal(barrier, inc=1, device_id={"mlp": (mlp + d) % 4}, device_id_type=MESH)
    pl.semaphore_signal(barrier, inc=1, device_id=pair, device_id_type=MESH)

    def shard(m):
        at = pl.multiple_of(m * D, D)
        half = pl.ds(pl.multiple_of(core * (D // 2), 16), D // 2)
        half_at = pl.ds(pl.multiple_of(m * D + core * (D // 2), 16), D // 2)
        return w1.at[half, pl.ds(at, D)], w2.at[half_at, :], b1.at[m]

    mine = shard(mlp)
    cols = pl.ds(pl.multiple_of(mlp * D, D), D)
    w1[:, cols] = fc1[...].astype(BF16)
    w2[cols, :] = fc2[...].astype(BF16)
    b1[mlp] = jnp.broadcast_to(fc1_b[...], (8, D))
    pl.semaphore_wait(barrier, 4)
    sends = []
    for d in range(1, 4):
        for n in range(3):
            copy = pltpu.make_async_remote_copy(
                src_ref=mine[n], dst_ref=mine[n], send_sem=ag_send.at[d - 1, n], recv_sem=ag_recv.at[d - 1, n],
                device_id={"mlp": (mlp + d) % 4}, device_id_type=MESH,
            )
            copy.start()
            sends.append(copy)
    prologue(region, table, x_ref, emask, bias, mask, tok)
    live = live_tokens[0]
    wq_b[...] = wq[...].astype(BF16)
    wp_b[...] = wp[...].astype(BF16)
    sums[...] = jnp.zeros_like(sums)
    b1_acc[...] = jnp.zeros_like(b1_acc)
    tacc[...] = jnp.zeros_like(tacc)
    att[...] = jnp.zeros_like(att)
    dqkv[...] = jnp.zeros_like(dqkv)

    for a in range(GROUPS):
        for r in range(0, G_TOK, 56):
            src = a * G_TOK + r
            low = src // 16 * 16
            rows = og[low : low + 64 if low + 64 <= TOK else TOK, :].astype(F32)[src - low : src - low + 56]
            keep = iota((56, D), 0) + src < live
            x = jnp.where(keep, rows, 0.0)
            s2[r : r + 56, :] = x
            sums[7] += fold_rows(x)
        s2[G_TOK:G_ROWS, :] = jnp.zeros((G_ROWS - G_TOK, D), F32)
        back[a * G_ROWS : (a + 1) * G_ROWS, :] = s2[...].astype(BF16)

    @pl.loop(0, ROWS // 80)
    def _(t):
        for c in range(5):
            rows = pl.ds(pl.multiple_of(t * 80 + c * 16, 16), 16)
            scaled, inverse = normalize(x_ref[rows, :])
            xh1[rows, :] = scaled
            inv1[rows, :] = inverse
            n1[rows, :] = (scaled * small[0:1, :] + small[1:2, :]).astype(BF16)

    for part in range(3):
        shift = None if part == 1 else small[2 + part // 2 : 3 + part // 2, :]

        @pl.loop(0, GROUPS)
        def _(a):
            rows = pl.ds(pl.multiple_of(a * G_ROWS, 16), G_ROWS)
            y = dot(n1[rows, :], wq_b[:, part * D : (part + 1) * D])
            if shift is not None:
                y = y + shift
            qkv[rows, part * D : (part + 1) * D] = y.astype(BF16)

    @pl.loop(0, GROUPS * PER)
    def _(w):
        rows = pl.ds(chunk_start(w), CHUNK)
        b = w % PER
        for g in range(SETS):
            q = qkv[rows, 128 * g : 128 * g + 128]
            k = qkv[rows, D + 128 * g : D + 128 * g + 128]
            v = qkv[rows, 2 * D + 128 * g : 2 * D + 128 * g + 128]
            scores = dot_nt(k, spread(q, emask[b]))[:KEYS] * SCALE + (bias[b, g] + mask[w])
            p = jnp.exp(scores - jnp.max(scores, axis=0, keepdims=True))
            p = p * (1.0 / jnp.sum(p, axis=0, keepdims=True))
            probs[w, g] = p
            o = collect(dot_tn(pad_keys(p).astype(BF16), v))
            i = iota((CHUNK, 128), 0)
            att[rows, 128 * g : 128 * g + 128] += jnp.where((i >= b) & (i < b + SPAN), o, 0.0)

    forwards = []
    for d in range(1, 4):
        came = shard((mlp + 4 - d) % 4)
        for n in range(3):
            sends[3 * (d - 1) + n].wait_recv()
            if n < 2:
                copy = pltpu.make_async_remote_copy(
                    src_ref=came[n], dst_ref=came[n], send_sem=pair_send.at[d - 1, n],
                    recv_sem=pair_recv.at[d - 1, n], device_id=pair, device_id_type=MESH,
                )
                copy.start()
                forwards.append(copy)

    @pl.loop(0, GROUPS)
    def _(a):
        rows = pl.ds(pl.multiple_of(a * G_ROWS, 16), G_ROWS)
        att_b[rows, :] = att[rows, :].astype(BF16)
        s1[...] = dot(att_b[rows, :], wp_b[...])

        @pl.loop(0, 5)
        def _(t):
            for c in range(5):
                here = pl.multiple_of(t * 80 + c * 16, 16)
                rows = pl.ds(pl.multiple_of(a * G_ROWS + here, 16), 16)
                middle = x_ref[rows, :] + (s1[pl.ds(here, 16), :] + small[4:5, :])
                x_ref[rows, :] = middle
                scaled, inverse = normalize(middle)
                xh2[rows, :] = scaled
                inv2[rows, :] = inverse
                n2[rows, :] = (scaled * small[5:6, :] + small[6:7, :]).astype(BF16)

    for copy in forwards:
        copy.wait()

    @pl.loop(0, 5)
    def _(mt):
        rows = pl.ds(pl.multiple_of(mt * 240, 16), 240)
        b1_row = jnp.concatenate([b1[m, 0:1, :] for m in range(4)], axis=1)
        for nt in range(6):
            cols = slice(256 * nt, 256 * nt + 256)
            inner = dot(n2[rows, :], w1[:, cols]) + b1_row[:, cols]
            up = dot_nt(back[rows, :], w2[cols, :])
            total = b1_acc[:, cols]
            for c in range(15):
                act, slope = gelu_parts(inner[16 * c : 16 * c + 16])
                here = pl.ds(pl.multiple_of(mt * 240 + 16 * c, 16), 16)
                hidden[here, cols] = act.astype(BF16)
                grad = (up[16 * c : 16 * c + 16] * slope).astype(BF16)
                ig[here, cols] = grad
                total = total + fold_rows(grad.astype(F32))
            b1_acc[:, cols] = total

    for a in range(GROUPS):
        rows = slice(a * G_ROWS, (a + 1) * G_ROWS)
        s1[...] = dot(hidden[rows, :], w2[...])
        s2[...] = dot_nt(ig[rows, :], w1[...])
        for c in range(25):
            here = slice(16 * c, 16 * c + 16)
            at = slice(a * G_ROWS + 16 * c, a * G_ROWS + 16 * c + 16)
            size = 16 if c < 24 else 8
            src = a * G_TOK + 16 * c
            y = x_ref[at, :] + (s1[here, :] + small[7:8, :])
            keep = iota((16, D), 0) + src < live
            out[src : src + size, :] = jnp.where(keep, y, 0.0)[:size]
            u = s2[here, :]
            scaled = xh2[at, :]
            sums[5] += fold_rows(u * scaled)
            sums[6] += fold_rows(u)
            mg = normalize_back(u, small[5:6, :], scaled, inv2[at, :]) + back[at, :].astype(F32)
            x_ref[at, :] = mg
            low = mg.astype(BF16)
            n2_low = low.astype(F32)
            sums[4] += fold_rows(n2_low)
            att[at, :] = n2_low

    fc2_g[...] = dot_tn(hidden[...], back[...]).astype(fc2_g.dtype)
    fc1_g[...] = dot_tn(n2[...], ig[...]).astype(fc1_g.dtype)

    @pl.loop(0, GROUPS)
    def _(a):
        rows = pl.ds(pl.multiple_of(a * G_ROWS, 16), G_ROWS)
        n2[rows, :] = att[rows, :].astype(BF16)

    proj_g[...] = dot_tn(att_b[...], n2[...]).astype(proj_g.dtype)

    @pl.loop(0, GROUPS)
    def _(a):
        rows = pl.ds(pl.multiple_of(a * G_ROWS, 16), G_ROWS)
        att_b[rows, :] = dot_nt(n2[rows, :], wp_b[...]).astype(BF16)

    @pl.loop(0, GROUPS * PER)
    def _(w):
        rows = pl.ds(chunk_start(w), CHUNK)
        b = w % PER
        for g in range(SETS):
            q = qkv[rows, 128 * g : 128 * g + 128]
            k = qkv[rows, D + 128 * g : D + 128 * g + 128]
            v = qkv[rows, 2 * D + 128 * g : 2 * D + 128 * g + 128]
            keep = emask[b]
            qe = spread(q, keep)
            da = spread(att_b[rows, 128 * g : 128 * g + 128], keep)
            p = probs[w, g]
            dp = dot_nt(v, da)[:KEYS]
            pd = p * dp
            ds = pad_keys(pd - p * jnp.sum(pd, axis=0, keepdims=True)).astype(BF16)
            tacc[b, g] += ds.astype(F32)[:KEYS]
            dv = dot(pad_keys(p).astype(BF16), da)
            dk = dot(ds, qe) * SCALE
            dq = collect(dot_tn(ds, k)) * SCALE
            dqkv[rows, 128 * g : 128 * g + 128] += dq
            dqkv[rows, D + 128 * g : D + 128 * g + 128] += dk
            dqkv[rows, 2 * D + 128 * g : 2 * D + 128 * g + 128] += dv

    @pl.loop(0, ROWS // 80)
    def _(t):
        for c in range(5):
            rows = pl.ds(pl.multiple_of(t * 80 + c * 16, 16), 16)
            low = dqkv[rows, :].astype(BF16)
            hidden[rows, :QKV] = low
            wide = low.astype(F32)
            sums[2] += fold_rows(wide[:, :D])
            sums[3] += fold_rows(wide[:, 2 * D :])

    qkv_g[...] = dot_tn(n1[...], hidden[:, :QKV]).astype(qkv_g.dtype)

    for a in range(GROUPS):
        rows = slice(a * G_ROWS, (a + 1) * G_ROWS)
        s1[...] = dot_nt(hidden[rows, :QKV], wq_b[...])
        for c in range(25):
            here = slice(16 * c, 16 * c + 16)
            at = slice(a * G_ROWS + 16 * c, a * G_ROWS + 16 * c + 16)
            size = 16 if c < 24 else 8
            src = a * G_TOK + 16 * c
            u = s1[here, :]
            scaled = xh1[at, :]
            sums[0] += fold_rows(u * scaled)
            sums[1] += fold_rows(u)
            y = normalize_back(u, small[0:1, :], scaled, inv1[at, :]) + x_ref[at, :]
            gin[src : src + size, :] = y[:size]

    for part in range(8):
        small_g[part : part + 1, :] = jnp.sum(sums[part], axis=0, keepdims=True)
    b1_g[...] = jnp.sum(b1_acc[...], axis=0, keepdims=True)

    j = iota((KEYS, 256), 0)
    amount = jnp.maximum(84 - embed(j), 0)
    for g in range(SETS):
        total = tacc[0, g]
        for b in range(1, PER):
            total = total + pltpu.roll(pltpu.roll(tacc[b, g], KEYS - b, 0), LANES - b, 1)
        for h in range(4):
            lane_from = iota((LANES, 256), 0) - CHUNK * h
            pick = (iota((LANES, 256), 1) == embed(lane_from)) & (lane_from >= 0) & (lane_from < SPAN)
            wide = barrel(dot_exact(total, jnp.where(pick, 1.0, 0.0)), amount, True)
            wide = jnp.where(j < SPAN, wide, 0.0)
            table_g[4 * g + h : 4 * g + h + 1, :] = jnp.sum(wide, axis=0, keepdims=True)
    table_g[HEADS:, :] = jnp.zeros((16 - HEADS, 256), F32)
    for copy in sends:
        copy.wait_send()


def local_block(live_tokens, tok, og, region, wq, wp, table, small, fc1, fc2, fc1_b, grad_type=BF16):
    sd = jax.ShapeDtypeStruct
    vm = pltpu.VMEM
    return pl.pallas_call(
        block_kernel,
        out_shape=[
            sd((TOK, D), F32),
            sd((TOK, D), F32),
            sd((D, QKV), grad_type),
            sd((D, D), grad_type),
            sd((D, FF), grad_type),
            sd((FF, D), grad_type),
            sd((8, D), F32),
            sd((1, FF), F32),
            sd((16, 256), F32),
        ],
        in_specs=[pl.BlockSpec(memory_space=pltpu.SMEM)] + [pl.BlockSpec(memory_space=vm)] * 10,
        out_specs=[pl.BlockSpec(memory_space=vm)] * 9,
        scratch_shapes=[
            vm((ROWS, D), F32),
            vm((ROWS, D), F32),
            vm((ROWS, 1), F32),
            vm((ROWS, D), F32),
            vm((ROWS, 1), F32),
            vm((ROWS, D), BF16),
            vm((ROWS, D), BF16),
            vm((ROWS, QKV), BF16),
            vm((ROWS, D), F32),
            vm((ROWS, D), BF16),
            vm((GROUPS * PER, SETS, KEYS, LANES), F32),
            vm((ROWS, D), BF16),
            vm((ROWS, FF), BF16),
            vm((ROWS, FF), BF16),
            vm((ROWS, QKV), F32),
            vm((PER, LANES, 128), BF16),
            vm((PER, SETS, KEYS, LANES), F32),
            vm((GROUPS * PER, KEYS, LANES), F32),
            vm((PER, SETS, KEYS, LANES), F32),
            vm((G_ROWS, D), F32),
            vm((G_ROWS, D), F32),
            vm((8, 8, D), F32),
            vm((8, FF), F32),
            vm((D, QKV), BF16),
            vm((D, D), BF16),
            vm((D, FF), BF16),
            vm((FF, D), BF16),
            vm((4, 8, D), F32),
            pltpu.SemaphoreType.DMA((3, 3)),
            pltpu.SemaphoreType.DMA((3, 3)),
            pltpu.SemaphoreType.DMA((3, 2)),
            pltpu.SemaphoreType.DMA((3, 2)),
        ],
        compiler_params=pltpu.CompilerParams(vmem_limit_bytes=63 * 1024 * 1024, collective_id=0, has_side_effects=True),
        cost_estimate=pl.CostEstimate(flops=14_000_000_000, bytes_accessed=20_000_000, transcendentals=3_000_000),
        name="block",
    )(live_tokens, tok, og, region, wq, wp, table, small, fc1, fc2, fc1_b)


def clip_scale(mean_square):
    return 1.0 / jnp.maximum(1.0, jnp.sqrt(mean_square))


def adafactor_matrix(grad, row, col, weight, rate):
    squares = grad * grad + EPS_SQ
    row_new = DECAY * row + (1.0 - DECAY) * jnp.mean(squares, axis=1)
    col_new = DECAY * col + (1.0 - DECAY) * jnp.mean(squares, axis=0)
    step = grad * lax.rsqrt(row_new[:, None] * col_new[None, :] / jnp.mean(row_new))
    return row_new, col_new, weight - rate * (step * clip_scale(jnp.mean(step * step)))


def vector_update(grad, state, weight):
    state_new = DECAY * state + (1.0 - DECAY) * (grad * grad + EPS_SQ)
    step = grad * lax.rsqrt(state_new)
    return state_new, weight - VEC_RATE * (step * clip_scale(jnp.mean(step * step)))


def per_device(
    tokens_in, out_grad, window_live, region_ids, qkv_weight, proj_weight, rel_table, small_params,
    fc1_weight, fc1_bias, fc2_weight, qkv_row, qkv_col, proj_row, proj_col, fc1_row, fc1_col,
    fc2_row, fc2_col, fc1_bias_state, small_state, table_state,
):
    live_tokens = (jnp.sum(window_live) * SPAN).reshape(1)
    region = jnp.pad(region_ids.astype(F32), (0, 104)).reshape(1, 1280)
    table = jnp.pad(rel_table.T, ((0, 4), (0, 87)))
    out, gin, qkv_l, proj_l, fc1_l, fc2_l, small_l, b1_l, table_l = local_block(
        live_tokens, tokens_in, out_grad, region, qkv_weight, proj_weight, table,
        small_params.reshape(8, D), fc1_weight, fc2_weight, fc1_bias.reshape(1, D),
    )
    qkv_l, proj_l, fc1_l, fc2_l = (g.astype(F32) for g in (qkv_l, proj_l, fc1_l, fc2_l))
    fc1_s = lax.psum_scatter(fc1_l, "mlp", scatter_dimension=1, tiled=True)
    fc2_s = lax.psum_scatter(fc2_l, "mlp", scatter_dimension=0, tiled=True)
    b1_s = lax.psum_scatter(b1_l.reshape(FF), "mlp", scatter_dimension=0, tiled=True)
    up_grad, down_grad, bias_grad = lax.psum((fc1_s, fc2_s, b1_s), "win")
    qkv_whole, proj_whole, small_grad, table_grad = lax.psum(
        (qkv_l, proj_l, small_l.reshape(8 * D), table_l[:HEADS, :169]), ("win", "mlp")
    )
    table_grad = table_grad.T

    up_squares = up_grad * up_grad + EPS_SQ
    down_squares = down_grad * down_grad + EPS_SQ
    fc1_col_new = DECAY * fc1_col + (1.0 - DECAY) * jnp.mean(up_squares, axis=0)
    fc2_row_new = DECAY * fc2_row + (1.0 - DECAY) * jnp.mean(down_squares, axis=1)
    fc1_bias_state_new = DECAY * fc1_bias_state + (1.0 - DECAY) * (bias_grad * bias_grad + EPS_SQ)
    bias_step = bias_grad * lax.rsqrt(fc1_bias_state_new)
    up_rows, up_over, down_cols, down_over, down_total, bias_norm = lax.psum(
        (
            jnp.sum(up_squares, axis=1),
            jnp.sum(up_grad * up_grad / fc1_col_new[None, :], axis=1),
            jnp.sum(down_squares, axis=0),
            jnp.sum(down_grad * down_grad / fc2_row_new[:, None], axis=0),
            jnp.sum(fc2_row_new),
            jnp.sum(bias_step * bias_step),
        ),
        "mlp",
    )
    fc1_row_new = DECAY * fc1_row + (1.0 - DECAY) * up_rows / FF
    fc2_col_new = DECAY * fc2_col + (1.0 - DECAY) * down_cols / FF
    up_mean = jnp.mean(fc1_row_new)
    down_mean = down_total / FF
    up_norm = up_mean * jnp.sum(up_over / fc1_row_new) / (D * FF)
    down_norm = down_mean * jnp.sum(down_over / fc2_col_new) / (D * FF)
    up_step = up_grad * lax.rsqrt(fc1_row_new[:, None] * fc1_col_new[None, :] / up_mean)
    down_step = down_grad * lax.rsqrt(fc2_row_new[:, None] * fc2_col_new[None, :] / down_mean)
    fc1_new = fc1_weight - D ** (-0.5) * (up_step * clip_scale(up_norm))
    fc2_new = fc2_weight - FF ** (-0.5) * (down_step * clip_scale(down_norm))
    fc1_bias_new = fc1_bias - VEC_RATE * (bias_step * clip_scale(bias_norm / FF))

    qkv_row_full, qkv_col_new, qkv_new_full = adafactor_matrix(
        qkv_whole, qkv_row, qkv_col, qkv_weight, D ** (-0.5)
    )
    proj_row_full, proj_col_new, proj_new_full = adafactor_matrix(
        proj_whole, proj_row, proj_col, proj_weight, (D // 8) ** (-0.5)
    )
    start = lax.axis_index(("win", "mlp")) * 3
    mine = lambda full: lax.dynamic_slice_in_dim(full, start, 3, 0)
    qkv_new = mine(qkv_new_full)
    proj_new = mine(proj_new_full)
    small_state_new, small_new = vector_update(small_grad, small_state, small_params)
    table_state_new, table_new = vector_update(table_grad, table_state, rel_table)
    return (
        out, gin,
        mine(qkv_whole), mine(qkv_row_full), qkv_col_new, qkv_new, qkv_new.astype(BF16),
        mine(proj_whole), mine(proj_row_full), proj_col_new, proj_new, proj_new.astype(BF16),
        up_grad, fc1_row_new, fc1_col_new, fc1_new, fc1_new.astype(BF16),
        down_grad, fc2_row_new, fc2_col_new, fc2_new, fc2_new.astype(BF16),
        bias_grad, fc1_bias_state_new, fc1_bias_new,
        small_grad, small_state_new, small_new,
        table_grad, table_state_new, table_new,
    )


def solution(mesh):
    tokens, owner = P(("win", "mlp"), None), P(("win", "mlp"))
    whole, part = P(), P("mlp")
    return jax.shard_map(
        per_device,
        mesh=mesh,
        in_specs=(
            tokens, tokens, owner, owner, whole, whole, whole, whole, P(None, "mlp"), part, P("mlp", None),
            whole, whole, whole, whole, whole, part, part, whole, part, whole, whole,
        ),
        out_specs=(
            tokens, tokens,
            tokens, owner, whole, tokens, tokens,
            tokens, owner, whole, tokens, tokens,
            P(None, "mlp"), whole, part, P(None, "mlp"), P(None, "mlp"),
            P("mlp", None), part, whole, P("mlp", None), P("mlp", None),
            part, part, part,
            whole, whole, whole,
            whole, whole, whole,
        ),
        check_vma=False,
    )
```

```python
import functools
import math

import jax
import jax.numpy as jnp
from jax import lax
from jax.experimental import pallas as pl
from jax.experimental.pallas import tpu as pltpu
from jax.sharding import PartitionSpec as P

D = 384
FF = 1536
QKV = 3 * D
HEADS = 12
WIN = 7
SPAN = WIN * WIN
STEP = 10
DECAY = 1.0 - STEP ** (-0.8)
EPS_NORM = 1e-05
EPS_SQ = 1e-30
VEC_RATE = 0.3
SCALE = 32 ** (-0.5)
FAR = -1e30

GROUPS = 3
PER = 8
G_TOK = PER * SPAN
G_ROWS = 400
ROWS = GROUPS * G_ROWS
TOK = GROUPS * G_TOK
CHUNK = 64
KEYS = 56
SETS = 3
LANES = 4 * CHUNK

MESH = pl.DeviceIdType.MESH
F32 = jnp.float32
BF16 = jnp.bfloat16


def dot(a, b):
    return jnp.dot(a, b, preferred_element_type=F32)


def dot_nt(a, b):
    return lax.dot_general(a, b, (((1,), (1,)), ((), ())), preferred_element_type=F32)


def dot_tn(a, b):
    return lax.dot_general(a, b, (((0,), (0,)), ((), ())), preferred_element_type=F32)


def dot_exact(a, b):
    return jnp.dot(a, b, precision=lax.Precision.HIGHEST, preferred_element_type=F32)


def iota(shape, dim):
    return lax.broadcasted_iota(jnp.int32, shape, dim)


def fold_rows(x):
    total = x[0:8]
    for i in range(1, x.shape[0] // 8):
        total = total + x[8 * i : 8 * i + 8]
    return total


def row_mean(x):
    return jnp.sum(x, axis=1, keepdims=True) * (1.0 / D)


def normalize(x):
    center = x - row_mean(x)
    inverse = lax.rsqrt(row_mean(center * center) + EPS_NORM)
    return center * inverse, inverse


def normalize_back(u, gain, scaled, inverse):
    weighted = u * gain
    return inverse * (weighted - row_mean(weighted) - scaled * row_mean(weighted * scaled))


def gelu_parts(v):
    e = jnp.exp(-0.5 * v * v)
    t = 1.0 / (1.0 + (0.3275911 * 0.5**0.5) * jnp.abs(v))
    poly = 1.061405429 * t - 1.453152027
    poly = poly * t + 1.421413741
    poly = poly * t - 0.284496736
    poly = poly * t + 0.254829592
    tail = (0.5 * e) * (poly * t)
    phi = jnp.where(v < 0.0, tail, 1.0 - tail)
    return v * phi, phi + v * e * (2.0 * math.pi) ** (-0.5)


def barrel(x, amount, right):
    width = x.shape[1]
    for k in range(7):
        step = 1 << k
        moved = pltpu.roll(x, step if right else width - step, 1)
        x = jnp.where((amount & step) != 0, moved, x)
    return x


def embed(i):
    return 13 * (i // WIN) + i % WIN


def chunk_start(w):
    return pl.multiple_of((w // PER) * G_ROWS + (w % PER) * 48, 16)


def prologue(region, table, x_ref, emask, bias, mask, tok):
    for a in range(GROUPS):
        for r in range(0, G_TOK, 56):
            src = a * G_TOK + r
            low = src // 16 * 16
            x_ref[a * G_ROWS + r : a * G_ROWS + r + 56, :] = (
                tok[low : low + 64 if low + 64 <= TOK else TOK, :].astype(F32)[src - low : src - low + 56]
            )
        x_ref[a * G_ROWS + G_TOK : (a + 1) * G_ROWS, :] = jnp.zeros((G_ROWS - G_TOK, D), F32)
    row = iota((LANES, 128), 0)
    lane = iota((LANES, 128), 1)
    for b in range(PER):
        i = row % CHUNK
        keep = (i >= b) & (i < b + SPAN) & (lane // 32 == row // CHUNK)
        emask[b] = jnp.where(keep, 1.0, 0.0).astype(BF16)
    j = iota((KEYS, 256), 0)
    amount = jnp.maximum(84 - embed(j), 0)
    jl = iota((KEYS, LANES), 0)
    il = iota((KEYS, LANES), 1) % CHUNK
    for g in range(SETS):
        base = jnp.zeros((KEYS, LANES), F32)
        for h in range(4):
            wide = jnp.broadcast_to(table[4 * g + h : 4 * g + h + 1, :], (KEYS, 256))
            wide = barrel(wide, amount, False)[:, :128]
            lane_to = iota((128, LANES), 1) - CHUNK * h
            pick = (iota((128, LANES), 0) == embed(lane_to)) & (lane_to >= 0) & (lane_to < SPAN)
            base = base + dot_exact(wide, jnp.where(pick, 1.0, 0.0))
        for b in range(PER):
            moved = pltpu.roll(pltpu.roll(base, b, 0), b, 1) if b else base
            key_ok = (jl >= b) & (jl < b + SPAN)
            query_ok = (il >= b) & (il < b + SPAN)
            bias[b, g] = jnp.where(key_ok, jnp.where(query_ok, moved, 0.0), FAR)
    eye = iota((CHUNK, CHUNK), 0) == iota((CHUNK, CHUNK), 1)
    for w in range(GROUPS * PER):
        start = (w // PER) * G_TOK + (w % PER) * 48
        line = region[:, start : start + CHUNK]
        column = jnp.sum(jnp.where(eye, jnp.broadcast_to(line, (CHUNK, CHUNK)), 0.0), axis=1, keepdims=True)
        wide = jnp.concatenate([line] * 4, axis=1)
        mask[w] = jnp.where(column[:KEYS] != wide, -100.0, 0.0)


def pad_keys(x):
    return jnp.concatenate([x, jnp.zeros((CHUNK - KEYS, x.shape[1]), x.dtype)], axis=0)


def spread(x, keep):
    return jnp.concatenate([x] * 4, axis=0) * keep


def collect(full):
    head = iota((CHUNK, 128), 1) // 32
    parts = [full[CHUNK * h : CHUNK * (h + 1)] for h in range(4)]
    low = jnp.where(head == 0, parts[0], parts[1])
    high = jnp.where(head == 2, parts[2], parts[3])
    return jnp.where(head < 2, low, high)


def block_kernel(
    live_tokens, tok, og, region, wq, wp, table, small, fc1, fc2, fc1_b, fc1_state, fc1_col, fc2_row, qkv_row, proj_row,
    out, gin, fin, vec, fc_sums, at_sums, own_g, own_r, own_wq, own_wp, b1,
    x_ref, xh1, inv1, inv2, n1, n2, qkv, att_b, probs, back, hidden, ig, dqkv,
    emask, bias, mask, tacc, s1, s2, sums, b1_acc, wq_b, wp_b, w1, w2,
    fcl, fr1, fr2, ft, fr3, fu, fr4, fst, atl, ar1, ar2, ar3, ar4, ast, vb,
    w_send, w_recv, pair_send, pair_recv, f1s, f1r, f2s, f2r, f3s, f3r, f4s, f4r, f5s, f5r, f6s, f6r, f7s, f7r, f8s, f8r,
    a1s, a1r, a2s, a2r, a3s, a3r, a4s, a4r, a5s, a5r, v1s, v1r, v2s, v2r, v3s, v3r, v4s, v4r,
):
    win, mlp = lax.axis_index("win"), lax.axis_index("mlp")
    z, y, core = win // 8, (win // 2) % 4, win % 2
    pair = win + 1 - 2 * core

    def along_x(d):
        return win, (mlp + d) % 4

    def along_y(d):
        return z * 8 + ((y + d) % 4) * 2 + core, mlp

    def along_z(d):
        return ((z + d) % 4) * 8 + y * 2 + core, mlp

    def class_peer(d):
        return pair if d >= 4 else win, (mlp + d) % 4

    barrier = pltpu.get_barrier_semaphore()
    peers = [class_peer(d) for d in range(1, 8)]
    peers += [along_y(d) for d in range(1, 4)] + [along_z(d) for d in range(1, 4)]
    for peer in peers:
        pl.semaphore_signal(barrier, inc=1, device_id=peer, device_id_type=MESH)

    def remote(src, dst, send, recv, peer):
        return pltpu.make_async_remote_copy(
            src_ref=src, dst_ref=dst, send_sem=send, recv_sem=recv, device_id=peer, device_id_type=MESH
        )

    def param(part):
        return small[:, D * part : D * part + D]

    pending = []

    def start(copy):
        copy.start()
        pending.append(copy)
        return copy

    def shard(m):
        at = pl.multiple_of(m * D, D)
        half = pl.ds(pl.multiple_of(core * (D // 2), 16), D // 2)
        half_at = pl.ds(pl.multiple_of(m * D + core * (D // 2), 16), D // 2)
        return w1.at[half, pl.ds(at, D)], w2.at[half_at, :], b1.at[m]

    mine = shard(mlp)
    cols = pl.ds(pl.multiple_of(mlp * D, D), D)
    w1[:, cols] = fc1[...].astype(BF16)
    w2[cols, :] = fc2[...].astype(BF16)
    b1[mlp, 0:4] = jnp.broadcast_to(fc1_b[...], (4, D))
    b1[mlp, 4:8] = jnp.broadcast_to(fc1_state[...], (4, D))
    pl.semaphore_wait(barrier, 13)
    sends = []
    for d in range(1, 4):
        for n in range(3):
            sends.append(start(remote(mine[n], mine[n], w_send.at[d - 1, n], w_recv.at[d - 1, n], along_x(d))))

    prologue(region, table, x_ref, emask, bias, mask, tok)
    live = live_tokens[0]
    wq_b[...] = wq[...].astype(BF16)
    wp_b[...] = wp[...].astype(BF16)
    sums[...] = jnp.zeros_like(sums)
    b1_acc[...] = jnp.zeros_like(b1_acc)
    tacc[...] = jnp.zeros_like(tacc)
    att = dqkv.at[:, :D]
    xh2 = dqkv.at[:, D : 2 * D]
    wide_q = ig.at[:D, :QKV]
    dqkv[:, :D] = jnp.zeros((ROWS, D), F32)

    for a in range(GROUPS):
        for r in range(0, G_TOK, 56):
            src = a * G_TOK + r
            low = src // 16 * 16
            rows = og[low : low + 64 if low + 64 <= TOK else TOK, :].astype(F32)[src - low : src - low + 56]
            keep = iota((56, D), 0) + src < live
            x = jnp.where(keep, rows, 0.0)
            s2[r : r + 56, :] = x
            sums[7] += fold_rows(x)
        s2[G_TOK:G_ROWS, :] = jnp.zeros((G_ROWS - G_TOK, D), F32)
        back[a * G_ROWS : (a + 1) * G_ROWS, :] = s2[...].astype(BF16)

    @pl.loop(0, ROWS // 80)
    def _(t):
        for c in range(5):
            rows = pl.ds(pl.multiple_of(t * 80 + c * 16, 16), 16)
            scaled, inverse = normalize(x_ref[rows, :])
            xh1[rows, :] = scaled
            inv1[rows, :] = inverse
            n1[rows, :] = (scaled * param(0) + param(1)).astype(BF16)

    for part in range(3):
        shift = None if part == 1 else param(2 + part // 2)

        @pl.loop(0, GROUPS)
        def _(a):
            rows = pl.ds(pl.multiple_of(a * G_ROWS, 16), G_ROWS)
            r = dot(n1[rows, :], wq_b[:, part * D : (part + 1) * D])
            if shift is not None:
                r = r + shift
            qkv[rows, part * D : (part + 1) * D] = r.astype(BF16)

    @pl.loop(0, PER)
    def _(b):
        for a in range(GROUPS):
            rows = pl.ds(pl.multiple_of(a * G_ROWS + b * 48, 16), CHUNK)
            w = a * PER + b
            for g in range(SETS):
                q = qkv[rows, 128 * g : 128 * g + 128]
                k = qkv[rows, D + 128 * g : D + 128 * g + 128]
                v = qkv[rows, 2 * D + 128 * g : 2 * D + 128 * g + 128]
                scores = dot_nt(k, spread(q, emask[b]))[:KEYS] * SCALE + (bias[b, g] + mask[w])
                p = jnp.exp(scores - jnp.max(scores, axis=0, keepdims=True))
                p = p * (1.0 / jnp.sum(p, axis=0, keepdims=True))
                probs[w, g] = p
                o = collect(dot_tn(pad_keys(p).astype(BF16), v))
                i = iota((CHUNK, 128), 0)
                att[rows, 128 * g : 128 * g + 128] += jnp.where((i >= b) & (i < b + SPAN), o, 0.0)

    forwards = []
    for d in range(1, 4):
        came = shard((mlp + 4 - d) % 4)
        for n in range(3):
            sends[3 * (d - 1) + n].wait_recv()
            if n < 2:
                copy = remote(came[n], came[n], pair_send.at[d - 1, n], pair_recv.at[d - 1, n], (pair, mlp))
                forwards.append(start(copy))

    @pl.loop(0, GROUPS)
    def _(a):
        rows = pl.ds(pl.multiple_of(a * G_ROWS, 16), G_ROWS)
        att_b[rows, :] = att[rows, :].astype(BF16)
        s1[...] = dot(att_b[rows, :], wp_b[...])

        @pl.loop(0, 5)
        def _(t):
            for c in range(5):
                here = pl.multiple_of(t * 80 + c * 16, 16)
                rows = pl.ds(pl.multiple_of(a * G_ROWS + here, 16), 16)
                middle = x_ref[rows, :] + (s1[pl.ds(here, 16), :] + param(4))
                x_ref[rows, :] = middle
                scaled, inverse = normalize(middle)
                xh2[rows, :] = scaled
                inv2[rows, :] = inverse
                n2[rows, :] = (scaled * param(5) + param(6)).astype(BF16)

    for copy in forwards:
        copy.wait_recv()

    @pl.loop(0, 5)
    def _(mt):
        rows = pl.ds(pl.multiple_of(mt * 240, 16), 240)
        b1_row = jnp.concatenate([b1[m, 0:1, :] for m in range(4)], axis=1)
        for nt in range(6):
            cols = slice(256 * nt, 256 * nt + 256)
            inner = dot(n2[rows, :], w1[:, cols]) + b1_row[:, cols]
            up = dot_nt(back[rows, :], w2[cols, :])
            total = b1_acc[:, cols]
            for c in range(15):
                act, slope = gelu_parts(inner[16 * c : 16 * c + 16])
                here = pl.ds(pl.multiple_of(mt * 240 + 16 * c, 16), 16)
                hidden[here, cols] = act.astype(BF16)
                grad = (up[16 * c : 16 * c + 16] * slope).astype(BF16)
                ig[here, cols] = grad
                total = total + fold_rows(grad.astype(F32))
            b1_acc[:, cols] = total

    g2 = dot_tn(hidden[...], back[...]).astype(BF16)
    g1 = dot_tn(n2[...], ig[...]).astype(BF16)
    for m in range(4):
        fcl[0, m] = g1[:, D * m : D * m + D].reshape(4, 96, D)
        fcl[1, m] = g2[D * m : D * m + D].reshape(4, 96, D)
    fc_one = [start(remote(fcl.at[1 - core, m], fr1.at[m], f1s.at[m], f1r.at[m], (pair, mlp))) for m in range(4)]

    for a in range(GROUPS):
        rows = slice(a * G_ROWS, (a + 1) * G_ROWS)
        s1[...] = dot(hidden[rows, :], w2[...])
        s2[...] = dot_nt(ig[rows, :], w1[...])
        for c in range(25):
            here = slice(16 * c, 16 * c + 16)
            at = slice(a * G_ROWS + 16 * c, a * G_ROWS + 16 * c + 16)
            size = 16 if c < 24 else 8
            src = a * G_TOK + 16 * c
            r = x_ref[at, :] + (s1[here, :] + param(7))
            keep = iota((16, D), 0) + src < live
            out[src : src + size, :] = jnp.where(keep, r, 0.0)[:size]
            u = s2[here, :]
            scaled = xh2[at, :]
            sums[5] += fold_rows(u * scaled)
            sums[6] += fold_rows(u)
            mg = normalize_back(u, param(5), scaled, inv2[at, :]) + back[at, :].astype(F32)
            x_ref[at, :] = mg
            low = mg.astype(BF16)
            n2[at, :] = low
            sums[4] += fold_rows(low.astype(F32))

    p = iota((D, D), 0)
    inner_p = p % 48
    owned = 24 * (inner_p // 3) + 12 * (p // 192) + 3 * ((p // 48) % 4) + inner_p % 3
    order = jnp.where(iota((D, D), 1) == owned, 1.0, 0.0).astype(BF16)

    def ordered(grad):
        return dot(order, grad.astype(BF16)).astype(BF16).reshape(2, 4, 48, D)

    def at_one(n):
        return remote(atl.at[n, 1 - core], ar1.at[n], a1s.at[n], a1r.at[n], (pair, mlp))

    def at_add_one(n):
        at_one(n).wait_recv()
        for i in range(4):
            ar1[n, i] = (ar1[n, i].astype(F32) + atl[n, core, i].astype(F32)).astype(BF16)
        for d in range(1, 4):
            start(remote(ar1.at[n, (mlp + d) % 4], ar2.at[n, d - 1], a2s.at[n, d - 1], a2r.at[n, d - 1], along_x(d)))

    def at_add_two(n):
        total = ar1[n, mlp].astype(F32)
        for d in range(1, 4):
            remote(ar1.at[n, 0], ar2.at[n, d - 1], a2s.at[n, d - 1], a2r.at[n, d - 1], along_x(d)).wait_recv()
            total = total + ar2[n, d - 1].astype(F32)
        ar3[n, y] = total.astype(BF16)
        for d in range(1, 4):
            start(remote(ar3.at[n, y], ar3.at[n, y], a3s.at[n, d - 1], a3r.at[n, d - 1], along_y(d)))

    def at_add_three(n):
        for d in range(1, 4):
            came = ar3.at[n, (y + 4 - d) % 4]
            remote(came, came, a3s.at[n, d - 1], a3r.at[n, d - 1], along_y(d)).wait_recv()
        total = ar3[n, 0].astype(F32) + ar3[n, 1].astype(F32)
        ar4[n, z] = (total + ar3[n, 2].astype(F32) + ar3[n, 3].astype(F32)).astype(BF16)
        for d in range(1, 4):
            start(remote(ar4.at[n, z], ar4.at[n, z], a4s.at[n, d - 1], a4r.at[n, d - 1], along_z(d)))

    def at_add_four(n):
        for d in range(1, 4):
            came = ar4.at[n, (z + 4 - d) % 4]
            remote(came, came, a4s.at[n, d - 1], a4r.at[n, d - 1], along_z(d)).wait_recv()
        total = ar4[n, 0].astype(F32) + ar4[n, 1].astype(F32)
        return total + ar4[n, 2].astype(F32) + ar4[n, 3].astype(F32)

    def first_axis(d):
        return z * 8 + ((y + d * core) % 4) * 2 + core, (mlp + d * (1 - core)) % 4

    def second_axis(d):
        return z * 8 + ((y + d * (1 - core)) % 4) * 2 + core, (mlp + d * core) % 4

    second = y * (1 - core) + mlp * core

    def fc_two(d):
        return remote(fr1.at[0], fr2.at[d - 1], f2s.at[d - 1], f2r.at[d - 1], first_axis(d))

    def fc_add_one():
        for m in range(4):
            fc_one[m].wait_recv()
            for i in range(4):
                fr1[m, i] = (fr1[m, i].astype(F32) + fcl[core, m, i].astype(F32)).astype(BF16)

        @pl.when(core == 0)
        def _():
            for d in range(1, 4):
                remote(fr1.at[(mlp + d) % 4], fr2.at[d - 1], f2s.at[d - 1], f2r.at[d - 1], first_axis(d)).start()

        @pl.when(core == 1)
        def _():
            for d in range(1, 4):
                remote(fr1.at[:, (y + d) % 4], fr2.at[d - 1], f2s.at[d - 1], f2r.at[d - 1], first_axis(d)).start()

    def fc_add_two():
        for d in range(1, 4):
            fc_two(d).wait_recv()
        for i in range(4):
            total = fr1[mlp * (1 - core) + i * core, i * (1 - core) + y * core].astype(F32)
            for d in range(1, 4):
                total = total + fr2[d - 1, i].astype(F32)
            ft[i] = total.astype(BF16)
        for d in range(1, 4):
            start(remote(ft.at[(second + d) % 4], fr3.at[d - 1], f3s.at[d - 1], f3r.at[d - 1], second_axis(d)))

    def fc_add_three():
        total = ft[second].astype(F32)
        for d in range(1, 4):
            remote(ft.at[0], fr3.at[d - 1], f3s.at[d - 1], f3r.at[d - 1], second_axis(d)).wait_recv()
            total = total + fr3[d - 1].astype(F32)
        fu[...] = total.reshape(4, 24, D)
        for d in range(1, 4):
            start(remote(fu.at[(z + d) % 4], fr4.at[d - 1], f4s.at[d - 1], f4r.at[d - 1], along_z(d)))

    def spread_first(d):
        return ((z + d * (1 - core)) % 4) * 8 + ((y + d * core) % 4) * 2 + core, mlp

    def spread_second(d):
        return ((z + d * core) % 4) * 8 + ((y + d * (1 - core)) % 4) * 2 + core, mlp

    def fc_add_four():
        total = fu[z]
        for d in range(1, 4):
            remote(fu.at[0], fr4.at[d - 1], f4s.at[d - 1], f4r.at[d - 1], along_z(d)).wait_recv()
            total = total + fr4[d - 1]
        fin[core, y, z] = total
        for d in range(1, 4):
            place = fin.at[core, y, z]
            start(remote(place, place, f5s.at[d - 1], f5r.at[d - 1], spread_first(d)))

    def fc_spread_two():
        for d in range(1, 4):
            place = fin.at[core, (y + 4 - d * core) % 4, (z + 4 - d * (1 - core)) % 4]
            remote(place, place, f5s.at[d - 1], f5r.at[d - 1], spread_first(d)).wait_recv()

        @pl.when(core == 0)
        def _():
            for d in range(1, 4):
                place = fin.at[core, y]
                remote(place, place, f6s.at[d - 1], f6r.at[d - 1], spread_second(d)).start()

        @pl.when(core == 1)
        def _():
            for d in range(1, 4):
                place = fin.at[core, :, z]
                remote(place, place, f6s.at[d - 1], f6r.at[d - 1], spread_second(d)).start()

    def fc_six(d):
        return remote(fin.at[core, y], fin.at[core, (y + 4 - d) % 4], f6s.at[d - 1], f6r.at[d - 1], spread_second(d))

    def fc_spread_three():
        @pl.when(core == 0)
        def _():
            for d in range(1, 4):
                place = fin.at[core, (y + 4 - d) % 4]
                remote(place, place, f6s.at[d - 1], f6r.at[d - 1], spread_second(d)).wait_recv()

        @pl.when(core == 1)
        def _():
            for d in range(1, 4):
                place = fin.at[core, :, (z + 4 - d) % 4]
                remote(place, place, f6s.at[d - 1], f6r.at[d - 1], spread_second(d)).wait_recv()

        start(remote(fin.at[core], fin.at[core], f7s.at[0], f7r.at[0], (pair, mlp)))

    atl[3] = ordered(dot_tn(att_b[...], n2[...]))
    start(at_one(3))

    @pl.loop(0, GROUPS)
    def _(a):
        rows = pl.ds(pl.multiple_of(a * G_ROWS, 16), G_ROWS)
        att_b[rows, :] = dot_nt(n2[rows, :], wp_b[...]).astype(BF16)

    dqkv[...] = jnp.zeros_like(dqkv)

    def attention_back(g, half):
        @pl.loop(4 * half, 4 * half + 4)
        def _(b):
            keep = emask[b]
            total = tacc[b, g]
            for a in range(GROUPS):
                rows = pl.ds(pl.multiple_of(a * G_ROWS + b * 48, 16), CHUNK)
                q = qkv[rows, 128 * g : 128 * g + 128]
                k = qkv[rows, D + 128 * g : D + 128 * g + 128]
                v = qkv[rows, 2 * D + 128 * g : 2 * D + 128 * g + 128]
                qe = spread(q, keep)
                da = spread(att_b[rows, 128 * g : 128 * g + 128], keep)
                p = probs[a * PER + b, g]
                dp = dot_nt(v, da)[:KEYS]
                pd = p * dp
                ds = pad_keys(pd - p * jnp.sum(pd, axis=0, keepdims=True)).astype(BF16)
                total = total + ds.astype(F32)[:KEYS]
                dv = dot(pad_keys(p).astype(BF16), da)
                dk = dot(ds, qe) * SCALE
                dq = collect(dot_tn(ds, k)) * SCALE
                dqkv[rows, 384 * g : 384 * g + 128] += dq
                dqkv[rows, 384 * g + 128 : 384 * g + 256] += dk
                dqkv[rows, 384 * g + 256 : 384 * g + 384] += dv
            tacc[b, g] = total

    def qkv_grad(g):
        group = slice(384 * g, 384 * g + 384)

        @pl.loop(0, ROWS // 80)
        def _(t):
            for c in range(5):
                rows = pl.ds(pl.multiple_of(t * 80 + c * 16, 16), 16)
                low = dqkv[rows, group].astype(BF16)
                hidden[rows, group] = low
                wide = low.astype(F32)
                sums[2, :, 128 * g : 128 * g + 128] += fold_rows(wide[:, :128])
                sums[3, :, 128 * g : 128 * g + 128] += fold_rows(wide[:, 256:])

        atl[g] = ordered(dot_tn(n1[...], hidden[:, group]))
        start(at_one(g))

    attention_back(0, 0)
    fc_add_one()
    at_add_one(3)
    attention_back(0, 1)
    qkv_grad(0)
    at_add_two(3)
    attention_back(1, 0)
    fc_add_two()
    at_add_one(0)
    at_add_three(3)
    attention_back(1, 1)
    qkv_grad(1)
    fc_add_three()
    at_add_two(0)
    attention_back(2, 0)
    fc_add_four()
    at_add_three(0)
    at_add_one(1)
    attention_back(2, 1)
    qkv_grad(2)
    fc_spread_two()
    at_add_two(1)

    for g in range(SETS):
        for part in range(3):
            wide_q[:, 128 * (3 * g + part) : 128 * (3 * g + part) + 128] = wq_b[
                :, D * part + 128 * g : D * part + 128 * g + 128
            ]

    def input_back(a):
        rows = slice(a * G_ROWS, (a + 1) * G_ROWS)
        s1[...] = dot_nt(hidden[rows, :QKV], wide_q[...])
        for c in range(25):
            here = slice(16 * c, 16 * c + 16)
            at = slice(a * G_ROWS + 16 * c, a * G_ROWS + 16 * c + 16)
            size = 16 if c < 24 else 8
            src = a * G_TOK + 16 * c
            u = s1[here, :]
            scaled = xh1[at, :]
            sums[0] += fold_rows(u * scaled)
            sums[1] += fold_rows(u)
            r = normalize_back(u, param(0), scaled, inv1[at, :]) + x_ref[at, :]
            gin[src : src + size, :] = r[:size]

    input_back(0)
    at_add_one(2)
    fc_spread_three()
    at_add_three(1)
    input_back(1)
    at_add_two(2)
    input_back(2)
    at_add_three(2)

    vec_own = vb.at[0, core]
    for part in range(8):
        vec_own[part : part + 1, :] = jnp.sum(sums[part], axis=0, keepdims=True)
    for m in range(4):
        vec_own[20 + m : 21 + m, :] = jnp.sum(b1_acc[:, D * m : D * m + D], axis=0, keepdims=True)
    j = iota((KEYS, 256), 0)
    amount = jnp.maximum(84 - embed(j), 0)
    for g in range(SETS):
        total = tacc[0, g]
        for b in range(1, PER):
            total = total + pltpu.roll(pltpu.roll(tacc[b, g], KEYS - b, 0), LANES - b, 1)
        for h in range(4):
            lane_from = iota((LANES, 256), 0) - CHUNK * h
            pick = (iota((LANES, 256), 1) == embed(lane_from)) & (lane_from >= 0) & (lane_from < SPAN)
            wide = barrel(dot_exact(total, jnp.where(pick, 1.0, 0.0)), amount, True)
            wide = jnp.where(j < SPAN, wide, 0.0)
            vec_own[8 + 4 * g + h : 9 + 4 * g + h, :] = jnp.concatenate(
                [jnp.sum(wide, axis=0, keepdims=True), jnp.zeros((1, 128), F32)], axis=1
            )
    start(remote(vec_own, vec_own, v1s.at[0], v1r.at[0], (pair, mlp)))
    remote(vec_own, vb.at[0, 1 - core], v1s.at[0], v1r.at[0], (pair, mlp)).wait_recv()
    vb[1, mlp] = vb[0, 0] + vb[0, 1]

    def vec_step(n, me, send, recv, peer):
        for d in range(1, 4):
            place = vb.at[n, me]
            start(remote(place, place, send.at[d - 1], recv.at[d - 1], peer(d)))

    def vec_total(n, me, send, recv, peer):
        for d in range(1, 4):
            place = vb.at[n, (me + 4 - d) % 4]
            remote(place, place, send.at[d - 1], recv.at[d - 1], peer(d)).wait_recv()
        return (vb[n, 0] + vb[n, 1]) + (vb[n, 2] + vb[n, 3])

    vec_step(1, mlp, v2s, v2r, along_x)

    remote(fin.at[1 - core], fin.at[1 - core], f7s.at[0], f7r.at[0], (pair, mlp)).wait_recv()
    eye = iota((D, D), 0) == iota((D, D), 1)

    def to_row(column):
        return jnp.sum(jnp.where(eye, column, 0.0), axis=0, keepdims=True)

    up = fin[0].reshape(D, D)
    down = fin[1].reshape(D, D)
    up_squares = up * up
    down_squares = down * down
    up_col = DECAY * fc1_col[...] + (1.0 - DECAY) * (jnp.sum(up_squares, axis=0, keepdims=True) * (1.0 / D) + EPS_SQ)
    down_row = DECAY * to_column(fc2_row[...], eye) + (1.0 - DECAY) * (row_mean(down_squares) + EPS_SQ)
    fst[mlp, 0:1] = to_row(jnp.sum(up_squares, axis=1, keepdims=True))
    fst[mlp, 1:2] = to_row(jnp.sum(up_squares * (1.0 / up_col), axis=1, keepdims=True))
    fst[mlp, 2:3] = jnp.sum(down_squares, axis=0, keepdims=True)
    fst[mlp, 3:4] = jnp.sum(down_squares * (1.0 / down_row), axis=0, keepdims=True)
    fst[mlp, 4:5] = jnp.broadcast_to(jnp.sum(down_row, axis=0, keepdims=True), (1, D))
    fst[mlp, 5:6] = up_col
    fst[mlp, 6:7] = to_row(down_row)
    fst[mlp, 7:8] = jnp.zeros((1, D), F32)
    for d in range(1, 4):
        start(remote(fst.at[mlp], fst.at[mlp], f8s.at[d - 1], f8r.at[d - 1], along_x(d)))

    vb[2, y] = vec_total(1, mlp, v2s, v2r, along_x)
    vec_step(2, y, v3s, v3r, along_y)

    totals = [at_add_four(n) for n in (3, 0, 1, 2)]
    totals = totals[1:] + totals[:1]
    r48 = iota((48, D), 0)
    pick = iota((48, D), 1) == 24 * (r48 // 3) + 12 * core + 3 * mlp + r48 % 3
    squares = [t * t for t in totals]

    def rows_new(state, mean):
        old = jnp.sum(jnp.where(pick, state, 0.0), axis=1, keepdims=True)
        return DECAY * old + (1.0 - DECAY) * (mean + EPS_SQ)

    qkv_new_row = rows_new(qkv_row[...], row_mean(squares[0] + squares[1] + squares[2]) * (1.0 / 3.0))
    proj_new_row = rows_new(proj_row[...], row_mean(squares[3]))
    mine_at = 4 * core + mlp
    for n in range(4):
        over = squares[n] * (1.0 / (qkv_new_row if n < 3 else proj_new_row))
        ast[mine_at, n : n + 1] = jnp.sum(squares[n], axis=0, keepdims=True)
        ast[mine_at, 4 + n : 5 + n] = jnp.sum(over, axis=0, keepdims=True)
    ast[mine_at, 8:9] = jnp.broadcast_to(jnp.sum(qkv_new_row, axis=0, keepdims=True), (1, D))
    ast[mine_at, 9:10] = jnp.broadcast_to(jnp.sum(proj_new_row, axis=0, keepdims=True), (1, D))
    ast[mine_at, 10:16] = jnp.zeros((6, D), F32)

    def at_five(d):
        place = ast.at[mine_at]
        return remote(place, place, a5s.at[d - 1], a5r.at[d - 1], class_peer(d))

    for d in range(1, 8):
        start(at_five(d))

    offset = 48 - 3 * (4 * z + y)
    for n in range(4):
        own_g[n] = pltpu.roll(totals[n], offset, 0)[:8]
    own_r[0] = pltpu.roll(jnp.broadcast_to(qkv_new_row, (48, 128)), offset, 0)[:8]
    own_r[1] = pltpu.roll(jnp.broadcast_to(proj_new_row, (48, 128)), offset, 0)[:8]
    block_rows = pl.ds(pl.multiple_of(24 * (win // 2), 8), 24)
    shift = 24 - 3 * (4 * core + mlp)
    own_wq[...] = pltpu.roll(wq[block_rows, :], shift, 0)[:8]
    own_wp[...] = pltpu.roll(wp[block_rows, :], shift, 0)[:8]

    vb[3, z] = vec_total(2, y, v3s, v3r, along_y)
    vec_step(3, z, v4s, v4r, along_z)

    for d in range(1, 4):
        place = fst.at[(mlp + 4 - d) % 4]
        remote(place, place, f8s.at[d - 1], f8r.at[d - 1], along_x(d)).wait_recv()
    total = (fst[0] + fst[1]) + (fst[2] + fst[3])
    fc_sums[0] = total
    fc_sums[1] = fst[mlp]

    for d in range(1, 8):
        place = ast.at[(4 * core + mlp + 8 - d) % 4 + 4 * (core if d < 4 else 1 - core)]
        remote(place, place, a5s.at[d - 1], a5r.at[d - 1], class_peer(d)).wait_recv()
    total = ast[0]
    for n in range(1, 8):
        total = total + ast[n]
    at_sums[...] = total

    vec[...] = vec_total(3, z, v4s, v4r, along_z)

    for copy in pending:
        copy.wait_send()
    for d in range(1, 4):
        fc_two(d).wait_send()
        fc_six(d).wait_send()


def to_column(row, eye):
    return jnp.sum(jnp.where(eye, row, 0.0), axis=1, keepdims=True)


def block(live_tokens, *arrays):
    sd = jax.ShapeDtypeStruct
    vm = pltpu.VMEM
    dma = pltpu.SemaphoreType.DMA
    return pl.pallas_call(
        block_kernel,
        out_shape=[
            sd((TOK, D), F32),
            sd((TOK, D), F32),
            sd((2, 4, 4, 24, D), F32),
            sd((24, D), F32),
            sd((2, 8, D), F32),
            sd((16, D), F32),
            sd((4, 8, D), F32),
            sd((2, 8, 128), F32),
            sd((8, QKV), F32),
            sd((8, D), F32),
            sd((4, 8, D), F32),
        ],
        in_specs=[pl.BlockSpec(memory_space=pltpu.SMEM)] + [pl.BlockSpec(memory_space=vm)] * len(arrays),
        out_specs=[pl.BlockSpec(memory_space=vm)] * 11,
        scratch_shapes=[
            vm((ROWS, D), F32),
            vm((ROWS, D), F32),
            vm((ROWS, 1), F32),
            vm((ROWS, 1), F32),
            vm((ROWS, D), BF16),
            vm((ROWS, D), BF16),
            vm((ROWS, QKV), BF16),
            vm((ROWS, D), BF16),
            vm((GROUPS * PER, SETS, KEYS, LANES), F32),
            vm((ROWS, D), BF16),
            vm((ROWS, FF), BF16),
            vm((ROWS, FF), BF16),
            vm((ROWS, QKV), F32),
            vm((PER, LANES, 128), BF16),
            vm((PER, SETS, KEYS, LANES), F32),
            vm((GROUPS * PER, KEYS, LANES), F32),
            vm((PER, SETS, KEYS, LANES), F32),
            vm((G_ROWS, D), F32),
            vm((G_ROWS, D), F32),
            vm((8, 8, D), F32),
            vm((8, FF), F32),
            vm((D, QKV), BF16),
            vm((D, D), BF16),
            vm((D, FF), BF16),
            vm((FF, D), BF16),
            vm((2, 4, 4, 96, D), BF16),
            vm((4, 4, 96, D), BF16),
            vm((3, 4, 96, D), BF16),
            vm((4, 96, D), BF16),
            vm((3, 96, D), BF16),
            vm((4, 24, D), F32),
            vm((3, 24, D), F32),
            vm((4, 8, D), F32),
            vm((4, 2, 4, 48, D), BF16),
            vm((4, 4, 48, D), BF16),
            vm((4, 3, 48, D), BF16),
            vm((4, 4, 48, D), BF16),
            vm((4, 4, 48, D), BF16),
            vm((8, 16, D), F32),
            vm((4, 4, 24, D), F32),
            dma((3, 3)), dma((3, 3)), dma((3, 2)), dma((3, 2)),
            dma((4,)), dma((4,)),
            dma((3,)), dma((3,)), dma((3,)), dma((3,)), dma((3,)), dma((3,)),
            dma((3,)), dma((3,)), dma((3,)), dma((3,)),
            dma((1,)), dma((1,)), dma((3,)), dma((3,)),
            dma((4,)), dma((4,)),
            dma((4, 3)), dma((4, 3)), dma((4, 3)), dma((4, 3)), dma((4, 3)), dma((4, 3)),
            dma((7,)), dma((7,)),
            dma((1,)), dma((1,)),
            dma((3,)), dma((3,)), dma((3,)), dma((3,)), dma((3,)), dma((3,)),
        ],
        compiler_params=pltpu.CompilerParams(
            vmem_limit_bytes=63 * 1024 * 1024, collective_id=0, has_side_effects=True
        ),
        cost_estimate=pl.CostEstimate(flops=14_000_000_000, bytes_accessed=20_000_000, transcendentals=3_000_000),
        name="block",
    )(live_tokens, *arrays)


def finish_kernel(
    fin, vec, fc_sums, at_sums, own_g, own_r, own_wq, own_wp, b1, fc1, fc2, fc1_b, fc1_row, fc2_col, qkv_col, proj_col,
    small, small_state, table, table_state,
    qkv_grad, qkv_row_new, qkv_col_new, qkv_new, qkv_low, proj_grad, proj_row_new, proj_col_new, proj_new, proj_low,
    fc1_grad, fc1_row_new, fc1_col_new, fc1_new, fc1_low, fc2_grad, fc2_row_new, fc2_col_new, fc2_new, fc2_low,
    b1_grad, b1_state_new, b1_new, small_grad, small_state_new, small_new, table_grad, table_state_new, table_new,
):
    mlp = lax.axis_index("mlp")
    eye = iota((D, D), 0) == iota((D, D), 1)
    eye8 = iota((8, 128), 0) == iota((8, 128), 1)

    def total(x):
        return jnp.sum(jnp.sum(x, axis=0, keepdims=True), axis=1, keepdims=True)

    def fresh(old, mean):
        return DECAY * old + (1.0 - DECAY) * (mean + EPS_SQ)

    def owned(grads, cols, over, row, row_total, weight, col_old, rate, outs):
        grad_out, row_out, col_out, new_out, low_out = outs
        width = grads.shape[1]
        col_new = fresh(col_old[...], cols * (1.0 / D))
        mean = row_total * (1.0 / D)
        norm = mean * jnp.sum(over * (1.0 / col_new), axis=1, keepdims=True) * (1.0 / (D * width))
        step = grads * lax.rsqrt(row * col_new * (1.0 / mean))
        new = weight - rate * (step * clip_scale(norm))
        grad_out[...] = grads[:3]
        row_out[...] = jnp.sum(jnp.where(eye8, row, 0.0), axis=0, keepdims=True)[:, :3]
        col_out[...] = col_new
        new_out[...] = new[:3]
        low_out[...] = new.astype(BF16)[:3]

    def by_part(take):
        return jnp.concatenate([take(g)[:, 128 * p : 128 * p + 128] for p in range(3) for g in range(SETS)], axis=1)

    owned(
        by_part(lambda g: own_g[g]), by_part(lambda g: at_sums[g : g + 1, :]),
        by_part(lambda g: at_sums[4 + g : 5 + g, :]), own_r[0][:, :1], at_sums[8:9, :1], own_wq[...], qkv_col,
        D ** (-0.5), (qkv_grad, qkv_row_new, qkv_col_new, qkv_new, qkv_low),
    )
    owned(
        own_g[3], at_sums[3:4, :], at_sums[7:8, :], own_r[1][:, :1], at_sums[9:10, :1], own_wp[...], proj_col,
        (D // 8) ** (-0.5), (proj_grad, proj_row_new, proj_col_new, proj_new, proj_low),
    )

    def update(grad, weight, row, col, mean, norm, rate, grad_out, new_out, low_out):
        row = row * (1.0 / mean)
        factor = rate * clip_scale(norm)
        for r in range(0, D, 48):
            rows = slice(r, r + 48)
            g = grad[rows, :]
            new = weight[rows, :] - (g * lax.rsqrt(row[rows] * col)) * factor
            grad_out[rows, :] = g
            new_out[rows, :] = new
            low_out[rows, :] = new.astype(BF16)

    row_new = fresh(fc1_row[...], fc_sums[0, 0:1, :] * (1.0 / FF))
    mean = row_mean(row_new)
    norm = mean * row_mean(fc_sums[0, 1:2, :] * (1.0 / row_new)) * (1.0 / FF)
    fc1_row_new[...] = row_new
    fc1_col_new[...] = fc_sums[1, 5:6, :]
    update(
        fin.at[0], fc1, to_column(row_new, eye), fc_sums[1, 5:6, :], mean, norm, D ** (-0.5),
        fc1_grad, fc1_new, fc1_low,
    )
    col_new = fresh(fc2_col[...], fc_sums[0, 2:3, :] * (1.0 / FF))
    mean = fc_sums[0, 4:5, :1] * (1.0 / FF)
    norm = mean * row_mean(fc_sums[0, 3:4, :] * (1.0 / col_new)) * (1.0 / FF)
    fc2_row_new[...] = fc_sums[1, 6:7, :]
    fc2_col_new[...] = col_new
    update(
        fin.at[1], fc2, to_column(fc_sums[1, 6:7, :], eye), col_new, mean, norm, FF ** (-0.5),
        fc2_grad, fc2_new, fc2_low,
    )

    def stepped(grad, old):
        state = fresh(old, grad * grad)
        return state, grad * lax.rsqrt(state)

    norm = jnp.zeros((1, 1), F32)
    for m in range(4):
        step = stepped(vec[20 + m : 21 + m, :], b1[m, 4:5, :])[1]
        norm = norm + jnp.sum(step * step, axis=1, keepdims=True)
    grad = vec[pl.ds(20 + mlp, 1), :]
    state, step = stepped(grad, b1[mlp, 4:5, :])
    b1_grad[...] = grad
    b1_state_new[...] = state
    b1_new[...] = fc1_b[...] - VEC_RATE * (step * clip_scale(norm * (1.0 / FF)))

    grad = jnp.concatenate([vec[n : n + 1, :] for n in range(8)], axis=1)
    state, step = stepped(grad, small_state[...])
    norm = jnp.sum(step * step, axis=1, keepdims=True) * (1.0 / (8 * D))
    small_grad[...] = grad
    small_state_new[...] = state
    small_new[...] = small[...] - VEC_RATE * (step * clip_scale(norm))

    grad = jnp.transpose(vec[8:24, :256])[:169, :HEADS]
    state, step = stepped(grad, table_state[...])
    norm = total(step * step) * (1.0 / (169 * HEADS))
    table_grad[...] = grad
    table_state_new[...] = state
    table_new[...] = table[...] - VEC_RATE * (step * clip_scale(norm))


def finish(*arrays):
    sd = jax.ShapeDtypeStruct
    vm = pltpu.VMEM

    def owned(width):
        return [sd((3, width), F32), sd((1, 3), F32), sd((1, width), F32), sd((3, width), F32), sd((3, width), BF16)]

    shard = [sd((D, D), F32), sd((1, D), F32), sd((1, D), F32), sd((D, D), F32), sd((D, D), BF16)]
    out_shape = owned(QKV) + owned(D) + shard + shard
    out_shape += [sd((1, D), F32)] * 3 + [sd((1, 8 * D), F32)] * 3 + [sd((169, HEADS), F32)] * 3
    return pl.pallas_call(
        finish_kernel,
        out_shape=out_shape,
        in_specs=[pl.BlockSpec(memory_space=vm)] * len(arrays),
        out_specs=[pl.BlockSpec(memory_space=vm)] * len(out_shape),
        compiler_params=pltpu.CompilerParams(vmem_limit_bytes=32 * 1024 * 1024),
        name="finish",
    )(*arrays)


def clip_scale(mean_square):
    return 1.0 / jnp.maximum(1.0, jnp.sqrt(mean_square))


def per_device(
    tokens_in, out_grad, window_live, region_ids, qkv_weight, proj_weight, rel_table, small_params,
    fc1_weight, fc1_bias, fc2_weight, qkv_row, qkv_col, proj_row, proj_col, fc1_row, fc1_col,
    fc2_row, fc2_col, fc1_bias_state, small_state, table_state,
):
    def line(x):
        return x.reshape(1, -1)

    live_tokens = (jnp.sum(window_live) * SPAN).reshape(1)
    region = jnp.pad(region_ids.astype(F32), (0, 104)).reshape(1, 1280)
    table = jnp.pad(rel_table.T, ((0, 4), (0, 87)))
    out, gin, fin, *parts = block(
        live_tokens, tokens_in, out_grad, region, qkv_weight, proj_weight, table, line(small_params),
        fc1_weight, fc2_weight, line(fc1_bias), line(fc1_bias_state), line(fc1_col), line(fc2_row),
        line(qkv_row), line(proj_row),
    )
    outs = finish(
        fin.reshape(2, D, D), *parts, fc1_weight, fc2_weight, line(fc1_bias), line(fc1_row), line(fc2_col),
        line(qkv_col), line(proj_col), line(small_params), line(small_state), rel_table, table_state,
    )
    flat = lambda x: x.reshape(-1) if x.shape[0] == 1 else x
    return (out, gin, *(flat(x) for x in outs))


def solution(mesh):
    tokens, owner = P(("win", "mlp"), None), P(("win", "mlp"))
    whole, part = P(), P("mlp")
    return jax.shard_map(
        per_device,
        mesh=mesh,
        in_specs=(
            tokens, tokens, owner, owner, whole, whole, whole, whole, P(None, "mlp"), part, P("mlp", None),
            whole, whole, whole, whole, whole, part, part, whole, part, whole, whole,
        ),
        out_specs=(
            tokens, tokens,
            tokens, owner, whole, tokens, tokens,
            tokens, owner, whole, tokens, tokens,
            P(None, "mlp"), whole, part, P(None, "mlp"), P(None, "mlp"),
            P("mlp", None), part, whole, P("mlp", None), P("mlp", None),
            part, part, part,
            whole, whole, whole,
            whole, whole, whole,
        ),
        check_vma=False,
    )
```

```python
import functools
import math

import jax
import jax.numpy as jnp
from jax import lax
from jax.experimental import pallas as pl
from jax.experimental.pallas import tpu as pltpu
from jax.sharding import PartitionSpec as P

D = 384
FF = 1536
QKV = 3 * D
HEADS = 12
WIN = 7
SPAN = WIN * WIN
STEP = 10
DECAY = 1.0 - STEP ** (-0.8)
EPS_NORM = 1e-05
EPS_SQ = 1e-30
VEC_RATE = 0.3
SCALE = 32 ** (-0.5)
FAR = -1e30

GROUPS = 3
PER = 8
G_TOK = PER * SPAN
G_ROWS = 400
ROWS = GROUPS * G_ROWS
TOK = GROUPS * G_TOK
CHUNK = 64
KEYS = 56
SETS = 3
LANES = 4 * CHUNK

MESH = pl.DeviceIdType.MESH
F32 = jnp.float32
BF16 = jnp.bfloat16


def dot(a, b):
    return jnp.dot(a, b, preferred_element_type=F32)


def dot_nt(a, b):
    return lax.dot_general(a, b, (((1,), (1,)), ((), ())), preferred_element_type=F32)


def dot_tn(a, b):
    return lax.dot_general(a, b, (((0,), (0,)), ((), ())), preferred_element_type=F32)


def dot_exact(a, b):
    return jnp.dot(a, b, precision=lax.Precision.HIGHEST, preferred_element_type=F32)


def iota(shape, dim):
    return lax.broadcasted_iota(jnp.int32, shape, dim)


def fold_rows(x):
    total = x[0:8]
    for i in range(1, x.shape[0] // 8):
        total = total + x[8 * i : 8 * i + 8]
    return total


def row_mean(x):
    return jnp.sum(x, axis=1, keepdims=True) * (1.0 / D)


def normalize(x):
    center = x - row_mean(x)
    inverse = lax.rsqrt(row_mean(center * center) + EPS_NORM)
    return center * inverse, inverse


def normalize_back(u, gain, scaled, inverse):
    weighted = u * gain
    return inverse * (weighted - row_mean(weighted) - scaled * row_mean(weighted * scaled))


def gelu_parts(v):
    e = jnp.exp(-0.5 * v * v)
    t = 1.0 / (1.0 + (0.3275911 * 0.5**0.5) * jnp.abs(v))
    poly = 1.061405429 * t - 1.453152027
    poly = poly * t + 1.421413741
    poly = poly * t - 0.284496736
    poly = poly * t + 0.254829592
    tail = (0.5 * e) * (poly * t)
    phi = jnp.where(v < 0.0, tail, 1.0 - tail)
    return v * phi, phi + v * e * (2.0 * math.pi) ** (-0.5)


def barrel(x, amount, right):
    width = x.shape[1]
    for k in range(7):
        step = 1 << k
        moved = pltpu.roll(x, step if right else width - step, 1)
        x = jnp.where((amount & step) != 0, moved, x)
    return x


def embed(i):
    return 13 * (i // WIN) + i % WIN


def chunk_start(w):
    return pl.multiple_of((w // PER) * G_ROWS + (w % PER) * 48, 16)


def prologue(region, table, x_ref, emask, bias, mask, tok):
    for a in range(GROUPS):
        for r in range(0, G_TOK, 56):
            src = a * G_TOK + r
            low = src // 16 * 16
            x_ref[a * G_ROWS + r : a * G_ROWS + r + 56, :] = (
                tok[low : low + 64 if low + 64 <= TOK else TOK, :].astype(F32)[src - low : src - low + 56]
            )
        x_ref[a * G_ROWS + G_TOK : (a + 1) * G_ROWS, :] = jnp.zeros((G_ROWS - G_TOK, D), F32)
    row = iota((LANES, 128), 0)
    lane = iota((LANES, 128), 1)
    for b in range(PER):
        i = row % CHUNK
        keep = (i >= b) & (i < b + SPAN) & (lane // 32 == row // CHUNK)
        emask[b] = jnp.where(keep, 1.0, 0.0).astype(BF16)
    j = iota((KEYS, 256), 0)
    amount = jnp.maximum(84 - embed(j), 0)
    jl = iota((KEYS, LANES), 0)
    il = iota((KEYS, LANES), 1) % CHUNK
    for g in range(SETS):
        base = jnp.zeros((KEYS, LANES), F32)
        for h in range(4):
            line = jnp.concatenate([table[4 * g + h : 4 * g + h + 1, :], jnp.zeros((1, 87), F32)], axis=1)
            wide = jnp.broadcast_to(line, (KEYS, 256))
            wide = barrel(wide, amount, False)[:, :128]
            lane_to = iota((128, LANES), 1) - CHUNK * h
            pick = (iota((128, LANES), 0) == embed(lane_to)) & (lane_to >= 0) & (lane_to < SPAN)
            base = base + dot_exact(wide, jnp.where(pick, 1.0, 0.0))
        for b in range(PER):
            moved = pltpu.roll(pltpu.roll(base, b, 0), b, 1) if b else base
            key_ok = (jl >= b) & (jl < b + SPAN)
            query_ok = (il >= b) & (il < b + SPAN)
            bias[b, g] = jnp.where(key_ok, jnp.where(query_ok, moved, 0.0), FAR)
    eye = iota((CHUNK, CHUNK), 0) == iota((CHUNK, CHUNK), 1)
    region_row = jnp.concatenate([region[...].reshape(1, TOK).astype(F32), jnp.zeros((1, 104), F32)], axis=1)
    for w in range(GROUPS * PER):
        start = (w // PER) * G_TOK + (w % PER) * 48
        line = region_row[:, start : start + CHUNK]
        column = jnp.sum(jnp.where(eye, jnp.broadcast_to(line, (CHUNK, CHUNK)), 0.0), axis=1, keepdims=True)
        wide = jnp.concatenate([line] * 4, axis=1)
        mask[w] = jnp.where(column[:KEYS] != wide, -100.0, 0.0)


def pad_keys(x):
    return jnp.concatenate([x, jnp.zeros((CHUNK - KEYS, x.shape[1]), x.dtype)], axis=0)


def spread(x, keep):
    return jnp.concatenate([x] * 4, axis=0) * keep


def collect(full):
    head = iota((CHUNK, 128), 1) // 32
    parts = [full[CHUNK * h : CHUNK * (h + 1)] for h in range(4)]
    low = jnp.where(head == 0, parts[0], parts[1])
    high = jnp.where(head == 2, parts[2], parts[3])
    return jnp.where(head < 2, low, high)


def block_kernel(
    live_windows, region, tok_in, og_in, wq_in, wp_in, table, small, fc1, fc2,
    fc1_b, fc1_state, fc1_col, fc2_row, qkv_row, proj_row,
    out_to, gin_to, fin, vec, fc_sums, at_sums, own_g, own_r, own_wq, own_wp, b1,
    x_ref, xh1, inv1, inv2, n1, n2, qkv, att_b, probs, back, hidden, ig, dqkv,
    emask, bias, mask, tacc, s1, s2, sums, b1_acc, wq_b, wp_b, w1, w2, tok, og, wq, wp, stage, in_sem, out_sem,
    fcl, fr1, fr2, ft, fr3, fr4, fst, atl, ar1, ar2, ar3, ar4, ast, vx, vy, at_total,
    w_send, w_recv, pair_send, pair_recv, f1s, f1r, f2s, f2r, f3s, f3r, f4s, f4r, f5s, f5r, f7s, f7r, f8s, f8r,
    a1s, a1r, a2s, a2r, a3s, a3r, a4s, a4r, a5s, a5r, vxs, vxr, vys, vyr,
):
    win, mlp = lax.axis_index("win"), lax.axis_index("mlp")
    z, y, core = win // 8, (win // 2) % 4, win % 2
    pair = win + 1 - 2 * core

    def along_x(d):
        return win, (mlp + d) % 4

    def along_y(d):
        return z * 8 + ((y + d) % 4) * 2 + core, mlp

    def along_z(d):
        return ((z + d) % 4) * 8 + y * 2 + core, mlp

    def plane_peer(d):
        return ((z + d // 4) % 4) * 8 + ((y + d % 4) % 4) * 2 + core, mlp

    def class_peer(d):
        return pair if d >= 4 else win, (mlp + d) % 4

    loads = [
        pltpu.make_async_copy(src, dst, in_sem.at[n])
        for n, (src, dst) in enumerate(((tok_in, tok), (og_in, og), (wq_in, wq), (wp_in, wp)))
    ]
    for copy in loads:
        copy.start()
    barrier = pltpu.get_barrier_semaphore()
    peers = [class_peer(d) for d in range(1, 8)]
    peers += [plane_peer(d) for d in range(1, 16)]
    for peer in peers:
        pl.semaphore_signal(barrier, inc=1, device_id=peer, device_id_type=MESH)

    def remote(src, dst, send, recv, peer):
        return pltpu.make_async_remote_copy(
            src_ref=src, dst_ref=dst, send_sem=send, recv_sem=recv, device_id=peer, device_id_type=MESH
        )

    def param(part):
        return small[D * part : D * part + D].reshape(1, D)

    pending = []

    def start(copy):
        copy.start()
        pending.append(copy)
        return copy

    def shard(m):
        at = pl.multiple_of(m * D, D)
        half = pl.ds(pl.multiple_of(core * (D // 2), 16), D // 2)
        half_at = pl.ds(pl.multiple_of(m * D + core * (D // 2), 16), D // 2)
        return w1.at[half, pl.ds(at, D)], w2.at[half_at, :], b1.at[m]

    mine = shard(mlp)
    cols = pl.ds(pl.multiple_of(mlp * D, D), D)
    w1[:, cols] = fc1[...].astype(BF16)
    w2[cols, :] = fc2[...].astype(BF16)
    b1[mlp, 0:4] = jnp.broadcast_to(fc1_b[...].reshape(1, D), (4, D))
    b1[mlp, 4:8] = jnp.broadcast_to(fc1_state[...].reshape(1, D), (4, D))
    pl.semaphore_wait(barrier, 22)
    sends = []
    for d in range(1, 4):
        for n in range(3):
            sends.append(start(remote(mine[n], mine[n], w_send.at[d - 1, n], w_recv.at[d - 1, n], along_x(d))))

    live = live_windows[0]
    for n in range(1, GROUPS * PER):
        live = live + live_windows[n]
    live = live * SPAN
    for copy in loads:
        copy.wait()
    prologue(region, table, x_ref, emask, bias, mask, tok)
    for g in range(SETS):
        for part in range(3):
            wq_b[:, D * g + 128 * part : D * g + 128 * part + 128] = wq[
                :, D * part + 128 * g : D * part + 128 * g + 128
            ].astype(BF16)
    wp_b[...] = wp[...].astype(BF16)
    sums[...] = jnp.zeros_like(sums)
    b1_acc[...] = jnp.zeros_like(b1_acc)
    tacc[...] = jnp.zeros_like(tacc)
    att = dqkv.at[:, :D]
    xh2 = dqkv.at[:, D : 2 * D]
    dqkv_b = ig.at[:, :QKV]
    dqkv[:, :D] = jnp.zeros((ROWS, D), F32)

    for a in range(GROUPS):
        for r in range(0, G_TOK, 56):
            src = a * G_TOK + r
            low = src // 16 * 16
            rows = og[low : low + 64 if low + 64 <= TOK else TOK, :].astype(F32)[src - low : src - low + 56]
            keep = iota((56, D), 0) + src < live
            x = jnp.where(keep, rows, 0.0)
            s2[r : r + 56, :] = x
            sums[7] += fold_rows(x)
        s2[G_TOK:G_ROWS, :] = jnp.zeros((G_ROWS - G_TOK, D), F32)
        back[a * G_ROWS : (a + 1) * G_ROWS, :] = s2[...].astype(BF16)

    shift_q = jnp.concatenate(
        [
            part[:, 128 * g : 128 * g + 128]
            for g in range(SETS)
            for part in (param(2), jnp.zeros((1, D), F32), param(3))
        ],
        axis=1,
    )

    @pl.loop(0, 5)
    def _(t):
        for c in range(15):
            rows = pl.ds(pl.multiple_of(t * 240 + c * 16, 16), 16)
            scaled, inverse = normalize(x_ref[rows, :])
            xh1[rows, :] = scaled
            inv1[rows, :] = inverse
            n1[rows, :] = (scaled * param(0) + param(1)).astype(BF16)

    @pl.loop(0, 5)
    def _(t):
        rows = pl.ds(pl.multiple_of(t * 240, 16), 240)
        qkv[rows, :] = (dot(n1[rows, :], wq_b[...]) + shift_q).astype(BF16)

    @pl.loop(0, PER)
    def _(b):
        for a in range(GROUPS):
            rows = pl.ds(pl.multiple_of(a * G_ROWS + b * 48, 16), CHUNK)
            w = a * PER + b
            for g in range(SETS):
                q = qkv[rows, D * g : D * g + 128]
                k = qkv[rows, D * g + 128 : D * g + 256]
                v = qkv[rows, D * g + 256 : D * g + 384]
                scores = dot_nt(k, spread(q, emask[b]))[:KEYS] * SCALE + (bias[b, g] + mask[w])
                p = jnp.exp(scores - jnp.max(scores, axis=0, keepdims=True))
                p = p * (1.0 / jnp.sum(p, axis=0, keepdims=True))
                probs[w, g] = p
                o = collect(dot_tn(pad_keys(p).astype(BF16), v))
                i = iota((CHUNK, 128), 0)
                att[rows, 128 * g : 128 * g + 128] += jnp.where((i >= b) & (i < b + SPAN), o, 0.0)

    forwards = []
    for d in range(1, 4):
        came = shard((mlp + 4 - d) % 4)
        for n in range(3):
            sends[3 * (d - 1) + n].wait_recv()
            if n < 2:
                copy = remote(came[n], came[n], pair_send.at[d - 1, n], pair_recv.at[d - 1, n], (pair, mlp))
                forwards.append(start(copy))

    @pl.loop(0, GROUPS)
    def _(a):
        rows = pl.ds(pl.multiple_of(a * G_ROWS, 16), G_ROWS)
        att_b[rows, :] = att[rows, :].astype(BF16)
        s1[...] = dot(att_b[rows, :], wp_b[...])

        for c in range(25):
            here = pl.ds(pl.multiple_of(a * G_ROWS + 16 * c, 16), 16)
            middle = x_ref[here, :] + (s1[16 * c : 16 * c + 16, :] + param(4))
            stage[here, :] = middle
            scaled, inverse = normalize(middle)
            xh2[here, :] = scaled
            inv2[here, :] = inverse
            n2[here, :] = (scaled * param(5) + param(6)).astype(BF16)

    for copy in forwards:
        copy.wait_recv()

    @pl.loop(0, 5)
    def _(mt):
        rows = pl.ds(pl.multiple_of(mt * 240, 16), 240)
        b1_row = jnp.concatenate([b1[m, 0:1, :] for m in range(4)], axis=1)
        for nt in range(6):
            cols = slice(256 * nt, 256 * nt + 256)
            inner = dot(n2[rows, :], w1[:, cols]) + b1_row[:, cols]
            up = dot_nt(back[rows, :], w2[cols, :])
            total = b1_acc[:, cols]
            for c in range(15):
                act, slope = gelu_parts(inner[16 * c : 16 * c + 16])
                here = pl.ds(pl.multiple_of(mt * 240 + 16 * c, 16), 16)
                hidden[here, cols] = act.astype(BF16)
                grad = (up[16 * c : 16 * c + 16] * slope).astype(BF16)
                ig[here, cols] = grad
                total = total + fold_rows(grad.astype(F32))
            b1_acc[:, cols] = total

    g2 = dot_tn(hidden[...], back[...]).astype(BF16)
    g1 = dot_tn(n2[...], ig[...]).astype(BF16)
    for m in range(4):
        fcl[0, m] = g1[:, D * m : D * m + D].reshape(4, 96, D)
        fcl[1, m] = g2[D * m : D * m + D].reshape(4, 96, D)
    fc_one = [start(remote(fcl.at[1 - core, m], fr1.at[m], f1s.at[m], f1r.at[m], (pair, mlp))) for m in range(4)]

    def middle_back(a):
        rows = slice(a * G_ROWS, (a + 1) * G_ROWS)
        s2[...] = dot_nt(ig[rows, :], w1[...])
        for c in range(25):
            here = slice(16 * c, 16 * c + 16)
            at = slice(a * G_ROWS + 16 * c, a * G_ROWS + 16 * c + 16)
            u = s2[here, :]
            scaled = xh2[at, :]
            sums[5] += fold_rows(u * scaled)
            sums[6] += fold_rows(u)
            mg = normalize_back(u, param(5), scaled, inv2[at, :]) + back[at, :].astype(F32)
            x_ref[at, :] = mg
            low = mg.astype(BF16)
            n2[at, :] = low
            sums[4] += fold_rows(low.astype(F32))

    def out_copy(a):
        return pltpu.make_async_copy(
            stage.at[pl.ds(a * G_ROWS, G_TOK)], out_to.at[pl.ds(a * G_TOK, G_TOK)], out_sem.at[a]
        )

    def block_out(a):
        rows = slice(a * G_ROWS, (a + 1) * G_ROWS)
        s1[...] = dot(hidden[rows, :], w2[...])
        for c in range(25):
            at = slice(a * G_ROWS + 16 * c, a * G_ROWS + 16 * c + 16)
            r = stage[at, :] + (s1[16 * c : 16 * c + 16, :] + param(7))
            keep = iota((16, D), 0) + (a * G_TOK + 16 * c) < live
            stage[at, :] = jnp.where(keep, r, 0.0)
        out_copy(a).start()

    p = iota((D, D), 0)
    inner_p = p % 48
    owned = 24 * (inner_p // 3) + 12 * (p // 192) + 3 * ((p // 48) % 4) + inner_p % 3
    order = jnp.where(iota((D, D), 1) == owned, 1.0, 0.0).astype(BF16)

    def ordered(grad):
        return dot(order, grad.astype(BF16)).astype(BF16).reshape(2, 4, 48, D)

    def at_one(n):
        return remote(atl.at[n, 1 - core], ar1.at[n], a1s.at[n], a1r.at[n], (pair, mlp))

    def at_add_one(n):
        at_one(n).wait_recv()
        for i in range(4):
            ar1[n, i] = (ar1[n, i].astype(F32) + atl[n, core, i].astype(F32)).astype(BF16)
        for d in range(1, 4):
            start(remote(ar1.at[n, (mlp + d) % 4], ar2.at[n, d - 1], a2s.at[n, d - 1], a2r.at[n, d - 1], along_x(d)))

    def at_add_two(n):
        total = ar1[n, mlp].astype(F32)
        for d in range(1, 4):
            remote(ar1.at[n, 0], ar2.at[n, d - 1], a2s.at[n, d - 1], a2r.at[n, d - 1], along_x(d)).wait_recv()
            total = total + ar2[n, d - 1].astype(F32)
        ar3[n, y] = total.astype(BF16)
        for d in range(1, 4):
            start(remote(ar3.at[n, y], ar3.at[n, y], a3s.at[n, d - 1], a3r.at[n, d - 1], along_y(d)))

    def at_add_three(n):
        for d in range(1, 4):
            came = ar3.at[n, (y + 4 - d) % 4]
            remote(came, came, a3s.at[n, d - 1], a3r.at[n, d - 1], along_y(d)).wait_recv()
        total = ar3[n, 0].astype(F32) + ar3[n, 1].astype(F32)
        ar4[n, z] = (total + ar3[n, 2].astype(F32) + ar3[n, 3].astype(F32)).astype(BF16)
        for d in range(1, 4):
            start(remote(ar4.at[n, z], ar4.at[n, z], a4s.at[n, d - 1], a4r.at[n, d - 1], along_z(d)))

    def at_finish(n):
        for d in range(1, 4):
            came = ar4.at[n, (z + 4 - d) % 4]
            remote(came, came, a4s.at[n, d - 1], a4r.at[n, d - 1], along_z(d)).wait_recv()
        total = ar4[n, 0].astype(F32) + ar4[n, 1].astype(F32)
        at_total[n] = total + ar4[n, 2].astype(F32) + ar4[n, 3].astype(F32)

    def to_axes(dx, dy, dz):
        return ((z + dz) % 4) * 8 + ((y + dy) % 4) * 2 + core, (mlp + dx) % 4

    def first_axis(d):
        return to_axes(d * (1 - core), 0, d * core)

    def second_axis(d):
        return to_axes(d * core, d * (1 - core), 0)

    def third_axis(d):
        return to_axes(0, d * core, d * (1 - core))

    def last_axis(d):
        return to_axes(0, d * (1 - core), d * core)

    block_at = y * (1 - core) + z * core
    second = y * (1 - core) + mlp * core
    third = z * (1 - core) + y * core

    def fc_two(d):
        return remote(fr1.at[0], fr2.at[d - 1], f2s.at[d - 1], f2r.at[d - 1], first_axis(d))

    def fc_add_one():
        for m in range(4):
            fc_one[m].wait_recv()
            for i in range(4):
                fr1[m, i] = (fr1[m, i].astype(F32) + fcl[core, m, i].astype(F32)).astype(BF16)

        @pl.when(core == 0)
        def _():
            for d in range(1, 4):
                remote(fr1.at[(mlp + d) % 4], fr2.at[d - 1], f2s.at[d - 1], f2r.at[d - 1], first_axis(d)).start()

        @pl.when(core == 1)
        def _():
            for d in range(1, 4):
                remote(fr1.at[:, (z + d) % 4], fr2.at[d - 1], f2s.at[d - 1], f2r.at[d - 1], first_axis(d)).start()

    def fc_add_two():
        for d in range(1, 4):
            fc_two(d).wait_recv()
        for i in range(4):
            total = fr1[mlp * (1 - core) + i * core, i * (1 - core) + z * core].astype(F32)
            for d in range(1, 4):
                total = total + fr2[d - 1, i].astype(F32)
            ft[i] = total.astype(BF16)
        for d in range(1, 4):
            start(remote(ft.at[(second + d) % 4], fr3.at[d - 1], f3s.at[d - 1], f3r.at[d - 1], second_axis(d)))

    def fc_add_three():
        total = ft[second].astype(F32)
        for d in range(1, 4):
            remote(ft.at[0], fr3.at[d - 1], f3s.at[d - 1], f3r.at[d - 1], second_axis(d)).wait_recv()
            total = total + fr3[d - 1].astype(F32)
        fr4[third] = total.astype(BF16)
        for d in range(1, 4):
            start(remote(fr4.at[third], fr4.at[third], f4s.at[d - 1], f4r.at[d - 1], third_axis(d)))

    def fc_add_four():
        for d in range(1, 4):
            came = fr4.at[(third + 4 - d) % 4]
            remote(came, came, f4s.at[d - 1], f4r.at[d - 1], third_axis(d)).wait_recv()
        total = fr4[0].astype(F32) + fr4[1].astype(F32)
        fin[core, block_at] = total + fr4[2].astype(F32) + fr4[3].astype(F32)
        for d in range(1, 4):
            place = fin.at[core, block_at]
            start(remote(place, place, f5s.at[d - 1], f5r.at[d - 1], last_axis(d)))

    def fc_spread():
        for d in range(1, 4):
            place = fin.at[core, (block_at + 4 - d) % 4]
            remote(place, place, f5s.at[d - 1], f5r.at[d - 1], last_axis(d)).wait_recv()
        start(remote(fin.at[core], fin.at[core], f7s.at[0], f7r.at[0], (pair, mlp)))

    mine_at, plane_at = 4 * core + mlp, 4 * z + y

    def vec_one(n):
        for d in range(1, 8):
            place = vx.at[n, mine_at]
            start(remote(place, place, vxs.at[n, d - 1], vxr.at[n, d - 1], class_peer(d)))

    def vec_two(n):
        for d in range(1, 8):
            place = vx.at[n, (mlp + 8 - d) % 4 + 4 * (core if d < 4 else 1 - core)]
            remote(place, place, vxs.at[n, d - 1], vxr.at[n, d - 1], class_peer(d)).wait_recv()
        total = vx[n, 0]
        for i in range(1, 8):
            total = total + vx[n, i]
        vy[n, plane_at] = total
        for d in range(1, 16):
            place = vy.at[n, plane_at]
            start(remote(place, place, vys.at[n, d - 1], vyr.at[n, d - 1], plane_peer(d)))

    def vec_three(n):
        for d in range(1, 16):
            place = vy.at[n, 4 * ((z + 4 - d // 4) % 4) + (y + 4 - d % 4) % 4]
            remote(place, place, vys.at[n, d - 1], vyr.at[n, d - 1], plane_peer(d)).wait_recv()
        total = vy[n, 0]
        for i in range(1, 16):
            total = total + vy[n, i]
        vec[8 * n : 8 * n + 8, :] = total

    middle_back(0)
    middle_back(1)
    fc_add_one()
    middle_back(2)

    atl[3] = ordered(dot_tn(att_b[...], n2[...]))
    start(at_one(3))

    @pl.loop(0, GROUPS)
    def _(a):
        rows = pl.ds(pl.multiple_of(a * G_ROWS, 16), G_ROWS)
        att_b[rows, :] = dot_nt(n2[rows, :], wp_b[...]).astype(BF16)

    dqkv[...] = jnp.zeros_like(dqkv)

    def attention_back(g, half):
        @pl.loop(4 * half, 4 * half + 4)
        def _(b):
            keep = emask[b]
            total = tacc[b, g]
            for a in range(GROUPS):
                rows = pl.ds(pl.multiple_of(a * G_ROWS + b * 48, 16), CHUNK)
                q = qkv[rows, D * g : D * g + 128]
                k = qkv[rows, D * g + 128 : D * g + 256]
                v = qkv[rows, D * g + 256 : D * g + 384]
                qe = spread(q, keep)
                da = spread(att_b[rows, 128 * g : 128 * g + 128], keep)
                p = probs[a * PER + b, g]
                dp = dot_nt(v, da)[:KEYS]
                pd = p * dp
                ds = pad_keys(pd - p * jnp.sum(pd, axis=0, keepdims=True)).astype(BF16)
                total = total + ds.astype(F32)[:KEYS]
                dv = dot(pad_keys(p).astype(BF16), da)
                dk = dot(ds, qe) * SCALE
                dq = collect(dot_tn(ds, k)) * SCALE
                dqkv[rows, 384 * g : 384 * g + 128] += dq
                dqkv[rows, 384 * g + 128 : 384 * g + 256] += dk
                dqkv[rows, 384 * g + 256 : 384 * g + 384] += dv
            tacc[b, g] = total

    def qkv_grad(g):
        group = slice(384 * g, 384 * g + 384)

        @pl.loop(0, 5)
        def _(t):
            for c in range(15):
                rows = pl.ds(pl.multiple_of(t * 240 + c * 16, 16), 16)
                low = dqkv[rows, group].astype(BF16)
                dqkv_b[rows, group] = low
                wide = low.astype(F32)
                sums[2, :, 128 * g : 128 * g + 128] += fold_rows(wide[:, :128])
                sums[3, :, 128 * g : 128 * g + 128] += fold_rows(wide[:, 256:])

        atl[g] = ordered(dot_tn(n1[...], dqkv_b[:, group]))
        start(at_one(g))

    for part in range(4):
        vx[0, mine_at, part : part + 1, :] = jnp.sum(sums[4 + part], axis=0, keepdims=True)
    for m in range(4):
        vx[0, mine_at, 4 + m : 5 + m, :] = jnp.sum(b1_acc[:, D * m : D * m + D], axis=0, keepdims=True)
    vec_one(0)

    def table_back(g, n):
        j = iota((KEYS, 256), 0)
        amount = jnp.maximum(84 - embed(j), 0)
        total = tacc[0, g]
        for b in range(1, PER):
            total = total + pltpu.roll(pltpu.roll(tacc[b, g], KEYS - b, 0), LANES - b, 1)
        for h in range(4):
            lane_from = iota((LANES, 256), 0) - CHUNK * h
            pick = (iota((LANES, 256), 1) == embed(lane_from)) & (lane_from >= 0) & (lane_from < SPAN)
            wide = barrel(dot_exact(total, jnp.where(pick, 1.0, 0.0)), amount, True)
            wide = jnp.where(j < SPAN, wide, 0.0)
            vx[n, mine_at, 4 * (g % 2) + h : 4 * (g % 2) + h + 1, :] = jnp.concatenate(
                [jnp.sum(wide, axis=0, keepdims=True), jnp.zeros((1, 128), F32)], axis=1
            )

    attention_back(0, 0)
    at_add_one(3)
    vec_two(0)
    attention_back(0, 1)
    qkv_grad(0)
    fc_add_two()
    at_add_two(3)
    table_back(0, 1)
    at_add_one(0)
    attention_back(1, 0)
    at_add_three(3)
    at_add_two(0)
    attention_back(1, 1)
    qkv_grad(1)
    fc_add_three()
    at_add_three(0)
    vec_three(0)
    table_back(1, 1)
    vec_one(1)
    at_add_one(1)
    attention_back(2, 0)
    at_finish(3)
    at_add_two(1)
    fc_add_four()
    attention_back(2, 1)
    qkv_grad(2)
    at_add_three(1)
    vec_two(1)
    table_back(2, 2)
    at_add_one(2)

    def gin_copy(a):
        return pltpu.make_async_copy(
            x_ref.at[pl.ds(a * G_ROWS, G_TOK)], gin_to.at[pl.ds(a * G_TOK, G_TOK)], out_sem.at[3 + a]
        )

    def input_back(a):
        rows = slice(a * G_ROWS, (a + 1) * G_ROWS)
        s2[...] = dot_nt(dqkv_b[rows, :], wq_b[...])
        for c in range(25):
            here = slice(16 * c, 16 * c + 16)
            at = slice(a * G_ROWS + 16 * c, a * G_ROWS + 16 * c + 16)
            u = s2[here, :]
            scaled = xh1[at, :]
            sums[0] += fold_rows(u * scaled)
            sums[1] += fold_rows(u)
            x_ref[at, :] = normalize_back(u, param(0), scaled, inv1[at, :]) + x_ref[at, :]
        gin_copy(a).start()

    for a in range(GROUPS):
        input_back(a)
    for part in range(4):
        vx[2, mine_at, 4 + part : 5 + part, :] = jnp.sum(sums[part], axis=0, keepdims=True)
    vec_one(2)
    at_add_two(2)
    at_finish(0)
    fc_spread()
    for a in range(GROUPS):
        block_out(a)
    at_finish(1)
    vec_three(1)
    vec_two(2)

    remote(fin.at[1 - core], fin.at[1 - core], f7s.at[0], f7r.at[0], (pair, mlp)).wait_recv()
    eye = iota((D, D), 0) == iota((D, D), 1)

    def to_row(column):
        return jnp.sum(jnp.where(eye, column, 0.0), axis=0, keepdims=True)

    up = fin[0].reshape(D, D)
    down = fin[1].reshape(D, D)
    up_squares = up * up
    down_squares = down * down
    up_col = DECAY * fc1_col[...].reshape(1, D) + (1.0 - DECAY) * (
        jnp.sum(up_squares, axis=0, keepdims=True) * (1.0 / D) + EPS_SQ
    )
    down_row = DECAY * to_column(fc2_row[...].reshape(1, D), eye) + (1.0 - DECAY) * (row_mean(down_squares) + EPS_SQ)
    fst[mlp, 0:1] = to_row(jnp.sum(up_squares, axis=1, keepdims=True))
    fst[mlp, 1:2] = to_row(jnp.sum(up_squares * (1.0 / up_col), axis=1, keepdims=True))
    fst[mlp, 2:3] = jnp.sum(down_squares, axis=0, keepdims=True)
    fst[mlp, 3:4] = jnp.sum(down_squares * (1.0 / down_row), axis=0, keepdims=True)
    fst[mlp, 4:5] = jnp.broadcast_to(jnp.sum(down_row, axis=0, keepdims=True), (1, D))
    fst[mlp, 5:6] = up_col
    fst[mlp, 6:7] = to_row(down_row)
    fst[mlp, 7:8] = jnp.zeros((1, D), F32)
    for d in range(1, 4):
        start(remote(fst.at[mlp], fst.at[mlp], f8s.at[d - 1], f8r.at[d - 1], along_x(d)))

    at_add_three(2)

    offset = 48 - 3 * plane_at
    block_rows = pl.ds(pl.multiple_of(24 * (win // 2), 8), 24)
    shift = 24 - 3 * mine_at
    own_wq[...] = pltpu.roll(wq[block_rows, :], shift, 0)[:8]
    own_wp[...] = pltpu.roll(wp[block_rows, :], shift, 0)[:8]

    r48 = iota((48, D), 0)
    pick = iota((48, D), 1) == 24 * (r48 // 3) + 12 * core + 3 * mlp + r48 % 3

    def rows_new(state, mean):
        old = jnp.sum(jnp.where(pick, state, 0.0), axis=1, keepdims=True)
        return DECAY * old + (1.0 - DECAY) * (mean + EPS_SQ)

    at_finish(2)
    squares = [at_total[n] * at_total[n] for n in range(4)]
    qkv_new_row = rows_new(
        qkv_row[...].reshape(1, D), row_mean(squares[0] + squares[1] + squares[2]) * (1.0 / 3.0)
    )
    proj_new_row = rows_new(proj_row[...].reshape(1, D), row_mean(squares[3]))
    for n in range(4):
        over = squares[n] * (1.0 / (qkv_new_row if n < 3 else proj_new_row))
        ast[mine_at, n : n + 1] = jnp.sum(squares[n], axis=0, keepdims=True)
        ast[mine_at, 4 + n : 5 + n] = jnp.sum(over, axis=0, keepdims=True)
    ast[mine_at, 8:9] = jnp.broadcast_to(jnp.sum(qkv_new_row, axis=0, keepdims=True), (1, D))
    ast[mine_at, 9:10] = jnp.broadcast_to(jnp.sum(proj_new_row, axis=0, keepdims=True), (1, D))
    ast[mine_at, 10:16] = jnp.zeros((6, D), F32)

    def at_five(d):
        place = ast.at[mine_at]
        return remote(place, place, a5s.at[d - 1], a5r.at[d - 1], class_peer(d))

    for d in range(1, 8):
        start(at_five(d))

    for n in range(4):
        own_g[n] = pltpu.roll(at_total[n], offset, 0)[:8]
    own_r[0] = pltpu.roll(jnp.broadcast_to(qkv_new_row, (48, 128)), offset, 0)[:8]
    own_r[1] = pltpu.roll(jnp.broadcast_to(proj_new_row, (48, 128)), offset, 0)[:8]

    for d in range(1, 4):
        place = fst.at[(mlp + 4 - d) % 4]
        remote(place, place, f8s.at[d - 1], f8r.at[d - 1], along_x(d)).wait_recv()
    fc_sums[0] = (fst[0] + fst[1]) + (fst[2] + fst[3])
    fc_sums[1] = fst[mlp]
    vec_three(2)

    for d in range(1, 8):
        place = ast.at[(mlp + 8 - d) % 4 + 4 * (core if d < 4 else 1 - core)]
        remote(place, place, a5s.at[d - 1], a5r.at[d - 1], class_peer(d)).wait_recv()
    total = ast[0]
    for n in range(1, 8):
        total = total + ast[n]
    at_sums[...] = total

    for a in range(GROUPS):
        gin_copy(a).wait()
        out_copy(a).wait()
    for copy in pending:
        copy.wait_send()
    for d in range(1, 4):
        fc_two(d).wait_send()


def to_column(row, eye):
    return jnp.sum(jnp.where(eye, row, 0.0), axis=1, keepdims=True)


def block(live_windows, region, tok, og, wq, wp, *arrays):
    sd = jax.ShapeDtypeStruct
    vm = pltpu.VMEM
    dma = pltpu.SemaphoreType.DMA
    return pl.pallas_call(
        block_kernel,
        out_shape=[
            sd((TOK, D), F32),
            sd((TOK, D), F32),
            sd((2, 4, 96, D), F32),
            sd((24, D), F32),
            sd((2, 8, D), F32),
            sd((16, D), F32),
            sd((4, 8, D), F32),
            sd((2, 8, 128), F32),
            sd((8, QKV), F32),
            sd((8, D), F32),
            sd((4, 8, D), F32),
        ],
        in_specs=[pl.BlockSpec(memory_space=pltpu.SMEM), pl.BlockSpec(memory_space=vm)]
        + [pl.BlockSpec(memory_space=pl.ANY)] * 4
        + [pl.BlockSpec(memory_space=vm)] * len(arrays),
        out_specs=[pl.BlockSpec(memory_space=pl.ANY)] * 2 + [pl.BlockSpec(memory_space=vm)] * 9,
        scratch_shapes=[
            vm((ROWS, D), F32),
            vm((ROWS, D), F32),
            vm((ROWS, 1), F32),
            vm((ROWS, 1), F32),
            vm((ROWS, D), BF16),
            vm((ROWS, D), BF16),
            vm((ROWS, QKV), BF16),
            vm((ROWS, D), BF16),
            vm((GROUPS * PER, SETS, KEYS, LANES), F32),
            vm((ROWS, D), BF16),
            vm((ROWS, FF), BF16),
            vm((ROWS, FF), BF16),
            vm((ROWS, QKV), F32),
            vm((PER, LANES, 128), BF16),
            vm((PER, SETS, KEYS, LANES), F32),
            vm((GROUPS * PER, KEYS, LANES), F32),
            vm((PER, SETS, KEYS, LANES), F32),
            vm((G_ROWS, D), F32),
            vm((G_ROWS, D), F32),
            vm((8, 8, D), F32),
            vm((8, FF), F32),
            vm((D, QKV), BF16),
            vm((D, D), BF16),
            vm((D, FF), BF16),
            vm((FF, D), BF16),
            vm((TOK, D), BF16),
            vm((TOK, D), BF16),
            vm((D, QKV), F32),
            vm((D, D), F32),
            vm((ROWS, D), F32),
            dma((4,)), dma((6,)),
            vm((2, 4, 4, 96, D), BF16),
            vm((4, 4, 96, D), BF16),
            vm((3, 4, 96, D), BF16),
            vm((4, 96, D), BF16),
            vm((3, 96, D), BF16),
            vm((4, 96, D), BF16),
            vm((4, 8, D), F32),
            vm((4, 2, 4, 48, D), BF16),
            vm((4, 4, 48, D), BF16),
            vm((4, 3, 48, D), BF16),
            vm((4, 4, 48, D), BF16),
            vm((4, 4, 48, D), BF16),
            vm((8, 16, D), F32),
            vm((3, 8, 8, D), F32),
            vm((3, 16, 8, D), F32),
            vm((4, 48, D), F32),
            dma((3, 3)), dma((3, 3)), dma((3, 2)), dma((3, 2)),
            dma((4,)), dma((4,)),
            dma((3,)), dma((3,)), dma((3,)), dma((3,)), dma((3,)), dma((3,)),
            dma((3,)), dma((3,)), dma((1,)), dma((1,)), dma((3,)), dma((3,)),
            dma((4,)), dma((4,)),
            dma((4, 3)), dma((4, 3)), dma((4, 3)), dma((4, 3)), dma((4, 3)), dma((4, 3)),
            dma((7,)), dma((7,)),
            dma((3, 7)), dma((3, 7)), dma((3, 15)), dma((3, 15)),
        ],
        compiler_params=pltpu.CompilerParams(
            vmem_limit_bytes=63 * 1024 * 1024, collective_id=0, has_side_effects=True
        ),
        cost_estimate=pl.CostEstimate(flops=14_000_000_000, bytes_accessed=20_000_000, transcendentals=3_000_000),
        name="block",
    )(live_windows, region, tok, og, wq, wp, *arrays)


def finish_kernel(
    fin, vec, fc_sums, at_sums, own_g, own_r, own_wq, own_wp, b1, fc1, fc2, fc1_b, fc1_row, fc2_col, qkv_col, proj_col,
    small, small_state, table, table_state, out_from, gin_from,
    qkv_grad, qkv_row_new, qkv_col_new, qkv_new, qkv_low, proj_grad, proj_row_new, proj_col_new, proj_new, proj_low,
    fc1_grad, fc1_row_new, fc1_col_new, fc1_new, fc1_low, fc2_grad, fc2_row_new, fc2_col_new, fc2_new, fc2_low,
    b1_grad, b1_state_new, b1_new, small_grad, small_state_new, small_new, table_grad, table_state_new, table_new,
    out_to, gin_to, held, sem_in, sem_out,
):
    def parts(src, dst, n):
        for i in range(4):
            rows = pl.ds(304 * i, 304 if i < 3 else TOK - 912)
            here = held.at[n, rows]
            yield (
                pltpu.make_async_copy(src.at[rows], here, sem_in.at[n, i]),
                pltpu.make_async_copy(here, dst.at[rows], sem_out.at[n, i]),
            )

    copies = list(parts(out_from, out_to, 0)) + list(parts(gin_from, gin_to, 1))
    for copy, _ in copies:
        copy.start()
    for copy, then in copies:
        copy.wait()
        then.start()
    mlp = lax.axis_index("mlp")
    eye = iota((D, D), 0) == iota((D, D), 1)
    eye8 = iota((8, 128), 0) == iota((8, 128), 1)

    def line(x):
        return x.reshape(1, -1)

    def total(x):
        return jnp.sum(jnp.sum(x, axis=0, keepdims=True), axis=1, keepdims=True)

    def fresh(old, mean):
        return DECAY * old + (1.0 - DECAY) * (mean + EPS_SQ)

    def owned(grads, cols, over, row, row_total, weight, col_old, rate, outs):
        grad_out, row_out, col_out, new_out, low_out = outs
        width = grads.shape[1]
        col_new = fresh(line(col_old[...]), cols * (1.0 / D))
        mean = row_total * (1.0 / D)
        norm = mean * jnp.sum(over * (1.0 / col_new), axis=1, keepdims=True) * (1.0 / (D * width))
        step = grads * lax.rsqrt(row * col_new * (1.0 / mean))
        new = weight - rate * (step * clip_scale(norm))
        grad_out[...] = grads[:3]
        row_out[...] = jnp.sum(jnp.where(eye8, row, 0.0), axis=0)[:3]
        col_out[...] = col_new.reshape(width)
        new_out[...] = new[:3]
        low_out[...] = new.astype(BF16)[:3]

    def by_part(take):
        return jnp.concatenate([take(g)[:, 128 * p : 128 * p + 128] for p in range(3) for g in range(SETS)], axis=1)

    owned(
        by_part(lambda g: own_g[g]), by_part(lambda g: at_sums[g : g + 1, :]),
        by_part(lambda g: at_sums[4 + g : 5 + g, :]), own_r[0][:, :1], at_sums[8:9, :1], own_wq[...], qkv_col,
        D ** (-0.5), (qkv_grad, qkv_row_new, qkv_col_new, qkv_new, qkv_low),
    )
    owned(
        own_g[3], at_sums[3:4, :], at_sums[7:8, :], own_r[1][:, :1], at_sums[9:10, :1], own_wp[...], proj_col,
        (D // 8) ** (-0.5), (proj_grad, proj_row_new, proj_col_new, proj_new, proj_low),
    )

    def update(grad, weight, row, col, mean, norm, rate, grad_out, new_out, low_out):
        row = row * (1.0 / mean)
        factor = rate * clip_scale(norm)
        for r in range(0, D, 48):
            rows = slice(r, r + 48)
            g = grad[rows, :]
            new = weight[rows, :] - (g * lax.rsqrt(row[rows] * col)) * factor
            grad_out[rows, :] = g
            new_out[rows, :] = new
            low_out[rows, :] = new.astype(BF16)

    row_new = fresh(line(fc1_row[...]), fc_sums[0, 0:1, :] * (1.0 / FF))
    mean = row_mean(row_new)
    norm = mean * row_mean(fc_sums[0, 1:2, :] * (1.0 / row_new)) * (1.0 / FF)
    fc1_row_new[...] = row_new.reshape(D)
    fc1_col_new[...] = fc_sums[1, 5]
    update(
        fin.at[0], fc1, to_column(row_new, eye), fc_sums[1, 5:6, :], mean, norm, D ** (-0.5),
        fc1_grad, fc1_new, fc1_low,
    )
    col_new = fresh(line(fc2_col[...]), fc_sums[0, 2:3, :] * (1.0 / FF))
    mean = fc_sums[0, 4:5, :1] * (1.0 / FF)
    norm = mean * row_mean(fc_sums[0, 3:4, :] * (1.0 / col_new)) * (1.0 / FF)
    fc2_row_new[...] = fc_sums[1, 6]
    fc2_col_new[...] = col_new.reshape(D)
    update(
        fin.at[1], fc2, to_column(fc_sums[1, 6:7, :], eye), col_new, mean, norm, FF ** (-0.5),
        fc2_grad, fc2_new, fc2_low,
    )

    def stepped(grad, old):
        state = fresh(old, grad * grad)
        return state, grad * lax.rsqrt(state)

    norm = jnp.zeros((1, 1), F32)
    for m in range(4):
        step = stepped(vec[4 + m : 5 + m, :], b1[m, 4:5, :])[1]
        norm = norm + jnp.sum(step * step, axis=1, keepdims=True)
    grad = vec[pl.ds(4 + mlp, 1), :]
    state, step = stepped(grad, b1[mlp, 4:5, :])
    b1_grad[...] = grad.reshape(D)
    b1_state_new[...] = state.reshape(D)
    b1_new[...] = (line(fc1_b[...]) - VEC_RATE * (step * clip_scale(norm * (1.0 / FF)))).reshape(D)

    grad = jnp.concatenate([vec[n : n + 1, :] for n in (20, 21, 22, 23, 0, 1, 2, 3)], axis=1)
    state, step = stepped(grad, line(small_state[...]))
    norm = jnp.sum(step * step, axis=1, keepdims=True) * (1.0 / (8 * D))
    small_grad[...] = grad.reshape(8 * D)
    small_state_new[...] = state.reshape(8 * D)
    small_new[...] = (line(small[...]) - VEC_RATE * (step * clip_scale(norm))).reshape(8 * D)

    grad = vec[8:20, :169]
    state, step = stepped(grad, table_state[...])
    norm = total(step * step) * (1.0 / (169 * HEADS))
    table_grad[...] = grad
    table_state_new[...] = state
    table_new[...] = table[...] - VEC_RATE * (step * clip_scale(norm))
    for _, then in copies:
        then.wait()


def finish(*arrays):
    sd = jax.ShapeDtypeStruct
    vm = pltpu.VMEM

    def owned(width):
        return [sd((3, width), F32), sd((3,), F32), sd((width,), F32), sd((3, width), F32), sd((3, width), BF16)]

    shard = [sd((D, D), F32), sd((D,), F32), sd((D,), F32), sd((D, D), F32), sd((D, D), BF16)]
    out_shape = owned(QKV) + owned(D) + shard + shard
    out_shape += [sd((D,), F32)] * 3 + [sd((8 * D,), F32)] * 3 + [sd((HEADS, 169), F32)] * 3 + [sd((TOK, D), F32)] * 2
    return pl.pallas_call(
        finish_kernel,
        out_shape=out_shape,
        in_specs=[pl.BlockSpec(memory_space=vm)] * (len(arrays) - 2) + [pl.BlockSpec(memory_space=pl.ANY)] * 2,
        out_specs=[pl.BlockSpec(memory_space=vm)] * (len(out_shape) - 2) + [pl.BlockSpec(memory_space=pl.ANY)] * 2,
        scratch_shapes=[vm((2, TOK, D), F32), pltpu.SemaphoreType.DMA((2, 4)), pltpu.SemaphoreType.DMA((2, 4))],
        compiler_params=pltpu.CompilerParams(vmem_limit_bytes=63 * 1024 * 1024),
        name="finish",
    )(*arrays)


def clip_scale(mean_square):
    return 1.0 / jnp.maximum(1.0, jnp.sqrt(mean_square))


def per_device(
    tokens_in, out_grad, window_live, region_ids, qkv_weight, proj_weight, rel_table, small_params,
    fc1_weight, fc1_bias, fc2_weight, qkv_row, qkv_col, proj_row, proj_col, fc1_row, fc1_col,
    fc2_row, fc2_col, fc1_bias_state, small_state, table_state,
):
    out, gin, fin, *parts = block(
        window_live, region_ids, tokens_in, out_grad, qkv_weight, proj_weight, rel_table.T, small_params,
        fc1_weight, fc2_weight, fc1_bias, fc1_bias_state, fc1_col, fc2_row, qkv_row, proj_row,
    )
    *outs, table_grad, table_state_new, table_new, out, gin = finish(
        fin.reshape(2, D, D), *parts, fc1_weight, fc2_weight, fc1_bias, fc1_row, fc2_col, qkv_col, proj_col,
        small_params, small_state, rel_table.T, table_state.T, out, gin,
    )
    return (out, gin, *outs, table_grad.T, table_state_new.T, table_new.T)


def solution(mesh):
    tokens, owner = P(("win", "mlp"), None), P(("win", "mlp"))
    whole, part = P(), P("mlp")
    return jax.shard_map(
        per_device,
        mesh=mesh,
        in_specs=(
            tokens, tokens, owner, owner, whole, whole, whole, whole, P(None, "mlp"), part, P("mlp", None),
            whole, whole, whole, whole, whole, part, part, whole, part, whole, whole,
        ),
        out_specs=(
            tokens, tokens,
            tokens, owner, whole, tokens, tokens,
            tokens, owner, whole, tokens, tokens,
            P(None, "mlp"), whole, part, P(None, "mlp"), P(None, "mlp"),
            P("mlp", None), part, whole, P("mlp", None), P("mlp", None),
            part, part, part,
            whole, whole, whole,
            whole, whole, whole,
        ),
        check_vma=False,
    )
```

```python
import functools
import math

import jax
import jax.numpy as jnp
from jax import lax
from jax.experimental import pallas as pl
from jax.experimental.pallas import tpu as pltpu
from jax.sharding import PartitionSpec as P

D = 384
FF = 1536
QKV = 3 * D
HEADS = 12
WIN = 7
SPAN = WIN * WIN
STEP = 10
DECAY = 1.0 - STEP ** (-0.8)
EPS_NORM = 1e-05
EPS_SQ = 1e-30
VEC_RATE = 0.3
SCALE = 32 ** (-0.5)
FAR = -1e30

GROUPS = 3
PER = 8
G_TOK = PER * SPAN
G_ROWS = 400
ROWS = GROUPS * G_ROWS
TOK = GROUPS * G_TOK
CHUNK = 64
KEYS = 56
SETS = 3
LANES = 4 * CHUNK

MESH = pl.DeviceIdType.MESH
F32 = jnp.float32
BF16 = jnp.bfloat16


def dot(a, b):
    return jnp.dot(a, b, preferred_element_type=F32)


def dot_nt(a, b):
    return lax.dot_general(a, b, (((1,), (1,)), ((), ())), preferred_element_type=F32)


def dot_tn(a, b):
    return lax.dot_general(a, b, (((0,), (0,)), ((), ())), preferred_element_type=F32)


def dot_exact(a, b):
    return jnp.dot(a, b, precision=lax.Precision.HIGHEST, preferred_element_type=F32)


def iota(shape, dim):
    return lax.broadcasted_iota(jnp.int32, shape, dim)


def fold_rows(x):
    total = x[0:8]
    for i in range(1, x.shape[0] // 8):
        total = total + x[8 * i : 8 * i + 8]
    return total


def row_mean(x):
    return jnp.sum(x, axis=1, keepdims=True) * (1.0 / D)


def normalize(x):
    center = x - row_mean(x)
    inverse = lax.rsqrt(row_mean(center * center) + EPS_NORM)
    return center * inverse, inverse


def normalize_back(u, gain, scaled, inverse):
    weighted = u * gain
    return inverse * (weighted - row_mean(weighted) - scaled * row_mean(weighted * scaled))


def gelu_parts(v):
    e = jnp.exp(-0.5 * v * v)
    t = 1.0 / (1.0 + (0.3275911 * 0.5**0.5) * jnp.abs(v))
    poly = 1.061405429 * t - 1.453152027
    poly = poly * t + 1.421413741
    poly = poly * t - 0.284496736
    poly = poly * t + 0.254829592
    tail = (0.5 * e) * (poly * t)
    phi = jnp.where(v < 0.0, tail, 1.0 - tail)
    return v * phi, phi + v * e * (2.0 * math.pi) ** (-0.5)


def barrel(x, amount, right):
    width = x.shape[1]
    for k in range(7):
        step = 1 << k
        moved = pltpu.roll(x, step if right else width - step, 1)
        x = jnp.where((amount & step) != 0, moved, x)
    return x


def embed(i):
    return 13 * (i // WIN) + i % WIN


def chunk_start(w):
    return pl.multiple_of((w // PER) * G_ROWS + (w % PER) * 48, 16)


def prologue(region, table, x_ref, emask, bias, mask, tok):
    for a in range(GROUPS):
        for r in range(0, G_TOK, 56):
            src = a * G_TOK + r
            low = src // 16 * 16
            x_ref[a * G_ROWS + r : a * G_ROWS + r + 56, :] = (
                tok[low : low + 64 if low + 64 <= TOK else TOK, :].astype(F32)[src - low : src - low + 56]
            )
        x_ref[a * G_ROWS + G_TOK : (a + 1) * G_ROWS, :] = jnp.zeros((G_ROWS - G_TOK, D), F32)
    row = iota((LANES, 128), 0)
    lane = iota((LANES, 128), 1)
    for b in range(PER):
        i = row % CHUNK
        keep = (i >= b) & (i < b + SPAN) & (lane // 32 == row // CHUNK)
        emask[b] = jnp.where(keep, 1.0, 0.0).astype(BF16)
    j = iota((KEYS, 256), 0)
    amount = jnp.maximum(84 - embed(j), 0)
    jl = iota((KEYS, LANES), 0)
    il = iota((KEYS, LANES), 1) % CHUNK
    for g in range(SETS):
        base = jnp.zeros((KEYS, LANES), F32)
        for h in range(4):
            line = jnp.concatenate([table[4 * g + h : 4 * g + h + 1, :], jnp.zeros((1, 87), F32)], axis=1)
            wide = jnp.broadcast_to(line, (KEYS, 256))
            wide = barrel(wide, amount, False)[:, :128]
            lane_to = iota((128, LANES), 1) - CHUNK * h
            pick = (iota((128, LANES), 0) == embed(lane_to)) & (lane_to >= 0) & (lane_to < SPAN)
            base = base + dot_exact(wide, jnp.where(pick, 1.0, 0.0))
        for b in range(PER):
            moved = pltpu.roll(pltpu.roll(base, b, 0), b, 1) if b else base
            key_ok = (jl >= b) & (jl < b + SPAN)
            query_ok = (il >= b) & (il < b + SPAN)
            bias[b, g] = jnp.where(key_ok, jnp.where(query_ok, moved, 0.0), FAR)
    eye = iota((CHUNK, CHUNK), 0) == iota((CHUNK, CHUNK), 1)
    region_row = jnp.concatenate([region[...].reshape(1, TOK).astype(F32), jnp.zeros((1, 104), F32)], axis=1)
    for w in range(GROUPS * PER):
        start = (w // PER) * G_TOK + (w % PER) * 48
        line = region_row[:, start : start + CHUNK]
        column = jnp.sum(jnp.where(eye, jnp.broadcast_to(line, (CHUNK, CHUNK)), 0.0), axis=1, keepdims=True)
        wide = jnp.concatenate([line] * 4, axis=1)
        mask[w] = jnp.where(column[:KEYS] != wide, -100.0, 0.0)


def pad_keys(x):
    return jnp.concatenate([x, jnp.zeros((CHUNK - KEYS, x.shape[1]), x.dtype)], axis=0)


def spread(x, keep):
    return jnp.concatenate([x] * 4, axis=0) * keep


def collect(full):
    head = iota((CHUNK, 128), 1) // 32
    parts = [full[CHUNK * h : CHUNK * (h + 1)] for h in range(4)]
    low = jnp.where(head == 0, parts[0], parts[1])
    high = jnp.where(head == 2, parts[2], parts[3])
    return jnp.where(head < 2, low, high)


def block_kernel(
    live_windows, region, tok_in, og_in, wq_in, wp_in, table, small, fc1, fc2,
    fc1_b, fc1_state, fc1_col, fc2_row, qkv_row, proj_row,
    out_to, gin_to, fin, vec, fc_sums, at_sums, own_g, own_r, own_wq, own_wp, b1,
    x_ref, xh1, inv1, inv2, n1, n2, qkv, att_b, probs, back, hidden, ig, dqkv,
    emask, bias, mask, tacc, s1, s2, sums, b1_acc, wq_b, wp_b, w1, w2, tok, og, wq, wp, stage, in_sem, out_sem,
    fcl, fr1, fr2, ft, fr3, fr4, fst, atl, ar1, ar2, ar3, ar4, ast, vx, vy, at_total,
    w_send, w_recv, pair_send, pair_recv, f1s, f1r, f2s, f2r, f3s, f3r, f4s, f4r, f5s, f5r, f7s, f7r, f8s, f8r,
    a1s, a1r, a2s, a2r, a3s, a3r, a4s, a4r, a5s, a5r, vxs, vxr, vys, vyr,
):
    win, mlp = lax.axis_index("win"), lax.axis_index("mlp")
    z, y, core = win // 8, (win // 2) % 4, win % 2
    pair = win + 1 - 2 * core

    def along_x(d):
        return win, (mlp + d) % 4

    def along_y(d):
        return z * 8 + ((y + d) % 4) * 2 + core, mlp

    def along_z(d):
        return ((z + d) % 4) * 8 + y * 2 + core, mlp

    def plane_peer(d):
        return ((z + d // 4) % 4) * 8 + ((y + d % 4) % 4) * 2 + core, mlp

    def class_peer(d):
        return pair if d >= 4 else win, (mlp + d) % 4

    loads = [
        pltpu.make_async_copy(src, dst, in_sem.at[n])
        for n, (src, dst) in enumerate(((tok_in, tok), (og_in, og), (wq_in, wq), (wp_in, wp)))
    ]
    for copy in loads:
        copy.start()
    barrier = pltpu.get_barrier_semaphore()
    peers = [class_peer(d) for d in range(1, 8)]
    peers += [plane_peer(d) for d in range(1, 16)]
    for peer in peers:
        pl.semaphore_signal(barrier, inc=1, device_id=peer, device_id_type=MESH)

    def remote(src, dst, send, recv, peer):
        return pltpu.make_async_remote_copy(
            src_ref=src, dst_ref=dst, send_sem=send, recv_sem=recv, device_id=peer, device_id_type=MESH
        )

    def param(part):
        return small[D * part : D * part + D].reshape(1, D)

    pending = []

    def start(copy):
        copy.start()
        pending.append(copy)
        return copy

    def shard(m):
        at = pl.multiple_of(m * D, D)
        half = pl.ds(pl.multiple_of(core * (D // 2), 16), D // 2)
        half_at = pl.ds(pl.multiple_of(m * D + core * (D // 2), 16), D // 2)
        return w1.at[half, pl.ds(at, D)], w2.at[half_at, :], b1.at[m]

    mine = shard(mlp)
    cols = pl.ds(pl.multiple_of(mlp * D, D), D)
    w1[:, cols] = fc1[...].astype(BF16)
    w2[cols, :] = fc2[...].astype(BF16)
    b1[mlp, 0:4] = jnp.broadcast_to(fc1_b[...].reshape(1, D), (4, D))
    b1[mlp, 4:8] = jnp.broadcast_to(fc1_state[...].reshape(1, D), (4, D))
    pl.semaphore_wait(barrier, 22)
    sends = []
    for d in range(1, 4):
        for n in range(3):
            sends.append(start(remote(mine[n], mine[n], w_send.at[d - 1, n], w_recv.at[d - 1, n], along_x(d))))

    live = live_windows[0]
    for n in range(1, GROUPS * PER):
        live = live + live_windows[n]
    live = live * SPAN
    for copy in loads:
        copy.wait()
    prologue(region, table, x_ref, emask, bias, mask, tok)
    for g in range(SETS):
        for part in range(3):
            wq_b[:, D * g + 128 * part : D * g + 128 * part + 128] = wq[
                :, D * part + 128 * g : D * part + 128 * g + 128
            ].astype(BF16)
    wp_b[...] = wp[...].astype(BF16)
    sums[...] = jnp.zeros_like(sums)
    b1_acc[...] = jnp.zeros_like(b1_acc)
    tacc[...] = jnp.zeros_like(tacc)
    att = dqkv.at[:, :D]
    xh2 = dqkv.at[:, D : 2 * D]
    dqkv_b = ig.at[:, :QKV]
    dqkv[:, :D] = jnp.zeros((ROWS, D), F32)

    for a in range(GROUPS):
        for r in range(0, G_TOK, 56):
            src = a * G_TOK + r
            low = src // 16 * 16
            rows = og[low : low + 64 if low + 64 <= TOK else TOK, :].astype(F32)[src - low : src - low + 56]
            keep = iota((56, D), 0) + src < live
            x = jnp.where(keep, rows, 0.0)
            s2[r : r + 56, :] = x
            sums[7] += fold_rows(x)
        s2[G_TOK:G_ROWS, :] = jnp.zeros((G_ROWS - G_TOK, D), F32)
        back[a * G_ROWS : (a + 1) * G_ROWS, :] = s2[...].astype(BF16)

    shift_q = jnp.concatenate(
        [
            part[:, 128 * g : 128 * g + 128]
            for g in range(SETS)
            for part in (param(2), jnp.zeros((1, D), F32), param(3))
        ],
        axis=1,
    )

    @pl.loop(0, 5, unroll=5)
    def _(t):
        for c in range(15):
            rows = pl.ds(pl.multiple_of(t * 240 + c * 16, 16), 16)
            scaled, inverse = normalize(x_ref[rows, :])
            xh1[rows, :] = scaled
            inv1[rows, :] = inverse
            n1[rows, :] = (scaled * param(0) + param(1)).astype(BF16)

    @pl.loop(0, 5, unroll=5)
    def _(t):
        rows = pl.ds(pl.multiple_of(t * 240, 16), 240)
        qkv[rows, :] = (dot(n1[rows, :], wq_b[...]) + shift_q).astype(BF16)

    @pl.loop(0, PER, unroll=4)
    def _(b):
        for a in range(GROUPS):
            rows = pl.ds(pl.multiple_of(a * G_ROWS + b * 48, 16), CHUNK)
            w = a * PER + b
            for g in range(SETS):
                q = qkv[rows, D * g : D * g + 128]
                k = qkv[rows, D * g + 128 : D * g + 256]
                v = qkv[rows, D * g + 256 : D * g + 384]
                scores = dot_nt(k, spread(q, emask[b]))[:KEYS] * SCALE + (bias[b, g] + mask[w])
                p = jnp.exp(scores - jnp.max(scores, axis=0, keepdims=True))
                p = p * (1.0 / jnp.sum(p, axis=0, keepdims=True))
                probs[w, g] = p
                o = collect(dot_tn(pad_keys(p).astype(BF16), v))
                i = iota((CHUNK, 128), 0)
                att[rows, 128 * g : 128 * g + 128] += jnp.where((i >= b) & (i < b + SPAN), o, 0.0)

    forwards = []
    for d in range(1, 4):
        came = shard((mlp + 4 - d) % 4)
        for n in range(3):
            sends[3 * (d - 1) + n].wait_recv()
            if n < 2:
                copy = remote(came[n], came[n], pair_send.at[d - 1, n], pair_recv.at[d - 1, n], (pair, mlp))
                forwards.append(start(copy))

    @pl.loop(0, GROUPS, unroll=3)
    def _(a):
        rows = pl.ds(pl.multiple_of(a * G_ROWS, 16), G_ROWS)
        att_b[rows, :] = att[rows, :].astype(BF16)
        s1[...] = dot(att_b[rows, :], wp_b[...])

        for c in range(25):
            here = pl.ds(pl.multiple_of(a * G_ROWS + 16 * c, 16), 16)
            middle = x_ref[here, :] + (s1[16 * c : 16 * c + 16, :] + param(4))
            stage[here, :] = middle
            scaled, inverse = normalize(middle)
            xh2[here, :] = scaled
            inv2[here, :] = inverse
            n2[here, :] = (scaled * param(5) + param(6)).astype(BF16)

    for copy in forwards:
        copy.wait_recv()

    @pl.loop(0, 5, unroll=5)
    def _(mt):
        rows = pl.ds(pl.multiple_of(mt * 240, 16), 240)
        b1_row = jnp.concatenate([b1[m, 0:1, :] for m in range(4)], axis=1)
        for nt in range(6):
            cols = slice(256 * nt, 256 * nt + 256)
            inner = dot(n2[rows, :], w1[:, cols]) + b1_row[:, cols]
            up = dot_nt(back[rows, :], w2[cols, :])
            total = b1_acc[:, cols]
            for c in range(15):
                act, slope = gelu_parts(inner[16 * c : 16 * c + 16])
                here = pl.ds(pl.multiple_of(mt * 240 + 16 * c, 16), 16)
                hidden[here, cols] = act.astype(BF16)
                grad = (up[16 * c : 16 * c + 16] * slope).astype(BF16)
                ig[here, cols] = grad
                total = total + fold_rows(grad.astype(F32))
            b1_acc[:, cols] = total

    g2 = dot_tn(hidden[...], back[...]).astype(BF16)
    g1 = dot_tn(n2[...], ig[...]).astype(BF16)
    for m in range(4):
        fcl[0, m] = g1[:, D * m : D * m + D].reshape(4, 96, D)
        fcl[1, m] = g2[D * m : D * m + D].reshape(4, 96, D)
    fc_one = [start(remote(fcl.at[1 - core, m], fr1.at[m], f1s.at[m], f1r.at[m], (pair, mlp))) for m in range(4)]

    def middle_back(a):
        rows = slice(a * G_ROWS, (a + 1) * G_ROWS)
        s2[...] = dot_nt(ig[rows, :], w1[...])
        for c in range(25):
            here = slice(16 * c, 16 * c + 16)
            at = slice(a * G_ROWS + 16 * c, a * G_ROWS + 16 * c + 16)
            u = s2[here, :]
            scaled = xh2[at, :]
            sums[5] += fold_rows(u * scaled)
            sums[6] += fold_rows(u)
            mg = normalize_back(u, param(5), scaled, inv2[at, :]) + back[at, :].astype(F32)
            x_ref[at, :] = mg
            low = mg.astype(BF16)
            n2[at, :] = low
            sums[4] += fold_rows(low.astype(F32))

    def out_copy(a):
        return pltpu.make_async_copy(
            stage.at[pl.ds(a * G_ROWS, G_TOK)], out_to.at[pl.ds(a * G_TOK, G_TOK)], out_sem.at[a]
        )

    def block_out(a):
        rows = slice(a * G_ROWS, (a + 1) * G_ROWS)
        s1[...] = dot(hidden[rows, :], w2[...])
        for c in range(25):
            at = slice(a * G_ROWS + 16 * c, a * G_ROWS + 16 * c + 16)
            r = stage[at, :] + (s1[16 * c : 16 * c + 16, :] + param(7))
            keep = iota((16, D), 0) + (a * G_TOK + 16 * c) < live
            stage[at, :] = jnp.where(keep, r, 0.0)
        out_copy(a).start()

    p = iota((D, D), 0)
    inner_p = p % 48
    owned = 24 * (inner_p // 3) + 12 * (p // 192) + 3 * ((p // 48) % 4) + inner_p % 3
    order = jnp.where(iota((D, D), 1) == owned, 1.0, 0.0).astype(BF16)

    def ordered(grad):
        return dot(order, grad.astype(BF16)).astype(BF16).reshape(2, 4, 48, D)

    def at_one(n):
        return remote(atl.at[n, 1 - core], ar1.at[n], a1s.at[n], a1r.at[n], (pair, mlp))

    def at_add_one(n):
        at_one(n).wait_recv()
        for i in range(4):
            ar1[n, i] = (ar1[n, i].astype(F32) + atl[n, core, i].astype(F32)).astype(BF16)
        for d in range(1, 4):
            start(remote(ar1.at[n, (mlp + d) % 4], ar2.at[n, d - 1], a2s.at[n, d - 1], a2r.at[n, d - 1], along_x(d)))

    def at_add_two(n):
        total = ar1[n, mlp].astype(F32)
        for d in range(1, 4):
            remote(ar1.at[n, 0], ar2.at[n, d - 1], a2s.at[n, d - 1], a2r.at[n, d - 1], along_x(d)).wait_recv()
            total = total + ar2[n, d - 1].astype(F32)
        ar3[n, y] = total.astype(BF16)
        for d in range(1, 4):
            start(remote(ar3.at[n, y], ar3.at[n, y], a3s.at[n, d - 1], a3r.at[n, d - 1], along_y(d)))

    def at_add_three(n):
        for d in range(1, 4):
            came = ar3.at[n, (y + 4 - d) % 4]
            remote(came, came, a3s.at[n, d - 1], a3r.at[n, d - 1], along_y(d)).wait_recv()
        total = ar3[n, 0].astype(F32) + ar3[n, 1].astype(F32)
        ar4[n, z] = (total + ar3[n, 2].astype(F32) + ar3[n, 3].astype(F32)).astype(BF16)
        for d in range(1, 4):
            start(remote(ar4.at[n, z], ar4.at[n, z], a4s.at[n, d - 1], a4r.at[n, d - 1], along_z(d)))

    def at_finish(n):
        for d in range(1, 4):
            came = ar4.at[n, (z + 4 - d) % 4]
            remote(came, came, a4s.at[n, d - 1], a4r.at[n, d - 1], along_z(d)).wait_recv()
        total = ar4[n, 0].astype(F32) + ar4[n, 1].astype(F32)
        at_total[n] = total + ar4[n, 2].astype(F32) + ar4[n, 3].astype(F32)

    def to_axes(dx, dy, dz):
        return ((z + dz) % 4) * 8 + ((y + dy) % 4) * 2 + core, (mlp + dx) % 4

    def first_axis(d):
        return to_axes(d * (1 - core), 0, d * core)

    def second_axis(d):
        return to_axes(d * core, d * (1 - core), 0)

    def third_axis(d):
        return to_axes(0, d * core, d * (1 - core))

    def last_axis(d):
        return to_axes(0, d * (1 - core), d * core)

    block_at = y * (1 - core) + z * core
    second = y * (1 - core) + mlp * core
    third = z * (1 - core) + y * core

    def fc_two(d):
        return remote(fr1.at[0], fr2.at[d - 1], f2s.at[d - 1], f2r.at[d - 1], first_axis(d))

    def fc_add_one():
        for m in range(4):
            fc_one[m].wait_recv()
            for i in range(4):
                fr1[m, i] = (fr1[m, i].astype(F32) + fcl[core, m, i].astype(F32)).astype(BF16)

        @pl.when(core == 0)
        def _():
            for d in range(1, 4):
                remote(fr1.at[(mlp + d) % 4], fr2.at[d - 1], f2s.at[d - 1], f2r.at[d - 1], first_axis(d)).start()

        @pl.when(core == 1)
        def _():
            for d in range(1, 4):
                remote(fr1.at[:, (z + d) % 4], fr2.at[d - 1], f2s.at[d - 1], f2r.at[d - 1], first_axis(d)).start()

    def fc_add_two():
        for d in range(1, 4):
            fc_two(d).wait_recv()
        for i in range(4):
            total = fr1[mlp * (1 - core) + i * core, i * (1 - core) + z * core].astype(F32)
            for d in range(1, 4):
                total = total + fr2[d - 1, i].astype(F32)
            ft[i] = total.astype(BF16)
        for d in range(1, 4):
            start(remote(ft.at[(second + d) % 4], fr3.at[d - 1], f3s.at[d - 1], f3r.at[d - 1], second_axis(d)))

    def fc_add_three():
        total = ft[second].astype(F32)
        for d in range(1, 4):
            remote(ft.at[0], fr3.at[d - 1], f3s.at[d - 1], f3r.at[d - 1], second_axis(d)).wait_recv()
            total = total + fr3[d - 1].astype(F32)
        fr4[third] = total.astype(BF16)
        for d in range(1, 4):
            start(remote(fr4.at[third], fr4.at[third], f4s.at[d - 1], f4r.at[d - 1], third_axis(d)))

    def fc_add_four():
        for d in range(1, 4):
            came = fr4.at[(third + 4 - d) % 4]
            remote(came, came, f4s.at[d - 1], f4r.at[d - 1], third_axis(d)).wait_recv()
        total = fr4[0].astype(F32) + fr4[1].astype(F32)
        fin[core, block_at] = total + fr4[2].astype(F32) + fr4[3].astype(F32)
        for d in range(1, 4):
            place = fin.at[core, block_at]
            start(remote(place, place, f5s.at[d - 1], f5r.at[d - 1], last_axis(d)))

    def fc_spread():
        for d in range(1, 4):
            place = fin.at[core, (block_at + 4 - d) % 4]
            remote(place, place, f5s.at[d - 1], f5r.at[d - 1], last_axis(d)).wait_recv()
        start(remote(fin.at[core], fin.at[core], f7s.at[0], f7r.at[0], (pair, mlp)))

    mine_at, plane_at = 4 * core + mlp, 4 * z + y

    def vec_one(n):
        for d in range(1, 8):
            place = vx.at[n, mine_at]
            start(remote(place, place, vxs.at[n, d - 1], vxr.at[n, d - 1], class_peer(d)))

    def vec_two(n):
        for d in range(1, 8):
            place = vx.at[n, (mlp + 8 - d) % 4 + 4 * (core if d < 4 else 1 - core)]
            remote(place, place, vxs.at[n, d - 1], vxr.at[n, d - 1], class_peer(d)).wait_recv()
        total = vx[n, 0]
        for i in range(1, 8):
            total = total + vx[n, i]
        vy[n, plane_at] = total
        for d in range(1, 16):
            place = vy.at[n, plane_at]
            start(remote(place, place, vys.at[n, d - 1], vyr.at[n, d - 1], plane_peer(d)))

    def vec_three(n):
        for d in range(1, 16):
            place = vy.at[n, 4 * ((z + 4 - d // 4) % 4) + (y + 4 - d % 4) % 4]
            remote(place, place, vys.at[n, d - 1], vyr.at[n, d - 1], plane_peer(d)).wait_recv()
        total = vy[n, 0]
        for i in range(1, 16):
            total = total + vy[n, i]
        vec[8 * n : 8 * n + 8, :] = total

    middle_back(0)
    middle_back(1)
    fc_add_one()
    middle_back(2)

    atl[3] = ordered(dot_tn(att_b[...], n2[...]))
    start(at_one(3))

    @pl.loop(0, GROUPS, unroll=3)
    def _(a):
        rows = pl.ds(pl.multiple_of(a * G_ROWS, 16), G_ROWS)
        att_b[rows, :] = dot_nt(n2[rows, :], wp_b[...]).astype(BF16)

    dqkv[...] = jnp.zeros_like(dqkv)

    def attention_back(g, half):
        @pl.loop(4 * half, 4 * half + 4, unroll=4)
        def _(b):
            keep = emask[b]
            total = tacc[b, g]
            for a in range(GROUPS):
                rows = pl.ds(pl.multiple_of(a * G_ROWS + b * 48, 16), CHUNK)
                q = qkv[rows, D * g : D * g + 128]
                k = qkv[rows, D * g + 128 : D * g + 256]
                v = qkv[rows, D * g + 256 : D * g + 384]
                qe = spread(q, keep)
                da = spread(att_b[rows, 128 * g : 128 * g + 128], keep)
                p = probs[a * PER + b, g]
                dp = dot_nt(v, da)[:KEYS]
                pd = p * dp
                ds = pad_keys(pd - p * jnp.sum(pd, axis=0, keepdims=True)).astype(BF16)
                total = total + ds.astype(F32)[:KEYS]
                dv = dot(pad_keys(p).astype(BF16), da)
                dk = dot(ds, qe) * SCALE
                dq = collect(dot_tn(ds, k)) * SCALE
                dqkv[rows, 384 * g : 384 * g + 128] += dq
                dqkv[rows, 384 * g + 128 : 384 * g + 256] += dk
                dqkv[rows, 384 * g + 256 : 384 * g + 384] += dv
            tacc[b, g] = total

    def qkv_grad(g):
        group = slice(384 * g, 384 * g + 384)

        @pl.loop(0, 5, unroll=5)
        def _(t):
            for c in range(15):
                rows = pl.ds(pl.multiple_of(t * 240 + c * 16, 16), 16)
                low = dqkv[rows, group].astype(BF16)
                dqkv_b[rows, group] = low
                wide = low.astype(F32)
                sums[2, :, 128 * g : 128 * g + 128] += fold_rows(wide[:, :128])
                sums[3, :, 128 * g : 128 * g + 128] += fold_rows(wide[:, 256:])

        atl[g] = ordered(dot_tn(n1[...], dqkv_b[:, group]))
        start(at_one(g))

    for part in range(4):
        vx[0, mine_at, part : part + 1, :] = jnp.sum(sums[4 + part], axis=0, keepdims=True)
    for m in range(4):
        vx[0, mine_at, 4 + m : 5 + m, :] = jnp.sum(b1_acc[:, D * m : D * m + D], axis=0, keepdims=True)
    vec_one(0)

    def table_back(g, n):
        j = iota((KEYS, 256), 0)
        amount = jnp.maximum(84 - embed(j), 0)
        total = tacc[0, g]
        for b in range(1, PER):
            total = total + pltpu.roll(pltpu.roll(tacc[b, g], KEYS - b, 0), LANES - b, 1)
        for h in range(4):
            lane_from = iota((LANES, 256), 0) - CHUNK * h
            pick = (iota((LANES, 256), 1) == embed(lane_from)) & (lane_from >= 0) & (lane_from < SPAN)
            wide = barrel(dot_exact(total, jnp.where(pick, 1.0, 0.0)), amount, True)
            wide = jnp.where(j < SPAN, wide, 0.0)
            vx[n, mine_at, 4 * (g % 2) + h : 4 * (g % 2) + h + 1, :] = jnp.concatenate(
                [jnp.sum(wide, axis=0, keepdims=True), jnp.zeros((1, 128), F32)], axis=1
            )

    attention_back(0, 0)
    at_add_one(3)
    vec_two(0)
    attention_back(0, 1)
    qkv_grad(0)
    fc_add_two()
    at_add_two(3)
    table_back(0, 1)
    at_add_one(0)
    attention_back(1, 0)
    at_add_three(3)
    at_add_two(0)
    attention_back(1, 1)
    qkv_grad(1)
    fc_add_three()
    at_add_three(0)
    vec_three(0)
    table_back(1, 1)
    vec_one(1)
    at_add_one(1)
    attention_back(2, 0)
    at_finish(3)
    at_add_two(1)
    fc_add_four()
    attention_back(2, 1)
    qkv_grad(2)
    at_add_three(1)
    vec_two(1)
    table_back(2, 2)
    at_add_one(2)

    def gin_copy(a):
        return pltpu.make_async_copy(
            x_ref.at[pl.ds(a * G_ROWS, G_TOK)], gin_to.at[pl.ds(a * G_TOK, G_TOK)], out_sem.at[3 + a]
        )

    def input_back(a):
        rows = slice(a * G_ROWS, (a + 1) * G_ROWS)
        s2[...] = dot_nt(dqkv_b[rows, :], wq_b[...])
        for c in range(25):
            here = slice(16 * c, 16 * c + 16)
            at = slice(a * G_ROWS + 16 * c, a * G_ROWS + 16 * c + 16)
            u = s2[here, :]
            scaled = xh1[at, :]
            sums[0] += fold_rows(u * scaled)
            sums[1] += fold_rows(u)
            x_ref[at, :] = normalize_back(u, param(0), scaled, inv1[at, :]) + x_ref[at, :]
        gin_copy(a).start()

    for a in range(GROUPS):
        input_back(a)
    for part in range(4):
        vx[2, mine_at, 4 + part : 5 + part, :] = jnp.sum(sums[part], axis=0, keepdims=True)
    vec_one(2)
    at_add_two(2)
    at_finish(0)
    fc_spread()
    for a in range(GROUPS):
        block_out(a)
    at_finish(1)
    vec_three(1)
    vec_two(2)

    remote(fin.at[1 - core], fin.at[1 - core], f7s.at[0], f7r.at[0], (pair, mlp)).wait_recv()
    eye = iota((D, D), 0) == iota((D, D), 1)

    def to_row(column):
        return jnp.sum(jnp.where(eye, column, 0.0), axis=0, keepdims=True)

    up = fin[0].reshape(D, D)
    down = fin[1].reshape(D, D)
    up_squares = up * up
    down_squares = down * down
    up_col = DECAY * fc1_col[...].reshape(1, D) + (1.0 - DECAY) * (
        jnp.sum(up_squares, axis=0, keepdims=True) * (1.0 / D) + EPS_SQ
    )
    down_row = DECAY * to_column(fc2_row[...].reshape(1, D), eye) + (1.0 - DECAY) * (row_mean(down_squares) + EPS_SQ)
    fst[mlp, 0:1] = to_row(jnp.sum(up_squares, axis=1, keepdims=True))
    fst[mlp, 1:2] = to_row(jnp.sum(up_squares * (1.0 / up_col), axis=1, keepdims=True))
    fst[mlp, 2:3] = jnp.sum(down_squares, axis=0, keepdims=True)
    fst[mlp, 3:4] = jnp.sum(down_squares * (1.0 / down_row), axis=0, keepdims=True)
    fst[mlp, 4:5] = jnp.broadcast_to(jnp.sum(down_row, axis=0, keepdims=True), (1, D))
    fst[mlp, 5:6] = up_col
    fst[mlp, 6:7] = to_row(down_row)
    fst[mlp, 7:8] = jnp.zeros((1, D), F32)
    for d in range(1, 4):
        start(remote(fst.at[mlp], fst.at[mlp], f8s.at[d - 1], f8r.at[d - 1], along_x(d)))

    at_add_three(2)

    offset = 48 - 3 * plane_at
    block_rows = pl.ds(pl.multiple_of(24 * (win // 2), 8), 24)
    shift = 24 - 3 * mine_at
    own_wq[...] = pltpu.roll(wq[block_rows, :], shift, 0)[:8]
    own_wp[...] = pltpu.roll(wp[block_rows, :], shift, 0)[:8]

    r48 = iota((48, D), 0)
    pick = iota((48, D), 1) == 24 * (r48 // 3) + 12 * core + 3 * mlp + r48 % 3

    def rows_new(state, mean):
        old = jnp.sum(jnp.where(pick, state, 0.0), axis=1, keepdims=True)
        return DECAY * old + (1.0 - DECAY) * (mean + EPS_SQ)

    at_finish(2)
    squares = [at_total[n] * at_total[n] for n in range(4)]
    qkv_new_row = rows_new(
        qkv_row[...].reshape(1, D), row_mean(squares[0] + squares[1] + squares[2]) * (1.0 / 3.0)
    )
    proj_new_row = rows_new(proj_row[...].reshape(1, D), row_mean(squares[3]))
    for n in range(4):
        over = squares[n] * (1.0 / (qkv_new_row if n < 3 else proj_new_row))
        ast[mine_at, n : n + 1] = jnp.sum(squares[n], axis=0, keepdims=True)
        ast[mine_at, 4 + n : 5 + n] = jnp.sum(over, axis=0, keepdims=True)
    ast[mine_at, 8:9] = jnp.broadcast_to(jnp.sum(qkv_new_row, axis=0, keepdims=True), (1, D))
    ast[mine_at, 9:10] = jnp.broadcast_to(jnp.sum(proj_new_row, axis=0, keepdims=True), (1, D))
    ast[mine_at, 10:16] = jnp.zeros((6, D), F32)

    def at_five(d):
        place = ast.at[mine_at]
        return remote(place, place, a5s.at[d - 1], a5r.at[d - 1], class_peer(d))

    for d in range(1, 8):
        start(at_five(d))

    for n in range(4):
        own_g[n] = pltpu.roll(at_total[n], offset, 0)[:8]
    own_r[0] = pltpu.roll(jnp.broadcast_to(qkv_new_row, (48, 128)), offset, 0)[:8]
    own_r[1] = pltpu.roll(jnp.broadcast_to(proj_new_row, (48, 128)), offset, 0)[:8]

    for d in range(1, 4):
        place = fst.at[(mlp + 4 - d) % 4]
        remote(place, place, f8s.at[d - 1], f8r.at[d - 1], along_x(d)).wait_recv()
    fc_sums[0] = (fst[0] + fst[1]) + (fst[2] + fst[3])
    fc_sums[1] = fst[mlp]
    vec_three(2)

    for d in range(1, 8):
        place = ast.at[(mlp + 8 - d) % 4 + 4 * (core if d < 4 else 1 - core)]
        remote(place, place, a5s.at[d - 1], a5r.at[d - 1], class_peer(d)).wait_recv()
    total = ast[0]
    for n in range(1, 8):
        total = total + ast[n]
    at_sums[...] = total

    for a in range(GROUPS):
        gin_copy(a).wait()
        out_copy(a).wait()
    for copy in pending:
        copy.wait_send()
    for d in range(1, 4):
        fc_two(d).wait_send()


def to_column(row, eye):
    return jnp.sum(jnp.where(eye, row, 0.0), axis=1, keepdims=True)


def block(live_windows, region, tok, og, wq, wp, *arrays):
    sd = jax.ShapeDtypeStruct
    vm = pltpu.VMEM
    dma = pltpu.SemaphoreType.DMA
    return pl.pallas_call(
        block_kernel,
        out_shape=[
            sd((TOK, D), F32),
            sd((TOK, D), F32),
            sd((2, 4, 96, D), F32),
            sd((24, D), F32),
            sd((2, 8, D), F32),
            sd((16, D), F32),
            sd((4, 8, D), F32),
            sd((2, 8, 128), F32),
            sd((8, QKV), F32),
            sd((8, D), F32),
            sd((4, 8, D), F32),
        ],
        in_specs=[pl.BlockSpec(memory_space=pltpu.SMEM), pl.BlockSpec(memory_space=vm)]
        + [pl.BlockSpec(memory_space=pl.ANY)] * 4
        + [pl.BlockSpec(memory_space=vm)] * len(arrays),
        out_specs=[pl.BlockSpec(memory_space=pl.ANY)] * 2 + [pl.BlockSpec(memory_space=vm)] * 9,
        scratch_shapes=[
            vm((ROWS, D), F32),
            vm((ROWS, D), F32),
            vm((ROWS, 1), F32),
            vm((ROWS, 1), F32),
            vm((ROWS, D), BF16),
            vm((ROWS, D), BF16),
            vm((ROWS, QKV), BF16),
            vm((ROWS, D), BF16),
            vm((GROUPS * PER, SETS, KEYS, LANES), F32),
            vm((ROWS, D), BF16),
            vm((ROWS, FF), BF16),
            vm((ROWS, FF), BF16),
            vm((ROWS, QKV), F32),
            vm((PER, LANES, 128), BF16),
            vm((PER, SETS, KEYS, LANES), F32),
            vm((GROUPS * PER, KEYS, LANES), F32),
            vm((PER, SETS, KEYS, LANES), F32),
            vm((G_ROWS, D), F32),
            vm((G_ROWS, D), F32),
            vm((8, 8, D), F32),
            vm((8, FF), F32),
            vm((D, QKV), BF16),
            vm((D, D), BF16),
            vm((D, FF), BF16),
            vm((FF, D), BF16),
            vm((TOK, D), BF16),
            vm((TOK, D), BF16),
            vm((D, QKV), F32),
            vm((D, D), F32),
            vm((ROWS, D), F32),
            dma((4,)), dma((6,)),
            vm((2, 4, 4, 96, D), BF16),
            vm((4, 4, 96, D), BF16),
            vm((3, 4, 96, D), BF16),
            vm((4, 96, D), BF16),
            vm((3, 96, D), BF16),
            vm((4, 96, D), BF16),
            vm((4, 8, D), F32),
            vm((4, 2, 4, 48, D), BF16),
            vm((4, 4, 48, D), BF16),
            vm((4, 3, 48, D), BF16),
            vm((4, 4, 48, D), BF16),
            vm((4, 4, 48, D), BF16),
            vm((8, 16, D), F32),
            vm((3, 8, 8, D), F32),
            vm((3, 16, 8, D), F32),
            vm((4, 48, D), F32),
            dma((3, 3)), dma((3, 3)), dma((3, 2)), dma((3, 2)),
            dma((4,)), dma((4,)),
            dma((3,)), dma((3,)), dma((3,)), dma((3,)), dma((3,)), dma((3,)),
            dma((3,)), dma((3,)), dma((1,)), dma((1,)), dma((3,)), dma((3,)),
            dma((4,)), dma((4,)),
            dma((4, 3)), dma((4, 3)), dma((4, 3)), dma((4, 3)), dma((4, 3)), dma((4, 3)),
            dma((7,)), dma((7,)),
            dma((3, 7)), dma((3, 7)), dma((3, 15)), dma((3, 15)),
        ],
        compiler_params=pltpu.CompilerParams(
            vmem_limit_bytes=63 * 1024 * 1024, collective_id=0, has_side_effects=True
        ),
        cost_estimate=pl.CostEstimate(flops=14_000_000_000, bytes_accessed=20_000_000, transcendentals=3_000_000),
        name="block",
    )(live_windows, region, tok, og, wq, wp, *arrays)


def finish_kernel(
    fin, vec, fc_sums, at_sums, own_g, own_r, own_wq, own_wp, b1, fc1, fc2, fc1_b, fc1_row, fc2_col, qkv_col, proj_col,
    small, small_state, table, table_state, out_from, gin_from,
    qkv_grad, qkv_row_new, qkv_col_new, qkv_new, qkv_low, proj_grad, proj_row_new, proj_col_new, proj_new, proj_low,
    fc1_grad, fc1_row_new, fc1_col_new, fc1_new, fc1_low, fc2_grad, fc2_row_new, fc2_col_new, fc2_new, fc2_low,
    b1_grad, b1_state_new, b1_new, small_grad, small_state_new, small_new, table_grad, table_state_new, table_new,
    out_to, gin_to, held, sem_in, sem_out,
):
    def parts(src, dst, n):
        for i in range(4):
            rows = pl.ds(304 * i, 304 if i < 3 else TOK - 912)
            here = held.at[n, rows]
            yield (
                pltpu.make_async_copy(src.at[rows], here, sem_in.at[n, i]),
                pltpu.make_async_copy(here, dst.at[rows], sem_out.at[n, i]),
            )

    copies = list(parts(out_from, out_to, 0)) + list(parts(gin_from, gin_to, 1))
    for copy, _ in copies:
        copy.start()
    for copy, then in copies:
        copy.wait()
        then.start()
    mlp = lax.axis_index("mlp")
    eye = iota((D, D), 0) == iota((D, D), 1)
    eye8 = iota((8, 128), 0) == iota((8, 128), 1)

    def line(x):
        return x.reshape(1, -1)

    def total(x):
        return jnp.sum(jnp.sum(x, axis=0, keepdims=True), axis=1, keepdims=True)

    def fresh(old, mean):
        return DECAY * old + (1.0 - DECAY) * (mean + EPS_SQ)

    def owned(grads, cols, over, row, row_total, weight, col_old, rate, outs):
        grad_out, row_out, col_out, new_out, low_out = outs
        width = grads.shape[1]
        col_new = fresh(line(col_old[...]), cols * (1.0 / D))
        mean = row_total * (1.0 / D)
        norm = mean * jnp.sum(over * (1.0 / col_new), axis=1, keepdims=True) * (1.0 / (D * width))
        step = grads * lax.rsqrt(row * col_new * (1.0 / mean))
        new = weight - rate * (step * clip_scale(norm))
        grad_out[...] = grads[:3]
        row_out[...] = jnp.sum(jnp.where(eye8, row, 0.0), axis=0)[:3]
        col_out[...] = col_new.reshape(width)
        new_out[...] = new[:3]
        low_out[...] = new.astype(BF16)[:3]

    def by_part(take):
        return jnp.concatenate([take(g)[:, 128 * p : 128 * p + 128] for p in range(3) for g in range(SETS)], axis=1)

    owned(
        by_part(lambda g: own_g[g]), by_part(lambda g: at_sums[g : g + 1, :]),
        by_part(lambda g: at_sums[4 + g : 5 + g, :]), own_r[0][:, :1], at_sums[8:9, :1], own_wq[...], qkv_col,
        D ** (-0.5), (qkv_grad, qkv_row_new, qkv_col_new, qkv_new, qkv_low),
    )
    owned(
        own_g[3], at_sums[3:4, :], at_sums[7:8, :], own_r[1][:, :1], at_sums[9:10, :1], own_wp[...], proj_col,
        (D // 8) ** (-0.5), (proj_grad, proj_row_new, proj_col_new, proj_new, proj_low),
    )

    def update(grad, weight, row, col, mean, norm, rate, grad_out, new_out, low_out):
        row = row * (1.0 / mean)
        factor = rate * clip_scale(norm)
        for r in range(0, D, 48):
            rows = slice(r, r + 48)
            g = grad[rows, :]
            new = weight[rows, :] - (g * lax.rsqrt(row[rows] * col)) * factor
            grad_out[rows, :] = g
            new_out[rows, :] = new
            low_out[rows, :] = new.astype(BF16)

    row_new = fresh(line(fc1_row[...]), fc_sums[0, 0:1, :] * (1.0 / FF))
    mean = row_mean(row_new)
    norm = mean * row_mean(fc_sums[0, 1:2, :] * (1.0 / row_new)) * (1.0 / FF)
    fc1_row_new[...] = row_new.reshape(D)
    fc1_col_new[...] = fc_sums[1, 5]
    update(
        fin.at[0], fc1, to_column(row_new, eye), fc_sums[1, 5:6, :], mean, norm, D ** (-0.5),
        fc1_grad, fc1_new, fc1_low,
    )
    col_new = fresh(line(fc2_col[...]), fc_sums[0, 2:3, :] * (1.0 / FF))
    mean = fc_sums[0, 4:5, :1] * (1.0 / FF)
    norm = mean * row_mean(fc_sums[0, 3:4, :] * (1.0 / col_new)) * (1.0 / FF)
    fc2_row_new[...] = fc_sums[1, 6]
    fc2_col_new[...] = col_new.reshape(D)
    update(
        fin.at[1], fc2, to_column(fc_sums[1, 6:7, :], eye), col_new, mean, norm, FF ** (-0.5),
        fc2_grad, fc2_new, fc2_low,
    )

    def stepped(grad, old):
        state = fresh(old, grad * grad)
        return state, grad * lax.rsqrt(state)

    norm = jnp.zeros((1, 1), F32)
    for m in range(4):
        step = stepped(vec[4 + m : 5 + m, :], b1[m, 4:5, :])[1]
        norm = norm + jnp.sum(step * step, axis=1, keepdims=True)
    grad = vec[pl.ds(4 + mlp, 1), :]
    state, step = stepped(grad, b1[mlp, 4:5, :])
    b1_grad[...] = grad.reshape(D)
    b1_state_new[...] = state.reshape(D)
    b1_new[...] = (line(fc1_b[...]) - VEC_RATE * (step * clip_scale(norm * (1.0 / FF)))).reshape(D)

    grad = jnp.concatenate([vec[n : n + 1, :] for n in (20, 21, 22, 23, 0, 1, 2, 3)], axis=1)
    state, step = stepped(grad, line(small_state[...]))
    norm = jnp.sum(step * step, axis=1, keepdims=True) * (1.0 / (8 * D))
    small_grad[...] = grad.reshape(8 * D)
    small_state_new[...] = state.reshape(8 * D)
    small_new[...] = (line(small[...]) - VEC_RATE * (step * clip_scale(norm))).reshape(8 * D)

    grad = vec[8:20, :169]
    state, step = stepped(grad, table_state[...])
    norm = total(step * step) * (1.0 / (169 * HEADS))
    table_grad[...] = grad
    table_state_new[...] = state
    table_new[...] = table[...] - VEC_RATE * (step * clip_scale(norm))
    for _, then in copies:
        then.wait()


def finish(*arrays):
    sd = jax.ShapeDtypeStruct
    vm = pltpu.VMEM

    def owned(width):
        return [sd((3, width), F32), sd((3,), F32), sd((width,), F32), sd((3, width), F32), sd((3, width), BF16)]

    shard = [sd((D, D), F32), sd((D,), F32), sd((D,), F32), sd((D, D), F32), sd((D, D), BF16)]
    out_shape = owned(QKV) + owned(D) + shard + shard
    out_shape += [sd((D,), F32)] * 3 + [sd((8 * D,), F32)] * 3 + [sd((HEADS, 169), F32)] * 3 + [sd((TOK, D), F32)] * 2
    return pl.pallas_call(
        finish_kernel,
        out_shape=out_shape,
        in_specs=[pl.BlockSpec(memory_space=vm)] * (len(arrays) - 2) + [pl.BlockSpec(memory_space=pl.ANY)] * 2,
        out_specs=[pl.BlockSpec(memory_space=vm)] * (len(out_shape) - 2) + [pl.BlockSpec(memory_space=pl.ANY)] * 2,
        scratch_shapes=[vm((2, TOK, D), F32), pltpu.SemaphoreType.DMA((2, 4)), pltpu.SemaphoreType.DMA((2, 4))],
        compiler_params=pltpu.CompilerParams(vmem_limit_bytes=63 * 1024 * 1024),
        name="finish",
    )(*arrays)


def clip_scale(mean_square):
    return 1.0 / jnp.maximum(1.0, jnp.sqrt(mean_square))


def per_device(
    tokens_in, out_grad, window_live, region_ids, qkv_weight, proj_weight, rel_table, small_params,
    fc1_weight, fc1_bias, fc2_weight, qkv_row, qkv_col, proj_row, proj_col, fc1_row, fc1_col,
    fc2_row, fc2_col, fc1_bias_state, small_state, table_state,
):
    out, gin, fin, *parts = block(
        window_live, region_ids, tokens_in, out_grad, qkv_weight, proj_weight, rel_table.T, small_params,
        fc1_weight, fc2_weight, fc1_bias, fc1_bias_state, fc1_col, fc2_row, qkv_row, proj_row,
    )
    *outs, table_grad, table_state_new, table_new, out, gin = finish(
        fin.reshape(2, D, D), *parts, fc1_weight, fc2_weight, fc1_bias, fc1_row, fc2_col, qkv_col, proj_col,
        small_params, small_state, rel_table.T, table_state.T, out, gin,
    )
    return (out, gin, *outs, table_grad.T, table_state_new.T, table_new.T)


def solution(mesh):
    tokens, owner = P(("win", "mlp"), None), P(("win", "mlp"))
    whole, part = P(), P("mlp")
    return jax.shard_map(
        per_device,
        mesh=mesh,
        in_specs=(
            tokens, tokens, owner, owner, whole, whole, whole, whole, P(None, "mlp"), part, P("mlp", None),
            whole, whole, whole, whole, whole, part, part, whole, part, whole, whole,
        ),
        out_specs=(
            tokens, tokens,
            tokens, owner, whole, tokens, tokens,
            tokens, owner, whole, tokens, tokens,
            P(None, "mlp"), whole, part, P(None, "mlp"), P(None, "mlp"),
            P("mlp", None), part, whole, P("mlp", None), P("mlp", None),
            part, part, part,
            whole, whole, whole,
            whole, whole, whole,
        ),
        check_vma=False,
    )
```

```python
import functools
import math

import jax
import jax.numpy as jnp
from jax import lax
from jax.experimental import pallas as pl
from jax.experimental.pallas import tpu as pltpu
from jax.sharding import PartitionSpec as P

D = 384
FF = 1536
QKV = 3 * D
HEADS = 12
WIN = 7
SPAN = WIN * WIN
STEP = 10
DECAY = 1.0 - STEP ** (-0.8)
EPS_NORM = 1e-05
EPS_SQ = 1e-30
VEC_RATE = 0.3
SCALE = 32 ** (-0.5)
FAR = -1e30

PLACE = (0, 1, 3, 2)
GROUPS = 3
PER = 8
G_TOK = PER * SPAN
G_ROWS = 400
ROWS = GROUPS * G_ROWS
TOK = GROUPS * G_TOK
CHUNK = 64
KEYS = 56
SETS = 3
LANES = 4 * CHUNK

MESH = pl.DeviceIdType.MESH
F32 = jnp.float32
BF16 = jnp.bfloat16


def dot(a, b):
    return jnp.dot(a, b, preferred_element_type=F32)


def dot_nt(a, b):
    return lax.dot_general(a, b, (((1,), (1,)), ((), ())), preferred_element_type=F32)


def dot_tn(a, b):
    return lax.dot_general(a, b, (((0,), (0,)), ((), ())), preferred_element_type=F32)


def dot_exact(a, b):
    return jnp.dot(a, b, precision=lax.Precision.HIGHEST, preferred_element_type=F32)


def iota(shape, dim):
    return lax.broadcasted_iota(jnp.int32, shape, dim)


def fold_rows(x):
    total = x[0:8]
    for i in range(1, x.shape[0] // 8):
        total = total + x[8 * i : 8 * i + 8]
    return total


def row_mean(x):
    return jnp.sum(x, axis=1, keepdims=True) * (1.0 / D)


def normalize(x):
    center = x - row_mean(x)
    inverse = lax.rsqrt(row_mean(center * center) + EPS_NORM)
    return center * inverse, inverse


def normalize_back(u, gain, scaled, inverse):
    weighted = u * gain
    return inverse * (weighted - row_mean(weighted) - scaled * row_mean(weighted * scaled))


def gelu_parts(v):
    e = jnp.exp(-0.5 * v * v)
    t = 1.0 / (1.0 + (0.3275911 * 0.5**0.5) * jnp.abs(v))
    poly = 1.061405429 * t - 1.453152027
    poly = poly * t + 1.421413741
    poly = poly * t - 0.284496736
    poly = poly * t + 0.254829592
    tail = (0.5 * e) * (poly * t)
    phi = jnp.where(v < 0.0, tail, 1.0 - tail)
    return v * phi, phi + v * e * (2.0 * math.pi) ** (-0.5)


def barrel(x, amount, right):
    width = x.shape[1]
    for k in range(7):
        step = 1 << k
        moved = pltpu.roll(x, step if right else width - step, 1)
        x = jnp.where((amount & step) != 0, moved, x)
    return x


def embed(i):
    return 13 * (i // WIN) + i % WIN


def chunk_start(w):
    return pl.multiple_of((w // PER) * G_ROWS + (w % PER) * 48, 16)


def prologue(region, table, x_ref, emask, bias, mask, tok):
    for a in range(GROUPS):
        for r in range(0, G_TOK, 56):
            src = a * G_TOK + r
            low = src // 16 * 16
            x_ref[a * G_ROWS + r : a * G_ROWS + r + 56, :] = (
                tok[low : low + 64 if low + 64 <= TOK else TOK, :].astype(F32)[src - low : src - low + 56]
            )
        x_ref[a * G_ROWS + G_TOK : (a + 1) * G_ROWS, :] = jnp.zeros((G_ROWS - G_TOK, D), F32)
    row = iota((LANES, 128), 0)
    lane = iota((LANES, 128), 1)
    for b in range(PER):
        i = row % CHUNK
        keep = (i >= b) & (i < b + SPAN) & (lane // 32 == row // CHUNK)
        emask[b] = jnp.where(keep, 1.0, 0.0).astype(BF16)
    j = iota((KEYS, 256), 0)
    amount = jnp.maximum(84 - embed(j), 0)
    jl = iota((KEYS, LANES), 0)
    il = iota((KEYS, LANES), 1) % CHUNK
    for g in range(SETS):
        base = jnp.zeros((KEYS, LANES), F32)
        for h in range(4):
            line = jnp.concatenate([table[4 * g + h : 4 * g + h + 1, :], jnp.zeros((1, 87), F32)], axis=1)
            wide = jnp.broadcast_to(line, (KEYS, 256))
            wide = barrel(wide, amount, False)[:, :128]
            lane_to = iota((128, LANES), 1) - CHUNK * h
            pick = (iota((128, LANES), 0) == embed(lane_to)) & (lane_to >= 0) & (lane_to < SPAN)
            base = base + dot_exact(wide, jnp.where(pick, 1.0, 0.0))
        for b in range(PER):
            moved = pltpu.roll(pltpu.roll(base, b, 0), b, 1) if b else base
            key_ok = (jl >= b) & (jl < b + SPAN)
            query_ok = (il >= b) & (il < b + SPAN)
            bias[b, g] = jnp.where(key_ok, jnp.where(query_ok, moved, 0.0), FAR)
    eye = iota((CHUNK, CHUNK), 0) == iota((CHUNK, CHUNK), 1)
    region_row = jnp.concatenate([region[...].reshape(1, TOK).astype(F32), jnp.zeros((1, 104), F32)], axis=1)
    for w in range(GROUPS * PER):
        start = (w // PER) * G_TOK + (w % PER) * 48
        line = region_row[:, start : start + CHUNK]
        column = jnp.sum(jnp.where(eye, jnp.broadcast_to(line, (CHUNK, CHUNK)), 0.0), axis=1, keepdims=True)
        wide = jnp.concatenate([line] * 4, axis=1)
        mask[w] = jnp.where(column[:KEYS] != wide, -100.0, 0.0)


def pad_keys(x):
    return jnp.concatenate([x, jnp.zeros((CHUNK - KEYS, x.shape[1]), x.dtype)], axis=0)


def spread(x, keep):
    return jnp.concatenate([x] * 4, axis=0) * keep


def collect(full):
    head = iota((CHUNK, 128), 1) // 32
    parts = [full[CHUNK * h : CHUNK * (h + 1)] for h in range(4)]
    low = jnp.where(head == 0, parts[0], parts[1])
    high = jnp.where(head == 2, parts[2], parts[3])
    return jnp.where(head < 2, low, high)


def block_kernel(
    live_windows, region, tok_in, og_in, wq_in, wp_in, table, small, fc1, fc2,
    fc1_b, fc1_state, fc1_col, fc2_row, qkv_row, proj_row,
    out_to, gin_to, fin, vec, fc_sums, at_sums, own_g, own_r, own_wq, own_wp, b1,
    x_ref, xh1, inv1, inv2, n1, n2, qkv, att_b, probs, back, hidden, ig, dqkv,
    emask, bias, mask, tacc, s1, s2, sums, b1_acc, wq_b, wp_b, w1, w2, tok, og, wq, wp, stage, in_sem, out_sem,
    fcl, fr1, fr2, ft, fr3, fr4, fst, atl, ar1, ar2, ar3, ar4, ast, vx, vy, at_total,
    w_send, w_recv, b_send, b_recv, pair_send, pair_recv, f1s, f1r, f2s, f2r, f3s, f3r, f4s, f4r, f5s, f5r, f7s, f7r, f8s, f8r,
    a1s, a1r, a2s, a2r, a3s, a3r, a4s, a4r, a5s, a5r, vxs, vxr, vys, vyr,
):
    win, mlp = lax.axis_index("win"), lax.axis_index("mlp")
    z, y, core = win // 8, (win // 2) % 4, win % 2
    pair = win + 1 - 2 * core

    def along_x(d):
        return win, (mlp + d) % 4

    def along_y(d):
        return z * 8 + ((y + d) % 4) * 2 + core, mlp

    def along_z(d):
        return ((z + d) % 4) * 8 + y * 2 + core, mlp

    def plane_peer(d):
        return ((z + d // 4) % 4) * 8 + ((y + d % 4) % 4) * 2 + core, mlp

    def class_peer(d):
        return pair if d >= 4 else win, (mlp + d) % 4

    loads = [
        pltpu.make_async_copy(src, dst, in_sem.at[n])
        for n, (src, dst) in enumerate(((tok_in, tok), (og_in, og), (wq_in, wq), (wp_in, wp)))
    ]
    for copy in loads:
        copy.start()
    barrier = pltpu.get_barrier_semaphore()
    peers = [class_peer(d) for d in range(1, 8)]
    peers += [plane_peer(d) for d in range(1, 16)]
    for peer in peers:
        pl.semaphore_signal(barrier, inc=1, device_id=peer, device_id_type=MESH)

    def remote(src, dst, send, recv, peer):
        return pltpu.make_async_remote_copy(
            src_ref=src, dst_ref=dst, send_sem=send, recv_sem=recv, device_id=peer, device_id_type=MESH
        )

    def param(part):
        return small[D * part : D * part + D].reshape(1, D)

    pending = []

    def start(copy):
        copy.start()
        pending.append(copy)
        return copy

    def shard(place):
        half = pl.ds(pl.multiple_of(core * (D // 2), 16), D // 2)
        half_at = pl.ds(pl.multiple_of(place * D + core * (D // 2), 16), D // 2)
        return w1.at[half, D * place : D * place + D], w2.at[half_at, :]

    def near(d, n):
        return remote(shard(0)[n], shard(PLACE[4 - d])[n], w_send.at[d // 2, n], w_recv.at[d // 2, n], along_x(d))

    def far(n):
        d = 3 - 2 * n
        return remote(shard(1 + n)[n], shard(3)[n], w_send.at[2, n], w_recv.at[2, n], along_x(d))

    def bias_copy(d):
        return remote(b1.at[0], b1.at[PLACE[4 - d]], b_send.at[d - 1], b_recv.at[d - 1], along_x(d))

    def across(place, n):
        came = shard(place)[n]
        return remote(came, came, pair_send.at[place - 1, n], pair_recv.at[place - 1, n], (pair, mlp))

    w1[:, :D] = fc1[...].astype(BF16)
    w2[:D, :] = fc2[...].astype(BF16)
    b1[0, 0:4] = jnp.broadcast_to(fc1_b[...].reshape(1, D), (4, D))
    b1[0, 4:8] = jnp.broadcast_to(fc1_state[...].reshape(1, D), (4, D))
    pl.semaphore_wait(barrier, 22)
    for n in range(2):
        for d in (1, 3):
            start(near(d, n))
    for d in range(1, 4):
        start(bias_copy(d))

    live = live_windows[0]
    for n in range(1, GROUPS * PER):
        live = live + live_windows[n]
    live = live * SPAN
    for copy in loads:
        copy.wait()
    prologue(region, table, x_ref, emask, bias, mask, tok)
    for g in range(SETS):
        for part in range(3):
            wq_b[:, D * g + 128 * part : D * g + 128 * part + 128] = wq[
                :, D * part + 128 * g : D * part + 128 * g + 128
            ].astype(BF16)
    wp_b[...] = wp[...].astype(BF16)
    sums[...] = jnp.zeros_like(sums)
    b1_acc[...] = jnp.zeros_like(b1_acc)
    tacc[...] = jnp.zeros_like(tacc)
    att = dqkv.at[:, :D]
    xh2 = dqkv.at[:, D : 2 * D]
    dqkv_b = ig.at[:, :QKV]
    dqkv[:, :D] = jnp.zeros((ROWS, D), F32)

    for a in range(GROUPS):
        for r in range(0, G_TOK, 56):
            src = a * G_TOK + r
            low = src // 16 * 16
            rows = og[low : low + 64 if low + 64 <= TOK else TOK, :].astype(F32)[src - low : src - low + 56]
            keep = iota((56, D), 0) + src < live
            x = jnp.where(keep, rows, 0.0)
            s2[r : r + 56, :] = x
            sums[7] += fold_rows(x)
        s2[G_TOK:G_ROWS, :] = jnp.zeros((G_ROWS - G_TOK, D), F32)
        back[a * G_ROWS : (a + 1) * G_ROWS, :] = s2[...].astype(BF16)

    shift_q = jnp.concatenate(
        [
            part[:, 128 * g : 128 * g + 128]
            for g in range(SETS)
            for part in (param(2), jnp.zeros((1, D), F32), param(3))
        ],
        axis=1,
    )

    @pl.loop(0, 5, unroll=5)
    def _(t):
        for c in range(15):
            rows = pl.ds(pl.multiple_of(t * 240 + c * 16, 16), 16)
            scaled, inverse = normalize(x_ref[rows, :])
            xh1[rows, :] = scaled
            inv1[rows, :] = inverse
            n1[rows, :] = (scaled * param(0) + param(1)).astype(BF16)

    @pl.loop(0, 5, unroll=5)
    def _(t):
        rows = pl.ds(pl.multiple_of(t * 240, 16), 240)
        qkv[rows, :] = (dot(n1[rows, :], wq_b[...]) + shift_q).astype(BF16)

    @pl.loop(0, PER, unroll=4)
    def _(b):
        for a in range(GROUPS):
            rows = pl.ds(pl.multiple_of(a * G_ROWS + b * 48, 16), CHUNK)
            w = a * PER + b
            for g in range(SETS):
                q = qkv[rows, D * g : D * g + 128]
                k = qkv[rows, D * g + 128 : D * g + 256]
                v = qkv[rows, D * g + 256 : D * g + 384]
                scores = dot_nt(k, spread(q, emask[b]))[:KEYS] * SCALE + (bias[b, g] + mask[w])
                p = jnp.exp(scores - jnp.max(scores, axis=0, keepdims=True))
                p = p * (1.0 / jnp.sum(p, axis=0, keepdims=True))
                probs[w, g] = p
                o = collect(dot_tn(pad_keys(p).astype(BF16), v))
                i = iota((CHUNK, 128), 0)
                att[rows, 128 * g : 128 * g + 128] += jnp.where((i >= b) & (i < b + SPAN), o, 0.0)

    for n in range(2):
        for d in (1, 3):
            near(d, n).wait_recv()
        start(far(n))
    for place in (1, 2):
        for n in range(2):
            start(across(place, n))
    for d in range(1, 4):
        bias_copy(d).wait_recv()

    @pl.loop(0, GROUPS, unroll=3)
    def _(a):
        rows = pl.ds(pl.multiple_of(a * G_ROWS, 16), G_ROWS)
        att_b[rows, :] = att[rows, :].astype(BF16)
        s1[...] = dot(att_b[rows, :], wp_b[...])

        for c in range(25):
            here = pl.ds(pl.multiple_of(a * G_ROWS + 16 * c, 16), 16)
            middle = x_ref[here, :] + (s1[16 * c : 16 * c + 16, :] + param(4))
            stage[here, :] = middle
            scaled, inverse = normalize(middle)
            xh2[here, :] = scaled
            inv2[here, :] = inverse
            n2[here, :] = (scaled * param(5) + param(6)).astype(BF16)

    for nt in range(6):
        if nt in (1, 3):
            for n in range(2):
                across(1 + nt // 2, n).wait_recv()
        if nt == 3:
            for n in range(2):
                far(n).wait_recv()
                start(across(3, n))
        if nt == 4:
            for n in range(2):
                across(3, n).wait_recv()
        cols = slice(256 * nt, 256 * nt + 256)
        shift = jnp.concatenate(
            [b1[c // 3, 0:1, 128 * (c % 3) : 128 * (c % 3) + 128] for c in (2 * nt, 2 * nt + 1)], axis=1
        )

        @pl.loop(0, 5, unroll=5)
        def _(mt):
            rows = pl.ds(pl.multiple_of(mt * 240, 16), 240)
            inner = dot(n2[rows, :], w1[:, cols]) + shift
            up = dot_nt(back[rows, :], w2[cols, :])
            total = b1_acc[:, cols]
            for c in range(15):
                act, slope = gelu_parts(inner[16 * c : 16 * c + 16])
                here = pl.ds(pl.multiple_of(mt * 240 + 16 * c, 16), 16)
                hidden[here, cols] = act.astype(BF16)
                grad = (up[16 * c : 16 * c + 16] * slope).astype(BF16)
                ig[here, cols] = grad
                total = total + fold_rows(grad.astype(F32))
            b1_acc[:, cols] = total

    g2 = dot_tn(hidden[...], back[...]).astype(BF16)
    g1 = dot_tn(n2[...], ig[...]).astype(BF16)
    for m in range(4):
        fcl[0, m] = g1[:, D * m : D * m + D].reshape(4, 96, D)
        fcl[1, m] = g2[D * m : D * m + D].reshape(4, 96, D)
    fc_one = [start(remote(fcl.at[1 - core, m], fr1.at[m], f1s.at[m], f1r.at[m], (pair, mlp))) for m in range(4)]

    def middle_back(a):
        rows = slice(a * G_ROWS, (a + 1) * G_ROWS)
        s2[...] = dot_nt(ig[rows, :], w1[...])
        for c in range(25):
            here = slice(16 * c, 16 * c + 16)
            at = slice(a * G_ROWS + 16 * c, a * G_ROWS + 16 * c + 16)
            u = s2[here, :]
            scaled = xh2[at, :]
            sums[5] += fold_rows(u * scaled)
            sums[6] += fold_rows(u)
            mg = normalize_back(u, param(5), scaled, inv2[at, :]) + back[at, :].astype(F32)
            x_ref[at, :] = mg
            low = mg.astype(BF16)
            n2[at, :] = low
            sums[4] += fold_rows(low.astype(F32))

    def out_copy(a):
        return pltpu.make_async_copy(
            stage.at[pl.ds(a * G_ROWS, G_TOK)], out_to.at[pl.ds(a * G_TOK, G_TOK)], out_sem.at[a]
        )

    def block_out(a):
        rows = slice(a * G_ROWS, (a + 1) * G_ROWS)
        s1[...] = dot(hidden[rows, :], w2[...])
        for c in range(25):
            at = slice(a * G_ROWS + 16 * c, a * G_ROWS + 16 * c + 16)
            r = stage[at, :] + (s1[16 * c : 16 * c + 16, :] + param(7))
            keep = iota((16, D), 0) + (a * G_TOK + 16 * c) < live
            stage[at, :] = jnp.where(keep, r, 0.0)
        out_copy(a).start()

    p = iota((D, D), 0)
    inner_p = p % 48
    owned = 24 * (inner_p // 3) + 12 * (p // 192) + 3 * ((p // 48) % 4) + inner_p % 3
    order = jnp.where(iota((D, D), 1) == owned, 1.0, 0.0).astype(BF16)

    def ordered(grad):
        return dot(order, grad.astype(BF16)).astype(BF16).reshape(2, 4, 48, D)

    def at_one(n):
        return remote(atl.at[n, 1 - core], ar1.at[n], a1s.at[n], a1r.at[n], (pair, mlp))

    def at_add_one(n):
        at_one(n).wait_recv()
        for i in range(4):
            ar1[n, i] = (ar1[n, i].astype(F32) + atl[n, core, i].astype(F32)).astype(BF16)
        for d in range(1, 4):
            start(remote(ar1.at[n, (mlp + d) % 4], ar2.at[n, d - 1], a2s.at[n, d - 1], a2r.at[n, d - 1], along_x(d)))

    def at_add_two(n):
        total = ar1[n, mlp].astype(F32)
        for d in range(1, 4):
            remote(ar1.at[n, 0], ar2.at[n, d - 1], a2s.at[n, d - 1], a2r.at[n, d - 1], along_x(d)).wait_recv()
            total = total + ar2[n, d - 1].astype(F32)
        ar3[n, y] = total.astype(BF16)
        for d in range(1, 4):
            start(remote(ar3.at[n, y], ar3.at[n, y], a3s.at[n, d - 1], a3r.at[n, d - 1], along_y(d)))

    def at_add_three(n):
        for d in range(1, 4):
            came = ar3.at[n, (y + 4 - d) % 4]
            remote(came, came, a3s.at[n, d - 1], a3r.at[n, d - 1], along_y(d)).wait_recv()
        total = ar3[n, 0].astype(F32) + ar3[n, 1].astype(F32)
        ar4[n, z] = (total + ar3[n, 2].astype(F32) + ar3[n, 3].astype(F32)).astype(BF16)
        for d in range(1, 4):
            start(remote(ar4.at[n, z], ar4.at[n, z], a4s.at[n, d - 1], a4r.at[n, d - 1], along_z(d)))

    def at_finish(n):
        for d in range(1, 4):
            came = ar4.at[n, (z + 4 - d) % 4]
            remote(came, came, a4s.at[n, d - 1], a4r.at[n, d - 1], along_z(d)).wait_recv()
        total = ar4[n, 0].astype(F32) + ar4[n, 1].astype(F32)
        at_total[n] = total + ar4[n, 2].astype(F32) + ar4[n, 3].astype(F32)

    def to_axes(dx, dy, dz):
        return ((z + dz) % 4) * 8 + ((y + dy) % 4) * 2 + core, (mlp + dx) % 4

    def first_axis(d):
        return to_axes(d * (1 - core), 0, d * core)

    def second_axis(d):
        return to_axes(d * core, d * (1 - core), 0)

    def third_axis(d):
        return to_axes(0, d * core, d * (1 - core))

    def last_axis(d):
        return to_axes(0, d * (1 - core), d * core)

    block_at = y * (1 - core) + z * core
    second = y * (1 - core)
    third = z * (1 - core) + y * core

    def fc_two(d):
        return remote(fr1.at[0], fr2.at[d - 1], f2s.at[d - 1], f2r.at[d - 1], first_axis(d))

    def fc_add_one():
        for m in range(4):
            fc_one[m].wait_recv()
            for i in range(4):
                fr1[m, i] = (fr1[m, i].astype(F32) + fcl[core, m, i].astype(F32)).astype(BF16)

        @pl.when(core == 0)
        def _():
            for d in range(1, 4):
                remote(fr1.at[PLACE[d]], fr2.at[d - 1], f2s.at[d - 1], f2r.at[d - 1], first_axis(d)).start()

        @pl.when(core == 1)
        def _():
            for d in range(1, 4):
                remote(fr1.at[:, (z + d) % 4], fr2.at[d - 1], f2s.at[d - 1], f2r.at[d - 1], first_axis(d)).start()

    def fc_add_two():
        for d in range(1, 4):
            fc_two(d).wait_recv()
        for i in range(4):
            total = fr1[i * core, i * (1 - core) + z * core].astype(F32)
            for d in range(1, 4):
                total = total + fr2[d - 1, i].astype(F32)
            ft[i] = total.astype(BF16)
        for d in range(1, 4):
            to = (1 - core) * ((y + d) % 4) + core * PLACE[d]
            start(remote(ft.at[to], fr3.at[d - 1], f3s.at[d - 1], f3r.at[d - 1], second_axis(d)))

    def fc_add_three():
        total = ft[second].astype(F32)
        for d in range(1, 4):
            remote(ft.at[0], fr3.at[d - 1], f3s.at[d - 1], f3r.at[d - 1], second_axis(d)).wait_recv()
            total = total + fr3[d - 1].astype(F32)
        fr4[third] = total.astype(BF16)
        for d in range(1, 4):
            start(remote(fr4.at[third], fr4.at[third], f4s.at[d - 1], f4r.at[d - 1], third_axis(d)))

    def fc_add_four():
        for d in range(1, 4):
            came = fr4.at[(third + 4 - d) % 4]
            remote(came, came, f4s.at[d - 1], f4r.at[d - 1], third_axis(d)).wait_recv()
        total = fr4[0].astype(F32) + fr4[1].astype(F32)
        fin[core, block_at] = total + fr4[2].astype(F32) + fr4[3].astype(F32)
        for d in range(1, 4):
            place = fin.at[core, block_at]
            start(remote(place, place, f5s.at[d - 1], f5r.at[d - 1], last_axis(d)))

    def fc_spread():
        for d in range(1, 4):
            place = fin.at[core, (block_at + 4 - d) % 4]
            remote(place, place, f5s.at[d - 1], f5r.at[d - 1], last_axis(d)).wait_recv()
        start(remote(fin.at[core], fin.at[core], f7s.at[0], f7r.at[0], (pair, mlp)))

    mine_at, plane_at = 4 * core + mlp, 4 * z + y

    def vec_one(n):
        for d in range(1, 8):
            place = vx.at[n, mine_at]
            start(remote(place, place, vxs.at[n, d - 1], vxr.at[n, d - 1], class_peer(d)))

    def vec_two(n):
        for d in range(1, 8):
            place = vx.at[n, (mlp + 8 - d) % 4 + 4 * (core if d < 4 else 1 - core)]
            remote(place, place, vxs.at[n, d - 1], vxr.at[n, d - 1], class_peer(d)).wait_recv()
        total = vx[n, 0]
        for i in range(1, 8):
            total = total + vx[n, i]
        vy[n, plane_at] = total
        for d in range(1, 16):
            place = vy.at[n, plane_at]
            start(remote(place, place, vys.at[n, d - 1], vyr.at[n, d - 1], plane_peer(d)))

    def vec_three(n):
        for d in range(1, 16):
            place = vy.at[n, 4 * ((z + 4 - d // 4) % 4) + (y + 4 - d % 4) % 4]
            remote(place, place, vys.at[n, d - 1], vyr.at[n, d - 1], plane_peer(d)).wait_recv()
        total = vy[n, 0]
        for i in range(1, 16):
            total = total + vy[n, i]
        vec[8 * n : 8 * n + 8, :] = total

    middle_back(0)
    middle_back(1)
    fc_add_one()
    middle_back(2)

    atl[3] = ordered(dot_tn(att_b[...], n2[...]))
    start(at_one(3))

    @pl.loop(0, GROUPS, unroll=3)
    def _(a):
        rows = pl.ds(pl.multiple_of(a * G_ROWS, 16), G_ROWS)
        att_b[rows, :] = dot_nt(n2[rows, :], wp_b[...]).astype(BF16)

    dqkv[...] = jnp.zeros_like(dqkv)

    def attention_back(g, half):
        @pl.loop(4 * half, 4 * half + 4, unroll=4)
        def _(b):
            keep = emask[b]
            total = tacc[b, g]
            for a in range(GROUPS):
                rows = pl.ds(pl.multiple_of(a * G_ROWS + b * 48, 16), CHUNK)
                q = qkv[rows, D * g : D * g + 128]
                k = qkv[rows, D * g + 128 : D * g + 256]
                v = qkv[rows, D * g + 256 : D * g + 384]
                qe = spread(q, keep)
                da = spread(att_b[rows, 128 * g : 128 * g + 128], keep)
                p = probs[a * PER + b, g]
                dp = dot_nt(v, da)[:KEYS]
                pd = p * dp
                ds = pad_keys(pd - p * jnp.sum(pd, axis=0, keepdims=True)).astype(BF16)
                total = total + ds.astype(F32)[:KEYS]
                dv = dot(pad_keys(p).astype(BF16), da)
                dk = dot(ds, qe) * SCALE
                dq = collect(dot_tn(ds, k)) * SCALE
                dqkv[rows, 384 * g : 384 * g + 128] += dq
                dqkv[rows, 384 * g + 128 : 384 * g + 256] += dk
                dqkv[rows, 384 * g + 256 : 384 * g + 384] += dv
            tacc[b, g] = total

    def qkv_grad(g):
        group = slice(384 * g, 384 * g + 384)

        @pl.loop(0, 5, unroll=5)
        def _(t):
            for c in range(15):
                rows = pl.ds(pl.multiple_of(t * 240 + c * 16, 16), 16)
                low = dqkv[rows, group].astype(BF16)
                dqkv_b[rows, group] = low
                wide = low.astype(F32)
                sums[2, :, 128 * g : 128 * g + 128] += fold_rows(wide[:, :128])
                sums[3, :, 128 * g : 128 * g + 128] += fold_rows(wide[:, 256:])

        atl[g] = ordered(dot_tn(n1[...], dqkv_b[:, group]))
        start(at_one(g))

    for part in range(4):
        vx[0, mine_at, part : part + 1, :] = jnp.sum(sums[4 + part], axis=0, keepdims=True)
    for m in range(4):
        d = (m + 4 - mlp) % 4
        place = d + d // 2 - 2 * (d // 3)
        cols = pl.ds(pl.multiple_of(place * D, 128), D)
        vx[0, mine_at, 4 + m : 5 + m, :] = jnp.sum(b1_acc[:, cols], axis=0, keepdims=True)
    vec_one(0)

    def table_back(g, n):
        j = iota((KEYS, 256), 0)
        amount = jnp.maximum(84 - embed(j), 0)
        total = tacc[0, g]
        for b in range(1, PER):
            total = total + pltpu.roll(pltpu.roll(tacc[b, g], KEYS - b, 0), LANES - b, 1)
        for h in range(4):
            lane_from = iota((LANES, 256), 0) - CHUNK * h
            pick = (iota((LANES, 256), 1) == embed(lane_from)) & (lane_from >= 0) & (lane_from < SPAN)
            wide = barrel(dot_exact(total, jnp.where(pick, 1.0, 0.0)), amount, True)
            wide = jnp.where(j < SPAN, wide, 0.0)
            vx[n, mine_at, 4 * (g % 2) + h : 4 * (g % 2) + h + 1, :] = jnp.concatenate(
                [jnp.sum(wide, axis=0, keepdims=True), jnp.zeros((1, 128), F32)], axis=1
            )

    attention_back(0, 0)
    attention_back(0, 1)
    qkv_grad(0)
    fc_add_two()
    table_back(0, 1)
    vec_two(0)
    attention_back(1, 0)
    at_add_one(3)
    at_add_one(0)
    attention_back(1, 1)
    qkv_grad(1)
    fc_add_three()
    table_back(1, 1)
    vec_one(1)
    attention_back(2, 0)
    at_add_one(1)
    at_add_two(3)
    at_add_two(0)
    vec_three(0)
    attention_back(2, 1)
    qkv_grad(2)
    table_back(2, 2)
    at_add_one(2)
    fc_add_four()

    def gin_copy(a):
        return pltpu.make_async_copy(
            x_ref.at[pl.ds(a * G_ROWS, G_TOK)], gin_to.at[pl.ds(a * G_TOK, G_TOK)], out_sem.at[3 + a]
        )

    def input_back(a):
        rows = slice(a * G_ROWS, (a + 1) * G_ROWS)
        s2[...] = dot_nt(dqkv_b[rows, :], wq_b[...])
        for c in range(25):
            here = slice(16 * c, 16 * c + 16)
            at = slice(a * G_ROWS + 16 * c, a * G_ROWS + 16 * c + 16)
            u = s2[here, :]
            scaled = xh1[at, :]
            sums[0] += fold_rows(u * scaled)
            sums[1] += fold_rows(u)
            x_ref[at, :] = normalize_back(u, param(0), scaled, inv1[at, :]) + x_ref[at, :]
        gin_copy(a).start()

    for a in range(GROUPS):
        input_back(a)
    for part in range(4):
        vx[2, mine_at, 4 + part : 5 + part, :] = jnp.sum(sums[part], axis=0, keepdims=True)
    vec_one(2)
    at_add_two(1)
    at_add_three(3)
    at_add_three(0)
    vec_two(1)
    for a in range(GROUPS):
        block_out(a)
    at_add_two(2)
    vec_two(2)
    fc_spread()
    at_finish(3)
    at_finish(0)
    at_add_three(1)

    remote(fin.at[1 - core], fin.at[1 - core], f7s.at[0], f7r.at[0], (pair, mlp)).wait_recv()
    eye = iota((D, D), 0) == iota((D, D), 1)

    def to_row(column):
        return jnp.sum(jnp.where(eye, column, 0.0), axis=0, keepdims=True)

    up = fin[0].reshape(D, D)
    down = fin[1].reshape(D, D)
    up_squares = up * up
    down_squares = down * down
    up_col = DECAY * fc1_col[...].reshape(1, D) + (1.0 - DECAY) * (
        jnp.sum(up_squares, axis=0, keepdims=True) * (1.0 / D) + EPS_SQ
    )
    down_row = DECAY * to_column(fc2_row[...].reshape(1, D), eye) + (1.0 - DECAY) * (row_mean(down_squares) + EPS_SQ)
    fst[mlp, 0:1] = to_row(jnp.sum(up_squares, axis=1, keepdims=True))
    fst[mlp, 1:2] = to_row(jnp.sum(up_squares * (1.0 / up_col), axis=1, keepdims=True))
    fst[mlp, 2:3] = jnp.sum(down_squares, axis=0, keepdims=True)
    fst[mlp, 3:4] = jnp.sum(down_squares * (1.0 / down_row), axis=0, keepdims=True)
    fst[mlp, 4:5] = jnp.broadcast_to(jnp.sum(down_row, axis=0, keepdims=True), (1, D))
    fst[mlp, 5:6] = up_col
    fst[mlp, 6:7] = to_row(down_row)
    fst[mlp, 7:8] = jnp.zeros((1, D), F32)
    for d in range(1, 4):
        start(remote(fst.at[mlp], fst.at[mlp], f8s.at[d - 1], f8r.at[d - 1], along_x(d)))

    at_add_three(2)
    at_finish(1)
    vec_three(1)

    offset = 48 - 3 * plane_at
    block_rows = pl.ds(pl.multiple_of(24 * (win // 2), 8), 24)
    shift = 24 - 3 * mine_at
    own_wq[...] = pltpu.roll(wq[block_rows, :], shift, 0)[:8]
    own_wp[...] = pltpu.roll(wp[block_rows, :], shift, 0)[:8]

    r48 = iota((48, D), 0)
    pick = iota((48, D), 1) == 24 * (r48 // 3) + 12 * core + 3 * mlp + r48 % 3

    def rows_new(state, mean):
        old = jnp.sum(jnp.where(pick, state, 0.0), axis=1, keepdims=True)
        return DECAY * old + (1.0 - DECAY) * (mean + EPS_SQ)

    at_finish(2)
    squares = [at_total[n] * at_total[n] for n in range(4)]
    qkv_new_row = rows_new(
        qkv_row[...].reshape(1, D), row_mean(squares[0] + squares[1] + squares[2]) * (1.0 / 3.0)
    )
    proj_new_row = rows_new(proj_row[...].reshape(1, D), row_mean(squares[3]))
    for n in range(4):
        over = squares[n] * (1.0 / (qkv_new_row if n < 3 else proj_new_row))
        ast[mine_at, n : n + 1] = jnp.sum(squares[n], axis=0, keepdims=True)
        ast[mine_at, 4 + n : 5 + n] = jnp.sum(over, axis=0, keepdims=True)
    ast[mine_at, 8:9] = jnp.broadcast_to(jnp.sum(qkv_new_row, axis=0, keepdims=True), (1, D))
    ast[mine_at, 9:10] = jnp.broadcast_to(jnp.sum(proj_new_row, axis=0, keepdims=True), (1, D))
    ast[mine_at, 10:16] = jnp.zeros((6, D), F32)

    def at_five(d):
        place = ast.at[mine_at]
        return remote(place, place, a5s.at[d - 1], a5r.at[d - 1], class_peer(d))

    for d in range(1, 8):
        start(at_five(d))

    for n in range(4):
        own_g[n] = pltpu.roll(at_total[n], offset, 0)[:8]
    own_r[0] = pltpu.roll(jnp.broadcast_to(qkv_new_row, (48, 128)), offset, 0)[:8]
    own_r[1] = pltpu.roll(jnp.broadcast_to(proj_new_row, (48, 128)), offset, 0)[:8]

    for d in range(1, 4):
        place = fst.at[(mlp + 4 - d) % 4]
        remote(place, place, f8s.at[d - 1], f8r.at[d - 1], along_x(d)).wait_recv()
    fc_sums[0] = (fst[0] + fst[1]) + (fst[2] + fst[3])
    fc_sums[1] = fst[mlp]
    vec_three(2)

    for d in range(1, 8):
        place = ast.at[(mlp + 8 - d) % 4 + 4 * (core if d < 4 else 1 - core)]
        remote(place, place, a5s.at[d - 1], a5r.at[d - 1], class_peer(d)).wait_recv()
    total = ast[0]
    for n in range(1, 8):
        total = total + ast[n]
    at_sums[...] = total

    for a in range(GROUPS):
        gin_copy(a).wait()
        out_copy(a).wait()
    for copy in pending:
        copy.wait_send()
    for d in range(1, 4):
        fc_two(d).wait_send()


def to_column(row, eye):
    return jnp.sum(jnp.where(eye, row, 0.0), axis=1, keepdims=True)


def block(live_windows, region, tok, og, wq, wp, *arrays):
    sd = jax.ShapeDtypeStruct
    vm = pltpu.VMEM
    dma = pltpu.SemaphoreType.DMA
    return pl.pallas_call(
        block_kernel,
        out_shape=[
            sd((TOK, D), F32),
            sd((TOK, D), F32),
            sd((2, 4, 96, D), F32),
            sd((24, D), F32),
            sd((2, 8, D), F32),
            sd((16, D), F32),
            sd((4, 8, D), F32),
            sd((2, 8, 128), F32),
            sd((8, QKV), F32),
            sd((8, D), F32),
            sd((4, 8, D), F32),
        ],
        in_specs=[pl.BlockSpec(memory_space=pltpu.SMEM), pl.BlockSpec(memory_space=vm)]
        + [pl.BlockSpec(memory_space=pl.ANY)] * 4
        + [pl.BlockSpec(memory_space=vm)] * len(arrays),
        out_specs=[pl.BlockSpec(memory_space=pl.ANY)] * 2 + [pl.BlockSpec(memory_space=vm)] * 9,
        scratch_shapes=[
            vm((ROWS, D), F32),
            vm((ROWS, D), F32),
            vm((ROWS, 1), F32),
            vm((ROWS, 1), F32),
            vm((ROWS, D), BF16),
            vm((ROWS, D), BF16),
            vm((ROWS, QKV), BF16),
            vm((ROWS, D), BF16),
            vm((GROUPS * PER, SETS, KEYS, LANES), F32),
            vm((ROWS, D), BF16),
            vm((ROWS, FF), BF16),
            vm((ROWS, FF), BF16),
            vm((ROWS, QKV), F32),
            vm((PER, LANES, 128), BF16),
            vm((PER, SETS, KEYS, LANES), F32),
            vm((GROUPS * PER, KEYS, LANES), F32),
            vm((PER, SETS, KEYS, LANES), F32),
            vm((G_ROWS, D), F32),
            vm((G_ROWS, D), F32),
            vm((8, 8, D), F32),
            vm((8, FF), F32),
            vm((D, QKV), BF16),
            vm((D, D), BF16),
            vm((D, FF), BF16),
            vm((FF, D), BF16),
            vm((TOK, D), BF16),
            vm((TOK, D), BF16),
            vm((D, QKV), F32),
            vm((D, D), F32),
            vm((ROWS, D), F32),
            dma((4,)), dma((6,)),
            vm((2, 4, 4, 96, D), BF16),
            vm((4, 4, 96, D), BF16),
            vm((3, 4, 96, D), BF16),
            vm((4, 96, D), BF16),
            vm((3, 96, D), BF16),
            vm((4, 96, D), BF16),
            vm((4, 8, D), F32),
            vm((4, 2, 4, 48, D), BF16),
            vm((4, 4, 48, D), BF16),
            vm((4, 3, 48, D), BF16),
            vm((4, 4, 48, D), BF16),
            vm((4, 4, 48, D), BF16),
            vm((8, 16, D), F32),
            vm((3, 8, 8, D), F32),
            vm((3, 16, 8, D), F32),
            vm((4, 48, D), F32),
            dma((3, 2)), dma((3, 2)), dma((3,)), dma((3,)), dma((3, 2)), dma((3, 2)),
            dma((4,)), dma((4,)),
            dma((3,)), dma((3,)), dma((3,)), dma((3,)), dma((3,)), dma((3,)),
            dma((3,)), dma((3,)), dma((1,)), dma((1,)), dma((3,)), dma((3,)),
            dma((4,)), dma((4,)),
            dma((4, 3)), dma((4, 3)), dma((4, 3)), dma((4, 3)), dma((4, 3)), dma((4, 3)),
            dma((7,)), dma((7,)),
            dma((3, 7)), dma((3, 7)), dma((3, 15)), dma((3, 15)),
        ],
        compiler_params=pltpu.CompilerParams(
            vmem_limit_bytes=63 * 1024 * 1024, collective_id=0, has_side_effects=True
        ),
        cost_estimate=pl.CostEstimate(flops=14_000_000_000, bytes_accessed=20_000_000, transcendentals=3_000_000),
        name="block",
    )(live_windows, region, tok, og, wq, wp, *arrays)


def finish_kernel(
    fin, vec, fc_sums, at_sums, own_g, own_r, own_wq, own_wp, b1, fc1, fc2, fc1_b, fc1_row, fc2_col, qkv_col, proj_col,
    small, small_state, table, table_state, out_from, gin_from,
    qkv_grad, qkv_row_new, qkv_col_new, qkv_new, qkv_low, proj_grad, proj_row_new, proj_col_new, proj_new, proj_low,
    fc1_grad, fc1_row_new, fc1_col_new, fc1_new, fc1_low, fc2_grad, fc2_row_new, fc2_col_new, fc2_new, fc2_low,
    b1_grad, b1_state_new, b1_new, small_grad, small_state_new, small_new, table_grad, table_state_new, table_new,
    out_to, gin_to, held, sem_in, sem_out,
):
    def parts(src, dst, n):
        for i in range(4):
            rows = pl.ds(304 * i, 304 if i < 3 else TOK - 912)
            here = held.at[n, rows]
            yield (
                pltpu.make_async_copy(src.at[rows], here, sem_in.at[n, i]),
                pltpu.make_async_copy(here, dst.at[rows], sem_out.at[n, i]),
            )

    copies = list(parts(out_from, out_to, 0)) + list(parts(gin_from, gin_to, 1))
    for copy, _ in copies:
        copy.start()
    for copy, then in copies:
        copy.wait()
        then.start()
    mlp = lax.axis_index("mlp")
    eye = iota((D, D), 0) == iota((D, D), 1)
    eye8 = iota((8, 128), 0) == iota((8, 128), 1)

    def line(x):
        return x.reshape(1, -1)

    def total(x):
        return jnp.sum(jnp.sum(x, axis=0, keepdims=True), axis=1, keepdims=True)

    def fresh(old, mean):
        return DECAY * old + (1.0 - DECAY) * (mean + EPS_SQ)

    def owned(grads, cols, over, row, row_total, weight, col_old, rate, outs):
        grad_out, row_out, col_out, new_out, low_out = outs
        width = grads.shape[1]
        col_new = fresh(line(col_old[...]), cols * (1.0 / D))
        mean = row_total * (1.0 / D)
        norm = mean * jnp.sum(over * (1.0 / col_new), axis=1, keepdims=True) * (1.0 / (D * width))
        step = grads * lax.rsqrt(row * col_new * (1.0 / mean))
        new = weight - rate * (step * clip_scale(norm))
        grad_out[...] = grads[:3]
        row_out[...] = jnp.sum(jnp.where(eye8, row, 0.0), axis=0)[:3]
        col_out[...] = col_new.reshape(width)
        new_out[...] = new[:3]
        low_out[...] = new.astype(BF16)[:3]

    def by_part(take):
        return jnp.concatenate([take(g)[:, 128 * p : 128 * p + 128] for p in range(3) for g in range(SETS)], axis=1)

    owned(
        by_part(lambda g: own_g[g]), by_part(lambda g: at_sums[g : g + 1, :]),
        by_part(lambda g: at_sums[4 + g : 5 + g, :]), own_r[0][:, :1], at_sums[8:9, :1], own_wq[...], qkv_col,
        D ** (-0.5), (qkv_grad, qkv_row_new, qkv_col_new, qkv_new, qkv_low),
    )
    owned(
        own_g[3], at_sums[3:4, :], at_sums[7:8, :], own_r[1][:, :1], at_sums[9:10, :1], own_wp[...], proj_col,
        (D // 8) ** (-0.5), (proj_grad, proj_row_new, proj_col_new, proj_new, proj_low),
    )

    def update(grad, weight, row, col, mean, norm, rate, grad_out, new_out, low_out):
        row = row * (1.0 / mean)
        factor = rate * clip_scale(norm)
        for r in range(0, D, 48):
            rows = slice(r, r + 48)
            g = grad[rows, :]
            new = weight[rows, :] - (g * lax.rsqrt(row[rows] * col)) * factor
            grad_out[rows, :] = g
            new_out[rows, :] = new
            low_out[rows, :] = new.astype(BF16)

    row_new = fresh(line(fc1_row[...]), fc_sums[0, 0:1, :] * (1.0 / FF))
    mean = row_mean(row_new)
    norm = mean * row_mean(fc_sums[0, 1:2, :] * (1.0 / row_new)) * (1.0 / FF)
    fc1_row_new[...] = row_new.reshape(D)
    fc1_col_new[...] = fc_sums[1, 5]
    update(
        fin.at[0], fc1, to_column(row_new, eye), fc_sums[1, 5:6, :], mean, norm, D ** (-0.5),
        fc1_grad, fc1_new, fc1_low,
    )
    col_new = fresh(line(fc2_col[...]), fc_sums[0, 2:3, :] * (1.0 / FF))
    mean = fc_sums[0, 4:5, :1] * (1.0 / FF)
    norm = mean * row_mean(fc_sums[0, 3:4, :] * (1.0 / col_new)) * (1.0 / FF)
    fc2_row_new[...] = fc_sums[1, 6]
    fc2_col_new[...] = col_new.reshape(D)
    update(
        fin.at[1], fc2, to_column(fc_sums[1, 6:7, :], eye), col_new, mean, norm, FF ** (-0.5),
        fc2_grad, fc2_new, fc2_low,
    )

    def stepped(grad, old):
        state = fresh(old, grad * grad)
        return state, grad * lax.rsqrt(state)

    norm = jnp.zeros((1, 1), F32)
    for m in range(4):
        d = (m + 4 - mlp) % 4
        step = stepped(vec[4 + m : 5 + m, :], b1[d + d // 2 - 2 * (d // 3), 4:5, :])[1]
        norm = norm + jnp.sum(step * step, axis=1, keepdims=True)
    grad = vec[pl.ds(4 + mlp, 1), :]
    state, step = stepped(grad, b1[0, 4:5, :])
    b1_grad[...] = grad.reshape(D)
    b1_state_new[...] = state.reshape(D)
    b1_new[...] = (line(fc1_b[...]) - VEC_RATE * (step * clip_scale(norm * (1.0 / FF)))).reshape(D)

    grad = jnp.concatenate([vec[n : n + 1, :] for n in (20, 21, 22, 23, 0, 1, 2, 3)], axis=1)
    state, step = stepped(grad, line(small_state[...]))
    norm = jnp.sum(step * step, axis=1, keepdims=True) * (1.0 / (8 * D))
    small_grad[...] = grad.reshape(8 * D)
    small_state_new[...] = state.reshape(8 * D)
    small_new[...] = (line(small[...]) - VEC_RATE * (step * clip_scale(norm))).reshape(8 * D)

    grad = vec[8:20, :169]
    state, step = stepped(grad, table_state[...])
    norm = total(step * step) * (1.0 / (169 * HEADS))
    table_grad[...] = grad
    table_state_new[...] = state
    table_new[...] = table[...] - VEC_RATE * (step * clip_scale(norm))
    for _, then in copies:
        then.wait()


def finish(*arrays):
    sd = jax.ShapeDtypeStruct
    vm = pltpu.VMEM

    def owned(width):
        return [sd((3, width), F32), sd((3,), F32), sd((width,), F32), sd((3, width), F32), sd((3, width), BF16)]

    shard = [sd((D, D), F32), sd((D,), F32), sd((D,), F32), sd((D, D), F32), sd((D, D), BF16)]
    out_shape = owned(QKV) + owned(D) + shard + shard
    out_shape += [sd((D,), F32)] * 3 + [sd((8 * D,), F32)] * 3 + [sd((HEADS, 169), F32)] * 3 + [sd((TOK, D), F32)] * 2
    return pl.pallas_call(
        finish_kernel,
        out_shape=out_shape,
        in_specs=[pl.BlockSpec(memory_space=vm)] * (len(arrays) - 2) + [pl.BlockSpec(memory_space=pl.ANY)] * 2,
        out_specs=[pl.BlockSpec(memory_space=vm)] * (len(out_shape) - 2) + [pl.BlockSpec(memory_space=pl.ANY)] * 2,
        scratch_shapes=[vm((2, TOK, D), F32), pltpu.SemaphoreType.DMA((2, 4)), pltpu.SemaphoreType.DMA((2, 4))],
        compiler_params=pltpu.CompilerParams(vmem_limit_bytes=63 * 1024 * 1024),
        name="finish",
    )(*arrays)


def clip_scale(mean_square):
    return 1.0 / jnp.maximum(1.0, jnp.sqrt(mean_square))


def per_device(
    tokens_in, out_grad, window_live, region_ids, qkv_weight, proj_weight, rel_table, small_params,
    fc1_weight, fc1_bias, fc2_weight, qkv_row, qkv_col, proj_row, proj_col, fc1_row, fc1_col,
    fc2_row, fc2_col, fc1_bias_state, small_state, table_state,
):
    out, gin, fin, *parts = block(
        window_live, region_ids, tokens_in, out_grad, qkv_weight, proj_weight, rel_table.T, small_params,
        fc1_weight, fc2_weight, fc1_bias, fc1_bias_state, fc1_col, fc2_row, qkv_row, proj_row,
    )
    *outs, table_grad, table_state_new, table_new, out, gin = finish(
        fin.reshape(2, D, D), *parts, fc1_weight, fc2_weight, fc1_bias, fc1_row, fc2_col, qkv_col, proj_col,
        small_params, small_state, rel_table.T, table_state.T, out, gin,
    )
    return (out, gin, *outs, table_grad.T, table_state_new.T, table_new.T)


def solution(mesh):
    tokens, owner = P(("win", "mlp"), None), P(("win", "mlp"))
    whole, part = P(), P("mlp")
    return jax.shard_map(
        per_device,
        mesh=mesh,
        in_specs=(
            tokens, tokens, owner, owner, whole, whole, whole, whole, P(None, "mlp"), part, P("mlp", None),
            whole, whole, whole, whole, whole, part, part, whole, part, whole, whole,
        ),
        out_specs=(
            tokens, tokens,
            tokens, owner, whole, tokens, tokens,
            tokens, owner, whole, tokens, tokens,
            P(None, "mlp"), whole, part, P(None, "mlp"), P(None, "mlp"),
            P("mlp", None), part, whole, P("mlp", None), P("mlp", None),
            part, part, part,
            whole, whole, whole,
            whole, whole, whole,
        ),
        check_vma=False,
    )
```

```python
import functools
import math

import jax
import jax.numpy as jnp
from jax import lax
from jax.experimental import pallas as pl
from jax.experimental.pallas import tpu as pltpu
from jax.sharding import PartitionSpec as P

D = 384
FF = 1536
QKV = 3 * D
HEADS = 12
WIN = 7
SPAN = WIN * WIN
STEP = 10
DECAY = 1.0 - STEP ** (-0.8)
EPS_NORM = 1e-05
EPS_SQ = 1e-30
VEC_RATE = 0.3
SCALE = 32 ** (-0.5)
FAR = -1e30
LOG2E = math.log2(math.e)
FACTOR = (2.0 * math.pi) ** (-0.5)

PLACE = (0, 1, 3, 2)
GROUPS = 3
PER = 8
G_TOK = PER * SPAN
G_ROWS = 400
ROWS = GROUPS * G_ROWS
TOK = GROUPS * G_TOK
CHUNK = 64
KEYS = 56
SETS = 3
LANES = 4 * CHUNK

MESH = pl.DeviceIdType.MESH
F32 = jnp.float32
BF16 = jnp.bfloat16


def dot(a, b):
    return jnp.dot(a, b, preferred_element_type=F32)


def dot_nt(a, b):
    return lax.dot_general(a, b, (((1,), (1,)), ((), ())), preferred_element_type=F32)


def dot_tn(a, b):
    return lax.dot_general(a, b, (((0,), (0,)), ((), ())), preferred_element_type=F32)


def dot_exact(a, b):
    return jnp.dot(a, b, precision=lax.Precision.HIGHEST, preferred_element_type=F32)


def iota(shape, dim):
    return lax.broadcasted_iota(jnp.int32, shape, dim)


def fold_rows(x):
    total = x[0:8]
    for i in range(1, x.shape[0] // 8):
        total = total + x[8 * i : 8 * i + 8]
    return total


def row_mean(x):
    return jnp.sum(x, axis=1, keepdims=True) * (1.0 / D)


def normalize(x):
    center = x - row_mean(x)
    inverse = lax.rsqrt(row_mean(center * center) + EPS_NORM)
    return center * inverse, inverse


def normalize_back(u, gain, scaled, inverse):
    weighted = u * gain
    return inverse * (weighted - row_mean(weighted) - scaled * row_mean(weighted * scaled))


def gelu_parts(v):
    density = jnp.exp2((v * v) * (-0.5 * LOG2E) + math.log2(FACTOR))
    t = 1.0 / (1.0 + (0.3275911 * 0.5**0.5) * jnp.abs(v))
    c = 0.5 / FACTOR
    poly = (1.061405429 * c) * t - 1.453152027 * c
    poly = poly * t + 1.421413741 * c
    poly = poly * t - 0.284496736 * c
    poly = poly * t + 0.254829592 * c
    tail = density * (poly * t)
    phi = jnp.where(v < 0.0, tail, 1.0 - tail)
    return v * phi, phi + v * density


def barrel(x, amount, right):
    width = x.shape[1]
    for k in range(7):
        step = 1 << k
        moved = pltpu.roll(x, step if right else width - step, 1)
        x = jnp.where((amount & step) != 0, moved, x)
    return x


def embed(i):
    return 13 * (i // WIN) + i % WIN


def chunk_start(w):
    return pl.multiple_of((w // PER) * G_ROWS + (w % PER) * 48, 16)


def widen(tok, x_ref):
    for a in range(GROUPS):
        for r in range(0, G_TOK, 56):
            src = a * G_TOK + r
            low = src // 16 * 16
            x_ref[a * G_ROWS + r : a * G_ROWS + r + 56, :] = (
                tok[low : low + 64 if low + 64 <= TOK else TOK, :].astype(F32)[src - low : src - low + 56]
            )
        x_ref[a * G_ROWS + G_TOK : (a + 1) * G_ROWS, :] = jnp.zeros((G_ROWS - G_TOK, D), F32)


def prologue(region, table, emask, bias, mask):
    row = iota((LANES, 128), 0)
    lane = iota((LANES, 128), 1)
    for b in range(PER):
        i = row % CHUNK
        keep = (i >= b) & (i < b + SPAN) & (lane // 32 == row // CHUNK)
        emask[b] = jnp.where(keep, 1.0, 0.0).astype(BF16)
    j = iota((KEYS, 256), 0)
    amount = jnp.maximum(84 - embed(j), 0)
    jl = iota((KEYS, LANES), 0)
    il = iota((KEYS, LANES), 1) % CHUNK
    for g in range(SETS):
        base = jnp.zeros((KEYS, LANES), F32)
        for h in range(4):
            line = jnp.concatenate([table[4 * g + h : 4 * g + h + 1, :], jnp.zeros((1, 87), F32)], axis=1)
            wide = jnp.broadcast_to(line, (KEYS, 256))
            wide = barrel(wide, amount, False)[:, :128]
            lane_to = iota((128, LANES), 1) - CHUNK * h
            pick = (iota((128, LANES), 0) == embed(lane_to)) & (lane_to >= 0) & (lane_to < SPAN)
            base = base + dot_exact(wide, jnp.where(pick, 1.0, 0.0))
        for b in range(PER):
            moved = pltpu.roll(pltpu.roll(base, b, 0), b, 1) if b else base
            key_ok = (jl >= b) & (jl < b + SPAN)
            query_ok = (il >= b) & (il < b + SPAN)
            bias[b, g] = jnp.where(key_ok, jnp.where(query_ok, moved, 0.0), FAR)
    eye = iota((CHUNK, CHUNK), 0) == iota((CHUNK, CHUNK), 1)
    region_row = jnp.concatenate([region[...].reshape(1, TOK).astype(F32), jnp.zeros((1, 104), F32)], axis=1)
    for w in range(GROUPS * PER):
        start = (w // PER) * G_TOK + (w % PER) * 48
        line = region_row[:, start : start + CHUNK]
        column = jnp.sum(jnp.where(eye, jnp.broadcast_to(line, (CHUNK, CHUNK)), 0.0), axis=1, keepdims=True)
        wide = jnp.concatenate([line] * 4, axis=1)
        mask[w] = jnp.where(column[:KEYS] != wide, -100.0, 0.0)


def pad_keys(x):
    return jnp.concatenate([x, jnp.zeros((CHUNK - KEYS, x.shape[1]), x.dtype)], axis=0)


def spread(x, keep):
    return jnp.concatenate([x] * 4, axis=0) * keep


def collect(full):
    head = iota((CHUNK, 128), 1) // 32
    parts = [full[CHUNK * h : CHUNK * (h + 1)] for h in range(4)]
    low = jnp.where(head == 0, parts[0], parts[1])
    high = jnp.where(head == 2, parts[2], parts[3])
    return jnp.where(head < 2, low, high)


def packed(ref):
    at, views = 0, []
    for rows in (24, 16, 16, 32, 24, 8, 32, 16):
        views.append(ref.at[at : at + rows])
        at += rows
    return views


def block_kernel(
    live_windows, region, tok_in, og_in, wq_in, wp_in, fc1_in, fc2_in, table, small,
    fc1_b, fc1_state, fc1_col, fc2_row, qkv_row, proj_row,
    out_to, gin_to, fin_to, pack,
    x_ref, xh1, inv1, inv2, n1, n2, qkv, att_b, probs, back, hidden, ig, dqkv,
    emask, bias, mask, tacc, s1, s2, sums, b1_acc, wq_b, wp_b, w1, w2, tok, og, wq, wp, fc1, fc2, fin, fin_b, b1, stage, in_sem, out_sem,
    fcl, fr1, fr2, ft, fr3, fr4, fst, atl, ar1, ar2, ar3, ar4, ast, vx, vy, at_total,
    w_send, w_recv, b_send, b_recv, pair_send, pair_recv, f1s, f1r, f2s, f2r, f3s, f3r, f4s, f4r, f5s, f5r, f7s, f7r, f8s, f8r,
    a1s, a1r, a2s, a2r, a3s, a3r, a4s, a4r, a5s, a5r, vxs, vxr, vys, vyr,
):
    win, mlp = lax.axis_index("win"), lax.axis_index("mlp")
    vec, fc_sums, at_sums, own_g, own_wq, own_wp, b1_all, own_r = packed(pack)
    z, y, core = win // 8, (win // 2) % 4, win % 2
    pair = win + 1 - 2 * core

    def along_x(d):
        return win, (mlp + d) % 4

    def along_y(d):
        return z * 8 + ((y + d) % 4) * 2 + core, mlp

    def along_z(d):
        return ((z + d) % 4) * 8 + y * 2 + core, mlp

    def plane_peer(d):
        return ((z + d // 4) % 4) * 8 + ((y + d % 4) % 4) * 2 + core, mlp

    def class_peer(d):
        return pair if d >= 4 else win, (mlp + d) % 4

    loads = [
        pltpu.make_async_copy(src, dst, in_sem.at[n])
        for n, (src, dst) in enumerate(
            ((fc1_in, fc1), (fc2_in, fc2), (tok_in, tok), (wq_in, wq), (og_in, og), (wp_in, wp))
        )
    ]
    for copy in loads:
        copy.start()
    barrier = pltpu.get_barrier_semaphore()
    peers = [class_peer(d) for d in range(1, 8)]
    peers += [plane_peer(d) for d in range(1, 16)]
    for peer in peers:
        pl.semaphore_signal(barrier, inc=1, device_id=peer, device_id_type=MESH)

    def remote(src, dst, send, recv, peer):
        return pltpu.make_async_remote_copy(
            src_ref=src, dst_ref=dst, send_sem=send, recv_sem=recv, device_id=peer, device_id_type=MESH
        )

    def param(part):
        return small[D * part : D * part + D].reshape(1, D)

    pending = []

    def start(copy):
        copy.start()
        pending.append(copy)
        return copy

    def shard(place):
        half = pl.ds(pl.multiple_of(core * (D // 2), 16), D // 2)
        half_at = pl.ds(pl.multiple_of(place * D + core * (D // 2), 16), D // 2)
        return w1.at[half, D * place : D * place + D], w2.at[half_at, :]

    def near(d, n):
        return remote(shard(0)[n], shard(PLACE[4 - d])[n], w_send.at[d // 2, n], w_recv.at[d // 2, n], along_x(d))

    def far(n):
        d = 3 - 2 * n
        return remote(shard(1 + n)[n], shard(3)[n], w_send.at[2, n], w_recv.at[2, n], along_x(d))

    def bias_copy(d):
        return remote(b1.at[0], b1.at[PLACE[4 - d]], b_send.at[d - 1], b_recv.at[d - 1], along_x(d))

    def across(place, n):
        came = shard(place)[n]
        return remote(came, came, pair_send.at[place - 1, n], pair_recv.at[place - 1, n], (pair, mlp))

    for copy in loads[:2]:
        copy.wait()
    w1[:, :D] = fc1[...].astype(BF16)
    w2[:D, :] = fc2[...].astype(BF16)
    b1[0, 0:4] = jnp.broadcast_to(fc1_b[...].reshape(1, D), (4, D))
    b1[0, 4:8] = jnp.broadcast_to(fc1_state[...].reshape(1, D), (4, D))
    pl.semaphore_wait(barrier, 22)
    for n in range(2):
        for d in (1, 3):
            start(near(d, n))
    for d in range(1, 4):
        start(bias_copy(d))

    live = live_windows[0]
    for n in range(1, GROUPS * PER):
        live = live + live_windows[n]
    live = live * SPAN
    prologue(region, table, emask, bias, mask)
    for copy in loads[2:]:
        copy.wait()
    widen(tok, x_ref)
    for g in range(SETS):
        for part in range(3):
            wq_b[:, D * g + 128 * part : D * g + 128 * part + 128] = wq[
                :, D * part + 128 * g : D * part + 128 * g + 128
            ].astype(BF16)
    wp_b[...] = wp[...].astype(BF16)
    sums[...] = jnp.zeros_like(sums)
    b1_acc[...] = jnp.zeros_like(b1_acc)
    tacc[...] = jnp.zeros_like(tacc)
    att = dqkv.at[:, :D]
    xh2 = dqkv.at[:, D : 2 * D]
    dqkv_b = ig.at[:, :QKV]
    dqkv[:, :D] = jnp.zeros((ROWS, D), F32)

    for a in range(GROUPS):
        for r in range(0, G_TOK, 56):
            src = a * G_TOK + r
            low = src // 16 * 16
            rows = og[low : low + 64 if low + 64 <= TOK else TOK, :].astype(F32)[src - low : src - low + 56]
            keep = iota((56, D), 0) + src < live
            x = jnp.where(keep, rows, 0.0)
            s2[r : r + 56, :] = x
            sums[7] += fold_rows(x)
        s2[G_TOK:G_ROWS, :] = jnp.zeros((G_ROWS - G_TOK, D), F32)
        back[a * G_ROWS : (a + 1) * G_ROWS, :] = s2[...].astype(BF16)

    shift_q = jnp.concatenate(
        [
            part[:, 128 * g : 128 * g + 128]
            for g in range(SETS)
            for part in (param(2), jnp.zeros((1, D), F32), param(3))
        ],
        axis=1,
    )

    @pl.loop(0, 5, unroll=5)
    def _(t):
        for c in range(15):
            rows = pl.ds(pl.multiple_of(t * 240 + c * 16, 16), 16)
            scaled, inverse = normalize(x_ref[rows, :])
            xh1[rows, :] = scaled
            inv1[rows, :] = inverse
            n1[rows, :] = (scaled * param(0) + param(1)).astype(BF16)

    @pl.loop(0, 5, unroll=5)
    def _(t):
        rows = pl.ds(pl.multiple_of(t * 240, 16), 240)
        qkv[rows, :] = (dot(n1[rows, :], wq_b[...]) + shift_q).astype(BF16)

    def scores_of(a, b, g):
        rows = pl.ds(a * G_ROWS + b * 48, CHUNK)
        q = qkv[rows, D * g : D * g + 128]
        k = qkv[rows, D * g + 128 : D * g + 256]
        return dot_nt(k, spread(q, emask[b]))

    def attend(a, b, g, raw):
        rows = pl.ds(a * G_ROWS + b * 48, CHUNK)
        v = qkv[rows, D * g + 256 : D * g + 384]
        scores = raw[:KEYS] * SCALE + (bias[b, g] + mask[a * PER + b])
        p = jnp.exp(scores - jnp.max(scores, axis=0, keepdims=True))
        p = p * (1.0 / jnp.sum(p, axis=0, keepdims=True))
        probs[a * PER + b, g] = p
        return dot_tn(pad_keys(p).astype(BF16), v)

    def attended(a, b, g, full):
        rows = pl.ds(a * G_ROWS + b * 48, CHUNK)
        i = iota((CHUNK, 128), 0)
        att[rows, 128 * g : 128 * g + 128] += jnp.where((i >= b) & (i < b + SPAN), collect(full), 0.0)

    blocks = [[(a, b, g) for a in range(GROUPS)] for b in range(PER) for g in range(SETS)]
    ahead = [scores_of(*unit) for unit in blocks[0]]
    for n, units in enumerate(blocks):
        raws = ahead
        if n + 1 < len(blocks):
            ahead = [scores_of(*unit) for unit in blocks[n + 1]]
        fulls = [attend(*unit, raw) for unit, raw in zip(units, raws)]
        for unit, full in zip(units, fulls):
            attended(*unit, full)

    for n in range(2):
        for d in (1, 3):
            near(d, n).wait_recv()
        start(far(n))
    for place in (1, 2):
        for n in range(2):
            start(across(place, n))
    for d in range(1, 4):
        bias_copy(d).wait_recv()

    @pl.loop(0, GROUPS, unroll=3)
    def _(a):
        rows = pl.ds(pl.multiple_of(a * G_ROWS, 16), G_ROWS)
        att_b[rows, :] = att[rows, :].astype(BF16)
        s1[...] = dot(att_b[rows, :], wp_b[...])

        for c in range(25):
            here = pl.ds(pl.multiple_of(a * G_ROWS + 16 * c, 16), 16)
            middle = x_ref[here, :] + (s1[16 * c : 16 * c + 16, :] + param(4))
            stage[here, :] = middle
            scaled, inverse = normalize(middle)
            xh2[here, :] = scaled
            inv2[here, :] = inverse
            n2[here, :] = (scaled * param(5) + param(6)).astype(BF16)

    for nt in range(6):
        if nt in (1, 3):
            for n in range(2):
                across(1 + nt // 2, n).wait_recv()
        if nt == 3:
            for n in range(2):
                far(n).wait_recv()
                start(across(3, n))
        if nt == 4:
            for n in range(2):
                across(3, n).wait_recv()
        cols = slice(256 * nt, 256 * nt + 256)
        shift = jnp.concatenate(
            [b1[c // 3, 0:1, 128 * (c % 3) : 128 * (c % 3) + 128] for c in (2 * nt, 2 * nt + 1)], axis=1
        )

        def products(mt):
            rows = pl.ds(mt * 240, 240)
            return dot(n2[rows, :], w1[:, cols]) + shift, dot_nt(back[rows, :], w2[cols, :])

        ahead = products(0)
        for mt in range(5):
            inner, up = ahead
            if mt < 4:
                ahead = products(mt + 1)
            total = b1_acc[:, cols]
            for c in range(15):
                act, slope = gelu_parts(inner[16 * c : 16 * c + 16])
                here = pl.ds(mt * 240 + 16 * c, 16)
                hidden[here, cols] = act.astype(BF16)
                grad = (up[16 * c : 16 * c + 16] * slope).astype(BF16)
                ig[here, cols] = grad
                total = total + fold_rows(grad.astype(F32))
            b1_acc[:, cols] = total

    g2 = dot_tn(hidden[...], back[...]).astype(BF16)
    g1 = dot_tn(n2[...], ig[...]).astype(BF16)
    for m in range(4):
        fcl[0, m] = g1[:, D * m : D * m + D].reshape(4, 96, D)
        fcl[1, m] = g2[D * m : D * m + D].reshape(4, 96, D)
    fc_one = [start(remote(fcl.at[1 - core, m], fr1.at[m], f1s.at[m], f1r.at[m], (pair, mlp))) for m in range(4)]

    def middle_back(a):
        rows = slice(a * G_ROWS, (a + 1) * G_ROWS)
        held = (s1, s2)[a % 2]
        held[...] = dot_nt(ig[rows, :], w1[...])
        for c in range(25):
            here = slice(16 * c, 16 * c + 16)
            at = slice(a * G_ROWS + 16 * c, a * G_ROWS + 16 * c + 16)
            u = held[here, :]
            scaled = xh2[at, :]
            sums[5] += fold_rows(u * scaled)
            sums[6] += fold_rows(u)
            mg = normalize_back(u, param(5), scaled, inv2[at, :]) + back[at, :].astype(F32)
            x_ref[at, :] = mg
            low = mg.astype(BF16)
            n2[at, :] = low
            sums[4] += fold_rows(low.astype(F32))

    def out_copy(a):
        return pltpu.make_async_copy(
            stage.at[pl.ds(a * G_ROWS, G_TOK)], out_to.at[pl.ds(a * G_TOK, G_TOK)], out_sem.at[a]
        )

    def block_out(a):
        rows = slice(a * G_ROWS, (a + 1) * G_ROWS)
        held = (s1, s2)[a % 2]
        held[...] = dot(hidden[rows, :], w2[...])
        for c in range(25):
            at = slice(a * G_ROWS + 16 * c, a * G_ROWS + 16 * c + 16)
            r = stage[at, :] + (held[16 * c : 16 * c + 16, :] + param(7))
            keep = iota((16, D), 0) + (a * G_TOK + 16 * c) < live
            stage[at, :] = jnp.where(keep, r, 0.0)
        out_copy(a).start()

    p = iota((D, D), 0)
    inner_p = p % 48
    owned = 24 * (inner_p // 3) + 12 * (p // 192) + 3 * ((p // 48) % 4) + inner_p % 3
    order = jnp.where(iota((D, D), 1) == owned, 1.0, 0.0).astype(BF16)

    def ordered(grad):
        return dot(order, grad.astype(BF16)).astype(BF16).reshape(2, 4, 48, D)

    def at_one(n):
        return remote(atl.at[n, 1 - core], ar1.at[n], a1s.at[n], a1r.at[n], (pair, mlp))

    def at_add_one(n):
        at_one(n).wait_recv()
        for i in range(4):
            ar1[n, i] = (ar1[n, i].astype(F32) + atl[n, core, i].astype(F32)).astype(BF16)
        for d in range(1, 4):
            start(remote(ar1.at[n, (mlp + d) % 4], ar2.at[n, d - 1], a2s.at[n, d - 1], a2r.at[n, d - 1], along_x(d)))

    def near_axis(d):
        return ((z + d * core) % 4) * 8 + ((y + d * (1 - core)) % 4) * 2 + core, mlp

    def other_axis(d):
        return ((z + d * (1 - core)) % 4) * 8 + ((y + d * core) % 4) * 2 + core, mlp

    near_at, other_at = y * (1 - core) + z * core, z * (1 - core) + y * core

    def at_add_two(n):
        total = ar1[n, mlp].astype(F32)
        for d in range(1, 4):
            remote(ar1.at[n, 0], ar2.at[n, d - 1], a2s.at[n, d - 1], a2r.at[n, d - 1], along_x(d)).wait_recv()
            total = total + ar2[n, d - 1].astype(F32)
        ar3[n, near_at] = total.astype(BF16)
        for d in range(1, 4):
            start(remote(ar3.at[n, near_at], ar3.at[n, near_at], a3s.at[n, d - 1], a3r.at[n, d - 1], near_axis(d)))

    def at_add_three(n):
        for d in range(1, 4):
            came = ar3.at[n, (near_at + 4 - d) % 4]
            remote(came, came, a3s.at[n, d - 1], a3r.at[n, d - 1], near_axis(d)).wait_recv()
        total = ar3[n, 0].astype(F32) + ar3[n, 1].astype(F32)
        ar4[n, other_at] = (total + ar3[n, 2].astype(F32) + ar3[n, 3].astype(F32)).astype(BF16)
        for d in range(1, 4):
            start(remote(ar4.at[n, other_at], ar4.at[n, other_at], a4s.at[n, d - 1], a4r.at[n, d - 1], other_axis(d)))

    def at_finish(n):
        for d in range(1, 4):
            came = ar4.at[n, (other_at + 4 - d) % 4]
            remote(came, came, a4s.at[n, d - 1], a4r.at[n, d - 1], other_axis(d)).wait_recv()
        total = ar4[n, 0].astype(F32) + ar4[n, 1].astype(F32)
        at_total[n] = total + ar4[n, 2].astype(F32) + ar4[n, 3].astype(F32)

    def to_axes(dx, dy, dz):
        return ((z + dz) % 4) * 8 + ((y + dy) % 4) * 2 + core, (mlp + dx) % 4

    def first_axis(d):
        return to_axes(d * (1 - core), 0, d * core)

    def second_axis(d):
        return to_axes(d * core, d * (1 - core), 0)

    def third_axis(d):
        return to_axes(0, d * core, d * (1 - core))

    def last_axis(d):
        return to_axes(0, d * (1 - core), d * core)

    block_at = y * (1 - core) + z * core
    second = y * (1 - core)
    third = z * (1 - core) + y * core

    def fc_two(d):
        return remote(fr1.at[0], fr2.at[d - 1], f2s.at[d - 1], f2r.at[d - 1], first_axis(d))

    def fc_add_one():
        for m in range(4):
            fc_one[m].wait_recv()
            for i in range(4):
                fr1[m, i] = (fr1[m, i].astype(F32) + fcl[core, m, i].astype(F32)).astype(BF16)

        @pl.when(core == 0)
        def _():
            for d in range(1, 4):
                remote(fr1.at[PLACE[d]], fr2.at[d - 1], f2s.at[d - 1], f2r.at[d - 1], first_axis(d)).start()

        @pl.when(core == 1)
        def _():
            for d in range(1, 4):
                remote(fr1.at[:, (z + d) % 4], fr2.at[d - 1], f2s.at[d - 1], f2r.at[d - 1], first_axis(d)).start()

    def fc_add_two():
        for d in range(1, 4):
            fc_two(d).wait_recv()
        for i in range(4):
            total = fr1[i * core, i * (1 - core) + z * core].astype(F32)
            for d in range(1, 4):
                total = total + fr2[d - 1, i].astype(F32)
            ft[i] = total.astype(BF16)
        for d in range(1, 4):
            to = (1 - core) * ((y + d) % 4) + core * PLACE[d]
            start(remote(ft.at[to], fr3.at[d - 1], f3s.at[d - 1], f3r.at[d - 1], second_axis(d)))

    def fc_add_three():
        total = ft[second].astype(F32)
        for d in range(1, 4):
            remote(ft.at[0], fr3.at[d - 1], f3s.at[d - 1], f3r.at[d - 1], second_axis(d)).wait_recv()
            total = total + fr3[d - 1].astype(F32)
        fr4[third] = total.astype(BF16)
        for d in range(1, 4):
            start(remote(fr4.at[third], fr4.at[third], f4s.at[d - 1], f4r.at[d - 1], third_axis(d)))

    def fc_add_four():
        for d in range(1, 4):
            came = fr4.at[(third + 4 - d) % 4]
            remote(came, came, f4s.at[d - 1], f4r.at[d - 1], third_axis(d)).wait_recv()
        total = fr4[0].astype(F32) + fr4[1].astype(F32)
        fin_b[core, block_at] = (total + fr4[2].astype(F32) + fr4[3].astype(F32)).astype(BF16)
        for d in range(1, 4):
            place = fin_b.at[core, block_at]
            start(remote(place, place, f5s.at[d - 1], f5r.at[d - 1], last_axis(d)))

    def fc_spread():
        for d in range(1, 4):
            place = fin_b.at[core, (block_at + 4 - d) % 4]
            remote(place, place, f5s.at[d - 1], f5r.at[d - 1], last_axis(d)).wait_recv()
        start(remote(fin_b.at[core], fin_b.at[core], f7s.at[0], f7r.at[0], (pair, mlp)))

    mine_at, plane_at = 4 * core + mlp, 4 * z + y

    def vec_one(n):
        for d in range(1, 8):
            place = vx.at[n, mine_at]
            start(remote(place, place, vxs.at[n, d - 1], vxr.at[n, d - 1], class_peer(d)))

    def vec_two(n):
        for d in range(1, 8):
            place = vx.at[n, (mlp + 8 - d) % 4 + 4 * (core if d < 4 else 1 - core)]
            remote(place, place, vxs.at[n, d - 1], vxr.at[n, d - 1], class_peer(d)).wait_recv()
        total = vx[n, 0]
        for i in range(1, 8):
            total = total + vx[n, i]
        vy[n, plane_at] = total
        for d in range(1, 16):
            place = vy.at[n, plane_at]
            start(remote(place, place, vys.at[n, d - 1], vyr.at[n, d - 1], plane_peer(d)))

    def vec_three(n):
        for d in range(1, 16):
            place = vy.at[n, 4 * ((z + 4 - d // 4) % 4) + (y + 4 - d % 4) % 4]
            remote(place, place, vys.at[n, d - 1], vyr.at[n, d - 1], plane_peer(d)).wait_recv()
        total = vy[n, 0]
        for i in range(1, 16):
            total = total + vy[n, i]
        vec[8 * n : 8 * n + 8, :] = total

    middle_back(0)
    middle_back(1)
    fc_add_one()
    middle_back(2)

    atl[3] = ordered(dot_tn(att_b[...], n2[...]))
    start(at_one(3))

    @pl.loop(0, GROUPS, unroll=3)
    def _(a):
        rows = pl.ds(pl.multiple_of(a * G_ROWS, 16), G_ROWS)
        att_b[rows, :] = dot_nt(n2[rows, :], wp_b[...]).astype(BF16)

    dqkv[...] = jnp.zeros_like(dqkv)

    def attention_back(g, half):
        def first(a, b):
            rows = pl.ds(a * G_ROWS + b * 48, CHUNK)
            v = qkv[rows, D * g + 256 : D * g + 384]
            da = spread(att_b[rows, 128 * g : 128 * g + 128], emask[b])
            return da, dot_nt(v, da)

        def inner_grad(a, b, dp):
            p = probs[a * PER + b, g]
            pd = p * dp[:KEYS]
            return pad_keys(p).astype(BF16), pad_keys(pd - p * jnp.sum(pd, axis=0, keepdims=True)).astype(BF16)

        def last(a, b, da, p, ds):
            rows = pl.ds(a * G_ROWS + b * 48, CHUNK)
            q = qkv[rows, D * g : D * g + 128]
            k = qkv[rows, D * g + 128 : D * g + 256]
            dv = dot(p, da)
            dk = dot(ds, spread(q, emask[b])) * SCALE
            dq = collect(dot_tn(ds, k)) * SCALE
            dqkv[rows, 384 * g : 384 * g + 128] += dq
            dqkv[rows, 384 * g + 128 : 384 * g + 256] += dk
            dqkv[rows, 384 * g + 256 : 384 * g + 384] += dv

        bs = range(4 * half, 4 * half + 4)
        ahead = [first(a, bs[0]) for a in range(GROUPS)]
        for b in bs:
            held = ahead
            if b + 1 in bs:
                ahead = [first(a, b + 1) for a in range(GROUPS)]
            grads = [inner_grad(a, b, held[a][1]) for a in range(GROUPS)]
            tacc[b, g] = sum(ds.astype(F32)[:KEYS] for _, ds in grads)
            for a in range(GROUPS):
                last(a, b, held[a][0], *grads[a])

    def qkv_grad(g):
        group = slice(384 * g, 384 * g + 384)

        @pl.loop(0, 5, unroll=5)
        def _(t):
            for c in range(15):
                rows = pl.ds(pl.multiple_of(t * 240 + c * 16, 16), 16)
                low = dqkv[rows, group].astype(BF16)
                dqkv_b[rows, group] = low
                wide = low.astype(F32)
                sums[2, :, 128 * g : 128 * g + 128] += fold_rows(wide[:, :128])
                sums[3, :, 128 * g : 128 * g + 128] += fold_rows(wide[:, 256:])

        atl[g] = ordered(dot_tn(n1[...], dqkv_b[:, group]))
        start(at_one(g))

    for part in range(4):
        vx[0, mine_at, part : part + 1, :] = jnp.sum(sums[4 + part], axis=0, keepdims=True)
    for m in range(4):
        d = (m + 4 - mlp) % 4
        place = d + d // 2 - 2 * (d // 3)
        cols = pl.ds(pl.multiple_of(place * D, 128), D)
        vx[0, mine_at, 4 + m : 5 + m, :] = jnp.sum(b1_acc[:, cols], axis=0, keepdims=True)
    vec_one(0)

    def table_back(g, n):
        j = iota((KEYS, 256), 0)
        amount = jnp.maximum(84 - embed(j), 0)
        total = tacc[0, g]
        for b in range(1, PER):
            total = total + pltpu.roll(pltpu.roll(tacc[b, g], KEYS - b, 0), LANES - b, 1)
        for h in range(4):
            lane_from = iota((LANES, 256), 0) - CHUNK * h
            pick = (iota((LANES, 256), 1) == embed(lane_from)) & (lane_from >= 0) & (lane_from < SPAN)
            wide = barrel(dot_exact(total, jnp.where(pick, 1.0, 0.0)), amount, True)
            wide = jnp.where(j < SPAN, wide, 0.0)
            vx[n, mine_at, 4 * (g % 2) + h : 4 * (g % 2) + h + 1, :] = jnp.concatenate(
                [jnp.sum(wide, axis=0, keepdims=True), jnp.zeros((1, 128), F32)], axis=1
            )

    attention_back(0, 0)
    attention_back(0, 1)
    qkv_grad(0)
    attention_back(1, 0)
    attention_back(1, 1)
    fc_add_two()
    qkv_grad(1)
    at_add_one(3)
    at_add_one(0)
    vec_two(0)
    attention_back(2, 0)
    at_add_one(1)
    attention_back(2, 1)
    qkv_grad(2)
    fc_add_three()
    at_add_one(2)

    def gin_copy(a):
        return pltpu.make_async_copy(
            x_ref.at[pl.ds(a * G_ROWS, G_TOK)], gin_to.at[pl.ds(a * G_TOK, G_TOK)], out_sem.at[3 + a]
        )

    def input_back(a):
        rows = slice(a * G_ROWS, (a + 1) * G_ROWS)
        held = (s1, s2)[a % 2]
        held[...] = dot_nt(dqkv_b[rows, :], wq_b[...])
        for c in range(25):
            here = slice(16 * c, 16 * c + 16)
            at = slice(a * G_ROWS + 16 * c, a * G_ROWS + 16 * c + 16)
            u = held[here, :]
            scaled = xh1[at, :]
            sums[0] += fold_rows(u * scaled)
            sums[1] += fold_rows(u)
            x_ref[at, :] = normalize_back(u, param(0), scaled, inv1[at, :]) + x_ref[at, :]
        gin_copy(a).start()

    for a in range(GROUPS):
        input_back(a)
    at_add_two(3)
    at_add_two(0)
    table_back(0, 1)
    table_back(1, 1)
    vec_one(1)
    at_add_two(1)
    table_back(2, 2)
    for part in range(4):
        vx[2, mine_at, 4 + part : 5 + part, :] = jnp.sum(sums[part], axis=0, keepdims=True)
    vec_one(2)
    vec_three(0)
    fc_add_four()
    at_add_two(2)
    block_out(0)
    block_out(1)
    at_add_three(3)
    at_add_three(0)
    block_out(2)
    at_add_three(1)
    vec_two(1)
    vec_two(2)
    at_add_three(2)
    fc_spread()
    at_finish(3)
    at_finish(0)
    at_finish(1)

    remote(fin_b.at[1 - core], fin_b.at[1 - core], f7s.at[0], f7r.at[0], (pair, mlp)).wait_recv()
    for half in range(2):
        for n in range(4):
            fin[half, n] = fin_b[half, n].astype(F32)
    fin_copy = pltpu.make_async_copy(fin, fin_to, out_sem.at[6])
    fin_copy.start()
    eye = iota((D, D), 0) == iota((D, D), 1)

    def to_row(column):
        return jnp.sum(jnp.where(eye, column, 0.0), axis=0, keepdims=True)

    up = fin[0].reshape(D, D)
    down = fin[1].reshape(D, D)
    up_squares = up * up
    down_squares = down * down
    up_col = DECAY * fc1_col[...].reshape(1, D) + (1.0 - DECAY) * (
        jnp.sum(up_squares, axis=0, keepdims=True) * (1.0 / D) + EPS_SQ
    )
    down_row = DECAY * to_column(fc2_row[...].reshape(1, D), eye) + (1.0 - DECAY) * (row_mean(down_squares) + EPS_SQ)
    fst[mlp, 0:1] = to_row(jnp.sum(up_squares, axis=1, keepdims=True))
    fst[mlp, 1:2] = to_row(jnp.sum(up_squares * (1.0 / up_col), axis=1, keepdims=True))
    fst[mlp, 2:3] = jnp.sum(down_squares, axis=0, keepdims=True)
    fst[mlp, 3:4] = jnp.sum(down_squares * (1.0 / down_row), axis=0, keepdims=True)
    fst[mlp, 4:5] = jnp.broadcast_to(jnp.sum(down_row, axis=0, keepdims=True), (1, D))
    fst[mlp, 5:6] = up_col
    fst[mlp, 6:7] = to_row(down_row)
    fst[mlp, 7:8] = jnp.zeros((1, D), F32)
    for d in range(1, 4):
        start(remote(fst.at[mlp], fst.at[mlp], f8s.at[d - 1], f8r.at[d - 1], along_x(d)))

    vec_three(1)

    offset = 48 - 3 * plane_at
    block_rows = pl.ds(pl.multiple_of(24 * (win // 2), 8), 24)
    shift = 24 - 3 * mine_at
    rolled = pltpu.roll(wq[block_rows, :], shift, 0)[:8]
    for part in range(3):
        own_wq[8 * part : 8 * part + 8, :] = rolled[:, D * part : D * part + D]
    own_wp[...] = pltpu.roll(wp[block_rows, :], shift, 0)[:8]

    r48 = iota((48, D), 0)
    pick = iota((48, D), 1) == 24 * (r48 // 3) + 12 * core + 3 * mlp + r48 % 3

    def rows_new(state, mean):
        old = jnp.sum(jnp.where(pick, state, 0.0), axis=1, keepdims=True)
        return DECAY * old + (1.0 - DECAY) * (mean + EPS_SQ)

    at_finish(2)
    squares = [at_total[n] * at_total[n] for n in range(4)]
    qkv_new_row = rows_new(
        qkv_row[...].reshape(1, D), row_mean(squares[0] + squares[1] + squares[2]) * (1.0 / 3.0)
    )
    proj_new_row = rows_new(proj_row[...].reshape(1, D), row_mean(squares[3]))
    for n in range(4):
        over = squares[n] * (1.0 / (qkv_new_row if n < 3 else proj_new_row))
        ast[mine_at, n : n + 1] = jnp.sum(squares[n], axis=0, keepdims=True)
        ast[mine_at, 4 + n : 5 + n] = jnp.sum(over, axis=0, keepdims=True)
    ast[mine_at, 8:9] = jnp.broadcast_to(jnp.sum(qkv_new_row, axis=0, keepdims=True), (1, D))
    ast[mine_at, 9:10] = jnp.broadcast_to(jnp.sum(proj_new_row, axis=0, keepdims=True), (1, D))
    ast[mine_at, 10:16] = jnp.zeros((6, D), F32)

    def at_five(d):
        place = ast.at[mine_at]
        return remote(place, place, a5s.at[d - 1], a5r.at[d - 1], class_peer(d))

    for d in range(1, 8):
        start(at_five(d))

    for n in range(4):
        own_g[8 * n : 8 * n + 8, :] = pltpu.roll(at_total[n], offset, 0)[:8]
        b1_all[8 * n : 8 * n + 8, :] = b1[n]
    own_r[0:8, :] = pltpu.roll(jnp.broadcast_to(qkv_new_row, (48, D)), offset, 0)[:8]
    own_r[8:16, :] = pltpu.roll(jnp.broadcast_to(proj_new_row, (48, D)), offset, 0)[:8]

    for d in range(1, 4):
        place = fst.at[(mlp + 4 - d) % 4]
        remote(place, place, f8s.at[d - 1], f8r.at[d - 1], along_x(d)).wait_recv()
    fc_sums[0:8, :] = (fst[0] + fst[1]) + (fst[2] + fst[3])
    fc_sums[8:16, :] = fst[mlp]
    vec_three(2)

    for d in range(1, 8):
        place = ast.at[(mlp + 8 - d) % 4 + 4 * (core if d < 4 else 1 - core)]
        remote(place, place, a5s.at[d - 1], a5r.at[d - 1], class_peer(d)).wait_recv()
    total = ast[0]
    for n in range(1, 8):
        total = total + ast[n]
    at_sums[...] = total

    for a in range(GROUPS):
        gin_copy(a).wait()
        out_copy(a).wait()
    fin_copy.wait()
    for copy in pending:
        copy.wait_send()
    for d in range(1, 4):
        fc_two(d).wait_send()


def to_column(row, eye):
    return jnp.sum(jnp.where(eye, row, 0.0), axis=1, keepdims=True)


def block(live_windows, region, tok, og, wq, wp, fc1, fc2, *arrays):
    sd = jax.ShapeDtypeStruct
    vm = pltpu.VMEM
    dma = pltpu.SemaphoreType.DMA
    return pl.pallas_call(
        block_kernel,
        out_shape=[
            sd((TOK, D), F32),
            sd((TOK, D), F32),
            sd((2, 4, 96, D), F32),
            sd((168, D), F32),
        ],
        in_specs=[pl.BlockSpec(memory_space=pltpu.SMEM), pl.BlockSpec(memory_space=vm)]
        + [pl.BlockSpec(memory_space=pl.ANY)] * 6
        + [pl.BlockSpec(memory_space=vm)] * len(arrays),
        out_specs=[pl.BlockSpec(memory_space=pl.ANY)] * 3 + [pl.BlockSpec(memory_space=vm)],
        scratch_shapes=[
            vm((ROWS, D), F32),
            vm((ROWS, D), F32),
            vm((ROWS, 1), F32),
            vm((ROWS, 1), F32),
            vm((ROWS, D), BF16),
            vm((ROWS, D), BF16),
            vm((ROWS, QKV), BF16),
            vm((ROWS, D), BF16),
            vm((GROUPS * PER, SETS, KEYS, LANES), F32),
            vm((ROWS, D), BF16),
            vm((ROWS, FF), BF16),
            vm((ROWS, FF), BF16),
            vm((ROWS, QKV), F32),
            vm((PER, LANES, 128), BF16),
            vm((PER, SETS, KEYS, LANES), F32),
            vm((GROUPS * PER, KEYS, LANES), F32),
            vm((PER, SETS, KEYS, LANES), F32),
            vm((G_ROWS, D), F32),
            vm((G_ROWS, D), F32),
            vm((8, 8, D), F32),
            vm((8, FF), F32),
            vm((D, QKV), BF16),
            vm((D, D), BF16),
            vm((D, FF), BF16),
            vm((FF, D), BF16),
            vm((TOK, D), BF16),
            vm((TOK, D), BF16),
            vm((D, QKV), F32),
            vm((D, D), F32),
            vm((D, D), F32),
            vm((D, D), F32),
            vm((2, 4, 96, D), F32),
            vm((2, 4, 96, D), BF16),
            vm((4, 8, D), F32),
            vm((ROWS, D), F32),
            dma((6,)), dma((7,)),
            vm((2, 4, 4, 96, D), BF16),
            vm((4, 4, 96, D), BF16),
            vm((3, 4, 96, D), BF16),
            vm((4, 96, D), BF16),
            vm((3, 96, D), BF16),
            vm((4, 96, D), BF16),
            vm((4, 8, D), F32),
            vm((4, 2, 4, 48, D), BF16),
            vm((4, 4, 48, D), BF16),
            vm((4, 3, 48, D), BF16),
            vm((4, 4, 48, D), BF16),
            vm((4, 4, 48, D), BF16),
            vm((8, 16, D), F32),
            vm((3, 8, 8, D), F32),
            vm((3, 16, 8, D), F32),
            vm((4, 48, D), F32),
            dma((3, 2)), dma((3, 2)), dma((3,)), dma((3,)), dma((3, 2)), dma((3, 2)),
            dma((4,)), dma((4,)),
            dma((3,)), dma((3,)), dma((3,)), dma((3,)), dma((3,)), dma((3,)),
            dma((3,)), dma((3,)), dma((1,)), dma((1,)), dma((3,)), dma((3,)),
            dma((4,)), dma((4,)),
            dma((4, 3)), dma((4, 3)), dma((4, 3)), dma((4, 3)), dma((4, 3)), dma((4, 3)),
            dma((7,)), dma((7,)),
            dma((3, 7)), dma((3, 7)), dma((3, 15)), dma((3, 15)),
        ],
        compiler_params=pltpu.CompilerParams(
            vmem_limit_bytes=63 * 1024 * 1024, collective_id=0, has_side_effects=True
        ),
        cost_estimate=pl.CostEstimate(flops=14_000_000_000, bytes_accessed=20_000_000, transcendentals=3_000_000),
        name="block",
    )(live_windows, region, tok, og, wq, wp, fc1, fc2, *arrays)


def finish_kernel(
    fin, fc1, fc2, out_from, gin_from, pack, fc1_b, fc1_row, fc2_col, qkv_col, proj_col,
    small, small_state, table, table_state,
    qkv_grad, qkv_row_new, qkv_col_new, qkv_new, qkv_low, proj_grad, proj_row_new, proj_col_new, proj_new, proj_low,
    fc1_grad, fc1_row_new, fc1_col_new, fc1_new, fc1_low, fc2_grad, fc2_row_new, fc2_col_new, fc2_new, fc2_low,
    b1_grad, b1_state_new, b1_new, small_grad, small_state_new, small_new, table_grad, table_state_new, table_new,
    out_to, gin_to, held, sem_in, sem_out,
):
    vec, fc_sums, at_sums, own_g, own_wq, own_wp, b1, own_r = packed(pack)
    def parts(src, dst, n):
        for i in range(4):
            rows = pl.ds(304 * i, 304 if i < 3 else TOK - 912)
            here = held.at[n, rows]
            yield (
                pltpu.make_async_copy(src.at[rows], here, sem_in.at[n, i]),
                pltpu.make_async_copy(here, dst.at[rows], sem_out.at[n, i]),
            )

    copies = list(parts(out_from, out_to, 0)) + list(parts(gin_from, gin_to, 1))
    for copy, _ in copies:
        copy.start()
    mlp = lax.axis_index("mlp")
    eye = iota((D, D), 0) == iota((D, D), 1)
    eye8 = iota((8, 128), 0) == iota((8, 128), 1)

    def line(x):
        return x.reshape(1, -1)

    def total(x):
        return jnp.sum(jnp.sum(x, axis=0, keepdims=True), axis=1, keepdims=True)

    def fresh(old, mean):
        return DECAY * old + (1.0 - DECAY) * (mean + EPS_SQ)

    def owned(grads, cols, over, row, row_total, weight, col_old, rate, outs):
        grad_out, row_out, col_out, new_out, low_out = outs
        width = grads.shape[1]
        col_new = fresh(line(col_old[...]), cols * (1.0 / D))
        mean = row_total * (1.0 / D)
        norm = mean * jnp.sum(over * (1.0 / col_new), axis=1, keepdims=True) * (1.0 / (D * width))
        step = grads * lax.rsqrt(row * col_new * (1.0 / mean))
        new = weight - rate * (step * clip_scale(norm))
        grad_out[...] = grads[:3]
        row_out[...] = jnp.sum(jnp.where(eye8, row, 0.0), axis=0)[:3]
        col_out[...] = col_new.reshape(width)
        new_out[...] = new[:3]
        low_out[...] = new.astype(BF16)[:3]

    def by_part(take):
        return jnp.concatenate([take(g)[:, 128 * p : 128 * p + 128] for p in range(3) for g in range(SETS)], axis=1)

    owned(
        by_part(lambda g: own_g[8 * g : 8 * g + 8, :]), by_part(lambda g: at_sums[g : g + 1, :]),
        by_part(lambda g: at_sums[4 + g : 5 + g, :]), own_r[0:8, :1], at_sums[8:9, :1],
        jnp.concatenate([own_wq[8 * part : 8 * part + 8, :] for part in range(3)], axis=1), qkv_col,
        D ** (-0.5), (qkv_grad, qkv_row_new, qkv_col_new, qkv_new, qkv_low),
    )
    owned(
        own_g[24:32, :], at_sums[3:4, :], at_sums[7:8, :], own_r[8:16, :1], at_sums[9:10, :1], own_wp[...], proj_col,
        (D // 8) ** (-0.5), (proj_grad, proj_row_new, proj_col_new, proj_new, proj_low),
    )

    for copy, then in copies:
        copy.wait()
        then.start()

    def update(grad, weight, row, col, mean, norm, rate, grad_out, new_out, low_out):
        row = row * (1.0 / mean)
        factor = rate * clip_scale(norm)
        for r in range(0, D, 48):
            rows = slice(r, r + 48)
            g = grad[rows, :]
            new = weight[rows, :] - (g * lax.rsqrt(row[rows] * col)) * factor
            grad_out[rows, :] = g
            new_out[rows, :] = new
            low_out[rows, :] = new.astype(BF16)

    row_new = fresh(line(fc1_row[...]), fc_sums[0:1, :] * (1.0 / FF))
    mean = row_mean(row_new)
    norm = mean * row_mean(fc_sums[1:2, :] * (1.0 / row_new)) * (1.0 / FF)
    fc1_row_new[...] = row_new.reshape(D)
    fc1_col_new[...] = fc_sums[13]
    update(
        fin.at[0], fc1, to_column(row_new, eye), fc_sums[13:14, :], mean, norm, D ** (-0.5),
        fc1_grad, fc1_new, fc1_low,
    )
    col_new = fresh(line(fc2_col[...]), fc_sums[2:3, :] * (1.0 / FF))
    mean = fc_sums[4:5, :1] * (1.0 / FF)
    norm = mean * row_mean(fc_sums[3:4, :] * (1.0 / col_new)) * (1.0 / FF)
    fc2_row_new[...] = fc_sums[14]
    fc2_col_new[...] = col_new.reshape(D)
    update(
        fin.at[1], fc2, to_column(fc_sums[14:15, :], eye), col_new, mean, norm, FF ** (-0.5),
        fc2_grad, fc2_new, fc2_low,
    )

    def stepped(grad, old):
        state = fresh(old, grad * grad)
        return state, grad * lax.rsqrt(state)

    norm = jnp.zeros((1, 1), F32)
    for m in range(4):
        d = (m + 4 - mlp) % 4
        step = stepped(vec[4 + m : 5 + m, :], b1[pl.ds(8 * (d + d // 2 - 2 * (d // 3)) + 4, 1), :])[1]
        norm = norm + jnp.sum(step * step, axis=1, keepdims=True)
    grad = vec[pl.ds(4 + mlp, 1), :]
    state, step = stepped(grad, b1[4:5, :])
    b1_grad[...] = grad.reshape(D)
    b1_state_new[...] = state.reshape(D)
    b1_new[...] = (line(fc1_b[...]) - VEC_RATE * (step * clip_scale(norm * (1.0 / FF)))).reshape(D)

    grad = jnp.concatenate([vec[n : n + 1, :] for n in (20, 21, 22, 23, 0, 1, 2, 3)], axis=1)
    state, step = stepped(grad, line(small_state[...]))
    norm = jnp.sum(step * step, axis=1, keepdims=True) * (1.0 / (8 * D))
    small_grad[...] = grad.reshape(8 * D)
    small_state_new[...] = state.reshape(8 * D)
    small_new[...] = (line(small[...]) - VEC_RATE * (step * clip_scale(norm))).reshape(8 * D)

    grad = vec[8:20, :169]
    state, step = stepped(grad, table_state[...])
    norm = total(step * step) * (1.0 / (169 * HEADS))
    table_grad[...] = grad
    table_state_new[...] = state
    table_new[...] = table[...] - VEC_RATE * (step * clip_scale(norm))
    for _, then in copies:
        then.wait()


def finish(*arrays):
    sd = jax.ShapeDtypeStruct
    vm = pltpu.VMEM
    dma = pltpu.SemaphoreType.DMA

    def owned(width):
        return [sd((3, width), F32), sd((3,), F32), sd((width,), F32), sd((3, width), F32), sd((3, width), BF16)]

    shard = [sd((D, D), F32), sd((D,), F32), sd((D,), F32), sd((D, D), F32), sd((D, D), BF16)]
    out_shape = owned(QKV) + owned(D) + shard + shard
    out_shape += [sd((D,), F32)] * 3 + [sd((8 * D,), F32)] * 3 + [sd((HEADS, 169), F32)] * 3 + [sd((TOK, D), F32)] * 2
    return pl.pallas_call(
        finish_kernel,
        out_shape=out_shape,
        in_specs=[pl.BlockSpec(memory_space=vm)] * 3
        + [pl.BlockSpec(memory_space=pl.ANY)] * 2
        + [pl.BlockSpec(memory_space=vm)] * (len(arrays) - 5),
        out_specs=[pl.BlockSpec(memory_space=vm)] * (len(out_shape) - 2) + [pl.BlockSpec(memory_space=pl.ANY)] * 2,
        scratch_shapes=[vm((2, TOK, D), F32), dma((2, 4)), dma((2, 4))],
        compiler_params=pltpu.CompilerParams(vmem_limit_bytes=63 * 1024 * 1024),
        name="finish",
    )(*arrays)


def clip_scale(mean_square):
    return 1.0 / jnp.maximum(1.0, jnp.sqrt(mean_square))


def per_device(
    tokens_in, out_grad, window_live, region_ids, qkv_weight, proj_weight, rel_table, small_params,
    fc1_weight, fc1_bias, fc2_weight, qkv_row, qkv_col, proj_row, proj_col, fc1_row, fc1_col,
    fc2_row, fc2_col, fc1_bias_state, small_state, table_state,
):
    out, gin, fin, pack = block(
        window_live, region_ids, tokens_in, out_grad, qkv_weight, proj_weight, fc1_weight, fc2_weight, rel_table.T,
        small_params, fc1_bias, fc1_bias_state, fc1_col, fc2_row, qkv_row, proj_row,
    )
    *outs, table_grad, table_state_new, table_new, out, gin = finish(
        fin.reshape(2, D, D), fc1_weight, fc2_weight, out, gin, pack, fc1_bias, fc1_row, fc2_col, qkv_col, proj_col,
        small_params, small_state, rel_table.T, table_state.T,
    )
    return (out, gin, *outs, table_grad.T, table_state_new.T, table_new.T)


def solution(mesh):
    tokens, owner = P(("win", "mlp"), None), P(("win", "mlp"))
    whole, part = P(), P("mlp")
    return jax.shard_map(
        per_device,
        mesh=mesh,
        in_specs=(
            tokens, tokens, owner, owner, whole, whole, whole, whole, P(None, "mlp"), part, P("mlp", None),
            whole, whole, whole, whole, whole, part, part, whole, part, whole, whole,
        ),
        out_specs=(
            tokens, tokens,
            tokens, owner, whole, tokens, tokens,
            tokens, owner, whole, tokens, tokens,
            P(None, "mlp"), whole, part, P(None, "mlp"), P(None, "mlp"),
            P("mlp", None), part, whole, P("mlp", None), P("mlp", None),
            part, part, part,
            whole, whole, whole,
            whole, whole, whole,
        ),
        check_vma=False,
    )
```

```python
import functools
import math

import jax
import jax.numpy as jnp
from jax import lax
from jax.experimental import pallas as pl
from jax.experimental.pallas import tpu as pltpu
from jax.sharding import PartitionSpec as P

D = 384
FF = 1536
QKV = 3 * D
HEADS = 12
WIN = 7
SPAN = WIN * WIN
STEP = 10
DECAY = 1.0 - STEP ** (-0.8)
EPS_NORM = 1e-05
EPS_SQ = 1e-30
VEC_RATE = 0.3
SCALE = 32 ** (-0.5)
FAR = -1e30
LOG2E = math.log2(math.e)
FACTOR = (2.0 * math.pi) ** (-0.5)

PLACE = (0, 1, 3, 2)
GROUPS = 3
PER = 8
G_TOK = PER * SPAN
G_ROWS = 400
ROWS = GROUPS * G_ROWS
TOK = GROUPS * G_TOK
CHUNK = 64
KEYS = 56
SETS = 3
LANES = 4 * CHUNK

MESH = pl.DeviceIdType.MESH
F32 = jnp.float32
BF16 = jnp.bfloat16


def dot(a, b):
    return jnp.dot(a, b, preferred_element_type=F32)


def dot_nt(a, b):
    return lax.dot_general(a, b, (((1,), (1,)), ((), ())), preferred_element_type=F32)


def dot_tn(a, b):
    return lax.dot_general(a, b, (((0,), (0,)), ((), ())), preferred_element_type=F32)


def dot_exact(a, b):
    return jnp.dot(a, b, precision=lax.Precision.HIGHEST, preferred_element_type=F32)


def iota(shape, dim):
    return lax.broadcasted_iota(jnp.int32, shape, dim)


def fold_rows(x):
    total = x[0:8]
    for i in range(1, x.shape[0] // 8):
        total = total + x[8 * i : 8 * i + 8]
    return total


def row_mean(x):
    return jnp.sum(x, axis=1, keepdims=True) * (1.0 / D)


def normalize(x):
    center = x - row_mean(x)
    inverse = lax.rsqrt(row_mean(center * center) + EPS_NORM)
    return center * inverse, inverse


def normalize_back(u, gain, scaled, inverse):
    weighted = u * gain
    return inverse * (weighted - row_mean(weighted) - scaled * row_mean(weighted * scaled))


def gelu_parts(v):
    density = jnp.exp2((v * v) * (-0.5 * LOG2E) + math.log2(FACTOR))
    t = 1.0 / (1.0 + (0.3275911 * 0.5**0.5) * jnp.abs(v))
    c = 0.5 / FACTOR
    poly = (1.061405429 * c) * t - 1.453152027 * c
    poly = poly * t + 1.421413741 * c
    poly = poly * t - 0.284496736 * c
    poly = poly * t + 0.254829592 * c
    tail = density * (poly * t)
    phi = jnp.where(v < 0.0, tail, 1.0 - tail)
    return v * phi, phi + v * density


def barrel(x, amount, right):
    width = x.shape[1]
    for k in range(7):
        step = 1 << k
        moved = pltpu.roll(x, step if right else width - step, 1)
        x = jnp.where((amount & step) != 0, moved, x)
    return x


def embed(i):
    return 13 * (i // WIN) + i % WIN


def chunk_start(w):
    return pl.multiple_of((w // PER) * G_ROWS + (w % PER) * 48, 16)


def widen(tok, x_ref):
    for a in range(GROUPS):
        for r in range(0, G_TOK, 56):
            src = a * G_TOK + r
            low = src // 16 * 16
            x_ref[a * G_ROWS + r : a * G_ROWS + r + 56, :] = (
                tok[low : low + 64 if low + 64 <= TOK else TOK, :].astype(F32)[src - low : src - low + 56]
            )
        x_ref[a * G_ROWS + G_TOK : (a + 1) * G_ROWS, :] = jnp.zeros((G_ROWS - G_TOK, D), F32)


def prologue(region, table, emask, bias, mask):
    row = iota((LANES, 128), 0)
    lane = iota((LANES, 128), 1)
    for b in range(PER):
        i = row % CHUNK
        keep = (i >= b) & (i < b + SPAN) & (lane // 32 == row // CHUNK)
        emask[b] = jnp.where(keep, 1.0, 0.0).astype(BF16)
    j = iota((KEYS, 256), 0)
    amount = jnp.maximum(84 - embed(j), 0)
    jl = iota((KEYS, LANES), 0)
    il = iota((KEYS, LANES), 1) % CHUNK
    for g in range(SETS):
        base = jnp.zeros((KEYS, LANES), F32)
        for h in range(4):
            line = jnp.concatenate([table[4 * g + h : 4 * g + h + 1, :], jnp.zeros((1, 87), F32)], axis=1)
            wide = jnp.broadcast_to(line, (KEYS, 256))
            wide = barrel(wide, amount, False)[:, :128]
            lane_to = iota((128, LANES), 1) - CHUNK * h
            pick = (iota((128, LANES), 0) == embed(lane_to)) & (lane_to >= 0) & (lane_to < SPAN)
            base = base + dot_exact(wide, jnp.where(pick, 1.0, 0.0))
        for b in range(PER):
            moved = pltpu.roll(pltpu.roll(base, b, 0), b, 1) if b else base
            key_ok = (jl >= b) & (jl < b + SPAN)
            query_ok = (il >= b) & (il < b + SPAN)
            bias[b, g] = jnp.where(key_ok, jnp.where(query_ok, moved, 0.0), FAR)
    eye = iota((CHUNK, CHUNK), 0) == iota((CHUNK, CHUNK), 1)
    region_row = jnp.concatenate([region[...].reshape(1, TOK).astype(F32), jnp.zeros((1, 104), F32)], axis=1)
    for w in range(GROUPS * PER):
        start = (w // PER) * G_TOK + (w % PER) * 48
        line = region_row[:, start : start + CHUNK]
        column = jnp.sum(jnp.where(eye, jnp.broadcast_to(line, (CHUNK, CHUNK)), 0.0), axis=1, keepdims=True)
        wide = jnp.concatenate([line] * 4, axis=1)
        mask[w] = jnp.where(column[:KEYS] != wide, -100.0, 0.0)


def pad_keys(x):
    return jnp.concatenate([x, jnp.zeros((CHUNK - KEYS, x.shape[1]), x.dtype)], axis=0)


def spread(x, keep):
    return jnp.concatenate([x] * 4, axis=0) * keep


def collect(full):
    head = iota((CHUNK, 128), 1) // 32
    parts = [full[CHUNK * h : CHUNK * (h + 1)] for h in range(4)]
    low = jnp.where(head == 0, parts[0], parts[1])
    high = jnp.where(head == 2, parts[2], parts[3])
    return jnp.where(head < 2, low, high)


def packed(ref):
    at, views = 0, []
    for rows in (24, 16, 16, 32, 24, 8, 32, 16):
        views.append(ref.at[at : at + rows])
        at += rows
    return views


def block_kernel(
    live_windows, region, tok_in, og_in, wq_in, wp_in, fc1_in, fc2_in, table, small,
    fc1_b, fc1_state, fc1_col, fc2_row, qkv_row, proj_row,
    out_to, gin_to, fin_to, pack,
    x_ref, xh1, inv1, inv2, n1, n2, qkv, att_b, probs, back, hidden, ig, dqkv,
    emask, bias, mask, tacc, s1, s2, sums, b1_acc, wq_b, wp_b, w1, w2, tok, og, wq, wp, fc1, fc2, fin, fin_b, b1, stage, in_sem, out_sem,
    fcl, fr1, fr2, ft, fr3, fr4, fst, atl, ar1, ar2, ar3, ar4, ast, vx, vy, at_total,
    w_send, w_recv, b_send, b_recv, pair_send, pair_recv, f1s, f1r, f2s, f2r, f3s, f3r, f4s, f4r, f5s, f5r, f7s, f7r, f8s, f8r,
    a1s, a1r, a2s, a2r, a3s, a3r, a4s, a4r, a5s, a5r, vxs, vxr, vys, vyr,
):
    win, mlp = lax.axis_index("win"), lax.axis_index("mlp")
    vec, fc_sums, at_sums, own_g, own_wq, own_wp, b1_all, own_r = packed(pack)
    z, y, core = win // 8, (win // 2) % 4, win % 2
    pair = win + 1 - 2 * core

    def along_x(d):
        return win, (mlp + d) % 4

    def along_y(d):
        return z * 8 + ((y + d) % 4) * 2 + core, mlp

    def along_z(d):
        return ((z + d) % 4) * 8 + y * 2 + core, mlp

    def plane_peer(d):
        return ((z + d // 4) % 4) * 8 + ((y + d % 4) % 4) * 2 + core, mlp

    def class_peer(d):
        return pair if d >= 4 else win, (mlp + d) % 4

    loads = [
        pltpu.make_async_copy(src, dst, in_sem.at[n])
        for n, (src, dst) in enumerate(
            ((fc1_in, fc1), (fc2_in, fc2), (tok_in, tok), (wq_in, wq), (og_in, og), (wp_in, wp))
        )
    ]
    for copy in loads:
        copy.start()
    barrier = pltpu.get_barrier_semaphore()
    peers = [class_peer(d) for d in range(1, 8)]
    peers += [plane_peer(d) for d in range(1, 16)]
    for peer in peers:
        pl.semaphore_signal(barrier, inc=1, device_id=peer, device_id_type=MESH)

    def remote(src, dst, send, recv, peer):
        return pltpu.make_async_remote_copy(
            src_ref=src, dst_ref=dst, send_sem=send, recv_sem=recv, device_id=peer, device_id_type=MESH
        )

    def param(part):
        return small[D * part : D * part + D].reshape(1, D)

    pending = []

    def start(copy):
        copy.start()
        pending.append(copy)
        return copy

    def shard(place):
        half = pl.ds(pl.multiple_of(core * (D // 2), 16), D // 2)
        half_at = pl.ds(pl.multiple_of(place * D + core * (D // 2), 16), D // 2)
        return w1.at[half, D * place : D * place + D], w2.at[half_at, :]

    def near(d, n):
        return remote(shard(0)[n], shard(PLACE[4 - d])[n], w_send.at[d // 2, n], w_recv.at[d // 2, n], along_x(d))

    def far(n):
        d = 3 - 2 * n
        return remote(shard(1 + n)[n], shard(3)[n], w_send.at[2, n], w_recv.at[2, n], along_x(d))

    def bias_copy(d):
        return remote(b1.at[0], b1.at[PLACE[4 - d]], b_send.at[d - 1], b_recv.at[d - 1], along_x(d))

    def across(place, n):
        came = shard(place)[n]
        return remote(came, came, pair_send.at[place - 1, n], pair_recv.at[place - 1, n], (pair, mlp))

    for copy in loads[:2]:
        copy.wait()
    w1[:, :D] = fc1[...].astype(BF16)
    w2[:D, :] = fc2[...].astype(BF16)
    b1[0, 0:4] = jnp.broadcast_to(fc1_b[...].reshape(1, D), (4, D))
    b1[0, 4:8] = jnp.broadcast_to(fc1_state[...].reshape(1, D), (4, D))
    pl.semaphore_wait(barrier, 22)
    for n in range(2):
        for d in (1, 3):
            start(near(d, n))
    for d in range(1, 4):
        start(bias_copy(d))

    live = live_windows[0]
    for n in range(1, GROUPS * PER):
        live = live + live_windows[n]
    live = live * SPAN
    prologue(region, table, emask, bias, mask)
    for copy in loads[2:]:
        copy.wait()
    widen(tok, x_ref)
    for g in range(SETS):
        for part in range(3):
            wq_b[:, D * g + 128 * part : D * g + 128 * part + 128] = wq[
                :, D * part + 128 * g : D * part + 128 * g + 128
            ].astype(BF16)
    wp_b[...] = wp[...].astype(BF16)
    sums[...] = jnp.zeros_like(sums)
    b1_acc[...] = jnp.zeros_like(b1_acc)
    tacc[...] = jnp.zeros_like(tacc)
    att = dqkv.at[:, :D]
    xh2 = dqkv.at[:, D : 2 * D]
    dqkv_b = ig.at[:, :QKV]
    dqkv[:, :D] = jnp.zeros((ROWS, D), F32)

    for a in range(GROUPS):
        for r in range(0, G_TOK, 56):
            src = a * G_TOK + r
            low = src // 16 * 16
            rows = og[low : low + 64 if low + 64 <= TOK else TOK, :].astype(F32)[src - low : src - low + 56]
            keep = iota((56, D), 0) + src < live
            x = jnp.where(keep, rows, 0.0)
            s2[r : r + 56, :] = x
            sums[7] += fold_rows(x)
        s2[G_TOK:G_ROWS, :] = jnp.zeros((G_ROWS - G_TOK, D), F32)
        back[a * G_ROWS : (a + 1) * G_ROWS, :] = s2[...].astype(BF16)

    shift_q = jnp.concatenate(
        [
            part[:, 128 * g : 128 * g + 128]
            for g in range(SETS)
            for part in (param(2), jnp.zeros((1, D), F32), param(3))
        ],
        axis=1,
    )

    @pl.loop(0, 5, unroll=5)
    def _(t):
        for c in range(15):
            rows = pl.ds(pl.multiple_of(t * 240 + c * 16, 16), 16)
            scaled, inverse = normalize(x_ref[rows, :])
            xh1[rows, :] = scaled
            inv1[rows, :] = inverse
            n1[rows, :] = (scaled * param(0) + param(1)).astype(BF16)

    @pl.loop(0, 5, unroll=5)
    def _(t):
        rows = pl.ds(pl.multiple_of(t * 240, 16), 240)
        qkv[rows, :] = (dot(n1[rows, :], wq_b[...]) + shift_q).astype(BF16)

    def scores_of(a, b, g):
        rows = pl.ds(pl.multiple_of(a * G_ROWS + b * 48, 16), CHUNK)
        q = qkv[rows, D * g : D * g + 128]
        k = qkv[rows, D * g + 128 : D * g + 256]
        return dot_nt(k, spread(q, emask[b]))

    def attend(a, b, g, raw):
        rows = pl.ds(pl.multiple_of(a * G_ROWS + b * 48, 16), CHUNK)
        v = qkv[rows, D * g + 256 : D * g + 384]
        scores = raw[:KEYS] * SCALE + (bias[b, g] + mask[a * PER + b])
        p = jnp.exp(scores - jnp.max(scores, axis=0, keepdims=True))
        p = p * (1.0 / jnp.sum(p, axis=0, keepdims=True))
        probs[a * PER + b, g] = p
        return dot_tn(pad_keys(p).astype(BF16), v)

    def attended(a, b, g, full):
        rows = pl.ds(pl.multiple_of(a * G_ROWS + b * 48, 16), CHUNK)
        i = iota((CHUNK, 128), 0)
        att[rows, 128 * g : 128 * g + 128] += jnp.where((i >= b) & (i < b + SPAN), collect(full), 0.0)

    @pl.loop(0, 4)
    def _(pair_at):
        blocks = [[(a, 2 * pair_at + b, g) for a in range(GROUPS)] for b in range(2) for g in range(SETS)]
        ahead = [scores_of(*unit) for unit in blocks[0]]
        for n, units in enumerate(blocks):
            raws = ahead
            if n + 1 < len(blocks):
                ahead = [scores_of(*unit) for unit in blocks[n + 1]]
            fulls = [attend(*unit, raw) for unit, raw in zip(units, raws)]
            for unit, full in zip(units, fulls):
                attended(*unit, full)

    for n in range(2):
        for d in (1, 3):
            near(d, n).wait_recv()
        start(far(n))
    for place in (1, 2):
        for n in range(2):
            start(across(place, n))
    for d in range(1, 4):
        bias_copy(d).wait_recv()

    @pl.loop(0, GROUPS, unroll=3)
    def _(a):
        rows = pl.ds(pl.multiple_of(a * G_ROWS, 16), G_ROWS)
        att_b[rows, :] = att[rows, :].astype(BF16)
        s1[...] = dot(att_b[rows, :], wp_b[...])

        for c in range(25):
            here = pl.ds(pl.multiple_of(a * G_ROWS + 16 * c, 16), 16)
            middle = x_ref[here, :] + (s1[16 * c : 16 * c + 16, :] + param(4))
            stage[here, :] = middle
            scaled, inverse = normalize(middle)
            xh2[here, :] = scaled
            inv2[here, :] = inverse
            n2[here, :] = (scaled * param(5) + param(6)).astype(BF16)

    for nt in range(6):
        if nt in (1, 3):
            for n in range(2):
                across(1 + nt // 2, n).wait_recv()
        if nt == 3:
            for n in range(2):
                far(n).wait_recv()
                start(across(3, n))
        if nt == 4:
            for n in range(2):
                across(3, n).wait_recv()
        cols = slice(256 * nt, 256 * nt + 256)
        shift = jnp.concatenate(
            [b1[c // 3, 0:1, 128 * (c % 3) : 128 * (c % 3) + 128] for c in (2 * nt, 2 * nt + 1)], axis=1
        )

        @pl.loop(0, 5)
        def _(mt):
            rows = pl.ds(pl.multiple_of(mt * 240, 16), 240)
            inner = dot(n2[rows, :], w1[:, cols]) + shift
            up = dot_nt(back[rows, :], w2[cols, :])
            total = b1_acc[:, cols]
            for c in range(15):
                act, slope = gelu_parts(inner[16 * c : 16 * c + 16])
                here = pl.ds(pl.multiple_of(mt * 240 + 16 * c, 16), 16)
                hidden[here, cols] = act.astype(BF16)
                grad = (up[16 * c : 16 * c + 16] * slope).astype(BF16)
                ig[here, cols] = grad
                total = total + fold_rows(grad.astype(F32))
            b1_acc[:, cols] = total

    g2 = dot_tn(hidden[...], back[...]).astype(BF16)
    g1 = dot_tn(n2[...], ig[...]).astype(BF16)
    for m in range(4):
        fcl[0, m] = g1[:, D * m : D * m + D].reshape(4, 96, D)
        fcl[1, m] = g2[D * m : D * m + D].reshape(4, 96, D)
    fc_one = [start(remote(fcl.at[1 - core, m], fr1.at[m], f1s.at[m], f1r.at[m], (pair, mlp))) for m in range(4)]

    def middle_back(a):
        rows = slice(a * G_ROWS, (a + 1) * G_ROWS)
        held = (s1, s2)[a % 2]
        held[...] = dot_nt(ig[rows, :], w1[...])
        for c in range(25):
            here = slice(16 * c, 16 * c + 16)
            at = slice(a * G_ROWS + 16 * c, a * G_ROWS + 16 * c + 16)
            u = held[here, :]
            scaled = xh2[at, :]
            sums[5] += fold_rows(u * scaled)
            sums[6] += fold_rows(u)
            mg = normalize_back(u, param(5), scaled, inv2[at, :]) + back[at, :].astype(F32)
            x_ref[at, :] = mg
            low = mg.astype(BF16)
            n2[at, :] = low
            sums[4] += fold_rows(low.astype(F32))

    def out_copy(a):
        return pltpu.make_async_copy(
            stage.at[pl.ds(a * G_ROWS, G_TOK)], out_to.at[pl.ds(a * G_TOK, G_TOK)], out_sem.at[a]
        )

    def block_out(a):
        rows = slice(a * G_ROWS, (a + 1) * G_ROWS)
        held = (s1, s2)[a % 2]
        held[...] = dot(hidden[rows, :], w2[...])
        for c in range(25):
            at = slice(a * G_ROWS + 16 * c, a * G_ROWS + 16 * c + 16)
            r = stage[at, :] + (held[16 * c : 16 * c + 16, :] + param(7))
            keep = iota((16, D), 0) + (a * G_TOK + 16 * c) < live
            stage[at, :] = jnp.where(keep, r, 0.0)
        out_copy(a).start()

    p = iota((D, D), 0)
    inner_p = p % 48
    owned = 24 * (inner_p // 3) + 12 * (p // 192) + 3 * ((p // 48) % 4) + inner_p % 3
    order = jnp.where(iota((D, D), 1) == owned, 1.0, 0.0).astype(BF16)

    def ordered(grad):
        return dot(order, grad.astype(BF16)).astype(BF16).reshape(2, 4, 48, D)

    def at_one(n):
        return remote(atl.at[n, 1 - core], ar1.at[n], a1s.at[n], a1r.at[n], (pair, mlp))

    def at_add_one(n):
        at_one(n).wait_recv()
        for i in range(4):
            ar1[n, i] = (ar1[n, i].astype(F32) + atl[n, core, i].astype(F32)).astype(BF16)
        for d in range(1, 4):
            start(remote(ar1.at[n, (mlp + d) % 4], ar2.at[n, d - 1], a2s.at[n, d - 1], a2r.at[n, d - 1], along_x(d)))

    def near_axis(d):
        return ((z + d * core) % 4) * 8 + ((y + d * (1 - core)) % 4) * 2 + core, mlp

    def other_axis(d):
        return ((z + d * (1 - core)) % 4) * 8 + ((y + d * core) % 4) * 2 + core, mlp

    near_at, other_at = y * (1 - core) + z * core, z * (1 - core) + y * core

    def at_add_two(n):
        total = ar1[n, mlp].astype(F32)
        for d in range(1, 4):
            remote(ar1.at[n, 0], ar2.at[n, d - 1], a2s.at[n, d - 1], a2r.at[n, d - 1], along_x(d)).wait_recv()
            total = total + ar2[n, d - 1].astype(F32)
        ar3[n, near_at] = total.astype(BF16)
        for d in range(1, 4):
            start(remote(ar3.at[n, near_at], ar3.at[n, near_at], a3s.at[n, d - 1], a3r.at[n, d - 1], near_axis(d)))

    def at_add_three(n):
        for d in range(1, 4):
            came = ar3.at[n, (near_at + 4 - d) % 4]
            remote(came, came, a3s.at[n, d - 1], a3r.at[n, d - 1], near_axis(d)).wait_recv()
        total = ar3[n, 0].astype(F32) + ar3[n, 1].astype(F32)
        ar4[n, other_at] = (total + ar3[n, 2].astype(F32) + ar3[n, 3].astype(F32)).astype(BF16)
        for d in range(1, 4):
            start(remote(ar4.at[n, other_at], ar4.at[n, other_at], a4s.at[n, d - 1], a4r.at[n, d - 1], other_axis(d)))

    def at_finish(n):
        for d in range(1, 4):
            came = ar4.at[n, (other_at + 4 - d) % 4]
            remote(came, came, a4s.at[n, d - 1], a4r.at[n, d - 1], other_axis(d)).wait_recv()
        total = ar4[n, 0].astype(F32) + ar4[n, 1].astype(F32)
        at_total[n] = total + ar4[n, 2].astype(F32) + ar4[n, 3].astype(F32)

    def to_axes(dx, dy, dz):
        return ((z + dz) % 4) * 8 + ((y + dy) % 4) * 2 + core, (mlp + dx) % 4

    def first_axis(d):
        return to_axes(d * (1 - core), 0, d * core)

    def second_axis(d):
        return to_axes(d * core, d * (1 - core), 0)

    def third_axis(d):
        return to_axes(0, d * core, d * (1 - core))

    def last_axis(d):
        return to_axes(0, d * (1 - core), d * core)

    block_at = y * (1 - core) + z * core
    second = y * (1 - core)
    third = z * (1 - core) + y * core

    def fc_two(d):
        return remote(fr1.at[0], fr2.at[d - 1], f2s.at[d - 1], f2r.at[d - 1], first_axis(d))

    def fc_add_one():
        for m in range(4):
            fc_one[m].wait_recv()
            for i in range(4):
                fr1[m, i] = (fr1[m, i].astype(F32) + fcl[core, m, i].astype(F32)).astype(BF16)

        @pl.when(core == 0)
        def _():
            for d in range(1, 4):
                remote(fr1.at[PLACE[d]], fr2.at[d - 1], f2s.at[d - 1], f2r.at[d - 1], first_axis(d)).start()

        @pl.when(core == 1)
        def _():
            for d in range(1, 4):
                remote(fr1.at[:, (z + d) % 4], fr2.at[d - 1], f2s.at[d - 1], f2r.at[d - 1], first_axis(d)).start()

    def fc_add_two():
        for d in range(1, 4):
            fc_two(d).wait_recv()
        for i in range(4):
            total = fr1[i * core, i * (1 - core) + z * core].astype(F32)
            for d in range(1, 4):
                total = total + fr2[d - 1, i].astype(F32)
            ft[i] = total.astype(BF16)
        for d in range(1, 4):
            to = (1 - core) * ((y + d) % 4) + core * PLACE[d]
            start(remote(ft.at[to], fr3.at[d - 1], f3s.at[d - 1], f3r.at[d - 1], second_axis(d)))

    def fc_add_three():
        total = ft[second].astype(F32)
        for d in range(1, 4):
            remote(ft.at[0], fr3.at[d - 1], f3s.at[d - 1], f3r.at[d - 1], second_axis(d)).wait_recv()
            total = total + fr3[d - 1].astype(F32)
        fr4[third] = total.astype(BF16)
        for d in range(1, 4):
            start(remote(fr4.at[third], fr4.at[third], f4s.at[d - 1], f4r.at[d - 1], third_axis(d)))

    def fc_add_four():
        for d in range(1, 4):
            came = fr4.at[(third + 4 - d) % 4]
            remote(came, came, f4s.at[d - 1], f4r.at[d - 1], third_axis(d)).wait_recv()
        total = fr4[0].astype(F32) + fr4[1].astype(F32)
        fin_b[core, block_at] = (total + fr4[2].astype(F32) + fr4[3].astype(F32)).astype(BF16)
        for d in range(1, 4):
            place = fin_b.at[core, block_at]
            start(remote(place, place, f5s.at[d - 1], f5r.at[d - 1], last_axis(d)))

    def fc_spread():
        for d in range(1, 4):
            place = fin_b.at[core, (block_at + 4 - d) % 4]
            remote(place, place, f5s.at[d - 1], f5r.at[d - 1], last_axis(d)).wait_recv()
        start(remote(fin_b.at[core], fin_b.at[core], f7s.at[0], f7r.at[0], (pair, mlp)))

    mine_at, plane_at = 4 * core + mlp, 4 * z + y

    def vec_one(n):
        for d in range(1, 8):
            place = vx.at[n, mine_at]
            start(remote(place, place, vxs.at[n, d - 1], vxr.at[n, d - 1], class_peer(d)))

    def vec_two(n):
        for d in range(1, 8):
            place = vx.at[n, (mlp + 8 - d) % 4 + 4 * (core if d < 4 else 1 - core)]
            remote(place, place, vxs.at[n, d - 1], vxr.at[n, d - 1], class_peer(d)).wait_recv()
        total = vx[n, 0]
        for i in range(1, 8):
            total = total + vx[n, i]
        vy[n, plane_at] = total
        for d in range(1, 16):
            place = vy.at[n, plane_at]
            start(remote(place, place, vys.at[n, d - 1], vyr.at[n, d - 1], plane_peer(d)))

    def vec_three(n):
        for d in range(1, 16):
            place = vy.at[n, 4 * ((z + 4 - d // 4) % 4) + (y + 4 - d % 4) % 4]
            remote(place, place, vys.at[n, d - 1], vyr.at[n, d - 1], plane_peer(d)).wait_recv()
        total = vy[n, 0]
        for i in range(1, 16):
            total = total + vy[n, i]
        vec[8 * n : 8 * n + 8, :] = total

    middle_back(0)
    middle_back(1)
    fc_add_one()
    middle_back(2)

    atl[3] = ordered(dot_tn(att_b[...], n2[...]))
    start(at_one(3))

    @pl.loop(0, GROUPS, unroll=3)
    def _(a):
        rows = pl.ds(pl.multiple_of(a * G_ROWS, 16), G_ROWS)
        att_b[rows, :] = dot_nt(n2[rows, :], wp_b[...]).astype(BF16)

    dqkv[...] = jnp.zeros_like(dqkv)

    def attention_back(g, half):
        def first(a, b):
            rows = pl.ds(a * G_ROWS + b * 48, CHUNK)
            v = qkv[rows, D * g + 256 : D * g + 384]
            da = spread(att_b[rows, 128 * g : 128 * g + 128], emask[b])
            return da, dot_nt(v, da)

        def inner_grad(a, b, dp):
            p = probs[a * PER + b, g]
            pd = p * dp[:KEYS]
            return pad_keys(p).astype(BF16), pad_keys(pd - p * jnp.sum(pd, axis=0, keepdims=True)).astype(BF16)

        def last(a, b, da, p, ds):
            rows = pl.ds(a * G_ROWS + b * 48, CHUNK)
            q = qkv[rows, D * g : D * g + 128]
            k = qkv[rows, D * g + 128 : D * g + 256]
            dv = dot(p, da)
            dk = dot(ds, spread(q, emask[b])) * SCALE
            dq = collect(dot_tn(ds, k)) * SCALE
            dqkv[rows, 384 * g : 384 * g + 128] += dq
            dqkv[rows, 384 * g + 128 : 384 * g + 256] += dk
            dqkv[rows, 384 * g + 256 : 384 * g + 384] += dv

        bs = range(4 * half, 4 * half + 4)
        ahead = [first(a, bs[0]) for a in range(GROUPS)]
        for b in bs:
            held = ahead
            if b + 1 in bs:
                ahead = [first(a, b + 1) for a in range(GROUPS)]
            grads = [inner_grad(a, b, held[a][1]) for a in range(GROUPS)]
            tacc[b, g] = sum(ds.astype(F32)[:KEYS] for _, ds in grads)
            for a in range(GROUPS):
                last(a, b, held[a][0], *grads[a])

    def qkv_grad(g):
        group = slice(384 * g, 384 * g + 384)

        @pl.loop(0, 5, unroll=5)
        def _(t):
            for c in range(15):
                rows = pl.ds(pl.multiple_of(t * 240 + c * 16, 16), 16)
                low = dqkv[rows, group].astype(BF16)
                dqkv_b[rows, group] = low
                wide = low.astype(F32)
                sums[2, :, 128 * g : 128 * g + 128] += fold_rows(wide[:, :128])
                sums[3, :, 128 * g : 128 * g + 128] += fold_rows(wide[:, 256:])

        atl[g] = ordered(dot_tn(n1[...], dqkv_b[:, group]))
        start(at_one(g))

    for part in range(4):
        vx[0, mine_at, part : part + 1, :] = jnp.sum(sums[4 + part], axis=0, keepdims=True)
    for m in range(4):
        d = (m + 4 - mlp) % 4
        place = d + d // 2 - 2 * (d // 3)
        cols = pl.ds(pl.multiple_of(place * D, 128), D)
        vx[0, mine_at, 4 + m : 5 + m, :] = jnp.sum(b1_acc[:, cols], axis=0, keepdims=True)
    vec_one(0)

    def table_back(g, n):
        j = iota((KEYS, 256), 0)
        amount = jnp.maximum(84 - embed(j), 0)
        total = tacc[0, g]
        for b in range(1, PER):
            total = total + pltpu.roll(pltpu.roll(tacc[b, g], KEYS - b, 0), LANES - b, 1)
        for h in range(4):
            lane_from = iota((LANES, 256), 0) - CHUNK * h
            pick = (iota((LANES, 256), 1) == embed(lane_from)) & (lane_from >= 0) & (lane_from < SPAN)
            wide = barrel(dot_exact(total, jnp.where(pick, 1.0, 0.0)), amount, True)
            wide = jnp.where(j < SPAN, wide, 0.0)
            vx[n, mine_at, 4 * (g % 2) + h : 4 * (g % 2) + h + 1, :] = jnp.concatenate(
                [jnp.sum(wide, axis=0, keepdims=True), jnp.zeros((1, 128), F32)], axis=1
            )

    attention_back(0, 0)
    attention_back(0, 1)
    qkv_grad(0)
    attention_back(1, 0)
    attention_back(1, 1)
    fc_add_two()
    qkv_grad(1)
    at_add_one(3)
    at_add_one(0)
    vec_two(0)
    attention_back(2, 0)
    at_add_one(1)
    attention_back(2, 1)
    qkv_grad(2)
    fc_add_three()
    at_add_one(2)

    def gin_copy(a):
        src = pl.ds(pl.multiple_of(a * G_ROWS, 8), G_TOK)
        dst = pl.ds(pl.multiple_of(a * G_TOK, 8), G_TOK)
        return pltpu.make_async_copy(x_ref.at[src], gin_to.at[dst], out_sem.at[3 + a])

    @pl.loop(0, GROUPS)
    def _(a):
        rows = pl.ds(pl.multiple_of(a * G_ROWS, 16), G_ROWS)
        s2[...] = dot_nt(dqkv_b[rows, :], wq_b[...])
        for c in range(25):
            here = slice(16 * c, 16 * c + 16)
            at = pl.ds(pl.multiple_of(a * G_ROWS + 16 * c, 16), 16)
            u = s2[here, :]
            scaled = xh1[at, :]
            sums[0] += fold_rows(u * scaled)
            sums[1] += fold_rows(u)
            x_ref[at, :] = normalize_back(u, param(0), scaled, inv1[at, :]) + x_ref[at, :]
        gin_copy(a).start()

    at_add_two(3)
    at_add_two(0)
    table_back(0, 1)
    table_back(1, 1)
    vec_one(1)
    at_add_two(1)
    table_back(2, 2)
    for part in range(4):
        vx[2, mine_at, 4 + part : 5 + part, :] = jnp.sum(sums[part], axis=0, keepdims=True)
    vec_one(2)
    vec_three(0)
    fc_add_four()
    at_add_two(2)
    block_out(0)
    block_out(1)
    at_add_three(3)
    at_add_three(0)
    block_out(2)
    at_add_three(1)
    vec_two(1)
    vec_two(2)
    at_add_three(2)
    fc_spread()
    at_finish(3)
    at_finish(0)
    at_finish(1)

    remote(fin_b.at[1 - core], fin_b.at[1 - core], f7s.at[0], f7r.at[0], (pair, mlp)).wait_recv()
    for half in range(2):
        for n in range(4):
            fin[half, n] = fin_b[half, n].astype(F32)
    fin_copy = pltpu.make_async_copy(fin, fin_to, out_sem.at[6])
    fin_copy.start()
    eye = iota((D, D), 0) == iota((D, D), 1)

    def to_row(column):
        return jnp.sum(jnp.where(eye, column, 0.0), axis=0, keepdims=True)

    up = fin[0].reshape(D, D)
    down = fin[1].reshape(D, D)
    up_squares = up * up
    down_squares = down * down
    up_col = DECAY * fc1_col[...].reshape(1, D) + (1.0 - DECAY) * (
        jnp.sum(up_squares, axis=0, keepdims=True) * (1.0 / D) + EPS_SQ
    )
    down_row = DECAY * to_column(fc2_row[...].reshape(1, D), eye) + (1.0 - DECAY) * (row_mean(down_squares) + EPS_SQ)
    fst[mlp, 0:1] = to_row(jnp.sum(up_squares, axis=1, keepdims=True))
    fst[mlp, 1:2] = to_row(jnp.sum(up_squares * (1.0 / up_col), axis=1, keepdims=True))
    fst[mlp, 2:3] = jnp.sum(down_squares, axis=0, keepdims=True)
    fst[mlp, 3:4] = jnp.sum(down_squares * (1.0 / down_row), axis=0, keepdims=True)
    fst[mlp, 4:5] = jnp.broadcast_to(jnp.sum(down_row, axis=0, keepdims=True), (1, D))
    fst[mlp, 5:6] = up_col
    fst[mlp, 6:7] = to_row(down_row)
    fst[mlp, 7:8] = jnp.zeros((1, D), F32)
    for d in range(1, 4):
        start(remote(fst.at[mlp], fst.at[mlp], f8s.at[d - 1], f8r.at[d - 1], along_x(d)))

    vec_three(1)

    offset = 48 - 3 * plane_at
    block_rows = pl.ds(pl.multiple_of(24 * (win // 2), 8), 24)
    shift = 24 - 3 * mine_at
    rolled = pltpu.roll(wq[block_rows, :], shift, 0)[:8]
    for part in range(3):
        own_wq[8 * part : 8 * part + 8, :] = rolled[:, D * part : D * part + D]
    own_wp[...] = pltpu.roll(wp[block_rows, :], shift, 0)[:8]

    r48 = iota((48, D), 0)
    pick = iota((48, D), 1) == 24 * (r48 // 3) + 12 * core + 3 * mlp + r48 % 3

    def rows_new(state, mean):
        old = jnp.sum(jnp.where(pick, state, 0.0), axis=1, keepdims=True)
        return DECAY * old + (1.0 - DECAY) * (mean + EPS_SQ)

    at_finish(2)
    squares = [at_total[n] * at_total[n] for n in range(4)]
    qkv_new_row = rows_new(
        qkv_row[...].reshape(1, D), row_mean(squares[0] + squares[1] + squares[2]) * (1.0 / 3.0)
    )
    proj_new_row = rows_new(proj_row[...].reshape(1, D), row_mean(squares[3]))
    for n in range(4):
        over = squares[n] * (1.0 / (qkv_new_row if n < 3 else proj_new_row))
        ast[mine_at, n : n + 1] = jnp.sum(squares[n], axis=0, keepdims=True)
        ast[mine_at, 4 + n : 5 + n] = jnp.sum(over, axis=0, keepdims=True)
    ast[mine_at, 8:9] = jnp.broadcast_to(jnp.sum(qkv_new_row, axis=0, keepdims=True), (1, D))
    ast[mine_at, 9:10] = jnp.broadcast_to(jnp.sum(proj_new_row, axis=0, keepdims=True), (1, D))
    ast[mine_at, 10:16] = jnp.zeros((6, D), F32)

    def at_five(d):
        place = ast.at[mine_at]
        return remote(place, place, a5s.at[d - 1], a5r.at[d - 1], class_peer(d))

    for d in range(1, 8):
        start(at_five(d))

    for n in range(4):
        own_g[8 * n : 8 * n + 8, :] = pltpu.roll(at_total[n], offset, 0)[:8]
        b1_all[8 * n : 8 * n + 8, :] = b1[n]
    own_r[0:8, :] = pltpu.roll(jnp.broadcast_to(qkv_new_row, (48, D)), offset, 0)[:8]
    own_r[8:16, :] = pltpu.roll(jnp.broadcast_to(proj_new_row, (48, D)), offset, 0)[:8]

    for d in range(1, 4):
        place = fst.at[(mlp + 4 - d) % 4]
        remote(place, place, f8s.at[d - 1], f8r.at[d - 1], along_x(d)).wait_recv()
    fc_sums[0:8, :] = (fst[0] + fst[1]) + (fst[2] + fst[3])
    fc_sums[8:16, :] = fst[mlp]
    vec_three(2)

    for d in range(1, 8):
        place = ast.at[(mlp + 8 - d) % 4 + 4 * (core if d < 4 else 1 - core)]
        remote(place, place, a5s.at[d - 1], a5r.at[d - 1], class_peer(d)).wait_recv()
    total = ast[0]
    for n in range(1, 8):
        total = total + ast[n]
    at_sums[...] = total

    for a in range(GROUPS):
        gin_copy(a).wait()
        out_copy(a).wait()
    fin_copy.wait()
    for copy in pending:
        copy.wait_send()
    for d in range(1, 4):
        fc_two(d).wait_send()


def to_column(row, eye):
    return jnp.sum(jnp.where(eye, row, 0.0), axis=1, keepdims=True)


def block(live_windows, region, tok, og, wq, wp, fc1, fc2, *arrays):
    sd = jax.ShapeDtypeStruct
    vm = pltpu.VMEM
    dma = pltpu.SemaphoreType.DMA
    return pl.pallas_call(
        block_kernel,
        out_shape=[
            sd((TOK, D), F32),
            sd((TOK, D), F32),
            sd((2, 4, 96, D), F32),
            sd((168, D), F32),
        ],
        in_specs=[pl.BlockSpec(memory_space=pltpu.SMEM), pl.BlockSpec(memory_space=vm)]
        + [pl.BlockSpec(memory_space=pl.ANY)] * 6
        + [pl.BlockSpec(memory_space=vm)] * len(arrays),
        out_specs=[pl.BlockSpec(memory_space=pl.ANY)] * 3 + [pl.BlockSpec(memory_space=vm)],
        scratch_shapes=[
            vm((ROWS, D), F32),
            vm((ROWS, D), F32),
            vm((ROWS, 1), F32),
            vm((ROWS, 1), F32),
            vm((ROWS, D), BF16),
            vm((ROWS, D), BF16),
            vm((ROWS, QKV), BF16),
            vm((ROWS, D), BF16),
            vm((GROUPS * PER, SETS, KEYS, LANES), F32),
            vm((ROWS, D), BF16),
            vm((ROWS, FF), BF16),
            vm((ROWS, FF), BF16),
            vm((ROWS, QKV), F32),
            vm((PER, LANES, 128), BF16),
            vm((PER, SETS, KEYS, LANES), F32),
            vm((GROUPS * PER, KEYS, LANES), F32),
            vm((PER, SETS, KEYS, LANES), F32),
            vm((G_ROWS, D), F32),
            vm((G_ROWS, D), F32),
            vm((8, 8, D), F32),
            vm((8, FF), F32),
            vm((D, QKV), BF16),
            vm((D, D), BF16),
            vm((D, FF), BF16),
            vm((FF, D), BF16),
            vm((TOK, D), BF16),
            vm((TOK, D), BF16),
            vm((D, QKV), F32),
            vm((D, D), F32),
            vm((D, D), F32),
            vm((D, D), F32),
            vm((2, 4, 96, D), F32),
            vm((2, 4, 96, D), BF16),
            vm((4, 8, D), F32),
            vm((ROWS, D), F32),
            dma((6,)), dma((7,)),
            vm((2, 4, 4, 96, D), BF16),
            vm((4, 4, 96, D), BF16),
            vm((3, 4, 96, D), BF16),
            vm((4, 96, D), BF16),
            vm((3, 96, D), BF16),
            vm((4, 96, D), BF16),
            vm((4, 8, D), F32),
            vm((4, 2, 4, 48, D), BF16),
            vm((4, 4, 48, D), BF16),
            vm((4, 3, 48, D), BF16),
            vm((4, 4, 48, D), BF16),
            vm((4, 4, 48, D), BF16),
            vm((8, 16, D), F32),
            vm((3, 8, 8, D), F32),
            vm((3, 16, 8, D), F32),
            vm((4, 48, D), F32),
            dma((3, 2)), dma((3, 2)), dma((3,)), dma((3,)), dma((3, 2)), dma((3, 2)),
            dma((4,)), dma((4,)),
            dma((3,)), dma((3,)), dma((3,)), dma((3,)), dma((3,)), dma((3,)),
            dma((3,)), dma((3,)), dma((1,)), dma((1,)), dma((3,)), dma((3,)),
            dma((4,)), dma((4,)),
            dma((4, 3)), dma((4, 3)), dma((4, 3)), dma((4, 3)), dma((4, 3)), dma((4, 3)),
            dma((7,)), dma((7,)),
            dma((3, 7)), dma((3, 7)), dma((3, 15)), dma((3, 15)),
        ],
        compiler_params=pltpu.CompilerParams(
            vmem_limit_bytes=63 * 1024 * 1024, collective_id=0, has_side_effects=True
        ),
        cost_estimate=pl.CostEstimate(flops=14_000_000_000, bytes_accessed=20_000_000, transcendentals=3_000_000),
        name="block",
    )(live_windows, region, tok, og, wq, wp, fc1, fc2, *arrays)


def finish_kernel(
    fin, fc1, fc2, out_from, gin_from, pack, fc1_b, fc1_row, fc2_col, qkv_col, proj_col,
    small, small_state, table, table_state,
    qkv_grad, qkv_row_new, qkv_col_new, qkv_new, qkv_low, proj_grad, proj_row_new, proj_col_new, proj_new, proj_low,
    fc1_grad, fc1_row_new, fc1_col_new, fc1_new, fc1_low, fc2_grad, fc2_row_new, fc2_col_new, fc2_new, fc2_low,
    b1_grad, b1_state_new, b1_new, small_grad, small_state_new, small_new, table_grad, table_state_new, table_new,
    out_to, gin_to, held, sem_in, sem_out,
):
    vec, fc_sums, at_sums, own_g, own_wq, own_wp, b1, own_r = packed(pack)
    def parts(src, dst, n):
        for i in range(4):
            rows = pl.ds(304 * i, 304 if i < 3 else TOK - 912)
            here = held.at[n, rows]
            yield (
                pltpu.make_async_copy(src.at[rows], here, sem_in.at[n, i]),
                pltpu.make_async_copy(here, dst.at[rows], sem_out.at[n, i]),
            )

    copies = list(parts(out_from, out_to, 0)) + list(parts(gin_from, gin_to, 1))
    for copy, _ in copies:
        copy.start()
    mlp = lax.axis_index("mlp")
    eye = iota((D, D), 0) == iota((D, D), 1)
    eye8 = iota((8, 128), 0) == iota((8, 128), 1)

    def line(x):
        return x.reshape(1, -1)

    def total(x):
        return jnp.sum(jnp.sum(x, axis=0, keepdims=True), axis=1, keepdims=True)

    def fresh(old, mean):
        return DECAY * old + (1.0 - DECAY) * (mean + EPS_SQ)

    def owned(grads, cols, over, row, row_total, weight, col_old, rate, outs):
        grad_out, row_out, col_out, new_out, low_out = outs
        width = grads.shape[1]
        col_new = fresh(line(col_old[...]), cols * (1.0 / D))
        mean = row_total * (1.0 / D)
        norm = mean * jnp.sum(over * (1.0 / col_new), axis=1, keepdims=True) * (1.0 / (D * width))
        step = grads * lax.rsqrt(row * col_new * (1.0 / mean))
        new = weight - rate * (step * clip_scale(norm))
        grad_out[...] = grads[:3]
        row_out[...] = jnp.sum(jnp.where(eye8, row, 0.0), axis=0)[:3]
        col_out[...] = col_new.reshape(width)
        new_out[...] = new[:3]
        low_out[...] = new.astype(BF16)[:3]

    def by_part(take):
        return jnp.concatenate([take(g)[:, 128 * p : 128 * p + 128] for p in range(3) for g in range(SETS)], axis=1)

    owned(
        by_part(lambda g: own_g[8 * g : 8 * g + 8, :]), by_part(lambda g: at_sums[g : g + 1, :]),
        by_part(lambda g: at_sums[4 + g : 5 + g, :]), own_r[0:8, :1], at_sums[8:9, :1],
        jnp.concatenate([own_wq[8 * part : 8 * part + 8, :] for part in range(3)], axis=1), qkv_col,
        D ** (-0.5), (qkv_grad, qkv_row_new, qkv_col_new, qkv_new, qkv_low),
    )
    owned(
        own_g[24:32, :], at_sums[3:4, :], at_sums[7:8, :], own_r[8:16, :1], at_sums[9:10, :1], own_wp[...], proj_col,
        (D // 8) ** (-0.5), (proj_grad, proj_row_new, proj_col_new, proj_new, proj_low),
    )

    for copy, then in copies:
        copy.wait()
        then.start()

    def update(grad, weight, row, col, mean, norm, rate, grad_out, new_out, low_out):
        row = row * (1.0 / mean)
        factor = rate * clip_scale(norm)
        for r in range(0, D, 48):
            rows = slice(r, r + 48)
            g = grad[rows, :]
            new = weight[rows, :] - (g * lax.rsqrt(row[rows] * col)) * factor
            grad_out[rows, :] = g
            new_out[rows, :] = new
            low_out[rows, :] = new.astype(BF16)

    row_new = fresh(line(fc1_row[...]), fc_sums[0:1, :] * (1.0 / FF))
    mean = row_mean(row_new)
    norm = mean * row_mean(fc_sums[1:2, :] * (1.0 / row_new)) * (1.0 / FF)
    fc1_row_new[...] = row_new.reshape(D)
    fc1_col_new[...] = fc_sums[13]
    update(
        fin.at[0], fc1, to_column(row_new, eye), fc_sums[13:14, :], mean, norm, D ** (-0.5),
        fc1_grad, fc1_new, fc1_low,
    )
    col_new = fresh(line(fc2_col[...]), fc_sums[2:3, :] * (1.0 / FF))
    mean = fc_sums[4:5, :1] * (1.0 / FF)
    norm = mean * row_mean(fc_sums[3:4, :] * (1.0 / col_new)) * (1.0 / FF)
    fc2_row_new[...] = fc_sums[14]
    fc2_col_new[...] = col_new.reshape(D)
    update(
        fin.at[1], fc2, to_column(fc_sums[14:15, :], eye), col_new, mean, norm, FF ** (-0.5),
        fc2_grad, fc2_new, fc2_low,
    )

    def stepped(grad, old):
        state = fresh(old, grad * grad)
        return state, grad * lax.rsqrt(state)

    norm = jnp.zeros((1, 1), F32)
    for m in range(4):
        d = (m + 4 - mlp) % 4
        step = stepped(vec[4 + m : 5 + m, :], b1[pl.ds(8 * (d + d // 2 - 2 * (d // 3)) + 4, 1), :])[1]
        norm = norm + jnp.sum(step * step, axis=1, keepdims=True)
    grad = vec[pl.ds(4 + mlp, 1), :]
    state, step = stepped(grad, b1[4:5, :])
    b1_grad[...] = grad.reshape(D)
    b1_state_new[...] = state.reshape(D)
    b1_new[...] = (line(fc1_b[...]) - VEC_RATE * (step * clip_scale(norm * (1.0 / FF)))).reshape(D)

    grad = jnp.concatenate([vec[n : n + 1, :] for n in (20, 21, 22, 23, 0, 1, 2, 3)], axis=1)
    state, step = stepped(grad, line(small_state[...]))
    norm = jnp.sum(step * step, axis=1, keepdims=True) * (1.0 / (8 * D))
    small_grad[...] = grad.reshape(8 * D)
    small_state_new[...] = state.reshape(8 * D)
    small_new[...] = (line(small[...]) - VEC_RATE * (step * clip_scale(norm))).reshape(8 * D)

    grad = vec[8:20, :169]
    state, step = stepped(grad, table_state[...])
    norm = total(step * step) * (1.0 / (169 * HEADS))
    table_grad[...] = grad
    table_state_new[...] = state
    table_new[...] = table[...] - VEC_RATE * (step * clip_scale(norm))
    for _, then in copies:
        then.wait()


def finish(*arrays):
    sd = jax.ShapeDtypeStruct
    vm = pltpu.VMEM
    dma = pltpu.SemaphoreType.DMA

    def owned(width):
        return [sd((3, width), F32), sd((3,), F32), sd((width,), F32), sd((3, width), F32), sd((3, width), BF16)]

    shard = [sd((D, D), F32), sd((D,), F32), sd((D,), F32), sd((D, D), F32), sd((D, D), BF16)]
    out_shape = owned(QKV) + owned(D) + shard + shard
    out_shape += [sd((D,), F32)] * 3 + [sd((8 * D,), F32)] * 3 + [sd((HEADS, 169), F32)] * 3 + [sd((TOK, D), F32)] * 2
    return pl.pallas_call(
        finish_kernel,
        out_shape=out_shape,
        in_specs=[pl.BlockSpec(memory_space=vm)] * 3
        + [pl.BlockSpec(memory_space=pl.ANY)] * 2
        + [pl.BlockSpec(memory_space=vm)] * (len(arrays) - 5),
        out_specs=[pl.BlockSpec(memory_space=vm)] * (len(out_shape) - 2) + [pl.BlockSpec(memory_space=pl.ANY)] * 2,
        scratch_shapes=[vm((2, TOK, D), F32), dma((2, 4)), dma((2, 4))],
        compiler_params=pltpu.CompilerParams(vmem_limit_bytes=63 * 1024 * 1024),
        name="finish",
    )(*arrays)


def clip_scale(mean_square):
    return 1.0 / jnp.maximum(1.0, jnp.sqrt(mean_square))


def per_device(
    tokens_in, out_grad, window_live, region_ids, qkv_weight, proj_weight, rel_table, small_params,
    fc1_weight, fc1_bias, fc2_weight, qkv_row, qkv_col, proj_row, proj_col, fc1_row, fc1_col,
    fc2_row, fc2_col, fc1_bias_state, small_state, table_state,
):
    out, gin, fin, pack = block(
        window_live, region_ids, tokens_in, out_grad, qkv_weight, proj_weight, fc1_weight, fc2_weight, rel_table.T,
        small_params, fc1_bias, fc1_bias_state, fc1_col, fc2_row, qkv_row, proj_row,
    )
    *outs, table_grad, table_state_new, table_new, out, gin = finish(
        fin.reshape(2, D, D), fc1_weight, fc2_weight, out, gin, pack, fc1_bias, fc1_row, fc2_col, qkv_col, proj_col,
        small_params, small_state, rel_table.T, table_state.T,
    )
    return (out, gin, *outs, table_grad.T, table_state_new.T, table_new.T)


def solution(mesh):
    tokens, owner = P(("win", "mlp"), None), P(("win", "mlp"))
    whole, part = P(), P("mlp")
    return jax.shard_map(
        per_device,
        mesh=mesh,
        in_specs=(
            tokens, tokens, owner, owner, whole, whole, whole, whole, P(None, "mlp"), part, P("mlp", None),
            whole, whole, whole, whole, whole, part, part, whole, part, whole, whole,
        ),
        out_specs=(
            tokens, tokens,
            tokens, owner, whole, tokens, tokens,
            tokens, owner, whole, tokens, tokens,
            P(None, "mlp"), whole, part, P(None, "mlp"), P(None, "mlp"),
            P("mlp", None), part, whole, P("mlp", None), P("mlp", None),
            part, part, part,
            whole, whole, whole,
            whole, whole, whole,
        ),
        check_vma=False,
    )
```

```python
import functools
import math

import jax
import jax.numpy as jnp
from jax import lax
from jax.experimental import pallas as pl
from jax.experimental.pallas import tpu as pltpu
from jax.sharding import PartitionSpec as P

D = 384
FF = 1536
QKV = 3 * D
HEADS = 12
WIN = 7
SPAN = WIN * WIN
STEP = 10
DECAY = 1.0 - STEP ** (-0.8)
EPS_NORM = 1e-05
EPS_SQ = 1e-30
VEC_RATE = 0.3
SCALE = 32 ** (-0.5)
FAR = -1e30
LOG2E = math.log2(math.e)
FACTOR = (2.0 * math.pi) ** (-0.5)

PLACE = (0, 1, 3, 2)
GROUPS = 3
PER = 8
G_TOK = PER * SPAN
G_ROWS = 400
ROWS = GROUPS * G_ROWS
TOK = GROUPS * G_TOK
CHUNK = 64
KEYS = 56
SETS = 3
LANES = 4 * CHUNK

MESH = pl.DeviceIdType.MESH
F32 = jnp.float32
BF16 = jnp.bfloat16


def dot(a, b):
    return jnp.dot(a, b, preferred_element_type=F32)


def dot_nt(a, b):
    return lax.dot_general(a, b, (((1,), (1,)), ((), ())), preferred_element_type=F32)


def dot_tn(a, b):
    return lax.dot_general(a, b, (((0,), (0,)), ((), ())), preferred_element_type=F32)


def dot_exact(a, b):
    return jnp.dot(a, b, precision=lax.Precision.HIGHEST, preferred_element_type=F32)


def iota(shape, dim):
    return lax.broadcasted_iota(jnp.int32, shape, dim)


def fold_rows(x):
    total = x[0:8]
    for i in range(1, x.shape[0] // 8):
        total = total + x[8 * i : 8 * i + 8]
    return total


def row_mean(x):
    return jnp.sum(x, axis=1, keepdims=True) * (1.0 / D)


def normalize(x):
    center = x - row_mean(x)
    inverse = lax.rsqrt(row_mean(center * center) + EPS_NORM)
    return center * inverse, inverse


def normalize_back(u, gain, scaled, inverse):
    weighted = u * gain
    return inverse * (weighted - row_mean(weighted) - scaled * row_mean(weighted * scaled))


def gelu_parts(v):
    density = jnp.exp2((v * v) * (-0.5 * LOG2E) + math.log2(FACTOR))
    t = 1.0 / (1.0 + (0.3275911 * 0.5**0.5) * jnp.abs(v))
    c = 0.5 / FACTOR
    poly = (1.061405429 * c) * t - 1.453152027 * c
    poly = poly * t + 1.421413741 * c
    poly = poly * t - 0.284496736 * c
    poly = poly * t + 0.254829592 * c
    tail = density * (poly * t)
    phi = jnp.where(v < 0.0, tail, 1.0 - tail)
    return v * phi, phi + v * density


def barrel(x, amount, right):
    width = x.shape[1]
    for k in range(7):
        step = 1 << k
        moved = pltpu.roll(x, step if right else width - step, 1)
        x = jnp.where((amount & step) != 0, moved, x)
    return x


def embed(i):
    return 13 * (i // WIN) + i % WIN


def chunk_start(w):
    return pl.multiple_of((w // PER) * G_ROWS + (w % PER) * 48, 16)


def widen(tok, x_ref):
    for a in range(GROUPS):
        for r in range(0, G_TOK, 56):
            src = a * G_TOK + r
            low = src // 16 * 16
            x_ref[a * G_ROWS + r : a * G_ROWS + r + 56, :] = (
                tok[low : low + 64 if low + 64 <= TOK else TOK, :].astype(F32)[src - low : src - low + 56]
            )
        x_ref[a * G_ROWS + G_TOK : (a + 1) * G_ROWS, :] = jnp.zeros((G_ROWS - G_TOK, D), F32)


def prologue(region, table, emask, bias, mask):
    row = iota((LANES, 128), 0)
    lane = iota((LANES, 128), 1)
    for b in range(PER):
        i = row % CHUNK
        keep = (i >= b) & (i < b + SPAN) & (lane // 32 == row // CHUNK)
        emask[b] = jnp.where(keep, 1.0, 0.0).astype(BF16)
    j = iota((KEYS, 256), 0)
    amount = jnp.maximum(84 - embed(j), 0)
    jl = iota((KEYS, LANES), 0)
    il = iota((KEYS, LANES), 1) % CHUNK
    for g in range(SETS):
        base = jnp.zeros((KEYS, LANES), F32)
        for h in range(4):
            line = jnp.concatenate([table[4 * g + h : 4 * g + h + 1, :], jnp.zeros((1, 87), F32)], axis=1)
            wide = jnp.broadcast_to(line, (KEYS, 256))
            wide = barrel(wide, amount, False)[:, :128]
            lane_to = iota((128, LANES), 1) - CHUNK * h
            pick = (iota((128, LANES), 0) == embed(lane_to)) & (lane_to >= 0) & (lane_to < SPAN)
            base = base + dot_exact(wide, jnp.where(pick, 1.0, 0.0))
        for b in range(PER):
            moved = pltpu.roll(pltpu.roll(base, b, 0), b, 1) if b else base
            key_ok = (jl >= b) & (jl < b + SPAN)
            query_ok = (il >= b) & (il < b + SPAN)
            bias[b, g] = jnp.where(key_ok, jnp.where(query_ok, moved, 0.0), FAR)
    eye = iota((CHUNK, CHUNK), 0) == iota((CHUNK, CHUNK), 1)
    region_row = jnp.concatenate([region[...].reshape(1, TOK).astype(F32), jnp.zeros((1, 104), F32)], axis=1)
    for w in range(GROUPS * PER):
        start = (w // PER) * G_TOK + (w % PER) * 48
        line = region_row[:, start : start + CHUNK]
        column = jnp.sum(jnp.where(eye, jnp.broadcast_to(line, (CHUNK, CHUNK)), 0.0), axis=1, keepdims=True)
        wide = jnp.concatenate([line] * 4, axis=1)
        mask[w] = jnp.where(column[:KEYS] != wide, -100.0, 0.0)


def pad_keys(x):
    return jnp.concatenate([x, jnp.zeros((CHUNK - KEYS, x.shape[1]), x.dtype)], axis=0)


def spread(x, keep):
    return jnp.concatenate([x] * 4, axis=0) * keep


def collect(full):
    head = iota((CHUNK, 128), 1) // 32
    parts = [full[CHUNK * h : CHUNK * (h + 1)] for h in range(4)]
    low = jnp.where(head == 0, parts[0], parts[1])
    high = jnp.where(head == 2, parts[2], parts[3])
    return jnp.where(head < 2, low, high)


def packed(ref):
    at, views = 0, []
    for rows in (24, 16, 16, 32, 24, 8, 32, 16):
        views.append(ref.at[at : at + rows])
        at += rows
    return views


def block_kernel(
    live_windows, region, tok_in, og_in, wq_in, wp_in, fc1_in, fc2_in, table, small,
    fc1_b, fc1_state, fc1_col, fc2_row, qkv_row, proj_row,
    out_to, gin_to, fin_to, pack,
    x_ref, xh1, inv1, inv2, n1, n2, qkv, att_b, probs, back, hidden, ig, dqkv,
    emask, bias, mask, tacc, s1, s2, sums, b1_acc, wq_b, wp_b, w1, w2, tok, og, wq, wp, fc1, fc2, fin, fin_b, b1, stage, in_sem, out_sem,
    fcl, fr1, fr2, ft, fr3, fr4, fst, atl, ar1, ar2, ar3, ar4, ast, vx, vy, at_total,
    w_send, w_recv, b_send, b_recv, pair_send, pair_recv, f1s, f1r, f2s, f2r, f3s, f3r, f4s, f4r, f5s, f5r, f7s, f7r, f8s, f8r,
    a1s, a1r, a2s, a2r, a3s, a3r, a4s, a4r, a5s, a5r, vxs, vxr, vys, vyr,
):
    win, mlp = lax.axis_index("win"), lax.axis_index("mlp")
    vec, fc_sums, at_sums, own_g, own_wq, own_wp, b1_all, own_r = packed(pack)
    z, y, core = win // 8, (win // 2) % 4, win % 2
    pair = win + 1 - 2 * core

    def along_x(d):
        return win, (mlp + d) % 4

    def along_y(d):
        return z * 8 + ((y + d) % 4) * 2 + core, mlp

    def along_z(d):
        return ((z + d) % 4) * 8 + y * 2 + core, mlp

    def plane_peer(d):
        return ((z + d // 4) % 4) * 8 + ((y + d % 4) % 4) * 2 + core, mlp

    def class_peer(d):
        return pair if d >= 4 else win, (mlp + d) % 4

    loads = [
        pltpu.make_async_copy(src, dst, in_sem.at[n])
        for n, (src, dst) in enumerate(
            ((fc1_in, fc1), (fc2_in, fc2), (tok_in, tok), (wq_in, wq), (og_in, og), (wp_in, wp))
        )
    ]
    for copy in loads:
        copy.start()
    barrier = pltpu.get_barrier_semaphore()
    peers = [class_peer(d) for d in range(1, 8)]
    peers += [plane_peer(d) for d in range(1, 16)]
    for peer in peers:
        pl.semaphore_signal(barrier, inc=1, device_id=peer, device_id_type=MESH)

    def remote(src, dst, send, recv, peer):
        return pltpu.make_async_remote_copy(
            src_ref=src, dst_ref=dst, send_sem=send, recv_sem=recv, device_id=peer, device_id_type=MESH
        )

    def param(part):
        return small[D * part : D * part + D].reshape(1, D)

    pending = []

    def start(copy):
        copy.start()
        pending.append(copy)
        return copy

    def shard(place):
        half = pl.ds(pl.multiple_of(core * (D // 2), 16), D // 2)
        half_at = pl.ds(pl.multiple_of(place * D + core * (D // 2), 16), D // 2)
        return w1.at[half, D * place : D * place + D], w2.at[half_at, :]

    def near(d, n):
        return remote(shard(0)[n], shard(PLACE[4 - d])[n], w_send.at[d // 2, n], w_recv.at[d // 2, n], along_x(d))

    def far(n):
        d = 3 - 2 * n
        return remote(shard(1 + n)[n], shard(3)[n], w_send.at[2, n], w_recv.at[2, n], along_x(d))

    def bias_copy(d):
        return remote(b1.at[0], b1.at[PLACE[4 - d]], b_send.at[d - 1], b_recv.at[d - 1], along_x(d))

    def across(place, n):
        came = shard(place)[n]
        return remote(came, came, pair_send.at[place - 1, n], pair_recv.at[place - 1, n], (pair, mlp))

    for copy in loads[:2]:
        copy.wait()
    w1[:, :D] = fc1[...].astype(BF16)
    w2[:D, :] = fc2[...].astype(BF16)
    b1[0, 0:4] = jnp.broadcast_to(fc1_b[...].reshape(1, D), (4, D))
    b1[0, 4:8] = jnp.broadcast_to(fc1_state[...].reshape(1, D), (4, D))
    pl.semaphore_wait(barrier, 22)
    for n in range(2):
        for d in (1, 3):
            start(near(d, n))
    for d in range(1, 4):
        start(bias_copy(d))

    live = live_windows[0]
    for n in range(1, GROUPS * PER):
        live = live + live_windows[n]
    live = live * SPAN
    prologue(region, table, emask, bias, mask)
    for copy in loads[2:]:
        copy.wait()
    widen(tok, x_ref)
    for g in range(SETS):
        for part in range(3):
            wq_b[:, D * g + 128 * part : D * g + 128 * part + 128] = wq[
                :, D * part + 128 * g : D * part + 128 * g + 128
            ].astype(BF16)
    wp_b[...] = wp[...].astype(BF16)
    sums[...] = jnp.zeros_like(sums)
    b1_acc[...] = jnp.zeros_like(b1_acc)
    tacc[...] = jnp.zeros_like(tacc)
    att = dqkv.at[:, :D]
    xh2 = dqkv.at[:, D : 2 * D]
    dqkv_b = ig.at[:, :QKV]
    dqkv[:, :D] = jnp.zeros((ROWS, D), F32)

    for a in range(GROUPS):
        for r in range(0, G_TOK, 56):
            src = a * G_TOK + r
            low = src // 16 * 16
            rows = og[low : low + 64 if low + 64 <= TOK else TOK, :].astype(F32)[src - low : src - low + 56]
            keep = iota((56, D), 0) + src < live
            x = jnp.where(keep, rows, 0.0)
            s2[r : r + 56, :] = x
            sums[7] += fold_rows(x)
        s2[G_TOK:G_ROWS, :] = jnp.zeros((G_ROWS - G_TOK, D), F32)
        back[a * G_ROWS : (a + 1) * G_ROWS, :] = s2[...].astype(BF16)

    shift_q = jnp.concatenate(
        [
            part[:, 128 * g : 128 * g + 128]
            for g in range(SETS)
            for part in (param(2), jnp.zeros((1, D), F32), param(3))
        ],
        axis=1,
    )

    @pl.loop(0, 5, unroll=5)
    def _(t):
        for c in range(15):
            rows = pl.ds(pl.multiple_of(t * 240 + c * 16, 16), 16)
            scaled, inverse = normalize(x_ref[rows, :])
            xh1[rows, :] = scaled
            inv1[rows, :] = inverse
            n1[rows, :] = (scaled * param(0) + param(1)).astype(BF16)

    @pl.loop(0, 5, unroll=5)
    def _(t):
        rows = pl.ds(pl.multiple_of(t * 240, 16), 240)
        qkv[rows, :] = (dot(n1[rows, :], wq_b[...]) + shift_q).astype(BF16)

    def scores_of(a, b, g):
        rows = pl.ds(pl.multiple_of(a * G_ROWS + b * 48, 16), CHUNK)
        q = qkv[rows, D * g : D * g + 128]
        k = qkv[rows, D * g + 128 : D * g + 256]
        return dot_nt(k, spread(q, emask[b]))

    def attend(a, b, g, raw):
        rows = pl.ds(pl.multiple_of(a * G_ROWS + b * 48, 16), CHUNK)
        v = qkv[rows, D * g + 256 : D * g + 384]
        scores = raw[:KEYS] * SCALE + (bias[b, g] + mask[a * PER + b])
        p = jnp.exp(scores - jnp.max(scores, axis=0, keepdims=True))
        p = p * (1.0 / jnp.sum(p, axis=0, keepdims=True))
        probs[a * PER + b, g] = p
        return dot_tn(pad_keys(p).astype(BF16), v)

    def attended(a, b, g, full):
        rows = pl.ds(pl.multiple_of(a * G_ROWS + b * 48, 16), CHUNK)
        i = iota((CHUNK, 128), 0)
        att[rows, 128 * g : 128 * g + 128] += jnp.where((i >= b) & (i < b + SPAN), collect(full), 0.0)

    @pl.loop(0, 2)
    def _(half):
        blocks = [[(a, 4 * half + b, g) for a in range(GROUPS)] for b in range(4) for g in range(SETS)]
        ahead = [scores_of(*unit) for unit in blocks[0]]
        for n, units in enumerate(blocks):
            raws = ahead
            if n + 1 < len(blocks):
                ahead = [scores_of(*unit) for unit in blocks[n + 1]]
            fulls = [attend(*unit, raw) for unit, raw in zip(units, raws)]
            for unit, full in zip(units, fulls):
                attended(*unit, full)

    for n in range(2):
        for d in (1, 3):
            near(d, n).wait_recv()
        start(far(n))
    for place in (1, 2):
        for n in range(2):
            start(across(place, n))
    for d in range(1, 4):
        bias_copy(d).wait_recv()

    @pl.loop(0, GROUPS, unroll=3)
    def _(a):
        rows = pl.ds(pl.multiple_of(a * G_ROWS, 16), G_ROWS)
        att_b[rows, :] = att[rows, :].astype(BF16)
        s1[...] = dot(att_b[rows, :], wp_b[...])

        for c in range(25):
            here = pl.ds(pl.multiple_of(a * G_ROWS + 16 * c, 16), 16)
            middle = x_ref[here, :] + (s1[16 * c : 16 * c + 16, :] + param(4))
            stage[here, :] = middle
            scaled, inverse = normalize(middle)
            xh2[here, :] = scaled
            inv2[here, :] = inverse
            n2[here, :] = (scaled * param(5) + param(6)).astype(BF16)

    for tiles in ((0, 1, 2), (3,), (4, 5)):
        if tiles[0] in (0, 3):
            for n in range(2):
                across(1 + tiles[0] // 3, n).wait_recv()
        if tiles[0] == 3:
            for n in range(2):
                far(n).wait_recv()
                start(across(3, n))
        if tiles[0] == 4:
            for n in range(2):
                across(3, n).wait_recv()

        @pl.loop(0, 5)
        def _(mt):
            rows = pl.ds(pl.multiple_of(mt * 240, 16), 240)

            def products(nt):
                cols = slice(256 * nt, 256 * nt + 256)
                shift = jnp.concatenate(
                    [b1[c // 3, 0:1, 128 * (c % 3) : 128 * (c % 3) + 128] for c in (2 * nt, 2 * nt + 1)], axis=1
                )
                return dot(n2[rows, :], w1[:, cols]) + shift, dot_nt(back[rows, :], w2[cols, :])

            ahead = products(tiles[0])
            for nt in tiles:
                inner, up = ahead
                if nt + 1 in tiles:
                    ahead = products(nt + 1)
                cols = slice(256 * nt, 256 * nt + 256)
                total = b1_acc[:, cols]
                for c in range(15):
                    act, slope = gelu_parts(inner[16 * c : 16 * c + 16])
                    here = pl.ds(pl.multiple_of(mt * 240 + 16 * c, 16), 16)
                    hidden[here, cols] = act.astype(BF16)
                    grad = (up[16 * c : 16 * c + 16] * slope).astype(BF16)
                    ig[here, cols] = grad
                    total = total + fold_rows(grad.astype(F32))
                b1_acc[:, cols] = total

    g2 = dot_tn(hidden[...], back[...]).astype(BF16)
    g1 = dot_tn(n2[...], ig[...]).astype(BF16)
    for m in range(4):
        fcl[0, m] = g1[:, D * m : D * m + D].reshape(4, 96, D)
        fcl[1, m] = g2[D * m : D * m + D].reshape(4, 96, D)
    fc_one = [start(remote(fcl.at[1 - core, m], fr1.at[m], f1s.at[m], f1r.at[m], (pair, mlp))) for m in range(4)]

    def middle_back(a):
        rows = slice(a * G_ROWS, (a + 1) * G_ROWS)
        held = (s1, s2)[a % 2]
        held[...] = dot_nt(ig[rows, :], w1[...])
        for c in range(25):
            here = slice(16 * c, 16 * c + 16)
            at = slice(a * G_ROWS + 16 * c, a * G_ROWS + 16 * c + 16)
            u = held[here, :]
            scaled = xh2[at, :]
            sums[5] += fold_rows(u * scaled)
            sums[6] += fold_rows(u)
            mg = normalize_back(u, param(5), scaled, inv2[at, :]) + back[at, :].astype(F32)
            x_ref[at, :] = mg
            low = mg.astype(BF16)
            n2[at, :] = low
            sums[4] += fold_rows(low.astype(F32))

    def out_copy(a):
        return pltpu.make_async_copy(
            stage.at[pl.ds(a * G_ROWS, G_TOK)], out_to.at[pl.ds(a * G_TOK, G_TOK)], out_sem.at[a]
        )

    def block_out(a):
        rows = slice(a * G_ROWS, (a + 1) * G_ROWS)
        held = (s1, s2)[a % 2]
        held[...] = dot(hidden[rows, :], w2[...])
        for c in range(25):
            at = slice(a * G_ROWS + 16 * c, a * G_ROWS + 16 * c + 16)
            r = stage[at, :] + (held[16 * c : 16 * c + 16, :] + param(7))
            keep = iota((16, D), 0) + (a * G_TOK + 16 * c) < live
            stage[at, :] = jnp.where(keep, r, 0.0)
        out_copy(a).start()

    p = iota((D, D), 0)
    inner_p = p % 48
    owned = 24 * (inner_p // 3) + 12 * (p // 192) + 3 * ((p // 48) % 4) + inner_p % 3
    order = jnp.where(iota((D, D), 1) == owned, 1.0, 0.0).astype(BF16)

    def ordered(grad):
        return dot(order, grad.astype(BF16)).astype(BF16).reshape(2, 4, 48, D)

    def at_one(n):
        return remote(atl.at[n, 1 - core], ar1.at[n], a1s.at[n], a1r.at[n], (pair, mlp))

    def at_add_one(n):
        at_one(n).wait_recv()
        for i in range(4):
            ar1[n, i] = (ar1[n, i].astype(F32) + atl[n, core, i].astype(F32)).astype(BF16)
        for d in range(1, 4):
            start(remote(ar1.at[n, (mlp + d) % 4], ar2.at[n, d - 1], a2s.at[n, d - 1], a2r.at[n, d - 1], along_x(d)))

    def near_axis(d):
        return ((z + d * core) % 4) * 8 + ((y + d * (1 - core)) % 4) * 2 + core, mlp

    def other_axis(d):
        return ((z + d * (1 - core)) % 4) * 8 + ((y + d * core) % 4) * 2 + core, mlp

    near_at, other_at = y * (1 - core) + z * core, z * (1 - core) + y * core

    def at_add_two(n):
        total = ar1[n, mlp].astype(F32)
        for d in range(1, 4):
            remote(ar1.at[n, 0], ar2.at[n, d - 1], a2s.at[n, d - 1], a2r.at[n, d - 1], along_x(d)).wait_recv()
            total = total + ar2[n, d - 1].astype(F32)
        ar3[n, near_at] = total.astype(BF16)
        for d in range(1, 4):
            start(remote(ar3.at[n, near_at], ar3.at[n, near_at], a3s.at[n, d - 1], a3r.at[n, d - 1], near_axis(d)))

    def at_add_three(n):
        for d in range(1, 4):
            came = ar3.at[n, (near_at + 4 - d) % 4]
            remote(came, came, a3s.at[n, d - 1], a3r.at[n, d - 1], near_axis(d)).wait_recv()
        total = ar3[n, 0].astype(F32) + ar3[n, 1].astype(F32)
        ar4[n, other_at] = (total + ar3[n, 2].astype(F32) + ar3[n, 3].astype(F32)).astype(BF16)
        for d in range(1, 4):
            start(remote(ar4.at[n, other_at], ar4.at[n, other_at], a4s.at[n, d - 1], a4r.at[n, d - 1], other_axis(d)))

    def at_finish(n):
        for d in range(1, 4):
            came = ar4.at[n, (other_at + 4 - d) % 4]
            remote(came, came, a4s.at[n, d - 1], a4r.at[n, d - 1], other_axis(d)).wait_recv()
        total = ar4[n, 0].astype(F32) + ar4[n, 1].astype(F32)
        at_total[n] = total + ar4[n, 2].astype(F32) + ar4[n, 3].astype(F32)

    def to_axes(dx, dy, dz):
        return ((z + dz) % 4) * 8 + ((y + dy) % 4) * 2 + core, (mlp + dx) % 4

    def first_axis(d):
        return to_axes(d * (1 - core), 0, d * core)

    def second_axis(d):
        return to_axes(d * core, d * (1 - core), 0)

    def third_axis(d):
        return to_axes(0, d * core, d * (1 - core))

    def last_axis(d):
        return to_axes(0, d * (1 - core), d * core)

    block_at = y * (1 - core) + z * core
    second = y * (1 - core)
    third = z * (1 - core) + y * core

    def fc_two(d):
        return remote(fr1.at[0], fr2.at[d - 1], f2s.at[d - 1], f2r.at[d - 1], first_axis(d))

    def fc_add_one():
        for m in range(4):
            fc_one[m].wait_recv()
            for i in range(4):
                fr1[m, i] = (fr1[m, i].astype(F32) + fcl[core, m, i].astype(F32)).astype(BF16)

        @pl.when(core == 0)
        def _():
            for d in range(1, 4):
                remote(fr1.at[PLACE[d]], fr2.at[d - 1], f2s.at[d - 1], f2r.at[d - 1], first_axis(d)).start()

        @pl.when(core == 1)
        def _():
            for d in range(1, 4):
                remote(fr1.at[:, (z + d) % 4], fr2.at[d - 1], f2s.at[d - 1], f2r.at[d - 1], first_axis(d)).start()

    def fc_add_two():
        for d in range(1, 4):
            fc_two(d).wait_recv()
        for i in range(4):
            total = fr1[i * core, i * (1 - core) + z * core].astype(F32)
            for d in range(1, 4):
                total = total + fr2[d - 1, i].astype(F32)
            ft[i] = total.astype(BF16)
        for d in range(1, 4):
            to = (1 - core) * ((y + d) % 4) + core * PLACE[d]
            start(remote(ft.at[to], fr3.at[d - 1], f3s.at[d - 1], f3r.at[d - 1], second_axis(d)))

    def fc_add_three():
        total = ft[second].astype(F32)
        for d in range(1, 4):
            remote(ft.at[0], fr3.at[d - 1], f3s.at[d - 1], f3r.at[d - 1], second_axis(d)).wait_recv()
            total = total + fr3[d - 1].astype(F32)
        fr4[third] = total.astype(BF16)
        for d in range(1, 4):
            start(remote(fr4.at[third], fr4.at[third], f4s.at[d - 1], f4r.at[d - 1], third_axis(d)))

    def fc_add_four():
        for d in range(1, 4):
            came = fr4.at[(third + 4 - d) % 4]
            remote(came, came, f4s.at[d - 1], f4r.at[d - 1], third_axis(d)).wait_recv()
        total = fr4[0].astype(F32) + fr4[1].astype(F32)
        fin_b[core, block_at] = (total + fr4[2].astype(F32) + fr4[3].astype(F32)).astype(BF16)
        for d in range(1, 4):
            place = fin_b.at[core, block_at]
            start(remote(place, place, f5s.at[d - 1], f5r.at[d - 1], last_axis(d)))

    def fc_spread():
        for d in range(1, 4):
            place = fin_b.at[core, (block_at + 4 - d) % 4]
            remote(place, place, f5s.at[d - 1], f5r.at[d - 1], last_axis(d)).wait_recv()
        start(remote(fin_b.at[core], fin_b.at[core], f7s.at[0], f7r.at[0], (pair, mlp)))

    mine_at, plane_at = 4 * core + mlp, 4 * z + y

    def vec_one(n):
        for d in range(1, 8):
            place = vx.at[n, mine_at]
            start(remote(place, place, vxs.at[n, d - 1], vxr.at[n, d - 1], class_peer(d)))

    def vec_two(n):
        for d in range(1, 8):
            place = vx.at[n, (mlp + 8 - d) % 4 + 4 * (core if d < 4 else 1 - core)]
            remote(place, place, vxs.at[n, d - 1], vxr.at[n, d - 1], class_peer(d)).wait_recv()
        total = vx[n, 0]
        for i in range(1, 8):
            total = total + vx[n, i]
        vy[n, plane_at] = total
        for d in range(1, 16):
            place = vy.at[n, plane_at]
            start(remote(place, place, vys.at[n, d - 1], vyr.at[n, d - 1], plane_peer(d)))

    def vec_three(n):
        for d in range(1, 16):
            place = vy.at[n, 4 * ((z + 4 - d // 4) % 4) + (y + 4 - d % 4) % 4]
            remote(place, place, vys.at[n, d - 1], vyr.at[n, d - 1], plane_peer(d)).wait_recv()
        total = vy[n, 0]
        for i in range(1, 16):
            total = total + vy[n, i]
        vec[8 * n : 8 * n + 8, :] = total

    middle_back(0)
    middle_back(1)
    fc_add_one()
    middle_back(2)

    atl[3] = ordered(dot_tn(att_b[...], n2[...]))
    start(at_one(3))

    @pl.loop(0, GROUPS, unroll=3)
    def _(a):
        rows = pl.ds(pl.multiple_of(a * G_ROWS, 16), G_ROWS)
        att_b[rows, :] = dot_nt(n2[rows, :], wp_b[...]).astype(BF16)

    dqkv[...] = jnp.zeros_like(dqkv)

    def attention_back(g, half):
        def first(a, b):
            rows = pl.ds(a * G_ROWS + b * 48, CHUNK)
            v = qkv[rows, D * g + 256 : D * g + 384]
            da = spread(att_b[rows, 128 * g : 128 * g + 128], emask[b])
            return da, dot_nt(v, da)

        def inner_grad(a, b, dp):
            p = probs[a * PER + b, g]
            pd = p * dp[:KEYS]
            return pad_keys(p).astype(BF16), pad_keys(pd - p * jnp.sum(pd, axis=0, keepdims=True)).astype(BF16)

        def last(a, b, da, p, ds):
            rows = pl.ds(a * G_ROWS + b * 48, CHUNK)
            q = qkv[rows, D * g : D * g + 128]
            k = qkv[rows, D * g + 128 : D * g + 256]
            dv = dot(p, da)
            dk = dot(ds, spread(q, emask[b])) * SCALE
            dq = collect(dot_tn(ds, k)) * SCALE
            dqkv[rows, 384 * g : 384 * g + 128] += dq
            dqkv[rows, 384 * g + 128 : 384 * g + 256] += dk
            dqkv[rows, 384 * g + 256 : 384 * g + 384] += dv

        bs = range(4 * half, 4 * half + 4)
        ahead = [first(a, bs[0]) for a in range(GROUPS)]
        for b in bs:
            held = ahead
            if b + 1 in bs:
                ahead = [first(a, b + 1) for a in range(GROUPS)]
            grads = [inner_grad(a, b, held[a][1]) for a in range(GROUPS)]
            tacc[b, g] = sum(ds.astype(F32)[:KEYS] for _, ds in grads)
            for a in range(GROUPS):
                last(a, b, held[a][0], *grads[a])

    def qkv_grad(g):
        group = slice(384 * g, 384 * g + 384)

        @pl.loop(0, 5, unroll=5)
        def _(t):
            for c in range(15):
                rows = pl.ds(pl.multiple_of(t * 240 + c * 16, 16), 16)
                low = dqkv[rows, group].astype(BF16)
                dqkv_b[rows, group] = low
                wide = low.astype(F32)
                sums[2, :, 128 * g : 128 * g + 128] += fold_rows(wide[:, :128])
                sums[3, :, 128 * g : 128 * g + 128] += fold_rows(wide[:, 256:])

        atl[g] = ordered(dot_tn(n1[...], dqkv_b[:, group]))
        start(at_one(g))

    for part in range(4):
        vx[0, mine_at, part : part + 1, :] = jnp.sum(sums[4 + part], axis=0, keepdims=True)
    for m in range(4):
        d = (m + 4 - mlp) % 4
        place = d + d // 2 - 2 * (d // 3)
        cols = pl.ds(pl.multiple_of(place * D, 128), D)
        vx[0, mine_at, 4 + m : 5 + m, :] = jnp.sum(b1_acc[:, cols], axis=0, keepdims=True)
    vec_one(0)

    def table_back(g, n):
        j = iota((KEYS, 256), 0)
        amount = jnp.maximum(84 - embed(j), 0)
        total = tacc[0, g]
        for b in range(1, PER):
            total = total + pltpu.roll(pltpu.roll(tacc[b, g], KEYS - b, 0), LANES - b, 1)
        for h in range(4):
            lane_from = iota((LANES, 256), 0) - CHUNK * h
            pick = (iota((LANES, 256), 1) == embed(lane_from)) & (lane_from >= 0) & (lane_from < SPAN)
            wide = barrel(dot_exact(total, jnp.where(pick, 1.0, 0.0)), amount, True)
            wide = jnp.where(j < SPAN, wide, 0.0)
            vx[n, mine_at, 4 * (g % 2) + h : 4 * (g % 2) + h + 1, :] = jnp.concatenate(
                [jnp.sum(wide, axis=0, keepdims=True), jnp.zeros((1, 128), F32)], axis=1
            )

    attention_back(0, 0)
    attention_back(0, 1)
    qkv_grad(0)
    attention_back(1, 0)
    attention_back(1, 1)
    fc_add_two()
    qkv_grad(1)
    at_add_one(3)
    at_add_one(0)
    vec_two(0)
    attention_back(2, 0)
    at_add_one(1)
    attention_back(2, 1)
    qkv_grad(2)
    fc_add_three()
    at_add_one(2)

    def gin_copy(a):
        src = pl.ds(pl.multiple_of(a * G_ROWS, 8), G_TOK)
        dst = pl.ds(pl.multiple_of(a * G_TOK, 8), G_TOK)
        return pltpu.make_async_copy(x_ref.at[src], gin_to.at[dst], out_sem.at[3 + a])

    @pl.loop(0, GROUPS)
    def _(a):
        rows = pl.ds(pl.multiple_of(a * G_ROWS, 16), G_ROWS)
        s2[...] = dot_nt(dqkv_b[rows, :], wq_b[...])
        for c in range(25):
            here = slice(16 * c, 16 * c + 16)
            at = pl.ds(pl.multiple_of(a * G_ROWS + 16 * c, 16), 16)
            u = s2[here, :]
            scaled = xh1[at, :]
            sums[0] += fold_rows(u * scaled)
            sums[1] += fold_rows(u)
            x_ref[at, :] = normalize_back(u, param(0), scaled, inv1[at, :]) + x_ref[at, :]
        gin_copy(a).start()

    at_add_two(3)
    at_add_two(0)
    table_back(0, 1)
    table_back(1, 1)
    vec_one(1)
    at_add_two(1)
    table_back(2, 2)
    for part in range(4):
        vx[2, mine_at, 4 + part : 5 + part, :] = jnp.sum(sums[part], axis=0, keepdims=True)
    vec_one(2)
    vec_three(0)
    fc_add_four()
    at_add_two(2)
    block_out(0)
    block_out(1)
    at_add_three(3)
    at_add_three(0)
    block_out(2)
    at_add_three(1)
    vec_two(1)
    vec_two(2)
    at_add_three(2)
    fc_spread()
    at_finish(3)
    at_finish(0)
    at_finish(1)

    remote(fin_b.at[1 - core], fin_b.at[1 - core], f7s.at[0], f7r.at[0], (pair, mlp)).wait_recv()
    for half in range(2):
        for n in range(4):
            fin[half, n] = fin_b[half, n].astype(F32)
    fin_copy = pltpu.make_async_copy(fin, fin_to, out_sem.at[6])
    fin_copy.start()
    eye = iota((D, D), 0) == iota((D, D), 1)

    def to_row(column):
        return jnp.sum(jnp.where(eye, column, 0.0), axis=0, keepdims=True)

    up = fin[0].reshape(D, D)
    down = fin[1].reshape(D, D)
    up_squares = up * up
    down_squares = down * down
    up_col = DECAY * fc1_col[...].reshape(1, D) + (1.0 - DECAY) * (
        jnp.sum(up_squares, axis=0, keepdims=True) * (1.0 / D) + EPS_SQ
    )
    down_row = DECAY * to_column(fc2_row[...].reshape(1, D), eye) + (1.0 - DECAY) * (row_mean(down_squares) + EPS_SQ)
    fst[mlp, 0:1] = to_row(jnp.sum(up_squares, axis=1, keepdims=True))
    fst[mlp, 1:2] = to_row(jnp.sum(up_squares * (1.0 / up_col), axis=1, keepdims=True))
    fst[mlp, 2:3] = jnp.sum(down_squares, axis=0, keepdims=True)
    fst[mlp, 3:4] = jnp.sum(down_squares * (1.0 / down_row), axis=0, keepdims=True)
    fst[mlp, 4:5] = jnp.broadcast_to(jnp.sum(down_row, axis=0, keepdims=True), (1, D))
    fst[mlp, 5:6] = up_col
    fst[mlp, 6:7] = to_row(down_row)
    fst[mlp, 7:8] = jnp.zeros((1, D), F32)
    for d in range(1, 4):
        start(remote(fst.at[mlp], fst.at[mlp], f8s.at[d - 1], f8r.at[d - 1], along_x(d)))

    vec_three(1)

    offset = 48 - 3 * plane_at
    block_rows = pl.ds(pl.multiple_of(24 * (win // 2), 8), 24)
    shift = 24 - 3 * mine_at
    rolled = pltpu.roll(wq[block_rows, :], shift, 0)[:8]
    for part in range(3):
        own_wq[8 * part : 8 * part + 8, :] = rolled[:, D * part : D * part + D]
    own_wp[...] = pltpu.roll(wp[block_rows, :], shift, 0)[:8]

    r48 = iota((48, D), 0)
    pick = iota((48, D), 1) == 24 * (r48 // 3) + 12 * core + 3 * mlp + r48 % 3

    def rows_new(state, mean):
        old = jnp.sum(jnp.where(pick, state, 0.0), axis=1, keepdims=True)
        return DECAY * old + (1.0 - DECAY) * (mean + EPS_SQ)

    at_finish(2)
    squares = [at_total[n] * at_total[n] for n in range(4)]
    qkv_new_row = rows_new(
        qkv_row[...].reshape(1, D), row_mean(squares[0] + squares[1] + squares[2]) * (1.0 / 3.0)
    )
    proj_new_row = rows_new(proj_row[...].reshape(1, D), row_mean(squares[3]))
    for n in range(4):
        over = squares[n] * (1.0 / (qkv_new_row if n < 3 else proj_new_row))
        ast[mine_at, n : n + 1] = jnp.sum(squares[n], axis=0, keepdims=True)
        ast[mine_at, 4 + n : 5 + n] = jnp.sum(over, axis=0, keepdims=True)
    ast[mine_at, 8:9] = jnp.broadcast_to(jnp.sum(qkv_new_row, axis=0, keepdims=True), (1, D))
    ast[mine_at, 9:10] = jnp.broadcast_to(jnp.sum(proj_new_row, axis=0, keepdims=True), (1, D))
    ast[mine_at, 10:16] = jnp.zeros((6, D), F32)

    def at_five(d):
        place = ast.at[mine_at]
        return remote(place, place, a5s.at[d - 1], a5r.at[d - 1], class_peer(d))

    for d in range(1, 8):
        start(at_five(d))

    for n in range(4):
        own_g[8 * n : 8 * n + 8, :] = pltpu.roll(at_total[n], offset, 0)[:8]
        b1_all[8 * n : 8 * n + 8, :] = b1[n]
    own_r[0:8, :] = pltpu.roll(jnp.broadcast_to(qkv_new_row, (48, D)), offset, 0)[:8]
    own_r[8:16, :] = pltpu.roll(jnp.broadcast_to(proj_new_row, (48, D)), offset, 0)[:8]

    for d in range(1, 4):
        place = fst.at[(mlp + 4 - d) % 4]
        remote(place, place, f8s.at[d - 1], f8r.at[d - 1], along_x(d)).wait_recv()
    fc_sums[0:8, :] = (fst[0] + fst[1]) + (fst[2] + fst[3])
    fc_sums[8:16, :] = fst[mlp]
    vec_three(2)

    for d in range(1, 8):
        place = ast.at[(mlp + 8 - d) % 4 + 4 * (core if d < 4 else 1 - core)]
        remote(place, place, a5s.at[d - 1], a5r.at[d - 1], class_peer(d)).wait_recv()
    total = ast[0]
    for n in range(1, 8):
        total = total + ast[n]
    at_sums[...] = total

    for a in range(GROUPS):
        gin_copy(a).wait()
        out_copy(a).wait()
    fin_copy.wait()
    for copy in pending:
        copy.wait_send()
    for d in range(1, 4):
        fc_two(d).wait_send()


def to_column(row, eye):
    return jnp.sum(jnp.where(eye, row, 0.0), axis=1, keepdims=True)


def block(live_windows, region, tok, og, wq, wp, fc1, fc2, *arrays):
    sd = jax.ShapeDtypeStruct
    vm = pltpu.VMEM
    dma = pltpu.SemaphoreType.DMA
    return pl.pallas_call(
        block_kernel,
        out_shape=[
            sd((TOK, D), F32),
            sd((TOK, D), F32),
            sd((2, 4, 96, D), F32),
            sd((168, D), F32),
        ],
        in_specs=[pl.BlockSpec(memory_space=pltpu.SMEM), pl.BlockSpec(memory_space=vm)]
        + [pl.BlockSpec(memory_space=pl.ANY)] * 6
        + [pl.BlockSpec(memory_space=vm)] * len(arrays),
        out_specs=[pl.BlockSpec(memory_space=pl.ANY)] * 3 + [pl.BlockSpec(memory_space=vm)],
        scratch_shapes=[
            vm((ROWS, D), F32),
            vm((ROWS, D), F32),
            vm((ROWS, 1), F32),
            vm((ROWS, 1), F32),
            vm((ROWS, D), BF16),
            vm((ROWS, D), BF16),
            vm((ROWS, QKV), BF16),
            vm((ROWS, D), BF16),
            vm((GROUPS * PER, SETS, KEYS, LANES), F32),
            vm((ROWS, D), BF16),
            vm((ROWS, FF), BF16),
            vm((ROWS, FF), BF16),
            vm((ROWS, QKV), F32),
            vm((PER, LANES, 128), BF16),
            vm((PER, SETS, KEYS, LANES), F32),
            vm((GROUPS * PER, KEYS, LANES), F32),
            vm((PER, SETS, KEYS, LANES), F32),
            vm((G_ROWS, D), F32),
            vm((G_ROWS, D), F32),
            vm((8, 8, D), F32),
            vm((8, FF), F32),
            vm((D, QKV), BF16),
            vm((D, D), BF16),
            vm((D, FF), BF16),
            vm((FF, D), BF16),
            vm((TOK, D), BF16),
            vm((TOK, D), BF16),
            vm((D, QKV), F32),
            vm((D, D), F32),
            vm((D, D), F32),
            vm((D, D), F32),
            vm((2, 4, 96, D), F32),
            vm((2, 4, 96, D), BF16),
            vm((4, 8, D), F32),
            vm((ROWS, D), F32),
            dma((6,)), dma((7,)),
            vm((2, 4, 4, 96, D), BF16),
            vm((4, 4, 96, D), BF16),
            vm((3, 4, 96, D), BF16),
            vm((4, 96, D), BF16),
            vm((3, 96, D), BF16),
            vm((4, 96, D), BF16),
            vm((4, 8, D), F32),
            vm((4, 2, 4, 48, D), BF16),
            vm((4, 4, 48, D), BF16),
            vm((4, 3, 48, D), BF16),
            vm((4, 4, 48, D), BF16),
            vm((4, 4, 48, D), BF16),
            vm((8, 16, D), F32),
            vm((3, 8, 8, D), F32),
            vm((3, 16, 8, D), F32),
            vm((4, 48, D), F32),
            dma((3, 2)), dma((3, 2)), dma((3,)), dma((3,)), dma((3, 2)), dma((3, 2)),
            dma((4,)), dma((4,)),
            dma((3,)), dma((3,)), dma((3,)), dma((3,)), dma((3,)), dma((3,)),
            dma((3,)), dma((3,)), dma((1,)), dma((1,)), dma((3,)), dma((3,)),
            dma((4,)), dma((4,)),
            dma((4, 3)), dma((4, 3)), dma((4, 3)), dma((4, 3)), dma((4, 3)), dma((4, 3)),
            dma((7,)), dma((7,)),
            dma((3, 7)), dma((3, 7)), dma((3, 15)), dma((3, 15)),
        ],
        compiler_params=pltpu.CompilerParams(
            vmem_limit_bytes=63 * 1024 * 1024, collective_id=0, has_side_effects=True
        ),
        cost_estimate=pl.CostEstimate(flops=14_000_000_000, bytes_accessed=20_000_000, transcendentals=3_000_000),
        name="block",
    )(live_windows, region, tok, og, wq, wp, fc1, fc2, *arrays)


def finish_kernel(
    fin, fc1, fc2, out_from, gin_from, pack, fc1_b, fc1_row, fc2_col, qkv_col, proj_col,
    small, small_state, table, table_state,
    qkv_grad, qkv_row_new, qkv_col_new, qkv_new, qkv_low, proj_grad, proj_row_new, proj_col_new, proj_new, proj_low,
    fc1_grad, fc1_row_new, fc1_col_new, fc1_new, fc1_low, fc2_grad, fc2_row_new, fc2_col_new, fc2_new, fc2_low,
    b1_grad, b1_state_new, b1_new, small_grad, small_state_new, small_new, table_grad, table_state_new, table_new,
    out_to, gin_to, held, sem_in, sem_out,
):
    vec, fc_sums, at_sums, own_g, own_wq, own_wp, b1, own_r = packed(pack)
    def parts(src, dst, n):
        for i in range(4):
            rows = pl.ds(304 * i, 304 if i < 3 else TOK - 912)
            here = held.at[n, rows]
            yield (
                pltpu.make_async_copy(src.at[rows], here, sem_in.at[n, i]),
                pltpu.make_async_copy(here, dst.at[rows], sem_out.at[n, i]),
            )

    copies = list(parts(out_from, out_to, 0)) + list(parts(gin_from, gin_to, 1))
    for copy, _ in copies:
        copy.start()
    mlp = lax.axis_index("mlp")
    eye = iota((D, D), 0) == iota((D, D), 1)
    eye8 = iota((8, 128), 0) == iota((8, 128), 1)

    def line(x):
        return x.reshape(1, -1)

    def total(x):
        return jnp.sum(jnp.sum(x, axis=0, keepdims=True), axis=1, keepdims=True)

    def fresh(old, mean):
        return DECAY * old + (1.0 - DECAY) * (mean + EPS_SQ)

    def owned(grads, cols, over, row, row_total, weight, col_old, rate, outs):
        grad_out, row_out, col_out, new_out, low_out = outs
        width = grads.shape[1]
        col_new = fresh(line(col_old[...]), cols * (1.0 / D))
        mean = row_total * (1.0 / D)
        norm = mean * jnp.sum(over * (1.0 / col_new), axis=1, keepdims=True) * (1.0 / (D * width))
        step = grads * lax.rsqrt(row * col_new * (1.0 / mean))
        new = weight - rate * (step * clip_scale(norm))
        grad_out[...] = grads[:3]
        row_out[...] = jnp.sum(jnp.where(eye8, row, 0.0), axis=0)[:3]
        col_out[...] = col_new.reshape(width)
        new_out[...] = new[:3]
        low_out[...] = new.astype(BF16)[:3]

    def by_part(take):
        return jnp.concatenate([take(g)[:, 128 * p : 128 * p + 128] for p in range(3) for g in range(SETS)], axis=1)

    owned(
        by_part(lambda g: own_g[8 * g : 8 * g + 8, :]), by_part(lambda g: at_sums[g : g + 1, :]),
        by_part(lambda g: at_sums[4 + g : 5 + g, :]), own_r[0:8, :1], at_sums[8:9, :1],
        jnp.concatenate([own_wq[8 * part : 8 * part + 8, :] for part in range(3)], axis=1), qkv_col,
        D ** (-0.5), (qkv_grad, qkv_row_new, qkv_col_new, qkv_new, qkv_low),
    )
    owned(
        own_g[24:32, :], at_sums[3:4, :], at_sums[7:8, :], own_r[8:16, :1], at_sums[9:10, :1], own_wp[...], proj_col,
        (D // 8) ** (-0.5), (proj_grad, proj_row_new, proj_col_new, proj_new, proj_low),
    )

    for copy, then in copies:
        copy.wait()
        then.start()

    def update(grad, weight, row, col, mean, norm, rate, grad_out, new_out, low_out):
        row = row * (1.0 / mean)
        factor = rate * clip_scale(norm)
        for r in range(0, D, 48):
            rows = slice(r, r + 48)
            g = grad[rows, :]
            new = weight[rows, :] - (g * lax.rsqrt(row[rows] * col)) * factor
            grad_out[rows, :] = g
            new_out[rows, :] = new
            low_out[rows, :] = new.astype(BF16)

    row_new = fresh(line(fc1_row[...]), fc_sums[0:1, :] * (1.0 / FF))
    mean = row_mean(row_new)
    norm = mean * row_mean(fc_sums[1:2, :] * (1.0 / row_new)) * (1.0 / FF)
    fc1_row_new[...] = row_new.reshape(D)
    fc1_col_new[...] = fc_sums[13]
    update(
        fin.at[0], fc1, to_column(row_new, eye), fc_sums[13:14, :], mean, norm, D ** (-0.5),
        fc1_grad, fc1_new, fc1_low,
    )
    col_new = fresh(line(fc2_col[...]), fc_sums[2:3, :] * (1.0 / FF))
    mean = fc_sums[4:5, :1] * (1.0 / FF)
    norm = mean * row_mean(fc_sums[3:4, :] * (1.0 / col_new)) * (1.0 / FF)
    fc2_row_new[...] = fc_sums[14]
    fc2_col_new[...] = col_new.reshape(D)
    update(
        fin.at[1], fc2, to_column(fc_sums[14:15, :], eye), col_new, mean, norm, FF ** (-0.5),
        fc2_grad, fc2_new, fc2_low,
    )

    def stepped(grad, old):
        state = fresh(old, grad * grad)
        return state, grad * lax.rsqrt(state)

    norm = jnp.zeros((1, 1), F32)
    for m in range(4):
        d = (m + 4 - mlp) % 4
        step = stepped(vec[4 + m : 5 + m, :], b1[pl.ds(8 * (d + d // 2 - 2 * (d // 3)) + 4, 1), :])[1]
        norm = norm + jnp.sum(step * step, axis=1, keepdims=True)
    grad = vec[pl.ds(4 + mlp, 1), :]
    state, step = stepped(grad, b1[4:5, :])
    b1_grad[...] = grad.reshape(D)
    b1_state_new[...] = state.reshape(D)
    b1_new[...] = (line(fc1_b[...]) - VEC_RATE * (step * clip_scale(norm * (1.0 / FF)))).reshape(D)

    grad = jnp.concatenate([vec[n : n + 1, :] for n in (20, 21, 22, 23, 0, 1, 2, 3)], axis=1)
    state, step = stepped(grad, line(small_state[...]))
    norm = jnp.sum(step * step, axis=1, keepdims=True) * (1.0 / (8 * D))
    small_grad[...] = grad.reshape(8 * D)
    small_state_new[...] = state.reshape(8 * D)
    small_new[...] = (line(small[...]) - VEC_RATE * (step * clip_scale(norm))).reshape(8 * D)

    grad = vec[8:20, :169]
    state, step = stepped(grad, table_state[...])
    norm = total(step * step) * (1.0 / (169 * HEADS))
    table_grad[...] = grad
    table_state_new[...] = state
    table_new[...] = table[...] - VEC_RATE * (step * clip_scale(norm))
    for _, then in copies:
        then.wait()


def finish(*arrays):
    sd = jax.ShapeDtypeStruct
    vm = pltpu.VMEM
    dma = pltpu.SemaphoreType.DMA

    def owned(width):
        return [sd((3, width), F32), sd((3,), F32), sd((width,), F32), sd((3, width), F32), sd((3, width), BF16)]

    shard = [sd((D, D), F32), sd((D,), F32), sd((D,), F32), sd((D, D), F32), sd((D, D), BF16)]
    out_shape = owned(QKV) + owned(D) + shard + shard
    out_shape += [sd((D,), F32)] * 3 + [sd((8 * D,), F32)] * 3 + [sd((HEADS, 169), F32)] * 3 + [sd((TOK, D), F32)] * 2
    return pl.pallas_call(
        finish_kernel,
        out_shape=out_shape,
        in_specs=[pl.BlockSpec(memory_space=vm)] * 3
        + [pl.BlockSpec(memory_space=pl.ANY)] * 2
        + [pl.BlockSpec(memory_space=vm)] * (len(arrays) - 5),
        out_specs=[pl.BlockSpec(memory_space=vm)] * (len(out_shape) - 2) + [pl.BlockSpec(memory_space=pl.ANY)] * 2,
        scratch_shapes=[vm((2, TOK, D), F32), dma((2, 4)), dma((2, 4))],
        compiler_params=pltpu.CompilerParams(vmem_limit_bytes=63 * 1024 * 1024),
        name="finish",
    )(*arrays)


def clip_scale(mean_square):
    return 1.0 / jnp.maximum(1.0, jnp.sqrt(mean_square))


def per_device(
    tokens_in, out_grad, window_live, region_ids, qkv_weight, proj_weight, rel_table, small_params,
    fc1_weight, fc1_bias, fc2_weight, qkv_row, qkv_col, proj_row, proj_col, fc1_row, fc1_col,
    fc2_row, fc2_col, fc1_bias_state, small_state, table_state,
):
    out, gin, fin, pack = block(
        window_live, region_ids, tokens_in, out_grad, qkv_weight, proj_weight, fc1_weight, fc2_weight, rel_table.T,
        small_params, fc1_bias, fc1_bias_state, fc1_col, fc2_row, qkv_row, proj_row,
    )
    *outs, table_grad, table_state_new, table_new, out, gin = finish(
        fin.reshape(2, D, D), fc1_weight, fc2_weight, out, gin, pack, fc1_bias, fc1_row, fc2_col, qkv_col, proj_col,
        small_params, small_state, rel_table.T, table_state.T,
    )
    return (out, gin, *outs, table_grad.T, table_state_new.T, table_new.T)


def solution(mesh):
    tokens, owner = P(("win", "mlp"), None), P(("win", "mlp"))
    whole, part = P(), P("mlp")
    return jax.shard_map(
        per_device,
        mesh=mesh,
        in_specs=(
            tokens, tokens, owner, owner, whole, whole, whole, whole, P(None, "mlp"), part, P("mlp", None),
            whole, whole, whole, whole, whole, part, part, whole, part, whole, whole,
        ),
        out_specs=(
            tokens, tokens,
            tokens, owner, whole, tokens, tokens,
            tokens, owner, whole, tokens, tokens,
            P(None, "mlp"), whole, part, P(None, "mlp"), P(None, "mlp"),
            P("mlp", None), part, whole, P("mlp", None), P("mlp", None),
            part, part, part,
            whole, whole, whole,
            whole, whole, whole,
        ),
        check_vma=False,
    )
```
